32 devices in a mesh: groups: 2 (over y), tensor: 4 (over z), store: 4 (over x, core).
Axes of the slice: x: 2, y: 2, z: 4, core: 2. Of those that a mesh axis runs over, the one named last changes fastest.
Arguments:
- hidden_activations: bfloat16 [2048, 28672], P('groups', 'tensor'), parts along dimension 0, may hold values from -6 to 6
- down_matrix: bfloat16 [28672, 8192], P('tensor', 'store'), may hold values from -0.03125 to 0.03125
- adapter_input_factor: bfloat16 [32, 28672, 128], P(('groups', 'store'), 'tensor'), parts along dimension 0, may hold values from -0.03125 to 0.03125
- adapter_output_factor: bfloat16 [32, 128, 8192], P(('groups', 'store'), 'tensor'), parts along dimension 0, may hold values from -0.5 to 0.5
- token_requests: int32 [2048], P('groups'), parts along dimension 0, may hold values from 0 to 3, never falling along the last dimension, each value on 1 to 512 neighbouring positions
- request_adapters: int32 [8], P('groups'), parts along dimension 0, may hold values from 0 to 15
- adapter_ranks: int32 [32], P('groups'), parts along dimension 0, may hold values from 16 to 128, as said below
- adapter_store_slot: int32 [32], P('groups'), parts along dimension 0, may hold values from 0 to 15, each once
Outputs:
- mixed: bfloat16 [2048, 8192], P(('groups', 'tensor'), 'store'), parts along dimension 0
The draws below stay inside these ranges and needn't reach their ends.
There are 2 independent parts, one for each index of `groups`. The reference program is written for one: setup_inputs(seed, part) draws one part's arguments, and reference() takes and returns one part's arrays. A program takes and returns all parts, laid end to end along the dimension named above; an argument that names none is the same for every part. Nothing has to cross between parts.
Inputs may be any that keep to these rules, and one draw needn't show every extreme that they name: `adapter_ranks`: each rank is 128, 64, 32 or 16; some adapter has rank 128.
All inputs are finite; a program needn't handle non-finite values.
Results may differ from the reference program's by a relative error of at most 0.013.
Values may be sent and summed in bfloat16 or wider, within the bound.
No kernel may reach another device: no remote copies, remote signals or barrier semaphores. Data moves between devices by JAX's collectives and lax.ppermute only.
A program may use at most 192 MiB of HBM per device.

```python
import math
import jax
import jax.numpy as jnp
import numpy as np
from jax import lax

MODEL_WIDTH = 8192
HIDDEN_UNITS = 28672
LARGEST_RANK = 128
SPAN_TOKENS = 1024
REQUEST_COUNT = 4
REQUEST_TOKENS = 512
ADAPTER_COUNT = 16
FBLK = 7168
RANK_BLOCK_ROWS = 32
N_TENSOR = 4


def draw_adapter_ranks(key, part):
    key = jax.random.fold_in(key, 11)
    halving_key, pick_key = jax.random.split(key)
    halvings = jax.random.randint(halving_key, (ADAPTER_COUNT,), 0, 4)
    rank_values = jnp.int32(LARGEST_RANK) // 2 ** halvings
    chosen = jax.random.randint(pick_key, (), 0, ADAPTER_COUNT)
    return jnp.where(jnp.arange(ADAPTER_COUNT) == chosen, LARGEST_RANK, rank_values).astype(jnp.int32)


def place_ends(values, stream_key, least, top_value):
    dims = values.shape
    spot = [jax.random.randint(jax.random.fold_in(stream_key, axis), (), 0, dims[axis]) for axis in range(len(dims))]
    values = values.at[tuple(spot)].set(least)
    longest = dims.index(max(dims))
    spot[longest] = (spot[longest] + 1) % dims[longest]
    return values.at[tuple(spot)].set(top_value)


def spiked(drawn, own_key, source, target, blocks, factor):
    def block_of(position):
        return (jnp.arange(drawn.shape[position]) // (drawn.shape[position] // blocks)).reshape((-1,) + (1,) * (drawn.ndim - 1 - position))

    one_side = jax.random.permutation(own_key, blocks)[block_of(target)]
    second = (block_of(target) + blocks // 2) % blocks
    return jnp.where((block_of(source) == one_side) | (block_of(source) == second), factor * drawn, drawn)


def levels(stream_key, shape, cuts, low, largest):
    level = 1.0
    for position, parts in cuts:
        heights = jax.random.uniform(jax.random.fold_in(jax.random.fold_in(stream_key, 6), position), (parts,), jnp.float32, low / len(cuts), largest / len(cuts))
        level = level * jnp.repeat(jnp.exp(heights), shape[position] // parts).reshape((-1,) + (1,) * (len(shape) - 1 - position))
    return level


def rank_bounds(count, lean):
    weights = [(1 << 20) // math.isqrt(grade ** lean) + 1 for grade in range(1, count + 1)]
    scale = 1 + sum(weights) // (1 << 30)
    return np.cumsum(np.array([max(1, weight // scale) for weight in weights]))


def ranked_ids(rng, extent, count, slope):
    table = rank_bounds(count, slope)
    pick = jax.random.randint(jax.random.fold_in(rng, 1), extent, 0, int(table[count - 1]))
    rank = jnp.searchsorted(jnp.asarray(table, jnp.int32), pick, side="right")
    return jax.random.permutation(jax.random.fold_in(rng, 2), count)[rank].astype(jnp.int32)


def length_profile(amount, total, limit, skew):
    weights = [(1 << 20) // math.isqrt(grade ** skew) + 1 for grade in range(2, amount + 1)]
    rest, holding = total - limit - (amount - 1), [1] * (amount - 1)
    while rest > 0:
        free = [i for i in range(amount - 1) if holding[i] < limit]
        whole, remaining = sum([weights[i] for i in free]), rest
        for i in free:
            extra = min(limit - holding[i], max(1, remaining * weights[i] // whole), rest)
            holding[i] = holding[i] + extra
            rest = rest - extra
    return np.array([limit] + holding)


def uneven(rng, number_of, total, bound, lean):
    if number_of == 2:
        one = jax.random.randint(rng, (), max(1, total - bound), min(bound, total - 1) + 1)
        return jnp.stack([one, total - one])
    sizes = jnp.asarray(length_profile(number_of, total, bound, lean), jnp.int32)
    couples = (number_of - 1) // 2
    giver, taker = sizes[1:1 + 2 * couples:2], sizes[2:2 + 2 * couples:2]
    room = jnp.minimum(giver - 1, bound - taker)
    shifted = jax.random.randint(jax.random.fold_in(rng, 1), (couples,), 0, 1 << 20) % (room + 1)
    sizes = sizes.at[1:1 + 2 * couples:2].set(giver - shifted).at[2:2 + 2 * couples:2].set(taker + shifted)
    return sizes[jax.random.permutation(jax.random.fold_in(rng, 2), number_of)]


def gaussian(rng, shape, deviation, bound, shards=(), held_as=jnp.bfloat16):
    loudness = levels(rng, shape, shards, -0.22, 0.18) if shards else 1.0
    entries = jax.random.normal(rng, shape, jnp.float32) * deviation * loudness
    return jnp.minimum(jnp.maximum(entries, -bound), bound).astype(held_as)


def gaussian_with(key, dims, deviation, most, shards, heavy, kind=jnp.bfloat16):
    values = deviation * jax.random.normal(key, dims, jnp.float32)
    if shards:
        values = values * levels(key, dims, shards, -0.22, 0.18)
    return jnp.clip(spiked(values, jax.random.fold_in(key, 3), *heavy), -most, most).astype(kind)


def setup_inputs(seed: int = 0, part: int = 0) -> dict:
    key_list = jax.random.split(jax.random.key(seed), 9)
    part_keys = jax.random.split(jax.random.fold_in(key_list[8], part), 9)
    return {
        "hidden_activations": gaussian_with(part_keys[0], (SPAN_TOKENS, HIDDEN_UNITS), 1.0, 6.0, ((1, 4),), (1, 0, 4, 2.0)),
        "down_matrix": gaussian(key_list[1], (HIDDEN_UNITS, MODEL_WIDTH), HIDDEN_UNITS ** -0.5, 0.03125, ((0, 4), (1, 4))),
        "adapter_input_factor": gaussian(part_keys[2], (ADAPTER_COUNT, HIDDEN_UNITS, LARGEST_RANK), HIDDEN_UNITS ** -0.5, 0.03125, ((0, 4), (1, 4))),
        "adapter_output_factor": gaussian(part_keys[3], (ADAPTER_COUNT, LARGEST_RANK, MODEL_WIDTH), LARGEST_RANK ** -0.5, 0.5, ((0, 4), (1, 4))),
        "token_requests": jnp.searchsorted(jnp.cumsum(uneven(part_keys[4], REQUEST_COUNT, SPAN_TOKENS, REQUEST_TOKENS, 1)), jnp.arange(SPAN_TOKENS), side="right").astype(jnp.int32),
        "request_adapters": place_ends(ranked_ids(part_keys[5], (REQUEST_COUNT,), ADAPTER_COUNT, 2), jax.random.fold_in(part_keys[5], 3), 0, ADAPTER_COUNT - 1).astype(jnp.int32),
        "adapter_ranks": draw_adapter_ranks(jax.random.fold_in(jax.random.fold_in(key_list[8], part), 71), part),
        "adapter_store_slot": jax.random.permutation(part_keys[7], ADAPTER_COUNT).astype(jnp.int32),
    }


def reference(hidden_activations, down_matrix, adapter_input_factor, adapter_output_factor, token_requests, request_adapters, adapter_ranks, adapter_store_slot):
    request_adapter_rank = adapter_ranks[request_adapters]
    request_store_slot = adapter_store_slot[request_adapters]
    adapter_scale = (0.25 * LARGEST_RANK) / request_adapter_rank.astype(jnp.float32)
    request_numbers = jnp.arange(REQUEST_COUNT, dtype=jnp.int32)
    first_token = jnp.sum((token_requests[None, :] < request_numbers[:, None]).astype(jnp.int32), axis=1)
    window_start = jnp.minimum(first_token, SPAN_TOKENS - REQUEST_TOKENS).astype(jnp.int32)
    columns = jnp.arange(LARGEST_RANK, dtype=jnp.int32)

    def accumulate_request(adapter_input_product, request_number):
        first_row = window_start[request_number]
        window_rows = lax.dynamic_slice_in_dim(hidden_activations, first_row, REQUEST_TOKENS, 0)
        adapter_row_block = adapter_input_factor[request_store_slot[request_number]]
        product = jnp.dot(window_rows, adapter_row_block, preferred_element_type=jnp.float32)
        window_ids = lax.dynamic_slice_in_dim(token_requests, first_row, REQUEST_TOKENS, 0)
        keep_mask = (window_ids == request_number)[:, None] & (columns < request_adapter_rank[request_number])[None, :]
        current_output = lax.dynamic_slice_in_dim(adapter_input_product, first_row, REQUEST_TOKENS, 0)
        updated_output = current_output + jnp.where(keep_mask, product, jnp.zeros_like(product))
        return lax.dynamic_update_slice_in_dim(adapter_input_product, updated_output, first_row, 0), None

    adapter_input_product, unused_value = lax.scan(accumulate_request, jnp.zeros((SPAN_TOKENS, LARGEST_RANK), jnp.float32), request_numbers)
    weight_matrices = jnp.where(token_requests[:, None] == request_numbers[None, :], adapter_scale[None, :], jnp.zeros((), jnp.float32))
    selected_output_factor = adapter_output_factor[request_store_slot]

    def block_term(total, rank_block_count):
        hidden_block = lax.dynamic_slice_in_dim(hidden_activations, rank_block_count * FBLK, FBLK, 1)
        weight_block = lax.dynamic_slice_in_dim(down_matrix, rank_block_count * FBLK, FBLK, 0)
        base_product = jnp.dot(hidden_block, weight_block, preferred_element_type=jnp.float32)
        adapter_block_term = lax.dynamic_slice_in_dim(adapter_input_product, rank_block_count * RANK_BLOCK_ROWS, RANK_BLOCK_ROWS, 1)
        expanded_rows = (weight_matrices[:, :, None] * adapter_block_term[:, None, :]).reshape(SPAN_TOKENS, REQUEST_COUNT * RANK_BLOCK_ROWS)
        output_factor_block = lax.dynamic_slice_in_dim(selected_output_factor, rank_block_count * RANK_BLOCK_ROWS, RANK_BLOCK_ROWS, 1).astype(jnp.float32).reshape(REQUEST_COUNT * RANK_BLOCK_ROWS, MODEL_WIDTH)
        adapter_product = jnp.dot(expanded_rows, output_factor_block, precision=lax.Precision.HIGHEST, preferred_element_type=jnp.float32)
        rounded_rank = lax.optimization_barrier((base_product + adapter_product).astype(jnp.bfloat16))
        return total + rounded_rank.astype(jnp.float32), None

    block_ids = jnp.arange(N_TENSOR, dtype=jnp.int32)
    summed, unused_value = lax.scan(block_term, jnp.zeros((SPAN_TOKENS, MODEL_WIDTH), jnp.float32), block_ids)
    return summed.astype(jnp.bfloat16)
```

```python
import functools

import jax
import jax.numpy as jnp
import numpy as np
from jax import lax
from jax.experimental import pallas as pl
from jax.experimental.pallas import tpu as pltpu
from jax.sharding import PartitionSpec as P

CHUNKS = 4


def line_order(n):
    order = []
    for z in range(n):
        sends = [(t, z >= n // 2, n - 1 - t + z) for t in range(z, n - 1)]
        sends += [(t, z < n // 2, t - (n - 1 - z)) for t in range(n - 1 - z, n - 1)]
        order.append([block for _, _, block in sorted(sends)] + [z])
    return order


def first_divisor(size, choices):
    for choice in choices:
        if size % choice == 0:
            return choice
    return size


def adapter_input_kernel(
    shard_ref, request_adapters_ref, ranks_ref, slots_ref, requests_ref, hidden_ref, factor_ref, out_ref, sums_ref
):
    step = pl.program_id(0)
    held, _, width = factor_ref.shape
    factors = jnp.concatenate([factor_ref[s] for s in range(held)], axis=1)
    product = jnp.dot(hidden_ref[...], factors, preferred_element_type=jnp.float32)

    @pl.when(step == 0)
    def _():
        for s in range(held):
            sums_ref[s] = product[:, s * width : (s + 1) * width]

    @pl.when(step > 0)
    def _():
        for s in range(held):
            sums_ref[s] += product[:, s * width : (s + 1) * width]

    @pl.when(step == pl.num_programs(0) - 1)
    def _():
        requests = requests_ref[...]
        row = lax.broadcasted_iota(jnp.int32, out_ref.shape, 0)
        column = lax.broadcasted_iota(jnp.int32, out_ref.shape, 1)
        total = jnp.zeros(out_ref.shape, jnp.float32)
        for r in range(request_adapters_ref.shape[0]):
            adapter = request_adapters_ref[r]
            local_slot = slots_ref[adapter] - shard_ref[0] * held
            owned = (local_slot >= 0) & (local_slot < held)
            start = jnp.sum((requests < r).astype(jnp.int32))
            end = jnp.where(owned, jnp.sum((requests <= r).astype(jnp.int32)), 0)
            keep = (row >= start) & (row < end) & (column < ranks_ref[adapter])
            total = jnp.where(keep, sums_ref[jnp.clip(local_slot, 0, held - 1)], total)
        out_ref[...] = total.astype(out_ref.dtype)


def adapter_input(hidden, factor, token_requests, request_adapters, ranks, slots, shard):
    tokens, depth = hidden.shape
    held, _, width = factor.shape
    tile = first_divisor(depth, (1024, 896, 512, 256, 128))
    smem = pl.BlockSpec(memory_space=pltpu.SMEM)
    return pl.pallas_call(
        adapter_input_kernel,
        out_shape=jax.ShapeDtypeStruct((tokens, width), jnp.bfloat16),
        grid=(depth // tile,),
        in_specs=[
            smem,
            smem,
            smem,
            smem,
            pl.BlockSpec((tokens // 128, 128), lambda k: (0, 0)),
            pl.BlockSpec((tokens, tile), lambda k: (0, k)),
            pl.BlockSpec((held, tile, width), lambda k: (0, k, 0)),
        ],
        out_specs=pl.BlockSpec((tokens, width), lambda k: (0, 0)),
        scratch_shapes=[pltpu.VMEM((held, tokens, width), jnp.float32)],
        compiler_params=pltpu.CompilerParams(vmem_limit_bytes=24 * 1024 * 1024),
        cost_estimate=pl.CostEstimate(
            flops=2 * tokens * depth * held * width,
            bytes_accessed=2 * depth * (tokens + held * width),
            transcendentals=0,
        ),
        name="adapter_input",
    )(shard[None], request_adapters, ranks, slots, token_requests.reshape(tokens // 128, 128), hidden, factor)


def swap(x, axis, bit):
    return lax.ppermute(x, axis, [(i, i ^ bit) for i in range(lax.axis_size(axis))])


def bits_of(size):
    return [1 << i for i in range(size.bit_length() - 1)]


def sum_to_shards(x, axis, dim):
    me = lax.axis_index(axis)
    for bit in bits_of(lax.axis_size(axis)):
        shape = x.shape
        x = x.reshape(shape[:dim] + (shape[dim] // 2, 2) + shape[dim + 1 :])
        side = (me // bit) % 2
        kept = lax.dynamic_index_in_dim(x, side, dim + 1, keepdims=False)
        sent = lax.dynamic_index_in_dim(x, 1 - side, dim + 1, keepdims=False)
        x = kept + swap(sent, axis, bit)
    return lax.squeeze(x, (dim,))


def gather_shards(x, axis, dim):
    me = lax.axis_index(axis)
    x = jnp.expand_dims(x, dim)
    for bit in reversed(bits_of(lax.axis_size(axis))):
        other = swap(x, axis, bit)
        high = (me // bit) % 2 == 1
        pair = jnp.where(high, jnp.stack([other, x], dim + 1), jnp.stack([x, other], dim + 1))
        x = pair.reshape(pair.shape[:dim] + (-1,) + pair.shape[dim + 2 :])
    return x


def sum_to_blocks(x, axis):
    n = lax.axis_size(axis)
    me = lax.axis_index(axis)
    total = lax.dynamic_index_in_dim(x, me, 0, keepdims=False).astype(jnp.float32)
    for shift in range(1, n):
        sent = lax.dynamic_index_in_dim(x, (me + shift) % n, 0, keepdims=False)
        total += lax.ppermute(sent, axis, [(i, (i + shift) % n) for i in range(n)]).astype(jnp.float32)
    return total.astype(x.dtype)


def gather_along_line(x, axis):
    n = lax.axis_size(axis)
    up, down = [x], [x]
    for j in range(1, n):
        up.append(lax.ppermute(up[-1], axis, [(i, i + 1) for i in range(j - 1, n - 1)]))
        down.append(lax.ppermute(down[-1], axis, [(i, i - 1) for i in range(n - j, 0, -1)]))
    return [x] + [up[j] + down[n - j] for j in range(1, n)]


def per_device(
    hidden_activations,
    down_matrix,
    adapter_input_factor,
    adapter_output_factor,
    token_requests,
    request_adapters,
    adapter_ranks,
    adapter_store_slot,
):
    n = lax.axis_size("tensor")
    place = lax.axis_index("tensor")
    shards = lax.axis_size("store")
    shard = lax.axis_index("store")
    tokens = hidden_activations.shape[0]
    block = tokens // n
    held, rank_rows, model_width = adapter_output_factor.shape
    width = down_matrix.shape[1]
    requests = request_adapters.shape[0]
    order = line_order(n)
    my_blocks = jnp.asarray(np.array(order, np.int32))[place]

    def slot_rows(s):
        return lax.dynamic_slice_in_dim(hidden_activations, my_blocks[s] * block, block, 0)

    def base_terms(matrix):
        return [
            lax.optimization_barrier(
                jnp.dot(slot_rows(s), matrix, preferred_element_type=jnp.float32).astype(jnp.bfloat16)
            )
            for s in range(n)
        ]

    chunk = width // CHUNKS
    first = base_terms(down_matrix[:, :chunk])
    later_matrix, factor, _ = lax.optimization_barrier((down_matrix, adapter_input_factor, first[n - 2]))

    partial = adapter_input(
        hidden_activations, factor, token_requests, request_adapters, adapter_ranks, adapter_store_slot, shard
    )
    later_matrix, partial = lax.optimization_barrier((later_matrix, partial))
    piece = tokens // (n * shards)
    pieces = sum_to_shards(partial.reshape(n, shards, piece, -1), "store", 1)
    lora = gather_shards(sum_to_blocks(pieces, "tensor"), "store", 0).reshape(block, -1)

    slot_of = adapter_store_slot[request_adapters]
    rank_of = adapter_ranks[request_adapters]
    offered = jnp.where(
        (slot_of // held == shard)[:, None, None], adapter_output_factor[slot_of % held], jnp.bfloat16(0)
    )
    rows = sum_to_shards(offered.reshape(requests * rank_rows, shards, width), "store", 1)
    rows = jnp.concatenate(gather_along_line(rows, "tensor"), axis=0)

    scale = 0.25 * lora.shape[1] / rank_of.astype(jnp.float32)
    my_requests = lax.dynamic_slice_in_dim(token_requests, place * block, block, 0)
    weights = jnp.where(my_requests[:, None] == jnp.arange(requests)[None, :], scale[None, :], 0.0)
    expanded = jnp.concatenate(
        [
            (
                weights[:, :, None]
                * lax.dynamic_slice_in_dim(lora, (place - j) % n * rank_rows, rank_rows, 1)[:, None, :]
            ).reshape(block, requests * rank_rows)
            for j in range(n)
        ],
        axis=1,
    ).astype(jnp.bfloat16)

    outputs = []
    for c in range(CHUNKS):
        columns = slice(c * chunk, (c + 1) * chunk)
        terms = first if c == 0 else base_terms(later_matrix[:, columns])
        arrived = {}
        for t in range(n - 1):
            for j in range(t + 1):
                sent = terms[order[j].index(n - 1 - t + j)]
                if j > 0:
                    sent = sent.astype(jnp.float32) + arrived[j - 1, t - 1].astype(jnp.float32)
                arrived[j, t] = lax.ppermute(
                    sent.astype(jnp.bfloat16), "tensor", [(j, j + 1), (n - 1 - j, n - 2 - j)]
                )
        total = jnp.dot(expanded, rows[:, columns], preferred_element_type=jnp.float32)
        total = lax.optimization_barrier(total + terms[n - 1].astype(jnp.float32))
        for j in range(n - 1):
            total += arrived[j, n - 2].astype(jnp.float32)
        outputs.append(total.astype(jnp.bfloat16))
    return jnp.concatenate(outputs, axis=1)


def solution(mesh):
    in_specs = (
        P("groups", "tensor"),
        P("tensor", "store"),
        P(("groups", "store"), "tensor", None),
        P(("groups", "store"), "tensor", None),
        P("groups"),
        P("groups"),
        P("groups"),
        P("groups"),
    )
    out_specs = P(("groups", "tensor"), "store")
    return jax.shard_map(
        per_device, mesh=mesh, in_specs=in_specs, out_specs=out_specs, check_vma=False
    )
```

```python
import jax
import jax.numpy as jnp
from jax import lax
from jax.experimental import pallas as pl
from jax.experimental.pallas import tpu as pltpu
from jax.sharding import PartitionSpec as P

VMEM_LIMIT = 52 * 1024 * 1024
LINE = 4


def line_order(n):
    order = []
    for z in range(n):
        sends = [(t, z >= n // 2, n - 1 - t + z) for t in range(z, n - 1)]
        sends += [(t, z < n // 2, t - (n - 1 - z)) for t in range(n - 1 - z, n - 1)]
        order.append([block for _, _, block in sorted(sends)] + [z])
    return order


def first_divisor(size, choices):
    for choice in choices:
        if size % choice == 0:
            return choice
    return size


def after(token, *done):
    return lax.optimization_barrier((token,) + done)[0]


def params():
    return pltpu.CompilerParams(vmem_limit_bytes=VMEM_LIMIT)


def base_kernel(count, place_ref, *refs):
    hidden, matrix, outs, sums = refs[:count], refs[count], refs[count + 1 : -1], refs[-1]
    step = pl.program_id(0)
    rows = jnp.concatenate([ref[...] for ref in hidden], axis=0) if count > 1 else hidden[0][...]
    product = jnp.dot(rows, matrix[...], preferred_element_type=jnp.float32)

    @pl.when(step == 0)
    def _():
        sums[...] = product

    @pl.when(step > 0)
    def _():
        sums[...] += product

    @pl.when(step == pl.num_programs(0) - 1)
    def _():
        block = outs[0].shape[0]
        for i in range(count):
            outs[i][...] = sums[pl.ds(i * block, block), :].astype(outs[i].dtype)


def base_terms(place, hidden, matrix, slots, half, n, halves):
    tokens, depth = hidden.shape
    block, columns = tokens // n, matrix.shape[1] // halves
    tile = first_divisor(depth, (512, 256, 128))
    order = line_order(n)

    def rows_of(slot):
        def index(k, place_ref):
            picked = jnp.int32(order[0][slot])
            for z in range(1, n):
                picked = jnp.where(place_ref[0] == z, order[z][slot], picked)
            return picked, k

        return pl.BlockSpec((block, tile), index)

    count = len(slots)
    return pl.pallas_call(
        lambda *refs: base_kernel(count, *refs),
        out_shape=[jax.ShapeDtypeStruct((block, columns), jnp.bfloat16)] * count,
        grid_spec=pltpu.PrefetchScalarGridSpec(
            num_scalar_prefetch=1,
            grid=(depth // tile,),
            in_specs=[rows_of(slot) for slot in slots] + [pl.BlockSpec((tile, columns), lambda k, _: (k, half))],
            out_specs=[pl.BlockSpec((block, columns), lambda k, _: (0, 0))] * count,
            scratch_shapes=[pltpu.VMEM((count * block, columns), jnp.float32)],
        ),
        compiler_params=params(),
        cost_estimate=pl.CostEstimate(flops=10**6, bytes_accessed=10**5, transcendentals=0),
        name="base_terms",
    )(place, *([hidden] * count), matrix)


def spans(requests_ref, r):
    requests = requests_ref[...]
    return jnp.sum((requests < r).astype(jnp.int32)), jnp.sum((requests <= r).astype(jnp.int32))


def adapter_input_kernel(
    place_ref, request_adapters_ref, ranks_ref, slots_ref, requests_ref, hidden_ref, factor_ref, out_ref, sums_ref
):
    step = pl.program_id(0)
    held, _, width = factor_ref.shape
    factors = jnp.concatenate([factor_ref[s] for s in range(held)], axis=1)
    product = jnp.dot(hidden_ref[...], factors, preferred_element_type=jnp.float32)

    @pl.when(step == 0)
    def _():
        sums_ref[...] = product

    @pl.when(step > 0)
    def _():
        sums_ref[...] += product

    @pl.when(step == pl.num_programs(0) - 1)
    def _():
        row = lax.broadcasted_iota(jnp.int32, out_ref.shape, 0)
        column = lax.broadcasted_iota(jnp.int32, out_ref.shape, 1)
        total = jnp.zeros(out_ref.shape, jnp.float32)
        for r in range(request_adapters_ref.shape[0]):
            adapter = request_adapters_ref[r]
            local_slot = slots_ref[adapter] - place_ref[1] * held
            owned = (local_slot >= 0) & (local_slot < held)
            start, end = spans(requests_ref, r)
            keep = (row >= start) & (row < jnp.where(owned, end, 0)) & (column < ranks_ref[adapter])
            lane = pl.multiple_of(jnp.clip(local_slot, 0, held - 1) * width, width)
            total = jnp.where(keep, sums_ref[:, pl.ds(lane, width)], total)
        out_ref[...] = total.astype(out_ref.dtype)


def adapter_input(place, hidden, factor, token_requests, request_adapters, ranks, slots):
    tokens, depth = hidden.shape
    held, _, width = factor.shape
    tile = first_divisor(depth, (1024, 896, 512, 256, 128))
    smem = pl.BlockSpec(memory_space=pltpu.SMEM)
    return pl.pallas_call(
        adapter_input_kernel,
        out_shape=jax.ShapeDtypeStruct((tokens, width), jnp.bfloat16),
        grid=(depth // tile,),
        in_specs=[
            smem,
            smem,
            smem,
            smem,
            pl.BlockSpec((tokens // 128, 128), lambda k: (0, 0)),
            pl.BlockSpec((tokens, tile), lambda k: (0, k)),
            pl.BlockSpec((held, tile, width), lambda k: (0, k, 0)),
        ],
        out_specs=pl.BlockSpec((tokens, width), lambda k: (0, 0)),
        scratch_shapes=[pltpu.VMEM((tokens, held * width), jnp.float32)],
        compiler_params=params(),
        cost_estimate=pl.CostEstimate(flops=10**6, bytes_accessed=10**5, transcendentals=0),
        name="adapter_input",
    )(place, request_adapters, ranks, slots, token_requests.reshape(tokens // 128, 128), hidden, factor)


def select_rows_kernel(place_ref, request_adapters_ref, slots_ref, kept_in, sent_in, kept_out, sent_out):
    slot = slots_ref[request_adapters_ref[pl.program_id(0)]] - place_ref[1] * place_ref[2]
    owned = (slot >= 0) & (slot < place_ref[2])
    zero = jnp.zeros(kept_out.shape, kept_out.dtype)
    kept_out[...] = jnp.where(owned, kept_in[...], zero)
    sent_out[...] = jnp.where(owned, sent_in[...], zero)


def select_rows(place, factor, request_adapters, slots, shards):
    held, rank_rows, model_width = factor.shape
    requests, width = request_adapters.shape[0], model_width // shards

    def columns_of(other):
        def index(r, i, place_ref, request_adapters_ref, slots_ref):
            slot = slots_ref[request_adapters_ref[r]] - place_ref[1] * held
            side = place_ref[1] % 2
            return jnp.clip(slot, 0, held - 1), 0, 2 * i + (1 - side if other else side)

        return pl.BlockSpec((1, rank_rows, width), index)

    out = jax.ShapeDtypeStruct((requests, rank_rows, shards // 2 * width), factor.dtype)
    return pl.pallas_call(
        select_rows_kernel,
        out_shape=[out, out],
        grid_spec=pltpu.PrefetchScalarGridSpec(
            num_scalar_prefetch=3,
            grid=(requests, shards // 2),
            in_specs=[columns_of(False), columns_of(True)],
            out_specs=[pl.BlockSpec((1, rank_rows, width), lambda r, i, *_: (r, 0, i))] * 2,
        ),
        compiler_params=params(),
        cost_estimate=pl.CostEstimate(flops=10**6, bytes_accessed=10**5, transcendentals=0),
        name="select_rows",
    )(place, request_adapters, slots, factor, factor)


def adapter_term_kernel(
    place_ref, request_adapters_ref, ranks_ref, requests_ref, lora_ref, rows_ref, out_ref
):
    block, width = lora_ref.shape
    row = lax.broadcasted_iota(jnp.int32, (block, width), 0) + place_ref[0] * block
    lora = lora_ref[...].astype(jnp.float32)
    parts = []
    for r in range(request_adapters_ref.shape[0]):
        start, end = spans(requests_ref, r)
        scale = 0.25 * width / ranks_ref[request_adapters_ref[r]].astype(jnp.float32)
        parts.append(jnp.where((row >= start) & (row < end), lora * scale, 0.0).astype(jnp.bfloat16))
    expanded = jnp.concatenate(parts, axis=1)
    out_ref[...] = jnp.dot(expanded, rows_ref[...], preferred_element_type=jnp.float32)


def adapter_term(place, lora, rows, token_requests, request_adapters, ranks):
    block, width = lora.shape
    depth, columns = rows.shape
    tokens = token_requests.shape[0]
    tile = first_divisor(columns, (512, 256, 128))
    smem = pl.BlockSpec(memory_space=pltpu.SMEM)
    return pl.pallas_call(
        adapter_term_kernel,
        out_shape=jax.ShapeDtypeStruct((block, columns), jnp.float32),
        grid=(columns // tile,),
        in_specs=[
            smem,
            smem,
            smem,
            pl.BlockSpec((tokens // 128, 128), lambda j: (0, 0)),
            pl.BlockSpec((block, width), lambda j: (0, 0)),
            pl.BlockSpec((depth, tile), lambda j: (0, j)),
        ],
        out_specs=pl.BlockSpec((block, tile), lambda j: (0, j)),
        compiler_params=params(),
        cost_estimate=pl.CostEstimate(flops=10**6, bytes_accessed=10**5, transcendentals=0),
        name="adapter_term",
    )(place, request_adapters, ranks, token_requests.reshape(tokens // 128, 128), lora, rows)


def swap(x, axis, bit):
    return lax.ppermute(x, axis, [(i, i ^ bit) for i in range(lax.axis_size(axis))])


def bits_of(size):
    return [1 << i for i in range(size.bit_length() - 1)]


def along_edge(x, edge):
    n = lax.axis_size("tensor")
    return lax.ppermute(x, "tensor", [(edge, edge + 1), (n - 1 - edge, n - 2 - edge)])


def sum_halves(x, dim, axis, bit):
    side = (lax.axis_index(axis) // bit) % 2
    size = x.shape[dim] // 2
    kept = lax.dynamic_slice_in_dim(x, side * size, size, dim)
    sent = lax.dynamic_slice_in_dim(x, (1 - side) * size, size, dim)
    return kept + swap(sent, axis, bit)


def join_halves(x, dim, axis, bit):
    other = swap(x, axis, bit)
    high = (lax.axis_index(axis) // bit) % 2 == 1
    return jnp.where(high, jnp.concatenate([other, x], dim), jnp.concatenate([x, other], dim))


def sum_to_blocks(x, axis):
    n = lax.axis_size(axis)
    me = lax.axis_index(axis)
    total = lax.dynamic_index_in_dim(x, me, 0, keepdims=False).astype(jnp.float32)
    for shift in range(1, n):
        sent = lax.dynamic_index_in_dim(x, (me + shift) % n, 0, keepdims=False)
        total += lax.ppermute(sent, axis, [(i, (i + shift) % n) for i in range(n)]).astype(jnp.float32)
    return total.astype(x.dtype)


def place_rows(own, received, place, n):
    full = [jnp.where(place == k, own, jnp.zeros_like(own)) for k in range(n)]
    for j, items in enumerate(received):
        for i in range(j + 1):
            zero = jnp.zeros_like(items[i])
            full[i] += jnp.where(place == j + 1, items[i], zero)
            full[n - 1 - i] += jnp.where(place == n - 2 - j, items[i], zero)
    return jnp.stack(full, axis=1)


def per_device(
    hidden_activations,
    down_matrix,
    adapter_input_factor,
    adapter_output_factor,
    token_requests,
    request_adapters,
    adapter_ranks,
    adapter_store_slot,
):
    n = lax.axis_size("tensor")
    z = lax.axis_index("tensor")
    shards = lax.axis_size("store")
    tokens = hidden_activations.shape[0]
    block = tokens // n
    held, rank_rows, model_width = adapter_output_factor.shape
    width = down_matrix.shape[1]
    requests = request_adapters.shape[0]
    lora_width = adapter_input_factor.shape[2]
    order = line_order(n)
    token = jnp.stack([z, lax.axis_index("store"), jnp.int32(held)]).astype(jnp.int32)
    on_line = n == LINE

    def base(token, slots, half):
        return base_terms(token, hidden_activations, down_matrix, slots, half, n, 2)

    def hop(token, term, came):
        term, came, _ = lax.optimization_barrier((term, came, token))
        return (term.astype(jnp.float32) + came.astype(jnp.float32)).astype(jnp.bfloat16)

    def input_product(token):
        return adapter_input(
            token,
            hidden_activations,
            adapter_input_factor,
            token_requests,
            request_adapters,
            adapter_ranks,
            adapter_store_slot,
        )

    store_bits = bits_of(shards)
    came, terms = {}, {}

    if on_line:
        terms[0, 0], = base(token, [0], 0)
        token = after(token, terms[0, 0])
        came[0, 0, 0] = along_edge(terms[0, 0], 0)
        terms[0, 1], terms[1, 1] = base(token, [0, 1], 1)
        token = after(token, terms[0, 1])
        came[0, 0, 1] = along_edge(terms[0, 1], 0)

    kept, sent = select_rows(token, adapter_output_factor, request_adapters, adapter_store_slot, shards)
    token = after(token, kept, sent)
    swapped = swap(sent, "store", 1)

    if on_line:
        sum_b10 = hop(token, terms[0, 0], came[0, 0, 0])
        token = after(token, sum_b10)
        came[1, 1, 0] = along_edge(sum_b10, 1)
        came[0, 1, 1] = along_edge(after(terms[1, 1], token), 0)

        terms[1, 0], terms[2, 0], terms[3, 0] = base(token, [1, 2, 3], 0)
        token = after(token, terms[1, 0])
        came[0, 1, 0] = along_edge(terms[1, 0], 0)

        sum_b11 = hop(token, terms[0, 1], came[0, 0, 1])
        token = after(token, sum_b11)
        came[1, 1, 1] = along_edge(sum_b11, 1)

    rows = kept + swapped
    for bit in reversed(store_bits[1:]):
        rows = sum_halves(rows, 2, "store", bit)

    partial = input_product(token)
    token = after(token, partial)
    piece = tokens // (n * shards)
    pieces = partial.reshape(n, tokens // n, lora_width)
    pieces = sum_halves(pieces, 1, "store", store_bits[0])

    if on_line:
        sum_c20 = hop(token, terms[2, 0], came[1, 1, 0])
        token = after(token, sum_c20)
        came[2, 2, 0] = along_edge(sum_c20, 2)
        came[0, 2, 0] = along_edge(after(terms[2, 0], token), 0)

        sum_b21 = hop(token, terms[1, 1], came[0, 1, 1])
        token = after(token, sum_b21)
        came[1, 2, 1] = along_edge(sum_b21, 1)

    token, rows, pieces = lax.optimization_barrier((token, rows, pieces))
    received = []
    bundle = rows[None]
    for edge in range(n - 1):
        received.append(along_edge(bundle, edge))
        bundle = jnp.concatenate([received[-1], rows[None]], axis=0)
    for bit in store_bits[1:]:
        pieces = sum_halves(pieces, 1, "store", bit)

    if on_line:
        terms[2, 1], terms[3, 1] = base(token, [2, 3], 1)
        token, pieces = lax.optimization_barrier((token, pieces, terms[2, 1]))[:2]

        sum_c21 = hop(token, terms[2, 1], came[1, 1, 1])
        token = after(token, sum_c21)
        came[2, 2, 1] = along_edge(sum_c21, 2)
        sum_b20 = hop(token, terms[1, 0], came[0, 1, 0])
        token = after(token, sum_b20)
        came[1, 2, 0] = along_edge(sum_b20, 1)
        came[0, 2, 1] = along_edge(after(terms[2, 1], token), 0)

    lora = sum_to_blocks(pieces, "tensor")
    for bit in reversed(store_bits):
        lora = join_halves(lora, 0, "store", bit)
    rows = place_rows(rows, received, z, n).reshape(requests * n * rank_rows, width)
    adapter = adapter_term(token, lora, rows, token_requests, request_adapters, adapter_ranks)

    if on_line:
        outputs = []
        half = width // 2
        adapter, last, _ = lax.optimization_barrier((adapter, came, token))
        for c in range(2):
            total = adapter[:, c * half : (c + 1) * half] + terms[n - 1, c].astype(jnp.float32)
            for edge in range(n - 1):
                total += last[edge, n - 2, c].astype(jnp.float32)
            outputs.append(total.astype(jnp.bfloat16))
        return jnp.concatenate(outputs, axis=1)

    term = jnp.dot(hidden_activations, down_matrix, preferred_element_type=jnp.float32)
    summed = lax.psum_scatter(term.astype(jnp.bfloat16), "tensor", scatter_dimension=0, tiled=True)
    return (summed.astype(jnp.float32) + adapter).astype(jnp.bfloat16)


def solution(mesh):
    in_specs = (
        P("groups", "tensor"),
        P("tensor", "store"),
        P(("groups", "store"), "tensor", None),
        P(("groups", "store"), "tensor", None),
        P("groups"),
        P("groups"),
        P("groups"),
        P("groups"),
    )
    out_specs = P(("groups", "tensor"), "store")
    return jax.shard_map(
        per_device, mesh=mesh, in_specs=in_specs, out_specs=out_specs, check_vma=False
    )
```

```python
import jax
import jax.numpy as jnp
from jax import lax
from jax.experimental import pallas as pl
from jax.experimental.pallas import tpu as pltpu
from jax.sharding import PartitionSpec as P

VMEM_LIMIT = 52 * 1024 * 1024
LINE = 4
LANES = 128
AHEAD = 4
PAIRS = 2


def line_order(n):
    order = []
    for z in range(n):
        sends = [(t, z >= n // 2, n - 1 - t + z) for t in range(z, n - 1)]
        sends += [(t, z < n // 2, t - (n - 1 - z)) for t in range(n - 1 - z, n - 1)]
        order.append([block for _, _, block in sorted(sends)] + [z])
    return order


def first_divisor(size, choices):
    for choice in choices:
        if size % choice == 0:
            return choice
    return size


def after(token, *done):
    return lax.optimization_barrier((token, done))[0]


def params():
    return pltpu.CompilerParams(vmem_limit_bytes=VMEM_LIMIT)


def small_cost():
    return pl.CostEstimate(flops=10**6, bytes_accessed=10**5, transcendentals=0)


def block_at(order, slot, place):
    picked = jnp.int32(order[0][slot])
    for z in range(1, len(order)):
        picked = jnp.where(place == z, order[z][slot], picked)
    return picked


def spans(requests_ref, r):
    requests = requests_ref[...]
    return jnp.sum((requests < r).astype(jnp.int32)), jnp.sum((requests <= r).astype(jnp.int32))


def adapter_inputs(sums, first_row, meta, requests_ref, held, width):
    place_ref, request_adapters_ref, ranks_ref, slots_ref = meta
    shape = (sums[0].shape[0], width)
    row = lax.broadcasted_iota(jnp.int32, shape, 0) + first_row
    column = lax.broadcasted_iota(jnp.int32, shape, 1)
    total = jnp.zeros(shape, jnp.float32)
    for r in range(request_adapters_ref.shape[0]):
        adapter = request_adapters_ref[r]
        local_slot = slots_ref[adapter] - place_ref[1] * held
        start, end = spans(requests_ref, r)
        for s in range(held):
            last = jnp.where(local_slot == s, end, 0)
            keep = (row >= start) & (row < last) & (column < ranks_ref[adapter])
            total = jnp.where(keep, sums[s], total)
    return total


def base_kernel(order, slots, half, held, *refs):
    meta, refs = refs[:4], refs[4:]
    count = len(slots)
    requests_ref, hidden, matrix, refs = refs[0], refs[1], refs[2], refs[3:]
    factor, refs = (refs[0], refs[1:]) if held else (None, refs)
    outs, (rows, right, sums, sems) = refs[:count], refs[count:]
    steps, _, tile = rows.shape
    columns = outs[0].shape[1]
    block = rows.shape[1] // count
    first_rows = [pl.multiple_of(block_at(order, slot, meta[0][0]) * block, block) for slot in slots]

    def copies(k):
        depth = pl.ds(pl.multiple_of(k * tile, tile), tile)
        moves = [
            (hidden.at[pl.ds(first_rows[i], block), depth], rows.at[k, pl.ds(i * block, block), :])
            for i in range(count)
        ]
        moves.append((matrix.at[depth, pl.ds(half * columns, columns)], right.at[k, :, pl.ds(0, columns)]))
        for s in range(held):
            width = factor.shape[2]
            moves.append((factor.at[s, depth, :], right.at[k, :, pl.ds(columns + s * width, width)]))
        return [pltpu.make_async_copy(a, b, sems.at[k, i]) for i, (a, b) in enumerate(moves)]

    def start(k):
        for copy in copies(k):
            copy.start()

    for k in range(min(AHEAD, steps)):
        start(k)
    sums[...] = jnp.zeros_like(sums)

    def step(k, _):
        @pl.when(k + AHEAD < steps)
        def _():
            start(k + AHEAD)

        for copy in copies(k):
            copy.wait()
        sums[...] += jnp.dot(rows[k], right[k], preferred_element_type=jnp.float32)
        return 0

    lax.fori_loop(0, steps, step, 0)
    for i in range(count):
        own = pl.ds(i * block, block)
        outs[i][:block, :] = sums[own, :columns].astype(jnp.bfloat16)
        if held:
            width = factor.shape[2]
            products = [sums[own, columns + s * width : columns + (s + 1) * width] for s in range(held)]
            inputs = adapter_inputs(products, first_rows[i], meta, requests_ref, held, width).astype(jnp.bfloat16)
            per_row = columns // width
            for j in range(per_row):
                size = block // per_row
                outs[i][block:, j * width : (j + 1) * width] = inputs[j * size : (j + 1) * size, :]


def base_terms(meta, requests, hidden, matrix, factor, slots, half, n):
    tokens, depth = hidden.shape
    block, columns = tokens // n, matrix.shape[1] // 2
    tile = first_divisor(depth, (512, 256, 128))
    steps = depth // tile
    count = len(slots)
    held, width = (factor.shape[0], factor.shape[2]) if factor is not None else (0, 0)
    out_rows = block + block * width // columns
    smem = pl.BlockSpec(memory_space=pltpu.SMEM)
    vmem = pl.BlockSpec(memory_space=pltpu.VMEM)
    hbm = pl.BlockSpec(memory_space=pltpu.HBM)
    arrays = [hidden, matrix] + ([factor] if held else [])
    return pl.pallas_call(
        lambda *refs: base_kernel(line_order(n), slots, half, held, *refs),
        out_shape=[jax.ShapeDtypeStruct((out_rows, columns), jnp.bfloat16)] * count,
        in_specs=[smem] * 4 + [vmem] + [hbm] * len(arrays),
        out_specs=[vmem] * count,
        scratch_shapes=[
            pltpu.VMEM((steps, count * block, tile), jnp.bfloat16),
            pltpu.VMEM((steps, tile, columns + held * width), jnp.bfloat16),
            pltpu.VMEM((count * block, columns + held * width), jnp.float32),
            pltpu.SemaphoreType.DMA((steps, count + 1 + held)),
        ],
        compiler_params=params(),
        cost_estimate=small_cost(),
        name="base_terms",
    )(*meta, requests, *arrays)


def select_rows_kernel(place_ref, request_adapters_ref, slots_ref, factor, kept, sent):
    held = factor.shape[0]
    shards = 2 * PAIRS
    width = factor.shape[2] // shards
    side = place_ref[1] % 2
    for r in range(request_adapters_ref.shape[0]):
        slot = slots_ref[request_adapters_ref[r]] - place_ref[1] * held
        owned = (slot >= 0) & (slot < held)
        slot = jnp.clip(slot, 0, held - 1)
        for out, core in ((kept, side), (sent, 1 - side)):
            for i in range(PAIRS):
                rows = factor[slot, :, pl.ds(pl.multiple_of((2 * i + core) * width, LANES), width)]
                out[r, :, i * width : (i + 1) * width] = jnp.where(owned, rows, jnp.zeros_like(rows))


def select_rows(meta, factor):
    place, request_adapters, _, slots = meta
    _, rank_rows, model_width = factor.shape
    smem = pl.BlockSpec(memory_space=pltpu.SMEM)
    vmem = pl.BlockSpec(memory_space=pltpu.VMEM)
    out = jax.ShapeDtypeStruct((request_adapters.shape[0], rank_rows, model_width // 2), factor.dtype)
    return pl.pallas_call(
        select_rows_kernel,
        out_shape=[out, out],
        in_specs=[smem, smem, smem, vmem],
        out_specs=[vmem, vmem],
        compiler_params=params(),
        cost_estimate=small_cost(),
        name="select_rows",
    )(place, request_adapters, slots, factor)


def expanded_inputs(meta, requests_ref, lora_ref):
    place_ref, request_adapters_ref, ranks_ref, _ = meta
    block, width = lora_ref.shape
    row = lax.broadcasted_iota(jnp.int32, (block, width), 0) + place_ref[0] * block
    lora = lora_ref[...].astype(jnp.float32)
    parts = []
    for r in range(request_adapters_ref.shape[0]):
        start, end = spans(requests_ref, r)
        scale = 0.25 * width / ranks_ref[request_adapters_ref[r]].astype(jnp.float32)
        parts.append(jnp.where((row >= start) & (row < end), lora * scale, 0.0).astype(jnp.bfloat16))
    return jnp.concatenate(parts, axis=1)


def finish_kernel(items, n, *refs):
    meta, requests_ref, lora_ref, refs = refs[:4], refs[4], refs[5], refs[6:]
    pieces, refs = refs[: len(items)], refs[len(items) :]
    added, out, rows = refs[:-2], refs[-2], refs[-1]
    place = meta[0][0]
    requests, rank_rows, width = pieces[0].shape
    rank = n * rank_rows
    for piece, (edge, item) in zip(pieces, items):
        if edge is None:
            targets = [(place >= 0, place)]
        else:
            targets = [(place == edge + 1, item), (place == n - 2 - edge, n - 1 - item)]
        for here, k in targets:

            @pl.when(here)
            def _(piece=piece, k=k):
                for r in range(requests):
                    first = pl.multiple_of(r * rank + k * rank_rows, rank_rows)
                    rows[pl.ds(first, rank_rows), :] = piece[r]

    expanded = expanded_inputs(meta, requests_ref, lora_ref)
    block = lora_ref.shape[0]
    half = width // 2
    for c in range(2):
        columns = slice(c * half, (c + 1) * half)
        total = jnp.dot(expanded, rows[:, columns], preferred_element_type=jnp.float32)
        for ref, which in zip(added, (0, 0, 0, 0, 1, 1)):
            if which == c:
                total += ref[:block, :].astype(jnp.float32)
        out[:, columns] = total.astype(out.dtype)


def finish(meta, requests, lora, items, pieces, added, n):
    smem = pl.BlockSpec(memory_space=pltpu.SMEM)
    vmem = pl.BlockSpec(memory_space=pltpu.VMEM)
    count, rank_rows, width = pieces[0].shape
    return pl.pallas_call(
        lambda *refs: finish_kernel(items, n, *refs),
        out_shape=jax.ShapeDtypeStruct((lora.shape[0], width), jnp.bfloat16),
        in_specs=[smem] * 4 + [vmem] * (2 + len(pieces) + len(added)),
        out_specs=vmem,
        scratch_shapes=[pltpu.VMEM((count * n * rank_rows, width), jnp.bfloat16)],
        compiler_params=params(),
        cost_estimate=small_cost(),
        name="finish",
    )(*meta, requests, lora, *pieces, *added)


def add_last_kernel(total, up, down, out):
    out[...] = (
        total[...].astype(jnp.float32) + up[...].astype(jnp.float32) + down[...].astype(jnp.float32)
    ).astype(out.dtype)


def add_last(total, up, down):
    block, width = total.shape
    half = width // 2
    tile = first_divisor(block, (64, 32, 16))
    arrival = pl.BlockSpec((tile, half), lambda i: (i, 0))
    second = pl.BlockSpec((tile, half), lambda i: (i, 1))
    return pl.pallas_call(
        add_last_kernel,
        out_shape=jax.ShapeDtypeStruct(total.shape, total.dtype),
        grid=(block // tile,),
        in_specs=[second, arrival, arrival],
        out_specs=second,
        input_output_aliases={0: 0},
        cost_estimate=small_cost(),
        name="add_last",
    )(total, up, down)


def swap(x, axis, bit):
    return lax.ppermute(x, axis, [(i, i ^ bit) for i in range(lax.axis_size(axis))])


def bits_of(size):
    return [1 << i for i in range(size.bit_length() - 1)]


def along_edge(x, edge):
    n = lax.axis_size("tensor")
    return lax.ppermute(x, "tensor", [(edge, edge + 1), (n - 1 - edge, n - 2 - edge)])


def take_half(x, dim, side):
    size = x.shape[dim] // 2
    return lax.dynamic_slice_in_dim(x, side * size, size, dim)


def on_line(hidden, matrix, input_factor, output_factor, requests, meta, n):
    shard = lax.axis_index("store")
    token, *rest = meta

    def base(token, slots, half):
        factor = input_factor if half == 0 else None
        return base_terms((token, *rest), requests, hidden, matrix, factor, slots, half, n)

    def hop(token, term, came):
        term, came, _ = lax.optimization_barrier((term, came, token))
        return (term.astype(jnp.float32) + came.astype(jnp.float32)).astype(jnp.bfloat16)

    s, came = {}, {}
    (s[0, 1],) = base(token, [0], 1)
    token = after(token, s[0, 1])
    came[0, 0, 1] = along_edge(s[0, 1], 0)
    kept, sent = select_rows((token, *rest), output_factor)
    token = after(token, kept, sent)
    swapped = swap(sent, "store", 1)
    (s[0, 0],) = base(token, [0], 0)
    token = after(token, s[0, 0])
    came[0, 0, 0] = along_edge(s[0, 0], 0)

    token = after(token, came[0, 0, 1], swapped)
    b11 = hop(token, s[0, 1], came[0, 0, 1])
    came[1, 1, 1] = along_edge(b11, 1)
    rows = kept + swapped
    token = after(token, b11, rows)
    side = shard // 2 % 2
    swapped = swap(take_half(rows, 2, 1 - side), "store", 2)
    rows = take_half(rows, 2, side)

    (s[1, 0],) = base(token, [1], 0)
    token = after(token, s[1, 0])
    came[0, 1, 0] = along_edge(s[1, 0], 0)
    token = after(token, came[0, 0, 0], swapped, came[1, 1, 1])
    b10 = hop(token, s[0, 0], came[0, 0, 0])
    came[1, 1, 0] = along_edge(b10, 1)
    rows = rows + swapped
    token = after(token, b10, rows)
    items = {(edge, edge): along_edge(rows, edge) for edge in range(3)}

    s[2, 0], s[3, 0] = base(token, [2, 3], 0)
    token = after(token, s[2, 0])
    came[0, 2, 0] = along_edge(s[2, 0], 0)
    token = after(token, came[0, 1, 0], came[1, 1, 0], items)
    b20 = hop(token, s[1, 0], came[0, 1, 0])
    came[1, 2, 0] = along_edge(b20, 1)
    c20 = hop(token, s[2, 0], came[1, 1, 0])
    came[2, 2, 0] = along_edge(c20, 2)
    token = after(token, b20, c20)
    items[1, 0] = along_edge(items[0, 0], 1)
    items[2, 1] = along_edge(items[1, 1], 2)

    s[1, 1], s[2, 1], s[3, 1] = base(token, [1, 2, 3], 1)
    token = after(token, s[1, 1])
    came[0, 1, 1] = along_edge(s[1, 1], 0)
    token = after(token, came[0, 2, 0], came[1, 2, 0], came[2, 2, 0], items)
    c21 = hop(token, s[2, 1], came[1, 1, 1])
    token = after(token, c21)
    came[2, 2, 1] = along_edge(c21, 2)
    items[2, 0] = along_edge(items[1, 0], 2)

    block = hidden.shape[0] // n
    width = input_factor.shape[2]
    arrived = [s[3, 0], came[0, 2, 0], came[1, 2, 0], came[2, 2, 0]]
    lora = sum(x[block:].astype(jnp.float32) for x in arrived).astype(jnp.bfloat16)
    lora = lora.reshape(lora.shape[0], -1, width).swapaxes(0, 1).reshape(block, width)
    lora = lora + swap(lora, "store", 1)
    token = after(token, lora)
    came[0, 2, 1] = along_edge(after(s[2, 1], token), 0)
    lora = lora + swap(lora, "store", 2)
    token = after(token, lora, came[0, 1, 1])
    b21 = hop(token, s[1, 1], came[0, 1, 1])
    token = after(token, b21)
    came[1, 2, 1] = along_edge(b21, 1)

    names = list(items)
    added = arrived + [s[3, 1], came[2, 2, 1]]
    out = finish(
        (token, *rest), requests, lora, [(None, None)] + names, [rows] + [items[name] for name in names], added, n
    )
    return add_last(out, came[0, 2, 1], came[1, 2, 1])


def anywhere(hidden, matrix, input_factor, output_factor, token_requests, meta):
    place, request_adapters, ranks, slots = meta
    held = input_factor.shape[0]
    width = input_factor.shape[2]
    rank, slot = ranks[request_adapters], slots[request_adapters]
    owned = slot // held == place[1]
    chosen = token_requests[:, None] == jnp.arange(request_adapters.shape[0])[None, :]
    lora = jnp.zeros((hidden.shape[0], width), jnp.float32)
    for r in range(request_adapters.shape[0]):
        product = jnp.dot(hidden, input_factor[slot[r] % held], preferred_element_type=jnp.float32)
        keep = (chosen[:, r] & owned[r])[:, None] & (jnp.arange(width) < rank[r])[None, :]
        lora = jnp.where(keep, product, lora)
    lora = lax.psum_scatter(lora.astype(jnp.bfloat16), "tensor", scatter_dimension=1, tiled=True)
    lora = lax.psum(lora, "store").astype(jnp.float32)
    rows = jnp.where(owned[:, None, None], output_factor[slot % held], jnp.zeros((), output_factor.dtype))
    rows = lax.psum_scatter(rows, "store", scatter_dimension=2, tiled=True)
    weights = jnp.where(chosen, 0.25 * width / rank.astype(jnp.float32)[None, :], 0.0)
    expanded = (weights[:, :, None] * lora[:, None, :]).reshape(hidden.shape[0], -1).astype(jnp.bfloat16)
    term = jnp.dot(hidden, matrix, preferred_element_type=jnp.float32)
    term += jnp.dot(expanded, rows.reshape(-1, rows.shape[2]), preferred_element_type=jnp.float32)
    return lax.psum_scatter(term.astype(jnp.bfloat16), "tensor", scatter_dimension=0, tiled=True)


def per_device(
    hidden_activations,
    down_matrix,
    adapter_input_factor,
    adapter_output_factor,
    token_requests,
    request_adapters,
    adapter_ranks,
    adapter_store_slot,
):
    n = lax.axis_size("tensor")
    place = jnp.stack([lax.axis_index("tensor"), lax.axis_index("store")]).astype(jnp.int32)
    meta = (place, request_adapters, adapter_ranks, adapter_store_slot)
    arrays = (hidden_activations, down_matrix, adapter_input_factor, adapter_output_factor)
    if n == LINE and lax.axis_size("store") == 2 * PAIRS:
        return on_line(*arrays, token_requests.reshape(-1, LANES), meta, n)
    return anywhere(*arrays, token_requests, meta)


def solution(mesh):
    in_specs = (
        P("groups", "tensor"),
        P("tensor", "store"),
        P(("groups", "store"), "tensor", None),
        P(("groups", "store"), "tensor", None),
        P("groups"),
        P("groups"),
        P("groups"),
        P("groups"),
    )
    out_specs = P(("groups", "tensor"), "store")
    return jax.shard_map(
        per_device, mesh=mesh, in_specs=in_specs, out_specs=out_specs, check_vma=False
    )
```

```python
import jax
import jax.numpy as jnp
from jax import lax
from jax.experimental import pallas as pl
from jax.experimental.pallas import tpu as pltpu
from jax.sharding import PartitionSpec as P

LINE = 4
LANES = 128
AHEAD = 3
PAIRS = 2
MIB = 1024 * 1024


def line_order(n):
    order = []
    for z in range(n):
        sends = [(t, z >= n // 2, n - 1 - t + z) for t in range(z, n - 1)]
        sends += [(t, z < n // 2, t - (n - 1 - z)) for t in range(n - 1 - z, n - 1)]
        order.append([block for _, _, block in sorted(sends)] + [z])
    return order


def first_divisor(size, choices):
    for choice in choices:
        if size % choice == 0:
            return choice
    return size


def after(token, *done):
    return lax.optimization_barrier((token, done))[0]


def params(mebibytes):
    return pltpu.CompilerParams(vmem_limit_bytes=mebibytes * MIB)


def small_cost():
    return pl.CostEstimate(flops=10**6, bytes_accessed=10**5, transcendentals=0)


def block_at(order, slot, place):
    picked = jnp.int32(order[0][slot])
    for z in range(1, len(order)):
        picked = jnp.where(place == z, order[z][slot], picked)
    return picked


def spans(requests_ref, count):
    requests = requests_ref[...]
    return [jnp.int32(0)] + [jnp.sum((requests <= r).astype(jnp.int32)) for r in range(count)]


def local_slots(meta, held):
    place_ref, request_adapters_ref, _, slots_ref = meta
    count = request_adapters_ref.shape[0]
    return [slots_ref[request_adapters_ref[r]] - place_ref[1] * held for r in range(count)]


def base_kernel(order, slots, half, held, *refs):
    count = len(slots)
    meta, refs = (refs[:4], refs[4:]) if held else (refs[:1], refs[1:])
    if held:
        requests_ref, factor, refs = refs[0], refs[1], refs[2:]
    hidden, matrix, refs = refs[0], refs[1], refs[2:]
    outs, (rows, right, sums, sems), refs = refs[:count], refs[count : count + 4], refs[count + 4 :]
    steps, _, tile = rows.shape
    columns = outs[0].shape[1]
    block = rows.shape[1] // count
    first_rows = [pl.multiple_of(block_at(order, slot, meta[0][0]) * block, block) for slot in slots]

    def depth_of(k):
        return pl.ds(pl.multiple_of(k * tile, tile), tile)

    def copies(k):
        moves = [
            (hidden.at[pl.ds(first_rows[i], block), depth_of(k)], rows.at[k, pl.ds(i * block, block), :])
            for i in range(count)
        ]
        moves.append((matrix.at[depth_of(k), pl.ds(half * columns, columns)], right.at[k]))
        return [pltpu.make_async_copy(a, b, sems.at[k, i]) for i, (a, b) in enumerate(moves)]

    if held:
        factors, inputs, factor_sems = refs
        width = factor.shape[2]

        def factor_copies(k, pair):
            return [
                pltpu.make_async_copy(
                    factor.at[2 * pair + i, depth_of(k), :],
                    factors.at[pair, k, :, pl.ds(i * width, width)],
                    factor_sems.at[k, 2 * pair + i],
                )
                for i in range(2)
            ]

    def start(k, pairs):
        for copy in copies(k):
            copy.start()
        for pair, used in enumerate(pairs):

            @pl.when(used)
            def _(pair=pair):
                for copy in factor_copies(k, pair):
                    copy.start()

    used = []
    if held:
        bounds = spans(requests_ref, meta[1].shape[0])
        local = local_slots(meta, held)
        for pair in range(held // 2):
            wanted = jnp.bool_(False)
            for r, slot in enumerate(local):
                for first in first_rows:
                    here = jnp.maximum(bounds[r], first) < jnp.minimum(bounds[r + 1], first + block)
                    wanted = wanted | (here & (slot // 2 == pair) & (slot >= 0))
            used.append(wanted)
        inputs[...] = jnp.zeros_like(inputs)
    for k in range(min(AHEAD, steps)):
        start(k, used)
    sums[...] = jnp.zeros_like(sums)

    def step(k, _):
        @pl.when(k + AHEAD < steps)
        def _():
            start(k + AHEAD, used)

        for copy in copies(k):
            copy.wait()
        sums[...] += jnp.dot(rows[k], right[k], preferred_element_type=jnp.float32)
        for pair, wanted in enumerate(used):

            @pl.when(wanted)
            def _(pair=pair):
                for copy in factor_copies(k, pair):
                    copy.wait()
                inputs[pair] += jnp.dot(rows[k], factors[pair, k], preferred_element_type=jnp.float32)

        return 0

    lax.fori_loop(0, steps, step, 0)
    for i in range(count):
        own = pl.ds(i * block, block)
        outs[i][:block, :] = sums[own, :].astype(jnp.bfloat16)
        if held:
            row = lax.broadcasted_iota(jnp.int32, (block, width), 0) + first_rows[i]
            column = lax.broadcasted_iota(jnp.int32, (block, width), 1)
            total = jnp.zeros((block, width), jnp.float32)
            for r, slot in enumerate(local):
                last = jnp.where((slot >= 0) & (slot < held), bounds[r + 1], 0)
                keep = (row >= bounds[r]) & (row < last) & (column < meta[2][meta[1][r]])
                slot = jnp.clip(slot, 0, held - 1)
                lanes = pl.ds(pl.multiple_of(slot % 2 * width, width), width)
                total = jnp.where(keep, inputs[slot // 2, own, lanes], total)
            total = total.astype(jnp.bfloat16)
            per_row = columns // width
            for j in range(per_row):
                size = block // per_row
                outs[i][block:, j * width : (j + 1) * width] = total[j * size : (j + 1) * size, :]


def base_terms(meta, requests, hidden, matrix, factor, slots, half, n):
    tokens, depth = hidden.shape
    block, columns = tokens // n, matrix.shape[1] // 2
    tile = first_divisor(depth, (1024, 512, 256, 128))
    steps = depth // tile
    count = len(slots)
    smem = pl.BlockSpec(memory_space=pltpu.SMEM)
    vmem = pl.BlockSpec(memory_space=pltpu.VMEM)
    hbm = pl.BlockSpec(memory_space=pltpu.HBM)
    held, out_rows = 0, block
    operands, in_specs = [meta[0]], [smem]
    scratch = [
        pltpu.VMEM((steps, count * block, tile), jnp.bfloat16),
        pltpu.VMEM((steps, tile, columns), jnp.bfloat16),
        pltpu.VMEM((count * block, columns), jnp.float32),
        pltpu.SemaphoreType.DMA((steps, count + 1)),
    ]
    if factor is not None:
        held, _, width = factor.shape
        out_rows += block * width // columns
        operands, in_specs = [*meta, requests, factor], [smem] * 4 + [vmem, hbm]
        scratch += [
            pltpu.VMEM((held // 2, steps, tile, 2 * width), jnp.bfloat16),
            pltpu.VMEM((held // 2, count * block, 2 * width), jnp.float32),
            pltpu.SemaphoreType.DMA((steps, held)),
        ]
    return pl.pallas_call(
        lambda *refs: base_kernel(line_order(n), slots, half, held, *refs),
        out_shape=[jax.ShapeDtypeStruct((out_rows, columns), jnp.bfloat16)] * count,
        in_specs=in_specs + [hbm, hbm],
        out_specs=[vmem] * count,
        scratch_shapes=scratch,
        compiler_params=params(44),
        cost_estimate=small_cost(),
        name="base_terms",
    )(*operands, hidden, matrix)


def select_rows_kernel(place_ref, request_adapters_ref, slots_ref, factor, kept, sent):
    held = factor.shape[0]
    shards = 2 * PAIRS
    width = factor.shape[2] // shards
    side = place_ref[1] % 2
    for r in range(request_adapters_ref.shape[0]):
        slot = slots_ref[request_adapters_ref[r]] - place_ref[1] * held
        owned = (slot >= 0) & (slot < held)
        slot = jnp.clip(slot, 0, held - 1)
        for out, core in ((kept, side), (sent, 1 - side)):
            for i in range(PAIRS):
                rows = factor[slot, :, pl.ds(pl.multiple_of((2 * i + core) * width, LANES), width)]
                out[r, :, i * width : (i + 1) * width] = jnp.where(owned, rows, jnp.zeros_like(rows))


def select_rows(meta, factor):
    place, request_adapters, _, slots = meta
    _, rank_rows, model_width = factor.shape
    smem = pl.BlockSpec(memory_space=pltpu.SMEM)
    vmem = pl.BlockSpec(memory_space=pltpu.VMEM)
    out = jax.ShapeDtypeStruct((request_adapters.shape[0], rank_rows, model_width // 2), factor.dtype)
    return pl.pallas_call(
        select_rows_kernel,
        out_shape=[out, out],
        in_specs=[smem, smem, smem, vmem],
        out_specs=[vmem, vmem],
        compiler_params=params(16),
        cost_estimate=small_cost(),
        name="select_rows",
    )(place, request_adapters, slots, factor)


def expanded_inputs(meta, requests_ref, lora_ref):
    place_ref, request_adapters_ref, ranks_ref, _ = meta
    block, width = lora_ref.shape
    row = lax.broadcasted_iota(jnp.int32, (block, width), 0) + place_ref[0] * block
    lora = lora_ref[...].astype(jnp.float32)
    count = request_adapters_ref.shape[0]
    bounds = spans(requests_ref, count)
    parts = []
    for r in range(count):
        scale = 0.25 * width / ranks_ref[request_adapters_ref[r]].astype(jnp.float32)
        keep = (row >= bounds[r]) & (row < bounds[r + 1])
        parts.append(jnp.where(keep, lora * scale, 0.0).astype(jnp.bfloat16))
    return jnp.concatenate(parts, axis=1)


def finish_kernel(items, n, *refs):
    meta, requests_ref, lora_ref, refs = refs[:4], refs[4], refs[5], refs[6:]
    count = 1 + max(index for index, *_ in items)
    pieces, refs = refs[:count], refs[count:]
    added, out, rows = refs[:-2], refs[-2], refs[-1]
    place = meta[0][0]
    requests, rank_rows, width = pieces[0].shape
    rank = n * rank_rows
    for index, sub, edge, item in items:
        if edge is None:
            targets = [(place >= 0, place)]
        else:
            targets = [(place == edge + 1, item), (place == n - 2 - edge, n - 1 - item)]
        piece = pieces[index] if sub is None else pieces[index].at[sub]
        for here, k in targets:

            @pl.when(here)
            def _(piece=piece, k=k):
                for r in range(requests):
                    first = pl.multiple_of(r * rank + k * rank_rows, rank_rows)
                    rows[pl.ds(first, rank_rows), :] = piece[r]

    expanded = expanded_inputs(meta, requests_ref, lora_ref)
    block = lora_ref.shape[0]
    half = width // 2
    for c in range(2):
        columns = slice(c * half, (c + 1) * half)
        total = jnp.dot(expanded, rows[:, columns], preferred_element_type=jnp.float32)
        for ref, which in zip(added, (0, 0, 0, 0, 1, 1)):
            if which == c:
                total += ref[:block, :].astype(jnp.float32)
        out[:, columns] = total.astype(out.dtype)


def finish(meta, requests, lora, items, pieces, added, n):
    smem = pl.BlockSpec(memory_space=pltpu.SMEM)
    vmem = pl.BlockSpec(memory_space=pltpu.VMEM)
    count, rank_rows, width = pieces[0].shape
    return pl.pallas_call(
        lambda *refs: finish_kernel(items, n, *refs),
        out_shape=jax.ShapeDtypeStruct((lora.shape[0], width), jnp.bfloat16),
        in_specs=[smem] * 4 + [vmem] * (2 + len(pieces) + len(added)),
        out_specs=vmem,
        scratch_shapes=[pltpu.VMEM((count * n * rank_rows, width), jnp.bfloat16)],
        compiler_params=params(20),
        cost_estimate=small_cost(),
        name="finish",
    )(*meta, requests, lora, *pieces, *added)


def add_last_kernel(total, up, down, out):
    half = up.shape[1]
    out[:, :half] = total[:, :half]
    last = total[:, half:].astype(jnp.float32) + up[...].astype(jnp.float32) + down[...].astype(jnp.float32)
    out[:, half:] = last.astype(out.dtype)


def add_last(total, up, down):
    vmem = pl.BlockSpec(memory_space=pltpu.VMEM)
    return pl.pallas_call(
        add_last_kernel,
        out_shape=jax.ShapeDtypeStruct(total.shape, total.dtype),
        in_specs=[vmem] * 3,
        out_specs=vmem,
        compiler_params=params(12),
        cost_estimate=small_cost(),
        name="add_last",
    )(total, up, down)


def hop_both_kernel(term_0, came_0, term_1, came_1, out):
    first = term_0.shape[0]
    out[:first, :] = (term_0[...].astype(jnp.float32) + came_0[...].astype(jnp.float32)).astype(out.dtype)
    out[first:, :] = (term_1[...].astype(jnp.float32) + came_1[...].astype(jnp.float32)).astype(out.dtype)


def hop_both(token, term_0, came_0, term_1, came_1):
    vmem = pl.BlockSpec(memory_space=pltpu.VMEM)
    arrays = lax.optimization_barrier((term_0, came_0, term_1, came_1, token))[:4]
    return pl.pallas_call(
        hop_both_kernel,
        out_shape=jax.ShapeDtypeStruct((term_0.shape[0] + term_1.shape[0], term_0.shape[1]), term_0.dtype),
        in_specs=[vmem] * 4,
        out_specs=vmem,
        compiler_params=params(12),
        cost_estimate=small_cost(),
        name="hop_both",
    )(*arrays)


def swap(x, axis, bit):
    return lax.ppermute(x, axis, [(i, i ^ bit) for i in range(lax.axis_size(axis))])


def bits_of(size):
    return [1 << i for i in range(size.bit_length() - 1)]


def along_edge(x, edge):
    n = lax.axis_size("tensor")
    return lax.ppermute(x, "tensor", [(edge, edge + 1), (n - 1 - edge, n - 2 - edge)])


def take_half(x, dim, side):
    size = x.shape[dim] // 2
    return lax.dynamic_slice_in_dim(x, side * size, size, dim)


def on_line(hidden, matrix, input_factor, output_factor, requests, meta, n):
    shard = lax.axis_index("store")
    token, *rest = meta

    def base(token, slots, half):
        factor = input_factor if half == 0 else None
        return base_terms((token, *rest), requests, hidden, matrix, factor, slots, half, n)

    def hop(token, term, came):
        term, came, _ = lax.optimization_barrier((term, came, token))
        return (term.astype(jnp.float32) + came.astype(jnp.float32)).astype(jnp.bfloat16)

    s = {}
    (s[0, 1],) = base(token, [0], 1)
    token = after(token, s[0, 1])
    a01 = along_edge(s[0, 1], 0)
    kept, sent = select_rows((token, *rest), output_factor)
    token = after(token, kept, sent)
    swapped = swap(sent, "store", 1)
    (s[0, 0],) = base(token, [0], 0)
    token = after(token, s[0, 0])
    a00 = along_edge(s[0, 0], 0)

    token = after(token, swapped)
    rows = kept + swapped
    side = shard // 2 % 2
    outgoing = take_half(rows, 2, 1 - side)
    token = after(token, outgoing)
    swapped = swap(outgoing, "store", 2)
    rows = take_half(rows, 2, side)

    s[1, 0], s[2, 0] = base(token, [1, 2], 0)
    token = after(token, s[1, 0])
    a10 = along_edge(s[1, 0], 0)
    token = after(token, a01, a00, swapped)
    b1 = hop_both(token, s[0, 0], a00, s[0, 1], a01)
    rows = rows + swapped
    token = after(token, b1, rows)
    b1 = along_edge(b1, 1)
    item_00, item_11, item_22 = (along_edge(rows, edge) for edge in range(3))
    a20 = along_edge(after(s[2, 0], token), 0)

    s[1, 1], s[2, 1], s[3, 1] = base(token, [1, 2, 3], 1)
    token = after(token, s[1, 1], a10, b1, item_00, item_11)
    piece = s[0, 0].shape[0]
    b20 = hop(token, s[1, 0], a10)
    token = after(token, b20)
    b20 = along_edge(b20, 1)
    c20 = hop(token, s[2, 0], b1[:piece])
    token = after(token, c20)
    c20 = along_edge(c20, 2)
    item_10 = along_edge(after(item_00, token), 1)
    a11 = along_edge(after(s[1, 1], token), 0)

    (s[3, 0],) = base(after(token, a20, item_22), [3], 0)
    token = after(token, s[3, 0], a20, b20, c20, item_10)
    c21 = hop(token, s[2, 1], b1[piece:])
    token = after(token, c21)
    c21 = along_edge(c21, 2)
    bundle = along_edge(after(jnp.stack([item_11, item_10]), token), 2)
    a21 = along_edge(after(s[2, 1], token), 0)

    block = hidden.shape[0] // n
    width = input_factor.shape[2]
    arrived = lax.optimization_barrier(([s[3, 0], a20, b20, c20], token))[0]
    lora = sum(x[block:].astype(jnp.float32) for x in arrived).astype(jnp.bfloat16)
    lora = lora.reshape(lora.shape[0], -1, width).swapaxes(0, 1).reshape(block, width)
    lora = lora + swap(lora, "store", 1)
    lora = lora + swap(lora, "store", 2)
    token = after(token, lora, a11)
    b21 = hop(token, s[1, 1], a11)
    token = after(token, b21)
    b21 = along_edge(b21, 1)

    pieces = [rows, item_00, item_11, item_10, item_22, bundle]
    items = [(0, None, None, None), (1, None, 0, 0), (2, None, 1, 1), (3, None, 1, 0), (4, None, 2, 2)]
    items += [(5, 0, 2, 1), (5, 1, 2, 0)]
    out = finish((token, *rest), requests, lora, items, pieces, arrived + [s[3, 1], c21], n)
    return add_last(out, a21, b21)


def anywhere(hidden, matrix, input_factor, output_factor, token_requests, meta):
    place, request_adapters, ranks, slots = meta
    held = input_factor.shape[0]
    width = input_factor.shape[2]
    rank, slot = ranks[request_adapters], slots[request_adapters]
    owned = slot // held == place[1]
    chosen = token_requests[:, None] == jnp.arange(request_adapters.shape[0])[None, :]
    lora = jnp.zeros((hidden.shape[0], width), jnp.float32)
    for r in range(request_adapters.shape[0]):
        product = jnp.dot(hidden, input_factor[slot[r] % held], preferred_element_type=jnp.float32)
        keep = (chosen[:, r] & owned[r])[:, None] & (jnp.arange(width) < rank[r])[None, :]
        lora = jnp.where(keep, product, lora)
    lora = lax.psum_scatter(lora.astype(jnp.bfloat16), "tensor", scatter_dimension=1, tiled=True)
    lora = lax.psum(lora, "store").astype(jnp.float32)
    rows = jnp.where(owned[:, None, None], output_factor[slot % held], jnp.zeros((), output_factor.dtype))
    rows = lax.psum_scatter(rows, "store", scatter_dimension=2, tiled=True)
    weights = jnp.where(chosen, 0.25 * width / rank.astype(jnp.float32)[None, :], 0.0)
    expanded = (weights[:, :, None] * lora[:, None, :]).reshape(hidden.shape[0], -1).astype(jnp.bfloat16)
    term = jnp.dot(hidden, matrix, preferred_element_type=jnp.float32)
    term += jnp.dot(expanded, rows.reshape(-1, rows.shape[2]), preferred_element_type=jnp.float32)
    return lax.psum_scatter(term.astype(jnp.bfloat16), "tensor", scatter_dimension=0, tiled=True)


def per_device(
    hidden_activations,
    down_matrix,
    adapter_input_factor,
    adapter_output_factor,
    token_requests,
    request_adapters,
    adapter_ranks,
    adapter_store_slot,
):
    n = lax.axis_size("tensor")
    place = jnp.stack([lax.axis_index("tensor"), lax.axis_index("store")]).astype(jnp.int32)
    meta = (place, request_adapters, adapter_ranks, adapter_store_slot)
    arrays = (hidden_activations, down_matrix, adapter_input_factor, adapter_output_factor)
    if n == LINE and lax.axis_size("store") == 2 * PAIRS and adapter_input_factor.shape[0] % 2 == 0:
        return on_line(*arrays, token_requests.reshape(-1, LANES), meta, n)
    return anywhere(*arrays, token_requests, meta)


def solution(mesh):
    in_specs = (
        P("groups", "tensor"),
        P("tensor", "store"),
        P(("groups", "store"), "tensor", None),
        P(("groups", "store"), "tensor", None),
        P("groups"),
        P("groups"),
        P("groups"),
        P("groups"),
    )
    out_specs = P(("groups", "tensor"), "store")
    return jax.shard_map(
        per_device, mesh=mesh, in_specs=in_specs, out_specs=out_specs, check_vma=False
    )
```

```python
import jax
import jax.numpy as jnp
from jax import lax
from jax.experimental import pallas as pl
from jax.experimental.pallas import tpu as pltpu
from jax.sharding import PartitionSpec as P

LINE = 4
LANES = 128
AHEAD = 3
PAIRS = 2
MIB = 1024 * 1024


def line_order(n):
    order = []
    for z in range(n):
        sends = [(t, z >= n // 2, n - 1 - t + z) for t in range(z, n - 1)]
        sends += [(t, z < n // 2, t - (n - 1 - z)) for t in range(n - 1 - z, n - 1)]
        order.append([block for _, _, block in sorted(sends)] + [z])
    return order


def first_divisor(size, choices):
    for choice in choices:
        if size % choice == 0:
            return choice
    return size


def after(token, *done):
    return lax.optimization_barrier((token, done))[0]


def params(mebibytes):
    return pltpu.CompilerParams(vmem_limit_bytes=mebibytes * MIB)


def small_cost():
    return pl.CostEstimate(flops=10**6, bytes_accessed=10**5, transcendentals=0)


def block_at(order, slot, place):
    picked = jnp.int32(order[0][slot])
    for z in range(1, len(order)):
        picked = jnp.where(place == z, order[z][slot], picked)
    return picked


def spans(requests_ref, count):
    requests = requests_ref[...]
    return [jnp.int32(0)] + [jnp.sum((requests <= r).astype(jnp.int32)) for r in range(count)]


class Meta:
    def __init__(self, ref, requests):
        self.ref, self.requests = ref, requests
        self.adapters = (ref.shape[0] - 2 - requests) // 2
        self.place, self.shard = ref[0], ref[1]

    def adapter(self, r):
        return self.ref[2 + r]

    def rank(self, r):
        return self.ref[2 + self.requests + self.adapter(r)]

    def local_slot(self, r, held):
        return self.ref[2 + self.requests + self.adapters + self.adapter(r)] - self.shard * held


def base_kernel(order, slots, half, held, request_count, *refs):
    count = len(slots)
    meta, refs = Meta(refs[0], request_count), refs[1:]
    if held:
        requests_ref, factor, refs = refs[0], refs[1], refs[2:]
    hidden, matrix, refs = refs[0], refs[1], refs[2:]
    outs, (rows, right, sums, sems), refs = refs[:count], refs[count : count + 4], refs[count + 4 :]
    steps, _, tile = rows.shape
    columns = outs[0].shape[1]
    block = rows.shape[1] // count
    first_rows = [pl.multiple_of(block_at(order, slot, meta.place) * block, block) for slot in slots]

    def depth_of(k):
        return pl.ds(pl.multiple_of(k * tile, tile), tile)

    def copies(k):
        moves = [
            (hidden.at[pl.ds(first_rows[i], block), depth_of(k)], rows.at[k, pl.ds(i * block, block), :])
            for i in range(count)
        ]
        moves.append((matrix.at[depth_of(k), pl.ds(half * columns, columns)], right.at[k]))
        return [pltpu.make_async_copy(a, b, sems.at[k, i]) for i, (a, b) in enumerate(moves)]

    if held:
        factors, inputs, factor_sems = refs
        width = factor.shape[2]

        def factor_copies(k, pair):
            return [
                pltpu.make_async_copy(
                    factor.at[2 * pair + i, depth_of(k), :],
                    factors.at[pair, k, :, pl.ds(i * width, width)],
                    factor_sems.at[k, 2 * pair + i],
                )
                for i in range(2)
            ]

    def start(k):
        for copy in copies(k):
            copy.start()

    def start_factors(k, pairs):
        for pair, used in enumerate(pairs):

            @pl.when(used)
            def _(pair=pair):
                for copy in factor_copies(k, pair):
                    copy.start()

    for k in range(min(AHEAD, steps)):
        start(k)
    used = []
    if held:
        bounds = spans(requests_ref, request_count)
        local = [meta.local_slot(r, held) for r in range(request_count)]
        for pair in range(held // 2):
            wanted = jnp.bool_(False)
            for r, slot in enumerate(local):
                for first in first_rows:
                    here = jnp.maximum(bounds[r], first) < jnp.minimum(bounds[r + 1], first + block)
                    wanted = wanted | (here & (slot // 2 == pair) & (slot >= 0))
            used.append(wanted)
        for k in range(min(AHEAD, steps)):
            start_factors(k, used)
        inputs[...] = jnp.zeros_like(inputs)
    sums[...] = jnp.zeros_like(sums)

    def step(k, _):
        @pl.when(k + AHEAD < steps)
        def _():
            start(k + AHEAD)
            start_factors(k + AHEAD, used)

        for copy in copies(k):
            copy.wait()
        sums[...] += jnp.dot(rows[k], right[k], preferred_element_type=jnp.float32)
        for pair, wanted in enumerate(used):

            @pl.when(wanted)
            def _(pair=pair):
                for copy in factor_copies(k, pair):
                    copy.wait()
                inputs[pair] += jnp.dot(rows[k], factors[pair, k], preferred_element_type=jnp.float32)

        return 0

    lax.fori_loop(0, steps, step, 0)
    for i in range(count):
        own = pl.ds(i * block, block)
        outs[i][:block, :] = sums[own, :].astype(jnp.bfloat16)
        if held:
            row = lax.broadcasted_iota(jnp.int32, (block, width), 0) + first_rows[i]
            column = lax.broadcasted_iota(jnp.int32, (block, width), 1)
            total = jnp.zeros((block, width), jnp.float32)
            for r, slot in enumerate(local):
                last = jnp.where((slot >= 0) & (slot < held), bounds[r + 1], 0)
                keep = (row >= bounds[r]) & (row < last) & (column < meta.rank(r))
                slot = jnp.clip(slot, 0, held - 1)
                lanes = pl.ds(pl.multiple_of(slot % 2 * width, width), width)
                total = jnp.where(keep, inputs[slot // 2, own, lanes], total)
            total = total.astype(jnp.bfloat16)
            per_row = columns // width
            for j in range(per_row):
                size = block // per_row
                outs[i][block:, j * width : (j + 1) * width] = total[j * size : (j + 1) * size, :]


def base_terms(meta, requests, request_count, hidden, matrix, factor, slots, half, n, grant):
    tokens, depth = hidden.shape
    block, columns = tokens // n, matrix.shape[1] // 2
    tile = first_divisor(depth, (1024, 512, 256, 128))
    steps = depth // tile
    count = len(slots)
    smem = pl.BlockSpec(memory_space=pltpu.SMEM)
    vmem = pl.BlockSpec(memory_space=pltpu.VMEM)
    hbm = pl.BlockSpec(memory_space=pltpu.HBM)
    held, out_rows = 0, block
    operands, in_specs = [meta], [smem]
    scratch = [
        pltpu.VMEM((steps, count * block, tile), jnp.bfloat16),
        pltpu.VMEM((steps, tile, columns), jnp.bfloat16),
        pltpu.VMEM((count * block, columns), jnp.float32),
        pltpu.SemaphoreType.DMA((steps, count + 1)),
    ]
    if factor is not None:
        held, _, width = factor.shape
        out_rows += block * width // columns
        operands, in_specs = [meta, requests, factor], [smem, vmem, hbm]
        scratch += [
            pltpu.VMEM((held // 2, steps, tile, 2 * width), jnp.bfloat16),
            pltpu.VMEM((held // 2, count * block, 2 * width), jnp.float32),
            pltpu.SemaphoreType.DMA((steps, held)),
        ]
    return pl.pallas_call(
        lambda *refs: base_kernel(line_order(n), slots, half, held, request_count, *refs),
        out_shape=[jax.ShapeDtypeStruct((out_rows, columns), jnp.bfloat16)] * count,
        in_specs=in_specs + [hbm, hbm],
        out_specs=[vmem] * count,
        scratch_shapes=scratch,
        compiler_params=params(grant),
        cost_estimate=small_cost(),
        name="base_terms",
    )(*operands, hidden, matrix)


def select_rows_kernel(request_count, meta_ref, factor, kept, sent):
    meta = Meta(meta_ref, request_count)
    held = factor.shape[0]
    width = factor.shape[2] // (2 * PAIRS)
    side = meta.shard % 2
    for r in range(request_count):
        slot = meta.local_slot(r, held)
        owned = (slot >= 0) & (slot < held)
        slot = jnp.clip(slot, 0, held - 1)
        for out, core in ((kept, side), (sent, 1 - side)):
            for i in range(PAIRS):
                rows = factor[slot, :, pl.ds(pl.multiple_of((2 * i + core) * width, LANES), width)]
                out[i, r] = jnp.where(owned, rows, jnp.zeros_like(rows))


def select_rows(meta, request_count, factor):
    _, rank_rows, model_width = factor.shape
    smem = pl.BlockSpec(memory_space=pltpu.SMEM)
    vmem = pl.BlockSpec(memory_space=pltpu.VMEM)
    shape = (PAIRS, request_count, rank_rows, model_width // (2 * PAIRS))
    out = jax.ShapeDtypeStruct(shape, factor.dtype)
    return pl.pallas_call(
        lambda *refs: select_rows_kernel(request_count, *refs),
        out_shape=[out, out],
        in_specs=[smem, vmem],
        out_specs=[vmem, vmem],
        compiler_params=params(16),
        cost_estimate=small_cost(),
        name="select_rows",
    )(meta, factor)


def expanded_inputs(meta, requests_ref, lora_ref):
    block, width = lora_ref.shape
    row = lax.broadcasted_iota(jnp.int32, (block, width), 0) + meta.place * block
    lora = lora_ref[...].astype(jnp.float32)
    bounds = spans(requests_ref, meta.requests)
    parts = []
    for r in range(meta.requests):
        scale = 0.25 * width / meta.rank(r).astype(jnp.float32)
        keep = (row >= bounds[r]) & (row < bounds[r + 1])
        parts.append(jnp.where(keep, lora * scale, 0.0).astype(jnp.bfloat16))
    return jnp.concatenate(parts, axis=1)


def finish_kernel(items, n, *refs):
    meta_ref, requests_ref, lora_ref, refs = refs[0], refs[1], refs[2], refs[3:]
    count = len(items)
    pieces, refs = refs[:count], refs[count:]
    added, out, rows = refs[:-2], refs[-2], refs[-1]
    requests, rank_rows, width = pieces[0].shape
    meta = Meta(meta_ref, requests)
    place = meta.place
    rank = n * rank_rows
    for piece, (edge, item) in zip(pieces, items):
        if edge is None:
            targets = [(place >= 0, place)]
        else:
            targets = [(place == edge + 1, item), (place == n - 2 - edge, n - 1 - item)]
        for here, k in targets:

            @pl.when(here)
            def _(piece=piece, k=k):
                for r in range(requests):
                    first = pl.multiple_of(r * rank + k * rank_rows, rank_rows)
                    rows[pl.ds(first, rank_rows), :] = piece[r]

    expanded = expanded_inputs(meta, requests_ref, lora_ref)
    block = lora_ref.shape[0]
    half = width // 2
    for c in range(2):
        columns = slice(c * half, (c + 1) * half)
        total = jnp.dot(expanded, rows[:, columns], preferred_element_type=jnp.float32)
        for ref, which in zip(added, (0, 0, 0, 0, 1, 1)):
            if which == c:
                total += ref[:block, :].astype(jnp.float32)
        out[:, columns] = total.astype(out.dtype)


def finish(meta, requests, lora, items, pieces, added, n):
    smem = pl.BlockSpec(memory_space=pltpu.SMEM)
    vmem = pl.BlockSpec(memory_space=pltpu.VMEM)
    count, rank_rows, width = pieces[0].shape
    return pl.pallas_call(
        lambda *refs: finish_kernel(items, n, *refs),
        out_shape=jax.ShapeDtypeStruct((lora.shape[0], width), jnp.bfloat16),
        in_specs=[smem] + [vmem] * (2 + len(pieces) + len(added)),
        out_specs=vmem,
        scratch_shapes=[pltpu.VMEM((count * n * rank_rows, width), jnp.bfloat16)],
        compiler_params=params(20),
        cost_estimate=small_cost(),
        name="finish",
    )(meta, requests, lora, *pieces, *added)


def add_last_kernel(total, up, down, out):
    half = up.shape[1]
    out[:, :half] = total[:, :half]
    last = total[:, half:].astype(jnp.float32) + up[...].astype(jnp.float32) + down[...].astype(jnp.float32)
    out[:, half:] = last.astype(out.dtype)


def add_last(total, up, down):
    vmem = pl.BlockSpec(memory_space=pltpu.VMEM)
    return pl.pallas_call(
        add_last_kernel,
        out_shape=jax.ShapeDtypeStruct(total.shape, total.dtype),
        in_specs=[vmem] * 3,
        out_specs=vmem,
        compiler_params=params(12),
        cost_estimate=small_cost(),
        name="add_last",
    )(total, up, down)


def swap(x, axis, bit):
    return lax.ppermute(x, axis, [(i, i ^ bit) for i in range(lax.axis_size(axis))])


def bits_of(size):
    return [1 << i for i in range(size.bit_length() - 1)]


def along_edge(x, edge):
    n = lax.axis_size("tensor")
    return lax.ppermute(x, "tensor", [(edge, edge + 1), (n - 1 - edge, n - 2 - edge)])


def on_line(hidden, matrix, input_factor, output_factor, requests, token, request_count, n):
    shard = lax.axis_index("store")

    def base(token, slots, half, grant):
        factor = input_factor if half == 0 else None
        return base_terms(token, requests, request_count, hidden, matrix, factor, slots, half, n, grant)

    def hop(token, term, came):
        term, came, _ = lax.optimization_barrier((term, came, token))
        return (term.astype(jnp.float32) + came.astype(jnp.float32)).astype(jnp.bfloat16)

    def send(x, edge, token):
        return along_edge(after(x, token), edge)

    kept, sent = select_rows(token, request_count, output_factor)
    token = after(token, kept, sent)
    swapped = swap(sent, "store", 1)
    (s00,) = base(token, [0], 0, 58)
    token = after(token, s00, swapped)
    a00 = along_edge(s00, 0)
    side = shard // 2 % 2
    kept, swapped, _ = lax.optimization_barrier((kept, swapped, token))
    outgoing = kept[1 - side] + swapped[1 - side]
    rows = kept[side] + swapped[side]
    token = after(token, outgoing, rows)
    swapped = swap(outgoing, "store", 2)
    (s01,) = base(token, [0], 1, 50)

    token = after(token, s01)
    a01 = send(s01, 0, token)
    token, swapped, a00 = lax.optimization_barrier((token, swapped, a00))
    b10 = hop(token, s00, a00)
    rows = rows + swapped
    token = after(token, b10, rows)
    b10 = along_edge(b10, 1)
    r00, r11, r22 = (along_edge(rows, edge) for edge in range(3))
    s10, s20, s30 = base(token, [1, 2, 3], 0, 42)

    token = after(token, s10)
    a10 = send(s10, 0, token)
    token = after(token, a01, b10, r00, r11, r22)
    b11 = hop(token, s01, a01)
    c20 = hop(token, s20, b10)
    token = after(token, b11, c20)
    b11 = along_edge(b11, 1)
    c20 = along_edge(c20, 2)
    r10 = send(r00, 1, token)
    r21 = send(r11, 2, token)
    a20 = send(s20, 0, token)
    s11, s21, s31 = base(token, [1, 2, 3], 1, 52)

    token = after(token, s11)
    a11 = send(s11, 0, token)
    token = after(token, a10, b11, c20, r10, r21, a20)
    b20 = hop(token, s10, a10)
    c21 = hop(token, s21, b11)
    token = after(token, b20, c21)
    b20 = along_edge(b20, 1)
    c21 = along_edge(c21, 2)
    r20 = send(r10, 2, token)
    a21 = send(s21, 0, token)

    block = hidden.shape[0] // n
    width = input_factor.shape[2]
    token = after(token, a11)
    b21 = hop(token, s11, a11)
    token = after(token, b21)
    b21 = along_edge(b21, 1)
    arrived = [s30, a20, b20, c20]
    lora = sum(x[block:].astype(jnp.float32) for x in arrived).astype(jnp.bfloat16)
    lora = lora.reshape(lora.shape[0], -1, width).swapaxes(0, 1).reshape(block, width)
    lora = lora + swap(lora, "store", 1)
    lora = lora + swap(lora, "store", 2)
    items = [(None, None), (0, 0), (1, 1), (1, 0), (2, 2), (2, 1), (2, 0)]
    out = finish(token, requests, lora, items, [rows, r00, r11, r10, r22, r21, r20], arrived + [s31, c21], n)
    return add_last(out, a21, b21)


def anywhere(hidden, matrix, input_factor, output_factor, token_requests, meta):
    request_adapters, ranks, slots = meta
    held = input_factor.shape[0]
    width = input_factor.shape[2]
    rank, slot = ranks[request_adapters], slots[request_adapters]
    owned = slot // held == lax.axis_index("store")
    chosen = token_requests[:, None] == jnp.arange(request_adapters.shape[0])[None, :]
    lora = jnp.zeros((hidden.shape[0], width), jnp.float32)
    for r in range(request_adapters.shape[0]):
        product = jnp.dot(hidden, input_factor[slot[r] % held], preferred_element_type=jnp.float32)
        keep = (chosen[:, r] & owned[r])[:, None] & (jnp.arange(width) < rank[r])[None, :]
        lora = jnp.where(keep, product, lora)
    lora = lax.psum_scatter(lora.astype(jnp.bfloat16), "tensor", scatter_dimension=1, tiled=True)
    lora = lax.psum(lora, "store").astype(jnp.float32)
    rows = jnp.where(owned[:, None, None], output_factor[slot % held], jnp.zeros((), output_factor.dtype))
    rows = lax.psum_scatter(rows, "store", scatter_dimension=2, tiled=True)
    weights = jnp.where(chosen, 0.25 * width / rank.astype(jnp.float32)[None, :], 0.0)
    expanded = (weights[:, :, None] * lora[:, None, :]).reshape(hidden.shape[0], -1).astype(jnp.bfloat16)
    term = jnp.dot(hidden, matrix, preferred_element_type=jnp.float32)
    term += jnp.dot(expanded, rows.reshape(-1, rows.shape[2]), preferred_element_type=jnp.float32)
    return lax.psum_scatter(term.astype(jnp.bfloat16), "tensor", scatter_dimension=0, tiled=True)


def per_device(
    hidden_activations,
    down_matrix,
    adapter_input_factor,
    adapter_output_factor,
    token_requests,
    request_adapters,
    adapter_ranks,
    adapter_store_slot,
):
    n = lax.axis_size("tensor")
    meta = (request_adapters, adapter_ranks, adapter_store_slot)
    arrays = (hidden_activations, down_matrix, adapter_input_factor, adapter_output_factor)
    if n == LINE and lax.axis_size("store") == 2 * PAIRS and adapter_input_factor.shape[0] % 2 == 0:
        place = jnp.stack([lax.axis_index("tensor"), lax.axis_index("store")]).astype(jnp.int32)
        token = jnp.concatenate([place, *meta])
        return on_line(*arrays, token_requests.reshape(-1, LANES), token, request_adapters.shape[0], n)
    return anywhere(*arrays, token_requests, meta)


def solution(mesh):
    in_specs = (
        P("groups", "tensor"),
        P("tensor", "store"),
        P(("groups", "store"), "tensor", None),
        P(("groups", "store"), "tensor", None),
        P("groups"),
        P("groups"),
        P("groups"),
        P("groups"),
    )
    out_specs = P(("groups", "tensor"), "store")
    return jax.shard_map(
        per_device, mesh=mesh, in_specs=in_specs, out_specs=out_specs, check_vma=False
    )
```

```python
import functools

import jax
import jax.numpy as jnp
from jax import lax
from jax.experimental import pallas as pl
from jax.experimental.pallas import tpu as pltpu
from jax.sharding import PartitionSpec as P

LINE = 4
LANES = 128
AHEAD = 3
PAIRS = 2
MIB = 1024 * 1024


def line_order(n):
    order = []
    for z in range(n):
        sends = [(t, z >= n // 2, n - 1 - t + z) for t in range(z, n - 1)]
        sends += [(t, z < n // 2, t - (n - 1 - z)) for t in range(n - 1 - z, n - 1)]
        order.append([block for _, _, block in sorted(sends)] + [z])
    return order


def first_divisor(size, choices):
    for choice in choices:
        if size % choice == 0:
            return choice
    return size


def after(token, *done):
    return lax.optimization_barrier((token, done))[0]


def params(mebibytes):
    return pltpu.CompilerParams(vmem_limit_bytes=mebibytes * MIB)


def small_cost():
    return pl.CostEstimate(flops=10**6, bytes_accessed=10**5, transcendentals=0)


def block_at(order, slot, place):
    picked = jnp.int32(order[0][slot])
    for z in range(1, len(order)):
        picked = jnp.where(place == z, order[z][slot], picked)
    return picked


def spans(requests_ref, count):
    requests = requests_ref[...]
    return [jnp.int32(0)] + [jnp.sum((requests <= r).astype(jnp.int32)) for r in range(count)]


class Meta:
    def __init__(self, ref, requests):
        self.ref, self.requests = ref, requests
        self.adapters = (ref.shape[0] - 2 - requests) // 2
        self.place, self.shard = ref[0], ref[1]

    def adapter(self, r):
        return self.ref[2 + r]

    def rank(self, r):
        return self.ref[2 + self.requests + self.adapter(r)]

    def local_slot(self, r, held):
        return self.ref[2 + self.requests + self.adapters + self.adapter(r)] - self.shard * held


def base_kernel(order, slots, half, held, request_count, *refs):
    count = len(slots)
    meta, refs = Meta(refs[0], request_count), refs[1:]
    if held:
        requests_ref, factor, refs = refs[0], refs[1], refs[2:]
    hidden, matrix, refs = refs[0], refs[1], refs[2:]
    outs, (rows, right, sums, sems), refs = refs[:count], refs[count : count + 4], refs[count + 4 :]
    steps, _, tile = rows.shape
    columns = outs[0].shape[1]
    block = rows.shape[1] // count
    first_rows = [pl.multiple_of(block_at(order, slot, meta.place) * block, block) for slot in slots]

    def depth_of(k):
        return pl.ds(pl.multiple_of(k * tile, tile), tile)

    def copies(k):
        moves = [
            (hidden.at[pl.ds(first_rows[i], block), depth_of(k)], rows.at[k, pl.ds(i * block, block), :])
            for i in range(count)
        ]
        moves.append((matrix.at[depth_of(k), pl.ds(half * columns, columns)], right.at[k]))
        return [pltpu.make_async_copy(a, b, sems.at[k, i]) for i, (a, b) in enumerate(moves)]

    if held:
        factors, inputs, factor_sems = refs
        width = factor.shape[2]

        def factor_copies(k, pair):
            return [
                pltpu.make_async_copy(
                    factor.at[2 * pair + i, depth_of(k), :],
                    factors.at[pair, k, :, pl.ds(i * width, width)],
                    factor_sems.at[k, 2 * pair + i],
                )
                for i in range(2)
            ]

    def start(k):
        for copy in copies(k):
            copy.start()

    def start_factors(k, pairs):
        for pair, used in enumerate(pairs):

            @pl.when(used)
            def _(pair=pair):
                for copy in factor_copies(k, pair):
                    copy.start()

    for k in range(min(AHEAD, steps)):
        start(k)
    used, blocks_using = [], []
    if held:
        bounds = spans(requests_ref, request_count)
        local = [meta.local_slot(r, held) for r in range(request_count)]
        for pair in range(held // 2):
            used_by = []
            for first in first_rows:
                wanted = jnp.bool_(False)
                for r, slot in enumerate(local):
                    here = jnp.maximum(bounds[r], first) < jnp.minimum(bounds[r + 1], first + block)
                    wanted = wanted | (here & (slot // 2 == pair) & (slot >= 0))
                used_by.append(wanted)
            blocks_using.append(used_by)
            used.append(functools.reduce(jnp.logical_or, used_by))
        for k in range(min(AHEAD, steps)):
            start_factors(k, used)
        inputs[...] = jnp.zeros_like(inputs)
    sums[...] = jnp.zeros_like(sums)

    def step(k, _):
        @pl.when(k + AHEAD < steps)
        def _():
            start(k + AHEAD)
            start_factors(k + AHEAD, used)

        for copy in copies(k):
            copy.wait()
        sums[...] += jnp.dot(rows[k], right[k], preferred_element_type=jnp.float32)
        for pair, wanted in enumerate(used):

            @pl.when(wanted)
            def _(pair=pair):
                for copy in factor_copies(k, pair):
                    copy.wait()

            for i, wanted_here in enumerate(blocks_using[pair]):

                @pl.when(wanted_here)
                def _(pair=pair, own=pl.ds(i * block, block)):
                    inputs[pair, own, :] += jnp.dot(
                        rows[k, own, :], factors[pair, k], preferred_element_type=jnp.float32
                    )

        return 0

    lax.fori_loop(0, steps, step, 0)
    for i in range(count):
        own = pl.ds(i * block, block)
        outs[i][:block, :] = sums[own, :].astype(jnp.bfloat16)
        if held:
            row = lax.broadcasted_iota(jnp.int32, (block, width), 0) + first_rows[i]
            column = lax.broadcasted_iota(jnp.int32, (block, width), 1)
            total = jnp.zeros((block, width), jnp.float32)
            for r, slot in enumerate(local):
                last = jnp.where((slot >= 0) & (slot < held), bounds[r + 1], 0)
                keep = (row >= bounds[r]) & (row < last) & (column < meta.rank(r))
                slot = jnp.clip(slot, 0, held - 1)
                lanes = pl.ds(pl.multiple_of(slot % 2 * width, width), width)
                total = jnp.where(keep, inputs[slot // 2, own, lanes], total)
            total = total.astype(jnp.bfloat16)
            per_row = columns // width
            for j in range(per_row):
                size = block // per_row
                outs[i][block:, j * width : (j + 1) * width] = total[j * size : (j + 1) * size, :]


def base_terms(meta, requests, request_count, hidden, matrix, factor, slots, half, n, grant):
    tokens, depth = hidden.shape
    block, columns = tokens // n, matrix.shape[1] // 2
    tile = first_divisor(depth, (1024, 512, 256, 128))
    steps = depth // tile
    count = len(slots)
    smem = pl.BlockSpec(memory_space=pltpu.SMEM)
    vmem = pl.BlockSpec(memory_space=pltpu.VMEM)
    hbm = pl.BlockSpec(memory_space=pltpu.HBM)
    held, out_rows = 0, block
    operands, in_specs = [meta], [smem]
    scratch = [
        pltpu.VMEM((steps, count * block, tile), jnp.bfloat16),
        pltpu.VMEM((steps, tile, columns), jnp.bfloat16),
        pltpu.VMEM((count * block, columns), jnp.float32),
        pltpu.SemaphoreType.DMA((steps, count + 1)),
    ]
    if factor is not None:
        held, _, width = factor.shape
        out_rows += block * width // columns
        operands, in_specs = [meta, requests, factor], [smem, vmem, hbm]
        scratch += [
            pltpu.VMEM((held // 2, steps, tile, 2 * width), jnp.bfloat16),
            pltpu.VMEM((held // 2, count * block, 2 * width), jnp.float32),
            pltpu.SemaphoreType.DMA((steps, held)),
        ]
    return pl.pallas_call(
        lambda *refs: base_kernel(line_order(n), slots, half, held, request_count, *refs),
        out_shape=[jax.ShapeDtypeStruct((out_rows, columns), jnp.bfloat16)] * count,
        in_specs=in_specs + [hbm, hbm],
        out_specs=[vmem] * count,
        scratch_shapes=scratch,
        compiler_params=params(grant),
        cost_estimate=small_cost(),
        name="base_terms",
    )(*operands, hidden, matrix)


def select_rows_kernel(request_count, meta_ref, factor, kept, sent):
    meta = Meta(meta_ref, request_count)
    held = factor.shape[0]
    width = factor.shape[2] // (2 * PAIRS)
    side = meta.shard % 2
    for r in range(request_count):
        slot = meta.local_slot(r, held)
        owned = (slot >= 0) & (slot < held)
        slot = jnp.clip(slot, 0, held - 1)
        for out, core in ((kept, side), (sent, 1 - side)):
            for i in range(PAIRS):
                rows = factor[slot, :, pl.ds(pl.multiple_of((2 * i + core) * width, LANES), width)]
                out[i, r] = jnp.where(owned, rows, jnp.zeros_like(rows))


def select_rows(meta, request_count, factor):
    _, rank_rows, model_width = factor.shape
    smem = pl.BlockSpec(memory_space=pltpu.SMEM)
    vmem = pl.BlockSpec(memory_space=pltpu.VMEM)
    shape = (PAIRS, request_count, rank_rows, model_width // (2 * PAIRS))
    out = jax.ShapeDtypeStruct(shape, factor.dtype)
    return pl.pallas_call(
        lambda *refs: select_rows_kernel(request_count, *refs),
        out_shape=[out, out],
        in_specs=[smem, vmem],
        out_specs=[vmem, vmem],
        compiler_params=params(16),
        cost_estimate=small_cost(),
        name="select_rows",
    )(meta, factor)


def expanded_inputs(meta, requests_ref, lora_ref):
    block, width = lora_ref.shape
    row = lax.broadcasted_iota(jnp.int32, (block, width), 0) + meta.place * block
    lora = lora_ref[...].astype(jnp.float32)
    bounds = spans(requests_ref, meta.requests)
    parts = []
    for r in range(meta.requests):
        scale = 0.25 * width / meta.rank(r).astype(jnp.float32)
        keep = (row >= bounds[r]) & (row < bounds[r + 1])
        parts.append(jnp.where(keep, lora * scale, 0.0).astype(jnp.bfloat16))
    return jnp.concatenate(parts, axis=1)


def finish_kernel(items, n, *refs):
    meta_ref, requests_ref, lora_ref, refs = refs[0], refs[1], refs[2], refs[3:]
    count = len(items)
    pieces, refs = refs[:count], refs[count:]
    added, out, rows = refs[:-2], refs[-2], refs[-1]
    requests, rank_rows, width = pieces[0].shape
    meta = Meta(meta_ref, requests)
    place = meta.place
    rank = n * rank_rows
    for piece, (edge, item) in zip(pieces, items):
        if edge is None:
            targets = [(place >= 0, place)]
        else:
            targets = [(place == edge + 1, item), (place == n - 2 - edge, n - 1 - item)]
        for here, k in targets:

            @pl.when(here)
            def _(piece=piece, k=k):
                for r in range(requests):
                    first = pl.multiple_of(r * rank + k * rank_rows, rank_rows)
                    rows[pl.ds(first, rank_rows), :] = piece[r]

    expanded = expanded_inputs(meta, requests_ref, lora_ref)
    block = lora_ref.shape[0]
    half = width // 2
    for c in range(2):
        columns = slice(c * half, (c + 1) * half)
        total = jnp.dot(expanded, rows[:, columns], preferred_element_type=jnp.float32)
        for ref, which in zip(added, (0, 0, 0, 0, 1, 1)):
            if which == c:
                total += ref[:block, :].astype(jnp.float32)
        out[:, columns] = total.astype(out.dtype)


def finish(meta, requests, lora, items, pieces, added, n):
    smem = pl.BlockSpec(memory_space=pltpu.SMEM)
    vmem = pl.BlockSpec(memory_space=pltpu.VMEM)
    count, rank_rows, width = pieces[0].shape
    return pl.pallas_call(
        lambda *refs: finish_kernel(items, n, *refs),
        out_shape=jax.ShapeDtypeStruct((lora.shape[0], width), jnp.bfloat16),
        in_specs=[smem] + [vmem] * (2 + len(pieces) + len(added)),
        out_specs=vmem,
        scratch_shapes=[pltpu.VMEM((count * n * rank_rows, width), jnp.bfloat16)],
        compiler_params=params(20),
        cost_estimate=small_cost(),
        name="finish",
    )(meta, requests, lora, *pieces, *added)


def add_last_kernel(total, up, down, out):
    half = up.shape[1]
    out[:, :half] = total[:, :half]
    last = total[:, half:].astype(jnp.float32) + up[...].astype(jnp.float32) + down[...].astype(jnp.float32)
    out[:, half:] = last.astype(out.dtype)


def add_last(total, up, down):
    vmem = pl.BlockSpec(memory_space=pltpu.VMEM)
    return pl.pallas_call(
        add_last_kernel,
        out_shape=jax.ShapeDtypeStruct(total.shape, total.dtype),
        in_specs=[vmem] * 3,
        out_specs=vmem,
        compiler_params=params(12),
        cost_estimate=small_cost(),
        name="add_last",
    )(total, up, down)


def swap(x, axis, bit):
    return lax.ppermute(x, axis, [(i, i ^ bit) for i in range(lax.axis_size(axis))])


def bits_of(size):
    return [1 << i for i in range(size.bit_length() - 1)]


def along_edge(x, edge):
    n = lax.axis_size("tensor")
    return lax.ppermute(x, "tensor", [(edge, edge + 1), (n - 1 - edge, n - 2 - edge)])


def on_line(hidden, matrix, input_factor, output_factor, requests, token, request_count, n):
    shard = lax.axis_index("store")

    def base(token, slots, half, grant):
        factor = input_factor if half == 0 else None
        return base_terms(token, requests, request_count, hidden, matrix, factor, slots, half, n, grant)

    def hop(token, term, came):
        term, came, _ = lax.optimization_barrier((term, came, token))
        return (term.astype(jnp.float32) + came.astype(jnp.float32)).astype(jnp.bfloat16)

    def send(x, edge, token):
        return along_edge(after(x, token), edge)

    kept, sent = select_rows(token, request_count, output_factor)
    token = after(token, kept, sent)
    swapped = swap(sent, "store", 1)
    (s00,) = base(token, [0], 0, 58)
    token = after(token, s00, swapped)
    a00 = along_edge(s00, 0)
    side = shard // 2 % 2
    kept, swapped, _ = lax.optimization_barrier((kept, swapped, token))
    outgoing = kept[1 - side] + swapped[1 - side]
    rows = kept[side] + swapped[side]
    token = after(token, outgoing, rows)
    swapped = swap(outgoing, "store", 2)
    s01, s11 = base(token, [0, 1], 1, 50)

    token = after(token, s01)
    a01 = send(s01, 0, token)
    token, swapped = lax.optimization_barrier((token, swapped))
    rows = rows + swapped
    token, a00 = lax.optimization_barrier((after(token, rows), a00))
    r11 = along_edge(rows, 1)
    b10 = hop(token, s00, a00)
    token = after(token, b10)
    b10 = along_edge(b10, 1)
    r22 = send(rows, 2, token)
    a11 = send(s11, 0, token)
    r00 = send(rows, 0, token)
    s10, s20, s30 = base(token, [1, 2, 3], 0, 42)

    token = after(token, s10)
    a10 = send(s10, 0, token)
    token = after(token, a01, b10, r11, r22)
    b11 = hop(token, s01, a01)
    c20 = hop(token, s20, b10)
    token = after(token, b11, c20)
    b11 = along_edge(b11, 1)
    c20 = along_edge(c20, 2)
    a20 = send(s20, 0, token)
    token = after(token, r00)
    r10 = send(r00, 1, token)
    r21 = send(r11, 2, token)
    s21, s31 = base(token, [2, 3], 1, 50)

    token = after(token, s21, a10, a11, b11, c20, r10, r21)
    a21 = send(s21, 0, token)
    b20 = hop(token, s10, a10)
    token = after(token, b20)
    b20 = along_edge(b20, 1)
    r20 = send(r10, 2, token)
    c21 = hop(token, s21, b11)
    token = after(token, c21)
    c21 = along_edge(c21, 2)
    b21 = hop(token, s11, a11)
    token = after(token, b21)
    b21 = along_edge(b21, 1)

    block = hidden.shape[0] // n
    width = input_factor.shape[2]
    token = after(token, a20)
    arrived = lax.optimization_barrier(([s30, a20, b20, c20], token))[0]
    lora = sum(x[block:].astype(jnp.float32) for x in arrived).astype(jnp.bfloat16)
    lora = lora.reshape(lora.shape[0], -1, width).swapaxes(0, 1).reshape(block, width)
    lora = lora + swap(lora, "store", 1)
    lora = lora + swap(lora, "store", 2)
    items = [(None, None), (0, 0), (1, 1), (1, 0), (2, 2), (2, 1), (2, 0)]
    out = finish(token, requests, lora, items, [rows, r00, r11, r10, r22, r21, r20], arrived + [s31, c21], n)
    return add_last(out, a21, b21)


def anywhere(hidden, matrix, input_factor, output_factor, token_requests, meta):
    request_adapters, ranks, slots = meta
    held = input_factor.shape[0]
    width = input_factor.shape[2]
    rank, slot = ranks[request_adapters], slots[request_adapters]
    owned = slot // held == lax.axis_index("store")
    chosen = token_requests[:, None] == jnp.arange(request_adapters.shape[0])[None, :]
    lora = jnp.zeros((hidden.shape[0], width), jnp.float32)
    for r in range(request_adapters.shape[0]):
        product = jnp.dot(hidden, input_factor[slot[r] % held], preferred_element_type=jnp.float32)
        keep = (chosen[:, r] & owned[r])[:, None] & (jnp.arange(width) < rank[r])[None, :]
        lora = jnp.where(keep, product, lora)
    lora = lax.psum_scatter(lora.astype(jnp.bfloat16), "tensor", scatter_dimension=1, tiled=True)
    lora = lax.psum(lora, "store").astype(jnp.float32)
    rows = jnp.where(owned[:, None, None], output_factor[slot % held], jnp.zeros((), output_factor.dtype))
    rows = lax.psum_scatter(rows, "store", scatter_dimension=2, tiled=True)
    weights = jnp.where(chosen, 0.25 * width / rank.astype(jnp.float32)[None, :], 0.0)
    expanded = (weights[:, :, None] * lora[:, None, :]).reshape(hidden.shape[0], -1).astype(jnp.bfloat16)
    term = jnp.dot(hidden, matrix, preferred_element_type=jnp.float32)
    term += jnp.dot(expanded, rows.reshape(-1, rows.shape[2]), preferred_element_type=jnp.float32)
    return lax.psum_scatter(term.astype(jnp.bfloat16), "tensor", scatter_dimension=0, tiled=True)


def per_device(
    hidden_activations,
    down_matrix,
    adapter_input_factor,
    adapter_output_factor,
    token_requests,
    request_adapters,
    adapter_ranks,
    adapter_store_slot,
):
    n = lax.axis_size("tensor")
    meta = (request_adapters, adapter_ranks, adapter_store_slot)
    arrays = (hidden_activations, down_matrix, adapter_input_factor, adapter_output_factor)
    if n == LINE and lax.axis_size("store") == 2 * PAIRS and adapter_input_factor.shape[0] % 2 == 0:
        place = jnp.stack([lax.axis_index("tensor"), lax.axis_index("store")]).astype(jnp.int32)
        token = jnp.concatenate([place, *meta])
        return on_line(*arrays, token_requests.reshape(-1, LANES), token, request_adapters.shape[0], n)
    return anywhere(*arrays, token_requests, meta)


def solution(mesh):
    in_specs = (
        P("groups", "tensor"),
        P("tensor", "store"),
        P(("groups", "store"), "tensor", None),
        P(("groups", "store"), "tensor", None),
        P("groups"),
        P("groups"),
        P("groups"),
        P("groups"),
    )
    out_specs = P(("groups", "tensor"), "store")
    return jax.shard_map(
        per_device, mesh=mesh, in_specs=in_specs, out_specs=out_specs, check_vma=False
    )
```

```python
import functools

import jax
import jax.numpy as jnp
from jax import lax
from jax.experimental import pallas as pl
from jax.experimental.pallas import tpu as pltpu
from jax.sharding import PartitionSpec as P

LINE = 4
LANES = 128
AHEAD = 3
PAIRS = 2
MIB = 1024 * 1024


def line_order(n):
    order = []
    for z in range(n):
        sends = [(t, z >= n // 2, n - 1 - t + z) for t in range(z, n - 1)]
        sends += [(t, z < n // 2, t - (n - 1 - z)) for t in range(n - 1 - z, n - 1)]
        order.append([block for _, _, block in sorted(sends)] + [z])
    return order


def first_divisor(size, choices):
    for choice in choices:
        if size % choice == 0:
            return choice
    return size


def after(token, *done):
    return lax.optimization_barrier((token, done))[0]


def params(mebibytes):
    return pltpu.CompilerParams(vmem_limit_bytes=mebibytes * MIB)


def small_cost():
    return pl.CostEstimate(flops=10**6, bytes_accessed=10**5, transcendentals=0)


def block_at(order, slot, place):
    picked = jnp.int32(order[0][slot])
    for z in range(1, len(order)):
        picked = jnp.where(place == z, order[z][slot], picked)
    return picked


def spans(requests_ref, count):
    requests = requests_ref[...]
    return [jnp.int32(0)] + [jnp.sum((requests <= r).astype(jnp.int32)) for r in range(count)]


class Meta:
    def __init__(self, ref, requests):
        self.ref, self.requests = ref, requests
        self.adapters = (ref.shape[0] - 2 - requests) // 2
        self.place, self.shard = ref[0], ref[1]

    def adapter(self, r):
        return self.ref[2 + r]

    def rank(self, r):
        return self.ref[2 + self.requests + self.adapter(r)]

    def local_slot(self, r, held):
        return self.ref[2 + self.requests + self.adapters + self.adapter(r)] - self.shard * held


def base_kernel(order, groups, half, held, request_count, *refs):
    slots = [slot for group in groups for slot in group]
    places = [(g, i) for g, group in enumerate(groups) for i in range(len(group))]
    count = len(slots)
    meta, refs = Meta(refs[0], request_count), refs[1:]
    if held:
        requests_ref, factor, refs = refs[0], refs[1], refs[2:]
    hidden, matrix, refs = refs[0], refs[1], refs[2:]
    outs, refs = refs[: len(groups)], refs[len(groups) :]
    (rows, right, sums, sems), refs = refs[:4], refs[4:]
    steps, _, tile = rows.shape
    columns = outs[0].shape[1]
    block = rows.shape[1] // count
    first_rows = [pl.multiple_of(block_at(order, slot, meta.place) * block, block) for slot in slots]

    def depth_of(k):
        return pl.ds(pl.multiple_of(k * tile, tile), tile)

    def copies(k):
        moves = [
            (hidden.at[pl.ds(first_rows[i], block), depth_of(k)], rows.at[k, pl.ds(i * block, block), :])
            for i in range(count)
        ]
        moves.append((matrix.at[depth_of(k), pl.ds(half * columns, columns)], right.at[k]))
        return [pltpu.make_async_copy(a, b, sems.at[k, i]) for i, (a, b) in enumerate(moves)]

    if held:
        factors, inputs, factor_sems = refs
        width = factor.shape[2]

        def factor_copies(k, pair):
            return [
                pltpu.make_async_copy(
                    factor.at[2 * pair + i, depth_of(k), :],
                    factors.at[pair, k, :, pl.ds(i * width, width)],
                    factor_sems.at[k, 2 * pair + i],
                )
                for i in range(2)
            ]

    def start(k):
        for copy in copies(k):
            copy.start()

    def start_factors(k, pairs):
        for pair, used in enumerate(pairs):

            @pl.when(used)
            def _(pair=pair):
                for copy in factor_copies(k, pair):
                    copy.start()

    for k in range(min(AHEAD, steps)):
        start(k)
    used, blocks_using = [], []
    if held:
        bounds = spans(requests_ref, request_count)
        local = [meta.local_slot(r, held) for r in range(request_count)]
        for pair in range(held // 2):
            used_by = []
            for first in first_rows:
                wanted = jnp.bool_(False)
                for r, slot in enumerate(local):
                    here = jnp.maximum(bounds[r], first) < jnp.minimum(bounds[r + 1], first + block)
                    wanted = wanted | (here & (slot // 2 == pair) & (slot >= 0))
                used_by.append(wanted)
            blocks_using.append(used_by)
            used.append(functools.reduce(jnp.logical_or, used_by))
        for k in range(min(AHEAD, steps)):
            start_factors(k, used)
        inputs[...] = jnp.zeros_like(inputs)
    sums[...] = jnp.zeros_like(sums)

    def step(k, _):
        @pl.when(k + AHEAD < steps)
        def _():
            start(k + AHEAD)
            start_factors(k + AHEAD, used)

        for copy in copies(k):
            copy.wait()
        sums[...] += jnp.dot(rows[k], right[k], preferred_element_type=jnp.float32)
        for pair, wanted in enumerate(used):

            @pl.when(wanted)
            def _(pair=pair):
                for copy in factor_copies(k, pair):
                    copy.wait()

            for i, wanted_here in enumerate(blocks_using[pair]):

                @pl.when(wanted_here)
                def _(pair=pair, own=pl.ds(i * block, block)):
                    inputs[pair, own, :] += jnp.dot(
                        rows[k, own, :], factors[pair, k], preferred_element_type=jnp.float32
                    )

        return 0

    lax.fori_loop(0, steps, step, 0)
    piece = outs[0].shape[0] // len(groups[0])
    for i, (group, position) in enumerate(places):
        own = pl.ds(i * block, block)
        out, top = outs[group], position * piece
        out[top : top + block, :] = sums[own, :].astype(jnp.bfloat16)
        if held:
            row = lax.broadcasted_iota(jnp.int32, (block, width), 0) + first_rows[i]
            column = lax.broadcasted_iota(jnp.int32, (block, width), 1)
            total = jnp.zeros((block, width), jnp.float32)
            for r, slot in enumerate(local):
                last = jnp.where((slot >= 0) & (slot < held), bounds[r + 1], 0)
                keep = (row >= bounds[r]) & (row < last) & (column < meta.rank(r))
                slot = jnp.clip(slot, 0, held - 1)
                lanes = pl.ds(pl.multiple_of(slot % 2 * width, width), width)
                total = jnp.where(keep, inputs[slot // 2, own, lanes], total)
            total = total.astype(jnp.bfloat16)
            size = block * width // columns
            for j in range(columns // width):
                lanes = slice(j * width, (j + 1) * width)
                out[top + block : top + block + size, lanes] = total[j * size : (j + 1) * size, :]


def base_terms(meta, requests, request_count, hidden, matrix, factor, groups, half, n, grant):
    tokens, depth = hidden.shape
    block, columns = tokens // n, matrix.shape[1] // 2
    tile = first_divisor(depth, (1024, 512, 256, 128))
    steps = depth // tile
    count = sum(len(group) for group in groups)
    smem = pl.BlockSpec(memory_space=pltpu.SMEM)
    vmem = pl.BlockSpec(memory_space=pltpu.VMEM)
    hbm = pl.BlockSpec(memory_space=pltpu.HBM)
    held, out_rows = 0, block
    operands, in_specs = [meta], [smem]
    scratch = [
        pltpu.VMEM((steps, count * block, tile), jnp.bfloat16),
        pltpu.VMEM((steps, tile, columns), jnp.bfloat16),
        pltpu.VMEM((count * block, columns), jnp.float32),
        pltpu.SemaphoreType.DMA((steps, count + 1)),
    ]
    if factor is not None:
        held, _, width = factor.shape
        out_rows += block * width // columns
        operands, in_specs = [meta, requests, factor], [smem, vmem, hbm]
        scratch += [
            pltpu.VMEM((held // 2, steps, tile, 2 * width), jnp.bfloat16),
            pltpu.VMEM((held // 2, count * block, 2 * width), jnp.float32),
            pltpu.SemaphoreType.DMA((steps, held)),
        ]
    return pl.pallas_call(
        lambda *refs: base_kernel(line_order(n), groups, half, held, request_count, *refs),
        out_shape=[jax.ShapeDtypeStruct((len(group) * out_rows, columns), jnp.bfloat16) for group in groups],
        in_specs=in_specs + [hbm, hbm],
        out_specs=[vmem] * len(groups),
        scratch_shapes=scratch,
        compiler_params=params(grant),
        cost_estimate=small_cost(),
        name="base_terms",
    )(*operands, hidden, matrix)


def select_rows_kernel(request_count, meta_ref, factor, kept, sent):
    meta = Meta(meta_ref, request_count)
    held, rank_rows, _ = factor.shape
    width = factor.shape[2] // (2 * PAIRS)
    side = meta.shard % 2
    for r in range(request_count):
        slot = meta.local_slot(r, held)
        owned = (slot >= 0) & (slot < held)
        slot = jnp.clip(slot, 0, held - 1)
        for out, core in ((kept, side), (sent, 1 - side)):
            for i in range(PAIRS):
                for c in range(2):
                    first = (2 * i + core) * width + c * (width // 2)
                    rows = factor[slot, :, pl.ds(pl.multiple_of(first, LANES), width // 2)]
                    top = (c * request_count + r) * rank_rows
                    out[i, top : top + rank_rows, :] = jnp.where(owned, rows, jnp.zeros_like(rows))


def select_rows(meta, request_count, factor):
    _, rank_rows, model_width = factor.shape
    smem = pl.BlockSpec(memory_space=pltpu.SMEM)
    vmem = pl.BlockSpec(memory_space=pltpu.VMEM)
    shape = (PAIRS, 2 * request_count * rank_rows, model_width // (4 * PAIRS))
    out = jax.ShapeDtypeStruct(shape, factor.dtype)
    return pl.pallas_call(
        lambda *refs: select_rows_kernel(request_count, *refs),
        out_shape=[out, out],
        in_specs=[smem, vmem],
        out_specs=[vmem, vmem],
        compiler_params=params(16),
        cost_estimate=small_cost(),
        name="select_rows",
    )(meta, factor)


def expanded_inputs(meta, requests_ref, lora_ref):
    block, width = lora_ref.shape
    row = lax.broadcasted_iota(jnp.int32, (block, width), 0) + meta.place * block
    lora = lora_ref[...].astype(jnp.float32)
    bounds = spans(requests_ref, meta.requests)
    parts = []
    for r in range(meta.requests):
        scale = 0.25 * width / meta.rank(r).astype(jnp.float32)
        keep = (row >= bounds[r]) & (row < bounds[r + 1])
        parts.append(jnp.where(keep, lora * scale, 0.0).astype(jnp.bfloat16))
    return jnp.concatenate(parts, axis=1)


def finish_kernel(items, added, requests, rank_rows, n, *refs):
    meta_ref, requests_ref, lora_ref, refs = refs[0], refs[1], refs[2], refs[3:]
    arrays, out, rows = refs[:-2], refs[-2], refs[-1]
    meta = Meta(meta_ref, requests)
    rank = n * rank_rows
    half = out.shape[1] // 2
    for index, top, targets in items:
        for place, k in targets:

            @pl.when(meta.place == place)
            def _(piece=arrays[index], top=top, k=k):
                for r in range(requests):
                    first = r * rank + k * rank_rows
                    for c in range(2):
                        start = top + (c * requests + r) * rank_rows
                        rows[first : first + rank_rows, c * half : (c + 1) * half] = piece[start : start + rank_rows, :]

    expanded = expanded_inputs(meta, requests_ref, lora_ref)
    block = lora_ref.shape[0]
    for c in range(2):
        columns = slice(c * half, (c + 1) * half)
        total = jnp.dot(expanded, rows[:, columns], preferred_element_type=jnp.float32)
        for index, top, which in added:
            if which == c:
                total += arrays[index][top : top + block, :].astype(jnp.float32)
        out[:, columns] = total.astype(out.dtype)


def finish(meta, requests, lora, arrays, items, added, request_count, rank_rows, n):
    smem = pl.BlockSpec(memory_space=pltpu.SMEM)
    vmem = pl.BlockSpec(memory_space=pltpu.VMEM)
    width = 2 * arrays[0].shape[1]
    return pl.pallas_call(
        lambda *refs: finish_kernel(items, added, request_count, rank_rows, n, *refs),
        out_shape=jax.ShapeDtypeStruct((lora.shape[0], width), jnp.bfloat16),
        in_specs=[smem] + [vmem] * (2 + len(arrays)),
        out_specs=vmem,
        scratch_shapes=[pltpu.VMEM((request_count * n * rank_rows, width), jnp.bfloat16)],
        compiler_params=params(20),
        cost_estimate=small_cost(),
        name="finish",
    )(meta, requests, lora, *arrays)


def join_kernel(count, term_top, came_top, under_top, term, came, *refs):
    out = refs[-1]
    total = term[term_top : term_top + count, :].astype(jnp.float32)
    total += came[came_top : came_top + count, :].astype(jnp.float32)
    out[:count, :] = total.astype(out.dtype)
    if len(refs) > 1:
        under = refs[0]
        out[count:, :] = under[under_top : under_top + out.shape[0] - count, :]


def join(token, count, term, term_top, came, came_top, under=None, under_top=0, under_count=0):
    arrays = [term, came] + ([] if under is None else [under])
    arrays = lax.optimization_barrier((arrays, token))[0]
    vmem = pl.BlockSpec(memory_space=pltpu.VMEM)
    return pl.pallas_call(
        lambda *refs: join_kernel(count, term_top, came_top, under_top, *refs),
        out_shape=jax.ShapeDtypeStruct((count + under_count, term.shape[1]), term.dtype),
        in_specs=[vmem] * len(arrays),
        out_specs=vmem,
        compiler_params=params(12),
        cost_estimate=small_cost(),
        name="join",
    )(*arrays)


def add_last_kernel(total, up, down, out):
    half = up.shape[1]
    out[:, :half] = total[:, :half]
    last = total[:, half:].astype(jnp.float32) + up[...].astype(jnp.float32) + down[...].astype(jnp.float32)
    out[:, half:] = last.astype(out.dtype)


def add_last(total, up, down):
    vmem = pl.BlockSpec(memory_space=pltpu.VMEM)
    return pl.pallas_call(
        add_last_kernel,
        out_shape=jax.ShapeDtypeStruct(total.shape, total.dtype),
        in_specs=[vmem] * 3,
        out_specs=vmem,
        compiler_params=params(12),
        cost_estimate=small_cost(),
        name="add_last",
    )(total, up, down)


def swap(x, axis, bit):
    return lax.ppermute(x, axis, [(i, i ^ bit) for i in range(lax.axis_size(axis))])


def bits_of(size):
    return [1 << i for i in range(size.bit_length() - 1)]


def along_edge(x, edge):
    n = lax.axis_size("tensor")
    return lax.ppermute(x, "tensor", [(edge, edge + 1), (n - 1 - edge, n - 2 - edge)])


def on_line(hidden, matrix, input_factor, output_factor, requests, token, request_count, n):
    shard = lax.axis_index("store")
    block = hidden.shape[0] // n
    width = input_factor.shape[2]
    rank_rows = output_factor.shape[1]
    piece = block + block * width // (matrix.shape[1] // 2)
    bundle = 2 * request_count * rank_rows

    def base(token, groups, half, grant):
        factor = input_factor if half == 0 else None
        return base_terms(token, requests, request_count, hidden, matrix, factor, groups, half, n, grant)

    def send(x, edge, token):
        return along_edge(after(x, token), edge)

    kept, sent = select_rows(token, request_count, output_factor)
    token = after(token, kept, sent)
    swapped = swap(sent, "store", 1)
    (s00,) = base(token, [[0]], 0, 58)
    token = after(token, s00, swapped)
    e0_1 = along_edge(s00, 0)
    side = shard // 2 % 2
    kept, swapped, _ = lax.optimization_barrier((kept, swapped, token))
    outgoing = kept[1 - side] + swapped[1 - side]
    rows = kept[side] + swapped[side]
    token = after(token, outgoing, rows)
    swapped = swap(outgoing, "store", 2)
    (s01_s11,) = base(token, [[0, 1]], 1, 50)

    token = after(token, s01_s11)
    e0_2 = send(s01_s11, 0, token)
    token, swapped = lax.optimization_barrier((token, swapped))
    rows = rows + swapped
    token = after(token, rows)
    near = lax.ppermute(rows, "tensor", [(0, 1), (n - 1, n - 2), (1, 0), (n - 2, n - 1)])
    b10 = join(token, piece, s00, 0, e0_1, 0, rows, 0, bundle)
    token = after(token, b10)
    e1_2 = along_edge(b10, 1)
    s10_s20, s30 = base(token, [[1, 2], [3]], 0, 42)

    token = after(token, s10_s20)
    e0_3 = send(s10_s20, 0, token)
    token = after(token, e0_2, near, e1_2)
    b11 = join(token, block, s01_s11, 0, e0_2, 0, near, 0, bundle)
    token = after(token, b11)
    e1_3 = along_edge(b11, 1)
    c20 = join(token, piece, s10_s20, piece, e1_2, 0, e1_2, piece, bundle)
    token = after(token, c20)
    e2_3 = along_edge(c20, 2)
    s21, s31 = base(token, [[2], [3]], 1, 50)

    token = after(token, s21)
    e0_4 = send(s21, 0, token)
    token = after(token, e0_3, e1_3, e2_3)
    b20 = join(token, piece, s10_s20, 0, e0_3, 0)
    token = after(token, b20)
    e1_4 = along_edge(b20, 1)
    c21 = join(token, block, s21, 0, e1_3, 0, e1_3, block, bundle)
    token = after(token, c21)
    e2_4 = along_edge(c21, 2)
    b21 = join(token, block, s01_s11, block, e0_2, block)
    token = after(token, b21)
    e1_5 = along_edge(b21, 1)

    lora = s30[block:].astype(jnp.float32) + e0_3[piece + block :].astype(jnp.float32)
    lora += e1_4[block:].astype(jnp.float32) + e2_3[block:piece].astype(jnp.float32)
    lora = lora.astype(jnp.bfloat16).reshape(piece - block, -1, width).swapaxes(0, 1).reshape(block, width)
    lora = lora + swap(lora, "store", 1)
    lora = lora + swap(lora, "store", 2)
    arrays = [s30, s31, rows, near, e1_2, e1_3, e2_3, e2_4, e0_3, e1_4]
    items = [
        (2, 0, [(z, z) for z in range(n)]),
        (3, 0, [(0, 1), (1, 0), (2, 3), (3, 2)]),
        (4, piece, [(1, 2), (2, 1)]),
        (5, block, [(1, 3), (2, 0)]),
        (6, piece, [(0, 2), (3, 1)]),
        (7, block, [(0, 3), (3, 0)]),
    ]
    added = [(0, 0, 0), (8, piece, 0), (9, 0, 0), (6, 0, 0), (1, 0, 1), (7, 0, 1)]
    out = finish(token, requests, lora, arrays, items, added, request_count, rank_rows, n)
    return add_last(out, e0_4, e1_5)


def anywhere(hidden, matrix, input_factor, output_factor, token_requests, meta):
    request_adapters, ranks, slots = meta
    held = input_factor.shape[0]
    width = input_factor.shape[2]
    rank, slot = ranks[request_adapters], slots[request_adapters]
    owned = slot // held == lax.axis_index("store")
    chosen = token_requests[:, None] == jnp.arange(request_adapters.shape[0])[None, :]
    lora = jnp.zeros((hidden.shape[0], width), jnp.float32)
    for r in range(request_adapters.shape[0]):
        product = jnp.dot(hidden, input_factor[slot[r] % held], preferred_element_type=jnp.float32)
        keep = (chosen[:, r] & owned[r])[:, None] & (jnp.arange(width) < rank[r])[None, :]
        lora = jnp.where(keep, product, lora)
    lora = lax.psum_scatter(lora.astype(jnp.bfloat16), "tensor", scatter_dimension=1, tiled=True)
    lora = lax.psum(lora, "store").astype(jnp.float32)
    rows = jnp.where(owned[:, None, None], output_factor[slot % held], jnp.zeros((), output_factor.dtype))
    rows = lax.psum_scatter(rows, "store", scatter_dimension=2, tiled=True)
    weights = jnp.where(chosen, 0.25 * width / rank.astype(jnp.float32)[None, :], 0.0)
    expanded = (weights[:, :, None] * lora[:, None, :]).reshape(hidden.shape[0], -1).astype(jnp.bfloat16)
    term = jnp.dot(hidden, matrix, preferred_element_type=jnp.float32)
    term += jnp.dot(expanded, rows.reshape(-1, rows.shape[2]), preferred_element_type=jnp.float32)
    return lax.psum_scatter(term.astype(jnp.bfloat16), "tensor", scatter_dimension=0, tiled=True)


def per_device(
    hidden_activations,
    down_matrix,
    adapter_input_factor,
    adapter_output_factor,
    token_requests,
    request_adapters,
    adapter_ranks,
    adapter_store_slot,
):
    n = lax.axis_size("tensor")
    meta = (request_adapters, adapter_ranks, adapter_store_slot)
    arrays = (hidden_activations, down_matrix, adapter_input_factor, adapter_output_factor)
    if n == LINE and lax.axis_size("store") == 2 * PAIRS and adapter_input_factor.shape[0] % 2 == 0:
        place = jnp.stack([lax.axis_index("tensor"), lax.axis_index("store")]).astype(jnp.int32)
        token = jnp.concatenate([place, *meta])
        return on_line(*arrays, token_requests.reshape(-1, LANES), token, request_adapters.shape[0], n)
    return anywhere(*arrays, token_requests, meta)


def solution(mesh):
    in_specs = (
        P("groups", "tensor"),
        P("tensor", "store"),
        P(("groups", "store"), "tensor", None),
        P(("groups", "store"), "tensor", None),
        P("groups"),
        P("groups"),
        P("groups"),
        P("groups"),
    )
    out_specs = P(("groups", "tensor"), "store")
    return jax.shard_map(
        per_device, mesh=mesh, in_specs=in_specs, out_specs=out_specs, check_vma=False
    )
```

```python
import functools

import jax
import jax.numpy as jnp
from jax import lax
from jax.experimental import pallas as pl
from jax.experimental.pallas import tpu as pltpu
from jax.sharding import PartitionSpec as P

LINE = 4
LANES = 128
AHEAD = 3
PAIRS = 2
MIB = 1024 * 1024


def line_order(n):
    order = []
    for z in range(n):
        sends = [(t, z >= n // 2, n - 1 - t + z) for t in range(z, n - 1)]
        sends += [(t, z < n // 2, t - (n - 1 - z)) for t in range(n - 1 - z, n - 1)]
        order.append([block for _, _, block in sorted(sends)] + [z])
    return order


def first_divisor(size, choices):
    for choice in choices:
        if size % choice == 0:
            return choice
    return size


def after(token, *done):
    return lax.optimization_barrier((token, done))[0]


def params(mebibytes):
    return pltpu.CompilerParams(vmem_limit_bytes=mebibytes * MIB)


def small_cost():
    return pl.CostEstimate(flops=10**6, bytes_accessed=10**5, transcendentals=0)


def block_at(order, slot, place):
    picked = jnp.int32(order[0][slot])
    for z in range(1, len(order)):
        picked = jnp.where(place == z, order[z][slot], picked)
    return picked


def spans(requests_ref, count):
    requests = requests_ref[...]
    return [jnp.int32(0)] + [jnp.sum((requests <= r).astype(jnp.int32)) for r in range(count)]


class Meta:
    def __init__(self, ref, requests):
        self.ref, self.requests = ref, requests
        self.adapters = (ref.shape[0] - 2 - requests) // 2
        self.place, self.shard = ref[0], ref[1]

    def adapter(self, r):
        return self.ref[2 + r]

    def rank(self, r):
        return self.ref[2 + self.requests + self.adapter(r)]

    def local_slot(self, r, held):
        return self.ref[2 + self.requests + self.adapters + self.adapter(r)] - self.shard * held


def base_kernel(order, groups, half, held, request_count, piece, handed_on, *refs):
    slots = [slot for group in groups for slot in group]
    places = [(g, i) for g, group in enumerate(groups) for i in range(len(group))]
    count = len(slots)
    meta, refs = Meta(refs[0], request_count), refs[1:]
    if held:
        requests_ref, factor, refs = refs[0], refs[1], refs[2:]
    hidden, matrix, refs = refs[0], refs[1], refs[2:]
    under, refs = (refs[0], refs[1:]) if handed_on else (None, refs)
    outs, refs = refs[: len(groups)], refs[len(groups) :]
    (rows, right, sums, sems), refs = refs[:4], refs[4:]
    steps, _, tile = rows.shape
    columns = outs[0].shape[1]
    block = rows.shape[1] // count
    first_rows = [pl.multiple_of(block_at(order, slot, meta.place) * block, block) for slot in slots]

    def depth_of(k):
        return pl.ds(pl.multiple_of(k * tile, tile), tile)

    def copies(k):
        moves = [
            (hidden.at[pl.ds(first_rows[i], block), depth_of(k)], rows.at[k, pl.ds(i * block, block), :])
            for i in range(count)
        ]
        moves.append((matrix.at[depth_of(k), pl.ds(half * columns, columns)], right.at[k]))
        return [pltpu.make_async_copy(a, b, sems.at[k, i]) for i, (a, b) in enumerate(moves)]

    if held:
        factors, inputs, factor_sems = refs
        width = factor.shape[2]

        def factor_copies(k, pair):
            return [
                pltpu.make_async_copy(
                    factor.at[2 * pair + i, depth_of(k), :],
                    factors.at[pair, k, :, pl.ds(i * width, width)],
                    factor_sems.at[k, 2 * pair + i],
                )
                for i in range(2)
            ]

    def start(k):
        for copy in copies(k):
            copy.start()

    def start_factors(k, pairs):
        for pair, used in enumerate(pairs):

            @pl.when(used)
            def _(pair=pair):
                for copy in factor_copies(k, pair):
                    copy.start()

    for k in range(min(AHEAD, steps)):
        start(k)
    used, blocks_using = [], []
    if held:
        bounds = spans(requests_ref, request_count)
        local = [meta.local_slot(r, held) for r in range(request_count)]
        for pair in range(held // 2):
            used_by = []
            for first in first_rows:
                wanted = jnp.bool_(False)
                for r, slot in enumerate(local):
                    here = jnp.maximum(bounds[r], first) < jnp.minimum(bounds[r + 1], first + block)
                    wanted = wanted | (here & (slot // 2 == pair) & (slot >= 0))
                used_by.append(wanted)
            blocks_using.append(used_by)
            used.append(functools.reduce(jnp.logical_or, used_by))
        for k in range(min(AHEAD, steps)):
            start_factors(k, used)
        inputs[...] = jnp.zeros_like(inputs)
    sums[...] = jnp.zeros_like(sums)

    def step(k, _):
        @pl.when(k + AHEAD < steps)
        def _():
            start(k + AHEAD)
            start_factors(k + AHEAD, used)

        for copy in copies(k):
            copy.wait()
        sums[...] += jnp.dot(rows[k], right[k], preferred_element_type=jnp.float32)
        for pair, wanted in enumerate(used):

            @pl.when(wanted)
            def _(pair=pair):
                for copy in factor_copies(k, pair):
                    copy.wait()

            for i, wanted_here in enumerate(blocks_using[pair]):

                @pl.when(wanted_here)
                def _(pair=pair, own=pl.ds(i * block, block)):
                    inputs[pair, own, :] += jnp.dot(
                        rows[k, own, :], factors[pair, k], preferred_element_type=jnp.float32
                    )

        return 0

    lax.fori_loop(0, steps, step, 0)
    if handed_on:
        outs[0][len(groups[0]) * piece :, :] = under[...]
    for i, (group, position) in enumerate(places):
        own = pl.ds(i * block, block)
        out, top = outs[group], position * piece
        out[top : top + block, :] = sums[own, :].astype(jnp.bfloat16)
        if held:
            row = lax.broadcasted_iota(jnp.int32, (block, width), 0) + first_rows[i]
            column = lax.broadcasted_iota(jnp.int32, (block, width), 1)
            total = jnp.zeros((block, width), jnp.float32)
            for r, slot in enumerate(local):
                last = jnp.where((slot >= 0) & (slot < held), bounds[r + 1], 0)
                keep = (row >= bounds[r]) & (row < last) & (column < meta.rank(r))
                slot = jnp.clip(slot, 0, held - 1)
                lanes = pl.ds(pl.multiple_of(slot % 2 * width, width), width)
                total = jnp.where(keep, inputs[slot // 2, own, lanes], total)
            total = total.astype(jnp.bfloat16)
            size = block * width // columns
            for j in range(columns // width):
                lanes = slice(j * width, (j + 1) * width)
                out[top + block : top + block + size, lanes] = total[j * size : (j + 1) * size, :]


def base_terms(meta, requests, request_count, hidden, matrix, factor, groups, half, n, grant, under=None):
    tokens, depth = hidden.shape
    block, columns = tokens // n, matrix.shape[1] // 2
    tile = first_divisor(depth, (1024, 512, 256, 128))
    steps = depth // tile
    count = sum(len(group) for group in groups)
    smem = pl.BlockSpec(memory_space=pltpu.SMEM)
    vmem = pl.BlockSpec(memory_space=pltpu.VMEM)
    hbm = pl.BlockSpec(memory_space=pltpu.HBM)
    held, out_rows = 0, block
    operands, in_specs = [meta], [smem]
    scratch = [
        pltpu.VMEM((steps, count * block, tile), jnp.bfloat16),
        pltpu.VMEM((steps, tile, columns), jnp.bfloat16),
        pltpu.VMEM((count * block, columns), jnp.float32),
        pltpu.SemaphoreType.DMA((steps, count + 1)),
    ]
    if factor is not None:
        held, _, width = factor.shape
        out_rows += block * width // columns
        operands, in_specs = [meta, requests, factor], [smem, vmem, hbm]
        scratch += [
            pltpu.VMEM((held // 2, steps, tile, 2 * width), jnp.bfloat16),
            pltpu.VMEM((held // 2, count * block, 2 * width), jnp.float32),
            pltpu.SemaphoreType.DMA((steps, held)),
        ]
    heights = [len(group) * out_rows for group in groups]
    operands, in_specs = operands + [hidden, matrix], in_specs + [hbm, hbm]
    if under is not None:
        heights[0] += under.shape[0]
        operands, in_specs = operands + [under], in_specs + [vmem]
    handed_on = under is not None
    return pl.pallas_call(
        lambda *refs: base_kernel(line_order(n), groups, half, held, request_count, out_rows, handed_on, *refs),
        out_shape=[jax.ShapeDtypeStruct((height, columns), jnp.bfloat16) for height in heights],
        in_specs=in_specs,
        out_specs=[vmem] * len(groups),
        scratch_shapes=scratch,
        compiler_params=params(grant),
        cost_estimate=small_cost(),
        name="base_terms",
    )(*operands)


def select_rows_kernel(request_count, meta_ref, factor, kept, sent):
    meta = Meta(meta_ref, request_count)
    held, rank_rows, _ = factor.shape
    width = factor.shape[2] // (2 * PAIRS)
    side = meta.shard % 2
    for r in range(request_count):
        slot = meta.local_slot(r, held)
        owned = (slot >= 0) & (slot < held)
        slot = jnp.clip(slot, 0, held - 1)
        for out, core in ((kept, side), (sent, 1 - side)):
            for i in range(PAIRS):
                for c in range(2):
                    first = (2 * i + core) * width + c * (width // 2)
                    rows = factor[slot, :, pl.ds(pl.multiple_of(first, LANES), width // 2)]
                    top = (c * request_count + r) * rank_rows
                    out[i, top : top + rank_rows, :] = jnp.where(owned, rows, jnp.zeros_like(rows))


def select_rows(meta, request_count, factor):
    _, rank_rows, model_width = factor.shape
    smem = pl.BlockSpec(memory_space=pltpu.SMEM)
    vmem = pl.BlockSpec(memory_space=pltpu.VMEM)
    shape = (PAIRS, 2 * request_count * rank_rows, model_width // (4 * PAIRS))
    out = jax.ShapeDtypeStruct(shape, factor.dtype)
    return pl.pallas_call(
        lambda *refs: select_rows_kernel(request_count, *refs),
        out_shape=[out, out],
        in_specs=[smem, vmem],
        out_specs=[vmem, vmem],
        compiler_params=params(16),
        cost_estimate=small_cost(),
        name="select_rows",
    )(meta, factor)


def expanded_inputs(meta, requests_ref, lora_ref):
    block, width = lora_ref.shape
    row = lax.broadcasted_iota(jnp.int32, (block, width), 0) + meta.place * block
    lora = lora_ref[...].astype(jnp.float32)
    bounds = spans(requests_ref, meta.requests)
    parts = []
    for r in range(meta.requests):
        scale = 0.25 * width / meta.rank(r).astype(jnp.float32)
        keep = (row >= bounds[r]) & (row < bounds[r + 1])
        parts.append(jnp.where(keep, lora * scale, 0.0).astype(jnp.bfloat16))
    return jnp.concatenate(parts, axis=1)


def finish_kernel(items, added, requests, rank_rows, n, *refs):
    meta_ref, requests_ref, lora_ref, refs = refs[0], refs[1], refs[2], refs[3:]
    arrays, out, rows = refs[:-2], refs[-2], refs[-1]
    meta = Meta(meta_ref, requests)
    rank = n * rank_rows
    half = out.shape[1] // 2
    for index, top, targets in items:
        for place, k in targets:

            @pl.when(meta.place == place)
            def _(piece=arrays[index], top=top, k=k):
                for r in range(requests):
                    first = r * rank + k * rank_rows
                    for c in range(2):
                        start = top + (c * requests + r) * rank_rows
                        rows[first : first + rank_rows, c * half : (c + 1) * half] = piece[start : start + rank_rows, :]

    expanded = expanded_inputs(meta, requests_ref, lora_ref)
    block = lora_ref.shape[0]
    for c in range(2):
        columns = slice(c * half, (c + 1) * half)
        total = jnp.dot(expanded, rows[:, columns], preferred_element_type=jnp.float32)
        for index, top, which in added:
            if which == c:
                total += arrays[index][top : top + block, :].astype(jnp.float32)
        out[:, columns] = total.astype(out.dtype)


def finish(meta, requests, lora, arrays, items, added, request_count, rank_rows, n):
    smem = pl.BlockSpec(memory_space=pltpu.SMEM)
    vmem = pl.BlockSpec(memory_space=pltpu.VMEM)
    width = 2 * arrays[0].shape[1]
    return pl.pallas_call(
        lambda *refs: finish_kernel(items, added, request_count, rank_rows, n, *refs),
        out_shape=jax.ShapeDtypeStruct((lora.shape[0], width), jnp.bfloat16),
        in_specs=[smem] + [vmem] * (2 + len(arrays)),
        out_specs=vmem,
        scratch_shapes=[pltpu.VMEM((request_count * n * rank_rows, width), jnp.bfloat16)],
        compiler_params=params(20),
        cost_estimate=small_cost(),
        name="finish",
    )(meta, requests, lora, *arrays)


def join_kernel(count, term_top, came_top, under_top, term, came, *refs):
    out = refs[-1]
    total = term[term_top : term_top + count, :].astype(jnp.float32)
    total += came[came_top : came_top + count, :].astype(jnp.float32)
    out[:count, :] = total.astype(out.dtype)
    if len(refs) > 1:
        under = refs[0]
        out[count:, :] = under[under_top : under_top + out.shape[0] - count, :]


def join(token, count, term, term_top, came, came_top, under=None, under_top=0, under_count=0):
    arrays = [term, came] + ([] if under is None else [under])
    arrays = lax.optimization_barrier((arrays, token))[0]
    vmem = pl.BlockSpec(memory_space=pltpu.VMEM)
    return pl.pallas_call(
        lambda *refs: join_kernel(count, term_top, came_top, under_top, *refs),
        out_shape=jax.ShapeDtypeStruct((count + under_count, term.shape[1]), term.dtype),
        in_specs=[vmem] * len(arrays),
        out_specs=vmem,
        compiler_params=params(12),
        cost_estimate=small_cost(),
        name="join",
    )(*arrays)


def add_last_kernel(total, up, down, out):
    half = up.shape[1]
    out[:, :half] = total[:, :half]
    last = total[:, half:].astype(jnp.float32) + up[...].astype(jnp.float32) + down[...].astype(jnp.float32)
    out[:, half:] = last.astype(out.dtype)


def add_last(total, up, down):
    vmem = pl.BlockSpec(memory_space=pltpu.VMEM)
    return pl.pallas_call(
        add_last_kernel,
        out_shape=jax.ShapeDtypeStruct(total.shape, total.dtype),
        in_specs=[vmem] * 3,
        out_specs=vmem,
        compiler_params=params(12),
        cost_estimate=small_cost(),
        name="add_last",
    )(total, up, down)


def swap(x, axis, bit):
    return lax.ppermute(x, axis, [(i, i ^ bit) for i in range(lax.axis_size(axis))])


def bits_of(size):
    return [1 << i for i in range(size.bit_length() - 1)]


def along_edge(x, edge):
    n = lax.axis_size("tensor")
    return lax.ppermute(x, "tensor", [(edge, edge + 1), (n - 1 - edge, n - 2 - edge)])


def on_line(hidden, matrix, input_factor, output_factor, requests, token, request_count, n):
    shard = lax.axis_index("store")
    block = hidden.shape[0] // n
    width = input_factor.shape[2]
    rank_rows = output_factor.shape[1]
    piece = block + block * width // (matrix.shape[1] // 2)
    bundle = 2 * request_count * rank_rows

    def base(token, groups, half, grant, under=None):
        factor = input_factor if half == 0 else None
        return base_terms(token, requests, request_count, hidden, matrix, factor, groups, half, n, grant, under)

    def send(x, edge, token):
        return along_edge(after(x, token), edge)

    kept, sent = select_rows(token, request_count, output_factor)
    token = after(token, kept, sent)
    swapped = swap(sent, "store", 1)
    (s00,) = base(token, [[0]], 0, 58)
    token = after(token, s00, swapped)
    e0_1 = along_edge(s00, 0)
    side = shard // 2 % 2
    kept, swapped, _ = lax.optimization_barrier((kept, swapped, token))
    outgoing = kept[1 - side] + swapped[1 - side]
    rows = kept[side] + swapped[side]
    token = after(token, outgoing, rows)
    swapped = swap(outgoing, "store", 2)
    s01, s11 = base(token, [[0], [1]], 1, 50)

    token = after(token, s01)
    e0_2 = send(s01, 0, token)
    token, swapped = lax.optimization_barrier((token, swapped))
    rows = rows + swapped
    token = after(token, rows)
    near = lax.ppermute(rows, "tensor", [(0, 1), (n - 1, n - 2), (1, 0), (n - 2, n - 1)])
    b10 = join(token, piece, s00, 0, e0_1, 0, rows, 0, bundle)
    token = after(token, b10)
    e1_2 = along_edge(b10, 1)
    s10_s11, s20, s30 = base(token, [[1], [2], [3]], 0, 42, s11)

    token = after(token, s10_s11)
    e0_3 = send(s10_s11, 0, token)
    token = after(token, e0_2, near)
    b11 = join(token, block, s01, 0, e0_2, 0, near, 0, bundle)
    token = after(token, b11)
    e1_3 = along_edge(b11, 1)
    c20 = join(token, piece, s20, 0, e1_2, 0, e1_2, piece, bundle)
    token = after(token, c20)
    e2_3 = along_edge(c20, 2)
    s21, s31 = base(token, [[2], [3]], 1, 50)

    token = after(token, s21, e0_3, e1_3, e2_3)
    e0_4 = send(s20, 0, token)
    b20 = join(token, piece, s10_s11, 0, e0_3, 0)
    token = after(token, b20)
    e1_4 = along_edge(b20, 1)
    c21 = join(token, block, s21, 0, e1_3, 0, e1_3, block, bundle)
    token = after(token, c21)
    e2_4 = along_edge(c21, 2)
    e0_5 = send(s21, 0, token)
    b21 = join(token, block, s10_s11, piece, e0_3, piece)
    token = after(token, b21)
    e1_5 = along_edge(b21, 1)

    token, e0_4 = lax.optimization_barrier((token, e0_4))
    e1_4 = lax.optimization_barrier((e1_4, token))[0]
    lora = s30[block:].astype(jnp.float32) + e0_4[block:].astype(jnp.float32)
    lora += e1_4[block:].astype(jnp.float32) + e2_3[block:piece].astype(jnp.float32)
    lora = lora.astype(jnp.bfloat16).reshape(piece - block, -1, width).swapaxes(0, 1).reshape(block, width)
    lora = lora + swap(lora, "store", 1)
    lora = lora + swap(lora, "store", 2)
    arrays = [s30, s31, rows, near, e1_2, e1_3, e2_3, e2_4, e0_4, e1_4]
    items = [
        (2, 0, [(z, z) for z in range(n)]),
        (3, 0, [(0, 1), (1, 0), (2, 3), (3, 2)]),
        (4, piece, [(1, 2), (2, 1)]),
        (5, block, [(1, 3), (2, 0)]),
        (6, piece, [(0, 2), (3, 1)]),
        (7, block, [(0, 3), (3, 0)]),
    ]
    added = [(0, 0, 0), (8, 0, 0), (9, 0, 0), (6, 0, 0), (1, 0, 1), (7, 0, 1)]
    out = finish(token, requests, lora, arrays, items, added, request_count, rank_rows, n)
    return add_last(out, e0_5, e1_5)


def anywhere(hidden, matrix, input_factor, output_factor, token_requests, meta):
    request_adapters, ranks, slots = meta
    held = input_factor.shape[0]
    width = input_factor.shape[2]
    rank, slot = ranks[request_adapters], slots[request_adapters]
    owned = slot // held == lax.axis_index("store")
    chosen = token_requests[:, None] == jnp.arange(request_adapters.shape[0])[None, :]
    lora = jnp.zeros((hidden.shape[0], width), jnp.float32)
    for r in range(request_adapters.shape[0]):
        product = jnp.dot(hidden, input_factor[slot[r] % held], preferred_element_type=jnp.float32)
        keep = (chosen[:, r] & owned[r])[:, None] & (jnp.arange(width) < rank[r])[None, :]
        lora = jnp.where(keep, product, lora)
    lora = lax.psum_scatter(lora.astype(jnp.bfloat16), "tensor", scatter_dimension=1, tiled=True)
    lora = lax.psum(lora, "store").astype(jnp.float32)
    rows = jnp.where(owned[:, None, None], output_factor[slot % held], jnp.zeros((), output_factor.dtype))
    rows = lax.psum_scatter(rows, "store", scatter_dimension=2, tiled=True)
    weights = jnp.where(chosen, 0.25 * width / rank.astype(jnp.float32)[None, :], 0.0)
    expanded = (weights[:, :, None] * lora[:, None, :]).reshape(hidden.shape[0], -1).astype(jnp.bfloat16)
    term = jnp.dot(hidden, matrix, preferred_element_type=jnp.float32)
    term += jnp.dot(expanded, rows.reshape(-1, rows.shape[2]), preferred_element_type=jnp.float32)
    return lax.psum_scatter(term.astype(jnp.bfloat16), "tensor", scatter_dimension=0, tiled=True)


def per_device(
    hidden_activations,
    down_matrix,
    adapter_input_factor,
    adapter_output_factor,
    token_requests,
    request_adapters,
    adapter_ranks,
    adapter_store_slot,
):
    n = lax.axis_size("tensor")
    meta = (request_adapters, adapter_ranks, adapter_store_slot)
    arrays = (hidden_activations, down_matrix, adapter_input_factor, adapter_output_factor)
    if n == LINE and lax.axis_size("store") == 2 * PAIRS and adapter_input_factor.shape[0] % 2 == 0:
        place = jnp.stack([lax.axis_index("tensor"), lax.axis_index("store")]).astype(jnp.int32)
        token = jnp.concatenate([place, *meta])
        return on_line(*arrays, token_requests.reshape(-1, LANES), token, request_adapters.shape[0], n)
    return anywhere(*arrays, token_requests, meta)


def solution(mesh):
    in_specs = (
        P("groups", "tensor"),
        P("tensor", "store"),
        P(("groups", "store"), "tensor", None),
        P(("groups", "store"), "tensor", None),
        P("groups"),
        P("groups"),
        P("groups"),
        P("groups"),
    )
    out_specs = P(("groups", "tensor"), "store")
    return jax.shard_map(
        per_device, mesh=mesh, in_specs=in_specs, out_specs=out_specs, check_vma=False
    )
```

```python
import functools

import jax
import jax.numpy as jnp
from jax import lax
from jax.experimental import pallas as pl
from jax.experimental.pallas import tpu as pltpu
from jax.sharding import PartitionSpec as P

LINE = 4
LANES = 128
AHEAD = 3
PAIRS = 2
MIB = 1024 * 1024


def line_order(n):
    order = []
    for z in range(n):
        sends = [(t, z >= n // 2, n - 1 - t + z) for t in range(z, n - 1)]
        sends += [(t, z < n // 2, t - (n - 1 - z)) for t in range(n - 1 - z, n - 1)]
        order.append([block for _, _, block in sorted(sends)] + [z])
    return order


def first_divisor(size, choices):
    for choice in choices:
        if size % choice == 0:
            return choice
    return size


def after(token, *done):
    return lax.optimization_barrier((token, done))[0]


def params(mebibytes):
    return pltpu.CompilerParams(vmem_limit_bytes=mebibytes * MIB)


def small_cost():
    return pl.CostEstimate(flops=10**6, bytes_accessed=10**5, transcendentals=0)


def block_at(order, slot, place):
    picked = jnp.int32(order[0][slot])
    for z in range(1, len(order)):
        picked = jnp.where(place == z, order[z][slot], picked)
    return picked


def spans(requests_ref, count):
    requests = requests_ref[...]
    return [jnp.int32(0)] + [jnp.sum((requests <= r).astype(jnp.int32)) for r in range(count)]


class Meta:
    def __init__(self, ref, requests):
        self.ref, self.requests = ref, requests
        self.adapters = (ref.shape[0] - 2 - requests) // 2
        self.place, self.shard = ref[0], ref[1]

    def adapter(self, r):
        return self.ref[2 + r]

    def rank(self, r):
        return self.ref[2 + self.requests + self.adapter(r)]

    def local_slot(self, r, held):
        return self.ref[2 + self.requests + self.adapters + self.adapter(r)] - self.shard * held


def base_kernel(order, groups, half, held, request_count, piece, *refs):
    slots = [slot for group in groups for slot in group]
    places = [(g, i) for g, group in enumerate(groups) for i in range(len(group))]
    count = len(slots)
    meta, refs = Meta(refs[0], request_count), refs[1:]
    if held:
        requests_ref, factor, refs = refs[0], refs[1], refs[2:]
    hidden, matrix, refs = refs[0], refs[1], refs[2:]
    outs, refs = refs[: len(groups)], refs[len(groups) :]
    (rows, right, sums, sems), refs = refs[:4], refs[4:]
    steps, _, tile = rows.shape
    columns = outs[0].shape[1]
    block = rows.shape[1] // count
    first_rows = [pl.multiple_of(block_at(order, slot, meta.place) * block, block) for slot in slots]

    def depth_of(k):
        return pl.ds(pl.multiple_of(k * tile, tile), tile)

    def copies(k):
        moves = [
            (hidden.at[pl.ds(first_rows[i], block), depth_of(k)], rows.at[k, pl.ds(i * block, block), :])
            for i in range(count)
        ]
        moves.append((matrix.at[depth_of(k), pl.ds(half * columns, columns)], right.at[k]))
        return [pltpu.make_async_copy(a, b, sems.at[k, i]) for i, (a, b) in enumerate(moves)]

    if held:
        factors, inputs, factor_sems = refs
        width = factor.shape[2]

        def factor_copies(k, pair):
            return [
                pltpu.make_async_copy(
                    factor.at[2 * pair + i, depth_of(k), :],
                    factors.at[pair, k, :, pl.ds(i * width, width)],
                    factor_sems.at[k, 2 * pair + i],
                )
                for i in range(2)
            ]

    def start(k):
        for copy in copies(k):
            copy.start()

    def start_factors(k, pairs):
        for pair, used in enumerate(pairs):

            @pl.when(used)
            def _(pair=pair):
                for copy in factor_copies(k, pair):
                    copy.start()

    for k in range(min(AHEAD, steps)):
        start(k)
    used, blocks_using = [], []
    if held:
        bounds = spans(requests_ref, request_count)
        local = [meta.local_slot(r, held) for r in range(request_count)]
        for pair in range(held // 2):
            used_by = []
            for first in first_rows:
                wanted = jnp.bool_(False)
                for r, slot in enumerate(local):
                    here = jnp.maximum(bounds[r], first) < jnp.minimum(bounds[r + 1], first + block)
                    wanted = wanted | (here & (slot // 2 == pair) & (slot >= 0))
                used_by.append(wanted)
            blocks_using.append(used_by)
            used.append(functools.reduce(jnp.logical_or, used_by))
        for k in range(min(AHEAD, steps)):
            start_factors(k, used)
        inputs[...] = jnp.zeros_like(inputs)
    sums[...] = jnp.zeros_like(sums)

    def step(k, _):
        @pl.when(k + AHEAD < steps)
        def _():
            start(k + AHEAD)
            start_factors(k + AHEAD, used)

        for copy in copies(k):
            copy.wait()
        sums[...] += jnp.dot(rows[k], right[k], preferred_element_type=jnp.float32)
        for pair, wanted in enumerate(used):

            @pl.when(wanted)
            def _(pair=pair):
                for copy in factor_copies(k, pair):
                    copy.wait()

            for i, wanted_here in enumerate(blocks_using[pair]):

                @pl.when(wanted_here)
                def _(pair=pair, own=pl.ds(i * block, block)):
                    inputs[pair, own, :] += jnp.dot(
                        rows[k, own, :], factors[pair, k], preferred_element_type=jnp.float32
                    )

        return 0

    lax.fori_loop(0, steps, step, 0)
    for i, (group, position) in enumerate(places):
        own = pl.ds(i * block, block)
        out, top = outs[group], position * piece
        out[top : top + block, :] = sums[own, :].astype(jnp.bfloat16)
        if held:
            row = lax.broadcasted_iota(jnp.int32, (block, width), 0) + first_rows[i]
            column = lax.broadcasted_iota(jnp.int32, (block, width), 1)
            total = jnp.zeros((block, width), jnp.float32)
            for r, slot in enumerate(local):
                last = jnp.where((slot >= 0) & (slot < held), bounds[r + 1], 0)
                keep = (row >= bounds[r]) & (row < last) & (column < meta.rank(r))
                slot = jnp.clip(slot, 0, held - 1)
                lanes = pl.ds(pl.multiple_of(slot % 2 * width, width), width)
                total = jnp.where(keep, inputs[slot // 2, own, lanes], total)
            total = total.astype(jnp.bfloat16)
            size = block * width // columns
            for j in range(columns // width):
                lanes = slice(j * width, (j + 1) * width)
                out[top + block : top + block + size, lanes] = total[j * size : (j + 1) * size, :]


def base_terms(meta, requests, request_count, hidden, matrix, factor, groups, half, n, grant):
    tokens, depth = hidden.shape
    block, columns = tokens // n, matrix.shape[1] // 2
    tile = first_divisor(depth, (1024, 512, 256, 128))
    steps = depth // tile
    count = sum(len(group) for group in groups)
    smem = pl.BlockSpec(memory_space=pltpu.SMEM)
    vmem = pl.BlockSpec(memory_space=pltpu.VMEM)
    hbm = pl.BlockSpec(memory_space=pltpu.HBM)
    held, out_rows = 0, block
    operands, in_specs = [meta], [smem]
    scratch = [
        pltpu.VMEM((steps, count * block, tile), jnp.bfloat16),
        pltpu.VMEM((steps, tile, columns), jnp.bfloat16),
        pltpu.VMEM((count * block, columns), jnp.float32),
        pltpu.SemaphoreType.DMA((steps, count + 1)),
    ]
    if factor is not None:
        held, _, width = factor.shape
        out_rows += block * width // columns
        operands, in_specs = [meta, requests, factor], [smem, vmem, hbm]
        scratch += [
            pltpu.VMEM((held // 2, steps, tile, 2 * width), jnp.bfloat16),
            pltpu.VMEM((held // 2, count * block, 2 * width), jnp.float32),
            pltpu.SemaphoreType.DMA((steps, held)),
        ]
    return pl.pallas_call(
        lambda *refs: base_kernel(line_order(n), groups, half, held, request_count, out_rows, *refs),
        out_shape=[jax.ShapeDtypeStruct((len(group) * out_rows, columns), jnp.bfloat16) for group in groups],
        in_specs=in_specs + [hbm, hbm],
        out_specs=[vmem] * len(groups),
        scratch_shapes=scratch,
        compiler_params=params(grant),
        cost_estimate=small_cost(),
        name="base_terms",
    )(*operands, hidden, matrix)


def select_rows_kernel(request_count, meta_ref, factor, kept, sent):
    meta = Meta(meta_ref, request_count)
    held, rank_rows, _ = factor.shape
    width = factor.shape[2] // (2 * PAIRS)
    side = meta.shard % 2
    for r in range(request_count):
        slot = meta.local_slot(r, held)
        owned = (slot >= 0) & (slot < held)
        slot = jnp.clip(slot, 0, held - 1)
        for out, core in ((kept, side), (sent, 1 - side)):
            for i in range(PAIRS):
                for c in range(2):
                    first = (2 * i + core) * width + c * (width // 2)
                    rows = factor[slot, :, pl.ds(pl.multiple_of(first, LANES), width // 2)]
                    top = (c * request_count + r) * rank_rows
                    out[i, top : top + rank_rows, :] = jnp.where(owned, rows, jnp.zeros_like(rows))


def select_rows(meta, request_count, factor):
    _, rank_rows, model_width = factor.shape
    smem = pl.BlockSpec(memory_space=pltpu.SMEM)
    vmem = pl.BlockSpec(memory_space=pltpu.VMEM)
    shape = (PAIRS, 2 * request_count * rank_rows, model_width // (4 * PAIRS))
    out = jax.ShapeDtypeStruct(shape, factor.dtype)
    return pl.pallas_call(
        lambda *refs: select_rows_kernel(request_count, *refs),
        out_shape=[out, out],
        in_specs=[smem, vmem],
        out_specs=[vmem, vmem],
        compiler_params=params(16),
        cost_estimate=small_cost(),
        name="select_rows",
    )(meta, factor)


def expanded_inputs(meta, requests_ref, lora_ref):
    block, width = lora_ref.shape
    row = lax.broadcasted_iota(jnp.int32, (block, width), 0) + meta.place * block
    lora = lora_ref[...].astype(jnp.float32)
    bounds = spans(requests_ref, meta.requests)
    parts = []
    for r in range(meta.requests):
        scale = 0.25 * width / meta.rank(r).astype(jnp.float32)
        keep = (row >= bounds[r]) & (row < bounds[r + 1])
        parts.append(jnp.where(keep, lora * scale, 0.0).astype(jnp.bfloat16))
    return jnp.concatenate(parts, axis=1)


def finish_kernel(items, added, requests, rank_rows, n, *refs):
    meta_ref, requests_ref, lora_ref, refs = refs[0], refs[1], refs[2], refs[3:]
    arrays, out, rows = refs[:-2], refs[-2], refs[-1]
    meta = Meta(meta_ref, requests)
    rank = n * rank_rows
    half = out.shape[1] // 2
    for index, top, targets in items:
        for place, k in targets:

            @pl.when(meta.place == place)
            def _(piece=arrays[index], top=top, k=k):
                for r in range(requests):
                    first = r * rank + k * rank_rows
                    for c in range(2):
                        start = top + (c * requests + r) * rank_rows
                        rows[first : first + rank_rows, c * half : (c + 1) * half] = piece[start : start + rank_rows, :]

    expanded = expanded_inputs(meta, requests_ref, lora_ref)
    block = lora_ref.shape[0]
    for c in range(2):
        columns = slice(c * half, (c + 1) * half)
        total = jnp.dot(expanded, rows[:, columns], preferred_element_type=jnp.float32)
        for index, top, which in added:
            if which == c:
                total += arrays[index][top : top + block, :].astype(jnp.float32)
        out[:, columns] = total.astype(out.dtype)


def finish(meta, requests, lora, arrays, items, added, request_count, rank_rows, n):
    smem = pl.BlockSpec(memory_space=pltpu.SMEM)
    vmem = pl.BlockSpec(memory_space=pltpu.VMEM)
    width = 2 * arrays[0].shape[1]
    return pl.pallas_call(
        lambda *refs: finish_kernel(items, added, request_count, rank_rows, n, *refs),
        out_shape=jax.ShapeDtypeStruct((lora.shape[0], width), jnp.bfloat16),
        in_specs=[smem] + [vmem] * (2 + len(arrays)),
        out_specs=vmem,
        scratch_shapes=[pltpu.VMEM((request_count * n * rank_rows, width), jnp.bfloat16)],
        compiler_params=params(20),
        cost_estimate=small_cost(),
        name="finish",
    )(meta, requests, lora, *arrays)


def join_kernel(count, term_top, came_top, under_top, term, came, *refs):
    out = refs[-1]
    total = term[term_top : term_top + count, :].astype(jnp.float32)
    total += came[came_top : came_top + count, :].astype(jnp.float32)
    out[:count, :] = total.astype(out.dtype)
    if len(refs) > 1:
        under = refs[0]
        out[count:, :] = under[under_top : under_top + out.shape[0] - count, :]


def join(token, count, term, term_top, came, came_top, under=None, under_top=0, under_count=0):
    arrays = [term, came] + ([] if under is None else [under])
    arrays = lax.optimization_barrier((arrays, token))[0]
    vmem = pl.BlockSpec(memory_space=pltpu.VMEM)
    return pl.pallas_call(
        lambda *refs: join_kernel(count, term_top, came_top, under_top, *refs),
        out_shape=jax.ShapeDtypeStruct((count + under_count, term.shape[1]), term.dtype),
        in_specs=[vmem] * len(arrays),
        out_specs=vmem,
        compiler_params=params(12),
        cost_estimate=small_cost(),
        name="join",
    )(*arrays)


def add_last_kernel(total, up, down, out):
    half = up.shape[1]
    out[:, :half] = total[:, :half]
    last = total[:, half:].astype(jnp.float32) + up[...].astype(jnp.float32) + down[...].astype(jnp.float32)
    out[:, half:] = last.astype(out.dtype)


def add_last(total, up, down):
    vmem = pl.BlockSpec(memory_space=pltpu.VMEM)
    return pl.pallas_call(
        add_last_kernel,
        out_shape=jax.ShapeDtypeStruct(total.shape, total.dtype),
        in_specs=[vmem] * 3,
        out_specs=vmem,
        compiler_params=params(12),
        cost_estimate=small_cost(),
        name="add_last",
    )(total, up, down)


def swap(x, axis, bit):
    return lax.ppermute(x, axis, [(i, i ^ bit) for i in range(lax.axis_size(axis))])


def bits_of(size):
    return [1 << i for i in range(size.bit_length() - 1)]


def along_edge(x, edge):
    n = lax.axis_size("tensor")
    return lax.ppermute(x, "tensor", [(edge, edge + 1), (n - 1 - edge, n - 2 - edge)])


def on_line(hidden, matrix, input_factor, output_factor, requests, token, request_count, n):
    shard = lax.axis_index("store")
    block = hidden.shape[0] // n
    width = input_factor.shape[2]
    rank_rows = output_factor.shape[1]
    piece = block + block * width // (matrix.shape[1] // 2)
    bundle = 2 * request_count * rank_rows

    def base(token, groups, half, grant):
        factor = input_factor if half == 0 else None
        return base_terms(token, requests, request_count, hidden, matrix, factor, groups, half, n, grant)

    def send(x, edge, token):
        return along_edge(after(x, token), edge)

    kept, sent = select_rows(token, request_count, output_factor)
    token = after(token, kept, sent)
    swapped = swap(sent, "store", 1)
    (s00,) = base(token, [[0]], 0, 58)
    token = after(token, s00, swapped)
    e0_1 = along_edge(s00, 0)
    side = shard // 2 % 2
    kept, swapped, _ = lax.optimization_barrier((kept, swapped, token))
    outgoing = kept[1 - side] + swapped[1 - side]
    rows = kept[side] + swapped[side]
    token = after(token, outgoing, rows)
    swapped = swap(outgoing, "store", 2)
    (s01,) = base(token, [[0]], 1, 50)

    token = after(token, s01)
    e0_2 = send(s01, 0, token)
    token, swapped = lax.optimization_barrier((token, swapped))
    rows = rows + swapped
    token = after(token, rows)
    near = lax.ppermute(rows, "tensor", [(0, 1), (n - 1, n - 2), (1, 0), (n - 2, n - 1)])
    b10 = join(token, piece, s00, 0, e0_1, 0, rows, 0, bundle)
    token = after(token, b10)
    e1_2 = along_edge(b10, 1)
    s10_s20, s30 = base(token, [[1, 2], [3]], 0, 42)

    token = after(token, s10_s20)
    e0_3 = send(s10_s20, 0, token)
    token = after(token, e0_2, near)
    b11 = join(token, block, s01, 0, e0_2, 0, near, 0, bundle)
    token = after(token, b11)
    e1_3 = along_edge(b11, 1)
    c20 = join(token, piece, s10_s20, piece, e1_2, 0, e1_2, piece, bundle)
    token = after(token, c20)
    e2_3 = along_edge(c20, 2)
    s11, s21, s31 = base(token, [[1], [2], [3]], 1, 50)

    token = after(token, s11, e0_3)
    e0_4 = send(s11, 0, token)
    b20 = join(token, piece, s10_s20, 0, e0_3, 0)
    token = after(token, b20)
    e1_4 = along_edge(b20, 1)
    token = after(token, e1_3, e2_3)
    c21 = join(token, block, s21, 0, e1_3, 0, e1_3, block, bundle)
    token = after(token, c21)
    e2_4 = along_edge(c21, 2)
    e0_5 = send(s21, 0, token)

    token, e0_4 = lax.optimization_barrier((token, e0_4))
    b21 = join(token, block, s11, 0, e0_4, 0)
    token = after(token, b21)
    e1_5 = along_edge(b21, 1)
    e1_4 = lax.optimization_barrier((e1_4, token))[0]
    lora = s30[block:].astype(jnp.float32) + e0_3[piece + block :].astype(jnp.float32)
    lora += e1_4[block:].astype(jnp.float32) + e2_3[block:piece].astype(jnp.float32)
    lora = lora.astype(jnp.bfloat16).reshape(piece - block, -1, width).swapaxes(0, 1).reshape(block, width)
    lora = lora + swap(lora, "store", 1)
    lora = lora + swap(lora, "store", 2)
    arrays = [s30, s31, rows, near, e1_2, e1_3, e2_3, e2_4, e0_3, e1_4]
    items = [
        (2, 0, [(z, z) for z in range(n)]),
        (3, 0, [(0, 1), (1, 0), (2, 3), (3, 2)]),
        (4, piece, [(1, 2), (2, 1)]),
        (5, block, [(1, 3), (2, 0)]),
        (6, piece, [(0, 2), (3, 1)]),
        (7, block, [(0, 3), (3, 0)]),
    ]
    added = [(0, 0, 0), (8, piece, 0), (9, 0, 0), (6, 0, 0), (1, 0, 1), (7, 0, 1)]
    out = finish(token, requests, lora, arrays, items, added, request_count, rank_rows, n)
    return add_last(out, e0_5, e1_5)


def anywhere(hidden, matrix, input_factor, output_factor, token_requests, meta):
    request_adapters, ranks, slots = meta
    held = input_factor.shape[0]
    width = input_factor.shape[2]
    rank, slot = ranks[request_adapters], slots[request_adapters]
    owned = slot // held == lax.axis_index("store")
    chosen = token_requests[:, None] == jnp.arange(request_adapters.shape[0])[None, :]
    lora = jnp.zeros((hidden.shape[0], width), jnp.float32)
    for r in range(request_adapters.shape[0]):
        product = jnp.dot(hidden, input_factor[slot[r] % held], preferred_element_type=jnp.float32)
        keep = (chosen[:, r] & owned[r])[:, None] & (jnp.arange(width) < rank[r])[None, :]
        lora = jnp.where(keep, product, lora)
    lora = lax.psum_scatter(lora.astype(jnp.bfloat16), "tensor", scatter_dimension=1, tiled=True)
    lora = lax.psum(lora, "store").astype(jnp.float32)
    rows = jnp.where(owned[:, None, None], output_factor[slot % held], jnp.zeros((), output_factor.dtype))
    rows = lax.psum_scatter(rows, "store", scatter_dimension=2, tiled=True)
    weights = jnp.where(chosen, 0.25 * width / rank.astype(jnp.float32)[None, :], 0.0)
    expanded = (weights[:, :, None] * lora[:, None, :]).reshape(hidden.shape[0], -1).astype(jnp.bfloat16)
    term = jnp.dot(hidden, matrix, preferred_element_type=jnp.float32)
    term += jnp.dot(expanded, rows.reshape(-1, rows.shape[2]), preferred_element_type=jnp.float32)
    return lax.psum_scatter(term.astype(jnp.bfloat16), "tensor", scatter_dimension=0, tiled=True)


def per_device(
    hidden_activations,
    down_matrix,
    adapter_input_factor,
    adapter_output_factor,
    token_requests,
    request_adapters,
    adapter_ranks,
    adapter_store_slot,
):
    n = lax.axis_size("tensor")
    meta = (request_adapters, adapter_ranks, adapter_store_slot)
    arrays = (hidden_activations, down_matrix, adapter_input_factor, adapter_output_factor)
    if n == LINE and lax.axis_size("store") == 2 * PAIRS and adapter_input_factor.shape[0] % 2 == 0:
        place = jnp.stack([lax.axis_index("tensor"), lax.axis_index("store")]).astype(jnp.int32)
        token = jnp.concatenate([place, *meta])
        return on_line(*arrays, token_requests.reshape(-1, LANES), token, request_adapters.shape[0], n)
    return anywhere(*arrays, token_requests, meta)


def solution(mesh):
    in_specs = (
        P("groups", "tensor"),
        P("tensor", "store"),
        P(("groups", "store"), "tensor", None),
        P(("groups", "store"), "tensor", None),
        P("groups"),
        P("groups"),
        P("groups"),
        P("groups"),
    )
    out_specs = P(("groups", "tensor"), "store")
    return jax.shard_map(
        per_device, mesh=mesh, in_specs=in_specs, out_specs=out_specs, check_vma=False
    )
```

```python
import functools

import jax
import jax.numpy as jnp
from jax import lax
from jax.experimental import pallas as pl
from jax.experimental.pallas import tpu as pltpu
from jax.sharding import PartitionSpec as P

LINE = 4
LANES = 128
AHEAD = 3
PAIRS = 2
MIB = 1024 * 1024


def line_order(n):
    order = []
    for z in range(n):
        sends = [(t, z >= n // 2, n - 1 - t + z) for t in range(z, n - 1)]
        sends += [(t, z < n // 2, t - (n - 1 - z)) for t in range(n - 1 - z, n - 1)]
        order.append([block for _, _, block in sorted(sends)] + [z])
    return order


def first_divisor(size, choices):
    for choice in choices:
        if size % choice == 0:
            return choice
    return size


def after(token, *done):
    return lax.optimization_barrier((token, done))[0]


def params(mebibytes):
    return pltpu.CompilerParams(vmem_limit_bytes=mebibytes * MIB)


def small_cost():
    return pl.CostEstimate(flops=10**6, bytes_accessed=10**5, transcendentals=0)


def block_at(order, slot, place):
    picked = jnp.int32(order[0][slot])
    for z in range(1, len(order)):
        picked = jnp.where(place == z, order[z][slot], picked)
    return picked


def spans(requests_ref, count):
    requests = requests_ref[...]
    return [jnp.int32(0)] + [jnp.sum((requests <= r).astype(jnp.int32)) for r in range(count)]


class Meta:
    def __init__(self, ref, requests):
        self.ref, self.requests = ref, requests
        self.adapters = (ref.shape[0] - 2 - requests) // 2
        self.place, self.shard = ref[0], ref[1]

    def adapter(self, r):
        return self.ref[2 + r]

    def rank(self, r):
        return self.ref[2 + self.requests + self.adapter(r)]

    def local_slot(self, r, held):
        return self.ref[2 + self.requests + self.adapters + self.adapter(r)] - self.shard * held


def base_kernel(order, groups, half, held, request_count, piece, handed_on, *refs):
    slots = [slot for group in groups for slot in group]
    places = [(g, i) for g, group in enumerate(groups) for i in range(len(group))]
    count = len(slots)
    meta, refs = Meta(refs[0], request_count), refs[1:]
    if held:
        requests_ref, factor, refs = refs[0], refs[1], refs[2:]
    hidden, matrix, refs = refs[0], refs[1], refs[2:]
    under, refs = (refs[0], refs[1:]) if handed_on else (None, refs)
    outs, refs = refs[: len(groups)], refs[len(groups) :]
    (rows, right, sums, sems), refs = refs[:4], refs[4:]
    steps, _, tile = rows.shape
    columns = outs[0].shape[1]
    block = rows.shape[1] // count
    first_rows = [pl.multiple_of(block_at(order, slot, meta.place) * block, block) for slot in slots]

    def depth_of(k):
        return pl.ds(pl.multiple_of(k * tile, tile), tile)

    def copies(k):
        moves = [
            (hidden.at[pl.ds(first_rows[i], block), depth_of(k)], rows.at[k, pl.ds(i * block, block), :])
            for i in range(count)
        ]
        moves.append((matrix.at[depth_of(k), pl.ds(half * columns, columns)], right.at[k]))
        return [pltpu.make_async_copy(a, b, sems.at[k, i]) for i, (a, b) in enumerate(moves)]

    if held:
        factors, inputs, factor_sems = refs
        width = factor.shape[2]

        def factor_copies(k, pair):
            return [
                pltpu.make_async_copy(
                    factor.at[2 * pair + i, depth_of(k), :],
                    factors.at[pair, k, :, pl.ds(i * width, width)],
                    factor_sems.at[k, 2 * pair + i],
                )
                for i in range(2)
            ]

    def start(k):
        for copy in copies(k):
            copy.start()

    def start_factors(k, pairs):
        for pair, used in enumerate(pairs):

            @pl.when(used)
            def _(pair=pair):
                for copy in factor_copies(k, pair):
                    copy.start()

    for k in range(min(AHEAD, steps)):
        start(k)
    used, blocks_using = [], []
    if held:
        bounds = spans(requests_ref, request_count)
        local = [meta.local_slot(r, held) for r in range(request_count)]
        for pair in range(held // 2):
            used_by = []
            for first in first_rows:
                wanted = jnp.bool_(False)
                for r, slot in enumerate(local):
                    here = jnp.maximum(bounds[r], first) < jnp.minimum(bounds[r + 1], first + block)
                    wanted = wanted | (here & (slot // 2 == pair) & (slot >= 0))
                used_by.append(wanted)
            blocks_using.append(used_by)
            used.append(functools.reduce(jnp.logical_or, used_by))
        for k in range(min(AHEAD, steps)):
            start_factors(k, used)
        inputs[...] = jnp.zeros_like(inputs)
    sums[...] = jnp.zeros_like(sums)

    def step(k, _):
        @pl.when(k + AHEAD < steps)
        def _():
            start(k + AHEAD)
            start_factors(k + AHEAD, used)

        for copy in copies(k):
            copy.wait()
        sums[...] += jnp.dot(rows[k], right[k], preferred_element_type=jnp.float32)
        for pair, wanted in enumerate(used):

            @pl.when(wanted)
            def _(pair=pair):
                for copy in factor_copies(k, pair):
                    copy.wait()

            for i, wanted_here in enumerate(blocks_using[pair]):

                @pl.when(wanted_here)
                def _(pair=pair, own=pl.ds(i * block, block)):
                    inputs[pair, own, :] += jnp.dot(
                        rows[k, own, :], factors[pair, k], preferred_element_type=jnp.float32
                    )

        return 0

    lax.fori_loop(0, steps, step, 0)
    if handed_on:
        outs[0][len(groups[0]) * piece :, :] = under[...]
    for i, (group, position) in enumerate(places):
        own = pl.ds(i * block, block)
        out, top = outs[group], position * piece
        out[top : top + block, :] = sums[own, :].astype(jnp.bfloat16)
        if held:
            row = lax.broadcasted_iota(jnp.int32, (block, width), 0) + first_rows[i]
            column = lax.broadcasted_iota(jnp.int32, (block, width), 1)
            total = jnp.zeros((block, width), jnp.float32)
            for r, slot in enumerate(local):
                last = jnp.where((slot >= 0) & (slot < held), bounds[r + 1], 0)
                keep = (row >= bounds[r]) & (row < last) & (column < meta.rank(r))
                slot = jnp.clip(slot, 0, held - 1)
                lanes = pl.ds(pl.multiple_of(slot % 2 * width, width), width)
                total = jnp.where(keep, inputs[slot // 2, own, lanes], total)
            total = total.astype(jnp.bfloat16)
            size = block * width // columns
            for j in range(columns // width):
                lanes = slice(j * width, (j + 1) * width)
                out[top + block : top + block + size, lanes] = total[j * size : (j + 1) * size, :]


def base_terms(meta, requests, request_count, hidden, matrix, factor, groups, half, n, grant, under=None):
    tokens, depth = hidden.shape
    block, columns = tokens // n, matrix.shape[1] // 2
    tile = first_divisor(depth, (1024, 512, 256, 128))
    steps = depth // tile
    count = sum(len(group) for group in groups)
    smem = pl.BlockSpec(memory_space=pltpu.SMEM)
    vmem = pl.BlockSpec(memory_space=pltpu.VMEM)
    hbm = pl.BlockSpec(memory_space=pltpu.HBM)
    held, out_rows = 0, block
    operands, in_specs = [meta], [smem]
    scratch = [
        pltpu.VMEM((steps, count * block, tile), jnp.bfloat16),
        pltpu.VMEM((steps, tile, columns), jnp.bfloat16),
        pltpu.VMEM((count * block, columns), jnp.float32),
        pltpu.SemaphoreType.DMA((steps, count + 1)),
    ]
    if factor is not None:
        held, _, width = factor.shape
        out_rows += block * width // columns
        operands, in_specs = [meta, requests, factor], [smem, vmem, hbm]
        scratch += [
            pltpu.VMEM((held // 2, steps, tile, 2 * width), jnp.bfloat16),
            pltpu.VMEM((held // 2, count * block, 2 * width), jnp.float32),
            pltpu.SemaphoreType.DMA((steps, held)),
        ]
    heights = [len(group) * out_rows for group in groups]
    operands, in_specs = operands + [hidden, matrix], in_specs + [hbm, hbm]
    if under is not None:
        heights[0] += under.shape[0]
        operands, in_specs = operands + [under], in_specs + [vmem]
    handed_on = under is not None
    return pl.pallas_call(
        lambda *refs: base_kernel(line_order(n), groups, half, held, request_count, out_rows, handed_on, *refs),
        out_shape=[jax.ShapeDtypeStruct((height, columns), jnp.bfloat16) for height in heights],
        in_specs=in_specs,
        out_specs=[vmem] * len(groups),
        scratch_shapes=scratch,
        compiler_params=params(grant),
        cost_estimate=small_cost(),
        name="base_terms",
    )(*operands)


def select_rows_kernel(request_count, meta_ref, factor, kept, sent):
    meta = Meta(meta_ref, request_count)
    held, rank_rows, _ = factor.shape
    width = factor.shape[2] // (2 * PAIRS)
    side = meta.shard % 2
    for r in range(request_count):
        slot = meta.local_slot(r, held)
        owned = (slot >= 0) & (slot < held)
        slot = jnp.clip(slot, 0, held - 1)
        for out, core in ((kept, side), (sent, 1 - side)):
            for i in range(PAIRS):
                for c in range(2):
                    first = (2 * i + core) * width + c * (width // 2)
                    rows = factor[slot, :, pl.ds(pl.multiple_of(first, LANES), width // 2)]
                    top = (c * request_count + r) * rank_rows
                    out[i, top : top + rank_rows, :] = jnp.where(owned, rows, jnp.zeros_like(rows))


def select_rows(meta, request_count, factor):
    _, rank_rows, model_width = factor.shape
    smem = pl.BlockSpec(memory_space=pltpu.SMEM)
    vmem = pl.BlockSpec(memory_space=pltpu.VMEM)
    shape = (PAIRS, 2 * request_count * rank_rows, model_width // (4 * PAIRS))
    out = jax.ShapeDtypeStruct(shape, factor.dtype)
    return pl.pallas_call(
        lambda *refs: select_rows_kernel(request_count, *refs),
        out_shape=[out, out],
        in_specs=[smem, vmem],
        out_specs=[vmem, vmem],
        compiler_params=params(16),
        cost_estimate=small_cost(),
        name="select_rows",
    )(meta, factor)


def expanded_inputs(meta, requests_ref, lora_ref):
    block, width = lora_ref.shape
    row = lax.broadcasted_iota(jnp.int32, (block, width), 0) + meta.place * block
    lora = lora_ref[...].astype(jnp.float32)
    bounds = spans(requests_ref, meta.requests)
    parts = []
    for r in range(meta.requests):
        scale = 0.25 * width / meta.rank(r).astype(jnp.float32)
        keep = (row >= bounds[r]) & (row < bounds[r + 1])
        parts.append(jnp.where(keep, lora * scale, 0.0).astype(jnp.bfloat16))
    return jnp.concatenate(parts, axis=1)


def finish_kernel(items, added, requests, rank_rows, n, *refs):
    meta_ref, requests_ref, lora_ref, refs = refs[0], refs[1], refs[2], refs[3:]
    arrays, out, rows = refs[:-2], refs[-2], refs[-1]
    meta = Meta(meta_ref, requests)
    rank = n * rank_rows
    half = out.shape[1] // 2
    for index, top, targets in items:
        for place, k in targets:

            @pl.when(meta.place == place)
            def _(piece=arrays[index], top=top, k=k):
                for r in range(requests):
                    first = r * rank + k * rank_rows
                    for c in range(2):
                        start = top + (c * requests + r) * rank_rows
                        rows[first : first + rank_rows, c * half : (c + 1) * half] = piece[start : start + rank_rows, :]

    expanded = expanded_inputs(meta, requests_ref, lora_ref)
    block = lora_ref.shape[0]
    for c in range(2):
        columns = slice(c * half, (c + 1) * half)
        total = jnp.dot(expanded, rows[:, columns], preferred_element_type=jnp.float32)
        for index, top, which in added:
            if which == c:
                total += arrays[index][top : top + block, :].astype(jnp.float32)
        out[:, columns] = total.astype(out.dtype)


def finish(meta, requests, lora, arrays, items, added, request_count, rank_rows, n):
    smem = pl.BlockSpec(memory_space=pltpu.SMEM)
    vmem = pl.BlockSpec(memory_space=pltpu.VMEM)
    width = 2 * arrays[0].shape[1]
    return pl.pallas_call(
        lambda *refs: finish_kernel(items, added, request_count, rank_rows, n, *refs),
        out_shape=jax.ShapeDtypeStruct((lora.shape[0], width), jnp.bfloat16),
        in_specs=[smem] + [vmem] * (2 + len(arrays)),
        out_specs=vmem,
        scratch_shapes=[pltpu.VMEM((request_count * n * rank_rows, width), jnp.bfloat16)],
        compiler_params=params(20),
        cost_estimate=small_cost(),
        name="finish",
    )(meta, requests, lora, *arrays)


def join_kernel(count, term_top, came_top, under_top, term, came, *refs):
    out = refs[-1]
    total = term[term_top : term_top + count, :].astype(jnp.float32)
    total += came[came_top : came_top + count, :].astype(jnp.float32)
    out[:count, :] = total.astype(out.dtype)
    if len(refs) > 1:
        under = refs[0]
        out[count:, :] = under[under_top : under_top + out.shape[0] - count, :]


def join(token, count, term, term_top, came, came_top, under=None, under_top=0, under_count=0):
    arrays = [term, came] + ([] if under is None else [under])
    arrays = lax.optimization_barrier((arrays, token))[0]
    vmem = pl.BlockSpec(memory_space=pltpu.VMEM)
    return pl.pallas_call(
        lambda *refs: join_kernel(count, term_top, came_top, under_top, *refs),
        out_shape=jax.ShapeDtypeStruct((count + under_count, term.shape[1]), term.dtype),
        in_specs=[vmem] * len(arrays),
        out_specs=vmem,
        compiler_params=params(12),
        cost_estimate=small_cost(),
        name="join",
    )(*arrays)


def add_last_kernel(total, up, down, out):
    half = up.shape[1]
    out[:, :half] = total[:, :half]
    last = total[:, half:].astype(jnp.float32) + up[...].astype(jnp.float32) + down[...].astype(jnp.float32)
    out[:, half:] = last.astype(out.dtype)


def add_last(total, up, down):
    vmem = pl.BlockSpec(memory_space=pltpu.VMEM)
    return pl.pallas_call(
        add_last_kernel,
        out_shape=jax.ShapeDtypeStruct(total.shape, total.dtype),
        in_specs=[vmem] * 3,
        out_specs=vmem,
        compiler_params=params(12),
        cost_estimate=small_cost(),
        name="add_last",
    )(total, up, down)


def pass_kernel(token_ref, out_ref):
    for i in range(token_ref.shape[0]):
        out_ref[i] = token_ref[i]


def pass_on(token):
    smem = pl.BlockSpec(memory_space=pltpu.SMEM)
    return pl.pallas_call(
        pass_kernel,
        out_shape=jax.ShapeDtypeStruct(token.shape, token.dtype),
        in_specs=[smem],
        out_specs=smem,
        cost_estimate=pl.CostEstimate(flops=4 * 10**9, bytes_accessed=10**3, transcendentals=0),
        name="pass_on",
    )(token)


def swap(x, axis, bit):
    return lax.ppermute(x, axis, [(i, i ^ bit) for i in range(lax.axis_size(axis))])


def bits_of(size):
    return [1 << i for i in range(size.bit_length() - 1)]


def along_edge(x, edge):
    n = lax.axis_size("tensor")
    return lax.ppermute(x, "tensor", [(edge, edge + 1), (n - 1 - edge, n - 2 - edge)])


def on_line(hidden, matrix, input_factor, output_factor, requests, token, request_count, n):
    shard = lax.axis_index("store")
    block = hidden.shape[0] // n
    width = input_factor.shape[2]
    rank_rows = output_factor.shape[1]
    piece = block + block * width // (matrix.shape[1] // 2)
    bundle = 2 * request_count * rank_rows

    def base(token, groups, half, grant, under=None):
        factor = input_factor if half == 0 else None
        return base_terms(token, requests, request_count, hidden, matrix, factor, groups, half, n, grant, under)

    def send(x, edge, token):
        return along_edge(after(x, token), edge)

    kept, sent = select_rows(token, request_count, output_factor)
    token = after(token, kept, sent)
    swapped = swap(sent, "store", 1)
    (s00,) = base(token, [[0]], 0, 58)
    token = after(token, s00, swapped)
    e0_1 = along_edge(s00, 0)
    side = shard // 2 % 2
    kept, swapped, _ = lax.optimization_barrier((kept, swapped, token))
    outgoing = kept[1 - side] + swapped[1 - side]
    rows = kept[side] + swapped[side]
    token = after(token, outgoing, rows)
    swapped = swap(outgoing, "store", 2)
    s01, s11 = base(token, [[0], [1]], 1, 50)

    token = after(token, s01)
    e0_2 = send(s01, 0, token)
    token, e0_1 = lax.optimization_barrier((token, e0_1))
    b10 = join(token, piece, s00, 0, e0_1, 0)
    token = after(token, b10)
    e1_2 = along_edge(b10, 1)
    token, swapped = lax.optimization_barrier((token, swapped))
    rows = rows + swapped
    token = after(token, rows)
    near = lax.ppermute(rows, "tensor", [(0, 1), (n - 1, n - 2), (1, 0), (n - 2, n - 1)])
    far = along_edge(rows, 1)
    s10_s11, s20, s30 = base(token, [[1], [2], [3]], 0, 42, s11)

    token = after(token, s10_s11)
    e0_3 = send(s10_s11, 0, token)
    token, e0_2 = lax.optimization_barrier((token, e0_2))
    token = pass_on(token)
    token, e1_2 = lax.optimization_barrier((token, e1_2))
    token, near = lax.optimization_barrier((token, near))
    b11 = join(token, block, s01, 0, e0_2, 0, near, 0, bundle)
    token = after(token, b11)
    e1_3 = along_edge(b11, 1)
    c20 = join(token, piece, s20, 0, e1_2, 0, far, 0, bundle)
    token = after(token, c20)
    e2_3 = along_edge(c20, 2)
    s21, s31 = base(token, [[2], [3]], 1, 50)

    token = after(token, s21)
    e0_4 = send(s20, 0, token)
    token, e0_3 = lax.optimization_barrier((token, e0_3))
    b20 = join(token, piece, s10_s11, 0, e0_3, 0)
    token = after(token, b20)
    e1_4 = along_edge(b20, 1)
    token = after(token, e1_3, e2_3)
    c21 = join(token, block, s21, 0, e1_3, 0, e1_3, block, bundle)
    token = after(token, c21)
    e2_4 = along_edge(c21, 2)
    e0_5 = send(s21, 0, token)
    b21 = join(token, block, s10_s11, piece, e0_3, piece)
    token = after(token, b21)
    e1_5 = along_edge(b21, 1)

    token, e0_4 = lax.optimization_barrier((token, e0_4))
    e1_4 = lax.optimization_barrier((e1_4, token))[0]
    lora = s30[block:].astype(jnp.float32) + e0_4[block:].astype(jnp.float32)
    lora += e1_4[block:].astype(jnp.float32) + e2_3[block:piece].astype(jnp.float32)
    lora = lora.astype(jnp.bfloat16).reshape(piece - block, -1, width).swapaxes(0, 1).reshape(block, width)
    lora = lora + swap(lora, "store", 1)
    lora = lora + swap(lora, "store", 2)
    arrays = [s30, s31, rows, near, far, e1_3, e2_3, e2_4, e0_4, e1_4]
    items = [
        (2, 0, [(z, z) for z in range(n)]),
        (3, 0, [(0, 1), (1, 0), (2, 3), (3, 2)]),
        (4, 0, [(1, 2), (2, 1)]),
        (5, block, [(1, 3), (2, 0)]),
        (6, piece, [(0, 2), (3, 1)]),
        (7, block, [(0, 3), (3, 0)]),
    ]
    added = [(0, 0, 0), (8, 0, 0), (9, 0, 0), (6, 0, 0), (1, 0, 1), (7, 0, 1)]
    out = finish(token, requests, lora, arrays, items, added, request_count, rank_rows, n)
    return add_last(out, e0_5, e1_5)


def anywhere(hidden, matrix, input_factor, output_factor, token_requests, meta):
    request_adapters, ranks, slots = meta
    held = input_factor.shape[0]
    width = input_factor.shape[2]
    rank, slot = ranks[request_adapters], slots[request_adapters]
    owned = slot // held == lax.axis_index("store")
    chosen = token_requests[:, None] == jnp.arange(request_adapters.shape[0])[None, :]
    lora = jnp.zeros((hidden.shape[0], width), jnp.float32)
    for r in range(request_adapters.shape[0]):
        product = jnp.dot(hidden, input_factor[slot[r] % held], preferred_element_type=jnp.float32)
        keep = (chosen[:, r] & owned[r])[:, None] & (jnp.arange(width) < rank[r])[None, :]
        lora = jnp.where(keep, product, lora)
    lora = lax.psum_scatter(lora.astype(jnp.bfloat16), "tensor", scatter_dimension=1, tiled=True)
    lora = lax.psum(lora, "store").astype(jnp.float32)
    rows = jnp.where(owned[:, None, None], output_factor[slot % held], jnp.zeros((), output_factor.dtype))
    rows = lax.psum_scatter(rows, "store", scatter_dimension=2, tiled=True)
    weights = jnp.where(chosen, 0.25 * width / rank.astype(jnp.float32)[None, :], 0.0)
    expanded = (weights[:, :, None] * lora[:, None, :]).reshape(hidden.shape[0], -1).astype(jnp.bfloat16)
    term = jnp.dot(hidden, matrix, preferred_element_type=jnp.float32)
    term += jnp.dot(expanded, rows.reshape(-1, rows.shape[2]), preferred_element_type=jnp.float32)
    return lax.psum_scatter(term.astype(jnp.bfloat16), "tensor", scatter_dimension=0, tiled=True)


def per_device(
    hidden_activations,
    down_matrix,
    adapter_input_factor,
    adapter_output_factor,
    token_requests,
    request_adapters,
    adapter_ranks,
    adapter_store_slot,
):
    n = lax.axis_size("tensor")
    meta = (request_adapters, adapter_ranks, adapter_store_slot)
    arrays = (hidden_activations, down_matrix, adapter_input_factor, adapter_output_factor)
    if n == LINE and lax.axis_size("store") == 2 * PAIRS and adapter_input_factor.shape[0] % 2 == 0:
        place = jnp.stack([lax.axis_index("tensor"), lax.axis_index("store")]).astype(jnp.int32)
        token = jnp.concatenate([place, *meta])
        return on_line(*arrays, token_requests.reshape(-1, LANES), token, request_adapters.shape[0], n)
    return anywhere(*arrays, token_requests, meta)


def solution(mesh):
    in_specs = (
        P("groups", "tensor"),
        P("tensor", "store"),
        P(("groups", "store"), "tensor", None),
        P(("groups", "store"), "tensor", None),
        P("groups"),
        P("groups"),
        P("groups"),
        P("groups"),
    )
    out_specs = P(("groups", "tensor"), "store")
    return jax.shard_map(
        per_device, mesh=mesh, in_specs=in_specs, out_specs=out_specs, check_vma=False
    )
```

```python
import functools

import jax
import jax.numpy as jnp
from jax import lax
from jax.experimental import pallas as pl
from jax.experimental.pallas import tpu as pltpu
from jax.sharding import PartitionSpec as P

LINE = 4
LANES = 128
AHEAD = 3
PAIRS = 2
HEAVY = 10**10
MIB = 1024 * 1024


def line_order(n):
    order = []
    for z in range(n):
        sends = [(t, z >= n // 2, n - 1 - t + z) for t in range(z, n - 1)]
        sends += [(t, z < n // 2, t - (n - 1 - z)) for t in range(n - 1 - z, n - 1)]
        order.append([block for _, _, block in sorted(sends)] + [z])
    return order


def first_divisor(size, choices):
    for choice in choices:
        if size % choice == 0:
            return choice
    return size


def after(token, *done):
    return lax.optimization_barrier((token, done))[0]


def params(mebibytes):
    return pltpu.CompilerParams(vmem_limit_bytes=mebibytes * MIB)


def small_cost():
    return pl.CostEstimate(flops=10**6, bytes_accessed=10**5, transcendentals=0)


def block_at(order, slot, place):
    picked = jnp.int32(order[0][slot])
    for z in range(1, len(order)):
        picked = jnp.where(place == z, order[z][slot], picked)
    return picked


def spans(requests_ref, count):
    requests = requests_ref[...]
    return [jnp.int32(0)] + [jnp.sum((requests <= r).astype(jnp.int32)) for r in range(count)]


class Meta:
    def __init__(self, ref, requests):
        self.ref, self.requests = ref, requests
        self.adapters = (ref.shape[0] - 2 - requests) // 2
        self.place, self.shard = ref[0], ref[1]

    def adapter(self, r):
        return self.ref[2 + r]

    def rank(self, r):
        return self.ref[2 + self.requests + self.adapter(r)]

    def local_slot(self, r, held):
        return self.ref[2 + self.requests + self.adapters + self.adapter(r)] - self.shard * held


def base_kernel(order, groups, half, held, request_count, piece, handed_on, *refs):
    slots = [slot for group in groups for slot in group]
    places = [(g, i) for g, group in enumerate(groups) for i in range(len(group))]
    count = len(slots)
    meta, refs = Meta(refs[0], request_count), refs[1:]
    if held:
        requests_ref, factor, refs = refs[0], refs[1], refs[2:]
    hidden, matrix, refs = refs[0], refs[1], refs[2:]
    under, refs = (refs[0], refs[1:]) if handed_on else (None, refs)
    outs, refs = refs[: len(groups)], refs[len(groups) :]
    (rows, right, sums, sems), refs = refs[:4], refs[4:]
    steps, _, tile = rows.shape
    columns = outs[0].shape[1]
    block = rows.shape[1] // count
    first_rows = [pl.multiple_of(block_at(order, slot, meta.place) * block, block) for slot in slots]

    def depth_of(k):
        return pl.ds(pl.multiple_of(k * tile, tile), tile)

    def copies(k):
        moves = [
            (hidden.at[pl.ds(first_rows[i], block), depth_of(k)], rows.at[k, pl.ds(i * block, block), :])
            for i in range(count)
        ]
        moves.append((matrix.at[depth_of(k), pl.ds(half * columns, columns)], right.at[k]))
        return [pltpu.make_async_copy(a, b, sems.at[k, i]) for i, (a, b) in enumerate(moves)]

    if held:
        factors, inputs, factor_sems = refs
        width = factor.shape[2]

        def factor_copies(k, pair):
            return [
                pltpu.make_async_copy(
                    factor.at[2 * pair + i, depth_of(k), :],
                    factors.at[pair, k, :, pl.ds(i * width, width)],
                    factor_sems.at[k, 2 * pair + i],
                )
                for i in range(2)
            ]

    def start(k):
        for copy in copies(k):
            copy.start()

    def start_factors(k, pairs):
        for pair, used in enumerate(pairs):

            @pl.when(used)
            def _(pair=pair):
                for copy in factor_copies(k, pair):
                    copy.start()

    for k in range(min(AHEAD, steps)):
        start(k)
    used, blocks_using = [], []
    if held:
        bounds = spans(requests_ref, request_count)
        local = [meta.local_slot(r, held) for r in range(request_count)]
        for pair in range(held // 2):
            used_by = []
            for first in first_rows:
                wanted = jnp.bool_(False)
                for r, slot in enumerate(local):
                    here = jnp.maximum(bounds[r], first) < jnp.minimum(bounds[r + 1], first + block)
                    wanted = wanted | (here & (slot // 2 == pair) & (slot >= 0))
                used_by.append(wanted)
            blocks_using.append(used_by)
            used.append(functools.reduce(jnp.logical_or, used_by))
        for k in range(min(AHEAD, steps)):
            start_factors(k, used)
        inputs[...] = jnp.zeros_like(inputs)
    sums[...] = jnp.zeros_like(sums)

    def step(k, _):
        @pl.when(k + AHEAD < steps)
        def _():
            start(k + AHEAD)
            start_factors(k + AHEAD, used)

        for copy in copies(k):
            copy.wait()
        sums[...] += jnp.dot(rows[k], right[k], preferred_element_type=jnp.float32)
        for pair, wanted in enumerate(used):

            @pl.when(wanted)
            def _(pair=pair):
                for copy in factor_copies(k, pair):
                    copy.wait()

            for i, wanted_here in enumerate(blocks_using[pair]):

                @pl.when(wanted_here)
                def _(pair=pair, own=pl.ds(i * block, block)):
                    inputs[pair, own, :] += jnp.dot(
                        rows[k, own, :], factors[pair, k], preferred_element_type=jnp.float32
                    )

        return 0

    lax.fori_loop(0, steps, step, 0)
    if handed_on:
        outs[0][len(groups[0]) * piece :, :] = under[...]
    for i, (group, position) in enumerate(places):
        own = pl.ds(i * block, block)
        out, top = outs[group], position * piece
        out[top : top + block, :] = sums[own, :].astype(jnp.bfloat16)
        if held:
            row = lax.broadcasted_iota(jnp.int32, (block, width), 0) + first_rows[i]
            column = lax.broadcasted_iota(jnp.int32, (block, width), 1)
            total = jnp.zeros((block, width), jnp.float32)
            for r, slot in enumerate(local):
                last = jnp.where((slot >= 0) & (slot < held), bounds[r + 1], 0)
                keep = (row >= bounds[r]) & (row < last) & (column < meta.rank(r))
                slot = jnp.clip(slot, 0, held - 1)
                lanes = pl.ds(pl.multiple_of(slot % 2 * width, width), width)
                total = jnp.where(keep, inputs[slot // 2, own, lanes], total)
            total = total.astype(jnp.bfloat16)
            size = block * width // columns
            for j in range(columns // width):
                lanes = slice(j * width, (j + 1) * width)
                out[top + block : top + block + size, lanes] = total[j * size : (j + 1) * size, :]


def base_terms(meta, requests, request_count, hidden, matrix, factor, groups, half, n, grant, under=None):
    tokens, depth = hidden.shape
    block, columns = tokens // n, matrix.shape[1] // 2
    tile = first_divisor(depth, (1024, 512, 256, 128))
    steps = depth // tile
    count = sum(len(group) for group in groups)
    smem = pl.BlockSpec(memory_space=pltpu.SMEM)
    vmem = pl.BlockSpec(memory_space=pltpu.VMEM)
    hbm = pl.BlockSpec(memory_space=pltpu.HBM)
    held, out_rows = 0, block
    operands, in_specs = [meta], [smem]
    scratch = [
        pltpu.VMEM((steps, count * block, tile), jnp.bfloat16),
        pltpu.VMEM((steps, tile, columns), jnp.bfloat16),
        pltpu.VMEM((count * block, columns), jnp.float32),
        pltpu.SemaphoreType.DMA((steps, count + 1)),
    ]
    if factor is not None:
        held, _, width = factor.shape
        out_rows += block * width // columns
        operands, in_specs = [meta, requests, factor], [smem, vmem, hbm]
        scratch += [
            pltpu.VMEM((held // 2, steps, tile, 2 * width), jnp.bfloat16),
            pltpu.VMEM((held // 2, count * block, 2 * width), jnp.float32),
            pltpu.SemaphoreType.DMA((steps, held)),
        ]
    heights = [len(group) * out_rows for group in groups]
    operands, in_specs = operands + [hidden, matrix], in_specs + [hbm, hbm]
    if under is not None:
        heights[0] += under.shape[0]
        operands, in_specs = operands + [under], in_specs + [vmem]
    handed_on = under is not None
    return pl.pallas_call(
        lambda *refs: base_kernel(line_order(n), groups, half, held, request_count, out_rows, handed_on, *refs),
        out_shape=[jax.ShapeDtypeStruct((height, columns), jnp.bfloat16) for height in heights],
        in_specs=in_specs,
        out_specs=[vmem] * len(groups),
        scratch_shapes=scratch,
        compiler_params=params(grant),
        cost_estimate=small_cost(),
        name="base_terms",
    )(*operands)


def select_rows_kernel(request_count, meta_ref, factor, kept, sent):
    meta = Meta(meta_ref, request_count)
    held, rank_rows, _ = factor.shape
    width = factor.shape[2] // (2 * PAIRS)
    side = meta.shard % 2
    for r in range(request_count):
        slot = meta.local_slot(r, held)
        owned = (slot >= 0) & (slot < held)
        slot = jnp.clip(slot, 0, held - 1)
        for out, core in ((kept, side), (sent, 1 - side)):
            for i in range(PAIRS):
                for c in range(2):
                    first = (2 * i + core) * width + c * (width // 2)
                    rows = factor[slot, :, pl.ds(pl.multiple_of(first, LANES), width // 2)]
                    top = (c * request_count + r) * rank_rows
                    out[i, top : top + rank_rows, :] = jnp.where(owned, rows, jnp.zeros_like(rows))


def select_rows(meta, request_count, factor):
    _, rank_rows, model_width = factor.shape
    smem = pl.BlockSpec(memory_space=pltpu.SMEM)
    vmem = pl.BlockSpec(memory_space=pltpu.VMEM)
    shape = (PAIRS, 2 * request_count * rank_rows, model_width // (4 * PAIRS))
    out = jax.ShapeDtypeStruct(shape, factor.dtype)
    return pl.pallas_call(
        lambda *refs: select_rows_kernel(request_count, *refs),
        out_shape=[out, out],
        in_specs=[smem, vmem],
        out_specs=[vmem, vmem],
        compiler_params=params(16),
        cost_estimate=small_cost(),
        name="select_rows",
    )(meta, factor)


def expanded_inputs(meta, requests_ref, lora_ref):
    block, width = lora_ref.shape
    row = lax.broadcasted_iota(jnp.int32, (block, width), 0) + meta.place * block
    lora = lora_ref[...].astype(jnp.float32)
    bounds = spans(requests_ref, meta.requests)
    parts = []
    for r in range(meta.requests):
        scale = 0.25 * width / meta.rank(r).astype(jnp.float32)
        keep = (row >= bounds[r]) & (row < bounds[r + 1])
        parts.append(jnp.where(keep, lora * scale, 0.0).astype(jnp.bfloat16))
    return jnp.concatenate(parts, axis=1)


def finish_kernel(items, added, requests, rank_rows, n, *refs):
    meta_ref, requests_ref, lora_ref, refs = refs[0], refs[1], refs[2], refs[3:]
    arrays, out, rows = refs[:-2], refs[-2], refs[-1]
    meta = Meta(meta_ref, requests)
    rank = n * rank_rows
    half = out.shape[1] // 2
    for index, top, targets in items:
        for place, k in targets:

            @pl.when(meta.place == place)
            def _(piece=arrays[index], top=top, k=k):
                for r in range(requests):
                    first = r * rank + k * rank_rows
                    for c in range(2):
                        start = top + (c * requests + r) * rank_rows
                        rows[first : first + rank_rows, c * half : (c + 1) * half] = piece[start : start + rank_rows, :]

    expanded = expanded_inputs(meta, requests_ref, lora_ref)
    block = lora_ref.shape[0]
    for c in range(2):
        columns = slice(c * half, (c + 1) * half)
        total = jnp.dot(expanded, rows[:, columns], preferred_element_type=jnp.float32)
        for index, top, which in added:
            if which == c:
                total += arrays[index][top : top + block, :].astype(jnp.float32)
        out[:, columns] = total.astype(out.dtype)


def finish(meta, requests, lora, arrays, items, added, request_count, rank_rows, n):
    smem = pl.BlockSpec(memory_space=pltpu.SMEM)
    vmem = pl.BlockSpec(memory_space=pltpu.VMEM)
    width = 2 * arrays[0].shape[1]
    return pl.pallas_call(
        lambda *refs: finish_kernel(items, added, request_count, rank_rows, n, *refs),
        out_shape=jax.ShapeDtypeStruct((lora.shape[0], width), jnp.bfloat16),
        in_specs=[smem] + [vmem] * (2 + len(arrays)),
        out_specs=vmem,
        scratch_shapes=[pltpu.VMEM((request_count * n * rank_rows, width), jnp.bfloat16)],
        compiler_params=params(20),
        cost_estimate=small_cost(),
        name="finish",
    )(meta, requests, lora, *arrays)


def join_kernel(count, term_top, came_top, under_top, term, came, *refs):
    out = refs[-1]
    total = term[term_top : term_top + count, :].astype(jnp.float32)
    total += came[came_top : came_top + count, :].astype(jnp.float32)
    out[:count, :] = total.astype(out.dtype)
    if len(refs) > 1:
        under = refs[0]
        out[count:, :] = under[under_top : under_top + out.shape[0] - count, :]


def join(token, count, term, term_top, came, came_top, under=None, under_top=0, under_count=0, weight=10**6):
    arrays = [term, came] + ([] if under is None else [under])
    arrays = lax.optimization_barrier((arrays, token))[0]
    vmem = pl.BlockSpec(memory_space=pltpu.VMEM)
    return pl.pallas_call(
        lambda *refs: join_kernel(count, term_top, came_top, under_top, *refs),
        out_shape=jax.ShapeDtypeStruct((count + under_count, term.shape[1]), term.dtype),
        in_specs=[vmem] * len(arrays),
        out_specs=vmem,
        compiler_params=params(12),
        cost_estimate=pl.CostEstimate(flops=weight, bytes_accessed=10**5, transcendentals=0),
        name="join",
    )(*arrays)


def add_last_kernel(total, *refs):
    arrivals, out = refs[:-1], refs[-1]
    half = arrivals[0].shape[1]
    out[:, :half] = total[:, :half]
    last = total[:, half:].astype(jnp.float32)
    for arrival in arrivals:
        last += arrival[...].astype(jnp.float32)
    out[:, half:] = last.astype(out.dtype)


def add_last(total, *arrivals):
    vmem = pl.BlockSpec(memory_space=pltpu.VMEM)
    return pl.pallas_call(
        add_last_kernel,
        out_shape=jax.ShapeDtypeStruct(total.shape, total.dtype),
        in_specs=[vmem] * (1 + len(arrivals)),
        out_specs=vmem,
        compiler_params=params(12),
        cost_estimate=small_cost(),
        name="add_last",
    )(total, *arrivals)


def swap(x, axis, bit):
    return lax.ppermute(x, axis, [(i, i ^ bit) for i in range(lax.axis_size(axis))])


def bits_of(size):
    return [1 << i for i in range(size.bit_length() - 1)]


def along_edge(x, edge):
    n = lax.axis_size("tensor")
    return lax.ppermute(x, "tensor", [(edge, edge + 1), (n - 1 - edge, n - 2 - edge)])


def on_line(hidden, matrix, input_factor, output_factor, requests, token, request_count, n):
    shard = lax.axis_index("store")
    block = hidden.shape[0] // n
    width = input_factor.shape[2]
    rank_rows = output_factor.shape[1]
    piece = block + block * width // (matrix.shape[1] // 2)
    bundle = 2 * request_count * rank_rows

    def base(token, groups, half, grant, under=None):
        factor = input_factor if half == 0 else None
        return base_terms(token, requests, request_count, hidden, matrix, factor, groups, half, n, grant, under)

    def send(x, edge, token):
        return along_edge(after(x, token), edge)

    kept, sent = select_rows(token, request_count, output_factor)
    token = after(token, kept, sent)
    swapped = swap(sent, "store", 1)
    (s00,) = base(token, [[0]], 0, 58)
    token = after(token, s00, swapped)
    e0_1 = along_edge(s00, 0)
    side = shard // 2 % 2
    kept, swapped, _ = lax.optimization_barrier((kept, swapped, token))
    outgoing = kept[1 - side] + swapped[1 - side]
    rows = kept[side] + swapped[side]
    token = after(token, outgoing, rows)
    swapped = swap(outgoing, "store", 2)
    s01, s11 = base(token, [[0], [1]], 1, 50)

    token = after(token, s01)
    e0_2 = send(s01, 0, token)
    token, e0_1 = lax.optimization_barrier((token, e0_1))
    b10 = join(token, piece, s00, 0, e0_1, 0)
    token = after(token, b10)
    e1_2 = along_edge(b10, 1)
    token, swapped = lax.optimization_barrier((token, swapped))
    rows = rows + swapped
    token = after(token, rows)
    near = lax.ppermute(rows, "tensor", [(0, 1), (n - 1, n - 2), (1, 0), (n - 2, n - 1)])
    far = along_edge(rows, 1)
    s10_s11, s20, s30 = base(token, [[1], [2], [3]], 0, 50, s11)

    token = after(token, s10_s11)
    e0_3 = send(s10_s11, 0, token)
    token, e0_2 = lax.optimization_barrier((token, e0_2))
    b11 = join(token, block, s01, 0, e0_2, 0, weight=HEAVY)
    token, near = lax.optimization_barrier((after(token, b11), near))
    e1_3 = along_edge(b11, 1)
    far_2 = send(near, 1, token)
    token, e1_2, far = lax.optimization_barrier((token, e1_2, far))
    c20 = join(token, piece, s20, 0, e1_2, 0, far, 0, bundle)
    token = after(token, c20)
    e2_3 = along_edge(c20, 2)
    s21, s31 = base(token, [[2], [3]], 1, 50)

    token = after(token, s21)
    e0_4 = send(s20, 0, token)
    token, e0_3 = lax.optimization_barrier((token, e0_3))
    b20 = join(token, piece, s10_s11, 0, e0_3, 0)
    token = after(token, b20)
    e1_4 = along_edge(b20, 1)
    token, far_2 = lax.optimization_barrier((token, far_2))
    last_rows = send(far_2, 2, token)
    token, e1_3 = lax.optimization_barrier((token, e1_3))
    c21 = join(token, block, s21, 0, e1_3, 0, weight=HEAVY)
    token = after(token, c21)
    e2_4 = along_edge(c21, 2)
    token, e2_3 = lax.optimization_barrier((token, e2_3))
    e0_5 = send(s21, 0, token)
    b21 = join(token, block, s10_s11, piece, e0_3, piece)
    token = after(token, b21)
    e1_5 = along_edge(b21, 1)

    token, e0_4 = lax.optimization_barrier((token, e0_4))
    token, e1_4 = lax.optimization_barrier((token, e1_4))
    token, last_rows = lax.optimization_barrier((token, last_rows))
    e1_4 = after(e1_4, token)
    lora = s30[block:].astype(jnp.float32) + e0_4[block:].astype(jnp.float32)
    lora += e1_4[block:].astype(jnp.float32) + e2_3[block:piece].astype(jnp.float32)
    lora = lora.astype(jnp.bfloat16).reshape(piece - block, -1, width).swapaxes(0, 1).reshape(block, width)
    lora = lora + swap(lora, "store", 1)
    lora = lora + swap(lora, "store", 2)
    arrays = [s30, s31, rows, near, far, far_2, e2_3, last_rows, e0_4, e1_4]
    items = [
        (2, 0, [(z, z) for z in range(n)]),
        (3, 0, [(0, 1), (1, 0), (2, 3), (3, 2)]),
        (4, 0, [(1, 2), (2, 1)]),
        (5, 0, [(1, 3), (2, 0)]),
        (6, piece, [(0, 2), (3, 1)]),
        (7, 0, [(0, 3), (3, 0)]),
    ]
    added = [(0, 0, 0), (8, 0, 0), (9, 0, 0), (6, 0, 0), (1, 0, 1)]
    out = finish(token, requests, lora, arrays, items, added, request_count, rank_rows, n)
    return add_last(out, e0_5, e1_5, e2_4)


def anywhere(hidden, matrix, input_factor, output_factor, token_requests, meta):
    request_adapters, ranks, slots = meta
    held = input_factor.shape[0]
    width = input_factor.shape[2]
    rank, slot = ranks[request_adapters], slots[request_adapters]
    owned = slot // held == lax.axis_index("store")
    chosen = token_requests[:, None] == jnp.arange(request_adapters.shape[0])[None, :]
    lora = jnp.zeros((hidden.shape[0], width), jnp.float32)
    for r in range(request_adapters.shape[0]):
        product = jnp.dot(hidden, input_factor[slot[r] % held], preferred_element_type=jnp.float32)
        keep = (chosen[:, r] & owned[r])[:, None] & (jnp.arange(width) < rank[r])[None, :]
        lora = jnp.where(keep, product, lora)
    lora = lax.psum_scatter(lora.astype(jnp.bfloat16), "tensor", scatter_dimension=1, tiled=True)
    lora = lax.psum(lora, "store").astype(jnp.float32)
    rows = jnp.where(owned[:, None, None], output_factor[slot % held], jnp.zeros((), output_factor.dtype))
    rows = lax.psum_scatter(rows, "store", scatter_dimension=2, tiled=True)
    weights = jnp.where(chosen, 0.25 * width / rank.astype(jnp.float32)[None, :], 0.0)
    expanded = (weights[:, :, None] * lora[:, None, :]).reshape(hidden.shape[0], -1).astype(jnp.bfloat16)
    term = jnp.dot(hidden, matrix, preferred_element_type=jnp.float32)
    term += jnp.dot(expanded, rows.reshape(-1, rows.shape[2]), preferred_element_type=jnp.float32)
    return lax.psum_scatter(term.astype(jnp.bfloat16), "tensor", scatter_dimension=0, tiled=True)


def per_device(
    hidden_activations,
    down_matrix,
    adapter_input_factor,
    adapter_output_factor,
    token_requests,
    request_adapters,
    adapter_ranks,
    adapter_store_slot,
):
    n = lax.axis_size("tensor")
    meta = (request_adapters, adapter_ranks, adapter_store_slot)
    arrays = (hidden_activations, down_matrix, adapter_input_factor, adapter_output_factor)
    if n == LINE and lax.axis_size("store") == 2 * PAIRS and adapter_input_factor.shape[0] % 2 == 0:
        place = jnp.stack([lax.axis_index("tensor"), lax.axis_index("store")]).astype(jnp.int32)
        token = jnp.concatenate([place, *meta])
        return on_line(*arrays, token_requests.reshape(-1, LANES), token, request_adapters.shape[0], n)
    return anywhere(*arrays, token_requests, meta)


def solution(mesh):
    in_specs = (
        P("groups", "tensor"),
        P("tensor", "store"),
        P(("groups", "store"), "tensor", None),
        P(("groups", "store"), "tensor", None),
        P("groups"),
        P("groups"),
        P("groups"),
        P("groups"),
    )
    out_specs = P(("groups", "tensor"), "store")
    return jax.shard_map(
        per_device, mesh=mesh, in_specs=in_specs, out_specs=out_specs, check_vma=False
    )
```

```python
import functools

import jax
import jax.numpy as jnp
from jax import lax
from jax.experimental import pallas as pl
from jax.experimental.pallas import tpu as pltpu
from jax.sharding import PartitionSpec as P

LINE = 4
LANES = 128
AHEAD = 3
PAIRS = 2
HEAVY = 10**10
MIB = 1024 * 1024


def line_order(n):
    order = []
    for z in range(n):
        sends = [(t, z >= n // 2, n - 1 - t + z) for t in range(z, n - 1)]
        sends += [(t, z < n // 2, t - (n - 1 - z)) for t in range(n - 1 - z, n - 1)]
        order.append([block for _, _, block in sorted(sends)] + [z])
    return order


def first_divisor(size, choices):
    for choice in choices:
        if size % choice == 0:
            return choice
    return size


def after(token, *done):
    return lax.optimization_barrier((token, done))[0]


def params(mebibytes):
    return pltpu.CompilerParams(vmem_limit_bytes=mebibytes * MIB)


def small_cost():
    return pl.CostEstimate(flops=10**6, bytes_accessed=10**5, transcendentals=0)


def block_at(order, slot, place):
    picked = jnp.int32(order[0][slot])
    for z in range(1, len(order)):
        picked = jnp.where(place == z, order[z][slot], picked)
    return picked


def spans(requests_ref, count):
    requests = requests_ref[...]
    return [jnp.int32(0)] + [jnp.sum((requests <= r).astype(jnp.int32)) for r in range(count)]


class Meta:
    def __init__(self, ref, requests):
        self.ref, self.requests = ref, requests
        self.adapters = (ref.shape[0] - 2 - requests) // 2
        self.place, self.shard = ref[0], ref[1]

    def adapter(self, r):
        return self.ref[2 + r]

    def rank(self, r):
        return self.ref[2 + self.requests + self.adapter(r)]

    def local_slot(self, r, held):
        return self.ref[2 + self.requests + self.adapters + self.adapter(r)] - self.shard * held


def base_kernel(order, groups, half, held, request_count, piece, handed_on, *refs):
    slots = [slot for group in groups for slot in group]
    places = [(g, i) for g, group in enumerate(groups) for i in range(len(group))]
    count = len(slots)
    meta, refs = Meta(refs[0], request_count), refs[1:]
    if held:
        requests_ref, factor, refs = refs[0], refs[1], refs[2:]
    hidden, matrix, refs = refs[0], refs[1], refs[2:]
    under, refs = (refs[0], refs[1:]) if handed_on else (None, refs)
    outs, refs = refs[: len(groups)], refs[len(groups) :]
    (rows, right, sums, sems), refs = refs[:4], refs[4:]
    steps, _, tile = rows.shape
    columns = outs[0].shape[1]
    block = rows.shape[1] // count
    first_rows = [pl.multiple_of(block_at(order, slot, meta.place) * block, block) for slot in slots]

    def depth_of(k):
        return pl.ds(pl.multiple_of(k * tile, tile), tile)

    def copies(k):
        moves = [
            (hidden.at[pl.ds(first_rows[i], block), depth_of(k)], rows.at[k, pl.ds(i * block, block), :])
            for i in range(count)
        ]
        moves.append((matrix.at[depth_of(k), pl.ds(half * columns, columns)], right.at[k]))
        return [pltpu.make_async_copy(a, b, sems.at[k, i]) for i, (a, b) in enumerate(moves)]

    if held:
        factors, inputs, factor_sems = refs
        width = factor.shape[2]

        def factor_copies(k, pair):
            return [
                pltpu.make_async_copy(
                    factor.at[2 * pair + i, depth_of(k), :],
                    factors.at[pair, k, :, pl.ds(i * width, width)],
                    factor_sems.at[k, 2 * pair + i],
                )
                for i in range(2)
            ]

    def start(k):
        for copy in copies(k):
            copy.start()

    def start_factors(k, pairs):
        for pair, used in enumerate(pairs):

            @pl.when(used)
            def _(pair=pair):
                for copy in factor_copies(k, pair):
                    copy.start()

    for k in range(min(AHEAD, steps)):
        start(k)
    used, blocks_using = [], []
    if held:
        bounds = spans(requests_ref, request_count)
        local = [meta.local_slot(r, held) for r in range(request_count)]
        for pair in range(held // 2):
            used_by = []
            for first in first_rows:
                wanted = jnp.bool_(False)
                for r, slot in enumerate(local):
                    here = jnp.maximum(bounds[r], first) < jnp.minimum(bounds[r + 1], first + block)
                    wanted = wanted | (here & (slot // 2 == pair) & (slot >= 0))
                used_by.append(wanted)
            blocks_using.append(used_by)
            used.append(functools.reduce(jnp.logical_or, used_by))
        for k in range(min(AHEAD, steps)):
            start_factors(k, used)
        inputs[...] = jnp.zeros_like(inputs)
    for k in range(steps):
        if k + AHEAD < steps:
            start(k + AHEAD)
            start_factors(k + AHEAD, used)
        for copy in copies(k):
            copy.wait()
        product = jnp.dot(rows[k], right[k], preferred_element_type=jnp.float32)
        if k == 0:
            sums[...] = product
        elif k < steps - 1:
            sums[...] += product
        else:
            total = (sums[...] + product).astype(jnp.bfloat16)
            for i, (group, position) in enumerate(places):
                top = position * piece
                outs[group][top : top + block, :] = total[i * block : (i + 1) * block, :]
        for pair, wanted in enumerate(used):

            @pl.when(wanted)
            def _(k=k, pair=pair):
                for copy in factor_copies(k, pair):
                    copy.wait()

            for i, wanted_here in enumerate(blocks_using[pair]):

                @pl.when(wanted_here)
                def _(k=k, pair=pair, own=pl.ds(i * block, block)):
                    inputs[pair, own, :] += jnp.dot(
                        rows[k, own, :], factors[pair, k], preferred_element_type=jnp.float32
                    )

    if handed_on:
        outs[0][len(groups[0]) * piece :, :] = under[...]
    for i, (group, position) in enumerate(places):
        if held:
            own = pl.ds(i * block, block)
            out, top = outs[group], position * piece
            row = lax.broadcasted_iota(jnp.int32, (block, width), 0) + first_rows[i]
            column = lax.broadcasted_iota(jnp.int32, (block, width), 1)
            total = jnp.zeros((block, width), jnp.float32)
            for r, slot in enumerate(local):
                last = jnp.where((slot >= 0) & (slot < held), bounds[r + 1], 0)
                keep = (row >= bounds[r]) & (row < last) & (column < meta.rank(r))
                slot = jnp.clip(slot, 0, held - 1)
                lanes = pl.ds(pl.multiple_of(slot % 2 * width, width), width)
                total = jnp.where(keep, inputs[slot // 2, own, lanes], total)
            total = total.astype(jnp.bfloat16)
            size = block * width // columns
            for j in range(columns // width):
                lanes = slice(j * width, (j + 1) * width)
                out[top + block : top + block + size, lanes] = total[j * size : (j + 1) * size, :]


def base_terms(meta, requests, request_count, hidden, matrix, factor, groups, half, n, grant, under=None):
    tokens, depth = hidden.shape
    block, columns = tokens // n, matrix.shape[1] // 2
    tile = first_divisor(depth, (1024, 512, 256, 128))
    steps = depth // tile
    count = sum(len(group) for group in groups)
    smem = pl.BlockSpec(memory_space=pltpu.SMEM)
    vmem = pl.BlockSpec(memory_space=pltpu.VMEM)
    hbm = pl.BlockSpec(memory_space=pltpu.HBM)
    held, out_rows = 0, block
    operands, in_specs = [meta], [smem]
    scratch = [
        pltpu.VMEM((steps, count * block, tile), jnp.bfloat16),
        pltpu.VMEM((steps, tile, columns), jnp.bfloat16),
        pltpu.VMEM((count * block, columns), jnp.float32),
        pltpu.SemaphoreType.DMA((steps, count + 1)),
    ]
    if factor is not None:
        held, _, width = factor.shape
        out_rows += block * width // columns
        operands, in_specs = [meta, requests, factor], [smem, vmem, hbm]
        scratch += [
            pltpu.VMEM((held // 2, steps, tile, 2 * width), jnp.bfloat16),
            pltpu.VMEM((held // 2, count * block, 2 * width), jnp.float32),
            pltpu.SemaphoreType.DMA((steps, held)),
        ]
    heights = [len(group) * out_rows for group in groups]
    operands, in_specs = operands + [hidden, matrix], in_specs + [hbm, hbm]
    if under is not None:
        heights[0] += under.shape[0]
        operands, in_specs = operands + [under], in_specs + [vmem]
    handed_on = under is not None
    return pl.pallas_call(
        lambda *refs: base_kernel(line_order(n), groups, half, held, request_count, out_rows, handed_on, *refs),
        out_shape=[jax.ShapeDtypeStruct((height, columns), jnp.bfloat16) for height in heights],
        in_specs=in_specs,
        out_specs=[vmem] * len(groups),
        scratch_shapes=scratch,
        compiler_params=params(grant),
        cost_estimate=small_cost(),
        name="base_terms",
    )(*operands)


def select_rows_kernel(request_count, meta_ref, factor, kept, sent):
    meta = Meta(meta_ref, request_count)
    held, rank_rows, _ = factor.shape
    width = factor.shape[2] // (2 * PAIRS)
    side = meta.shard % 2
    for r in range(request_count):
        slot = meta.local_slot(r, held)
        owned = (slot >= 0) & (slot < held)
        slot = jnp.clip(slot, 0, held - 1)
        for out, core in ((kept, side), (sent, 1 - side)):
            for i in range(PAIRS):
                for c in range(2):
                    first = (2 * i + core) * width + c * (width // 2)
                    rows = factor[slot, :, pl.ds(pl.multiple_of(first, LANES), width // 2)]
                    top = (c * request_count + r) * rank_rows
                    out[i, top : top + rank_rows, :] = jnp.where(owned, rows, jnp.zeros_like(rows))


def select_rows(meta, request_count, factor):
    _, rank_rows, model_width = factor.shape
    smem = pl.BlockSpec(memory_space=pltpu.SMEM)
    vmem = pl.BlockSpec(memory_space=pltpu.VMEM)
    shape = (PAIRS, 2 * request_count * rank_rows, model_width // (4 * PAIRS))
    out = jax.ShapeDtypeStruct(shape, factor.dtype)
    return pl.pallas_call(
        lambda *refs: select_rows_kernel(request_count, *refs),
        out_shape=[out, out],
        in_specs=[smem, vmem],
        out_specs=[vmem, vmem],
        compiler_params=params(16),
        cost_estimate=small_cost(),
        name="select_rows",
    )(meta, factor)


def expanded_inputs(meta, requests_ref, lora_ref):
    block, width = lora_ref.shape
    row = lax.broadcasted_iota(jnp.int32, (block, width), 0) + meta.place * block
    lora = lora_ref[...].astype(jnp.float32)
    bounds = spans(requests_ref, meta.requests)
    parts = []
    for r in range(meta.requests):
        scale = 0.25 * width / meta.rank(r).astype(jnp.float32)
        keep = (row >= bounds[r]) & (row < bounds[r + 1])
        parts.append(jnp.where(keep, lora * scale, 0.0).astype(jnp.bfloat16))
    return jnp.concatenate(parts, axis=1)


def finish_kernel(items, added, requests, rank_rows, n, *refs):
    meta_ref, requests_ref, lora_ref, refs = refs[0], refs[1], refs[2], refs[3:]
    arrays, out, rows = refs[:-2], refs[-2], refs[-1]
    meta = Meta(meta_ref, requests)
    rank = n * rank_rows
    half = out.shape[1] // 2
    for index, top, targets in items:
        for place, k in targets:

            @pl.when(meta.place == place)
            def _(piece=arrays[index], top=top, k=k):
                for r in range(requests):
                    first = r * rank + k * rank_rows
                    for c in range(2):
                        start = top + (c * requests + r) * rank_rows
                        rows[first : first + rank_rows, c * half : (c + 1) * half] = piece[start : start + rank_rows, :]

    expanded = expanded_inputs(meta, requests_ref, lora_ref)
    block = lora_ref.shape[0]
    for c in range(2):
        columns = slice(c * half, (c + 1) * half)
        total = jnp.dot(expanded, rows[:, columns], preferred_element_type=jnp.float32)
        for index, top, which in added:
            if which == c:
                total += arrays[index][top : top + block, :].astype(jnp.float32)
        out[:, columns] = total.astype(out.dtype)


def finish(meta, requests, lora, arrays, items, added, request_count, rank_rows, n):
    smem = pl.BlockSpec(memory_space=pltpu.SMEM)
    vmem = pl.BlockSpec(memory_space=pltpu.VMEM)
    width = 2 * arrays[0].shape[1]
    return pl.pallas_call(
        lambda *refs: finish_kernel(items, added, request_count, rank_rows, n, *refs),
        out_shape=jax.ShapeDtypeStruct((lora.shape[0], width), jnp.bfloat16),
        in_specs=[smem] + [vmem] * (2 + len(arrays)),
        out_specs=vmem,
        scratch_shapes=[pltpu.VMEM((request_count * n * rank_rows, width), jnp.bfloat16)],
        compiler_params=params(20),
        cost_estimate=small_cost(),
        name="finish",
    )(meta, requests, lora, *arrays)


def join_kernel(count, term_top, came_top, under_top, term, came, *refs):
    out = refs[-1]
    total = term[term_top : term_top + count, :].astype(jnp.float32)
    total += came[came_top : came_top + count, :].astype(jnp.float32)
    out[:count, :] = total.astype(out.dtype)
    if len(refs) > 1:
        under = refs[0]
        out[count:, :] = under[under_top : under_top + out.shape[0] - count, :]


def join(token, count, term, term_top, came, came_top, under=None, under_top=0, under_count=0, weight=10**6):
    arrays = [term, came] + ([] if under is None else [under])
    arrays = lax.optimization_barrier((arrays, token))[0]
    vmem = pl.BlockSpec(memory_space=pltpu.VMEM)
    return pl.pallas_call(
        lambda *refs: join_kernel(count, term_top, came_top, under_top, *refs),
        out_shape=jax.ShapeDtypeStruct((count + under_count, term.shape[1]), term.dtype),
        in_specs=[vmem] * len(arrays),
        out_specs=vmem,
        compiler_params=params(12),
        cost_estimate=pl.CostEstimate(flops=weight, bytes_accessed=10**5, transcendentals=0),
        name="join",
    )(*arrays)


def add_last_kernel(total, *refs):
    arrivals, out = refs[:-1], refs[-1]
    half = arrivals[0].shape[1]
    out[:, :half] = total[:, :half]
    last = total[:, half:].astype(jnp.float32)
    for arrival in arrivals:
        last += arrival[...].astype(jnp.float32)
    out[:, half:] = last.astype(out.dtype)


def add_last(total, *arrivals):
    vmem = pl.BlockSpec(memory_space=pltpu.VMEM)
    return pl.pallas_call(
        add_last_kernel,
        out_shape=jax.ShapeDtypeStruct(total.shape, total.dtype),
        in_specs=[vmem] * (1 + len(arrivals)),
        out_specs=vmem,
        compiler_params=params(12),
        cost_estimate=small_cost(),
        name="add_last",
    )(total, *arrivals)


def swap(x, axis, bit):
    return lax.ppermute(x, axis, [(i, i ^ bit) for i in range(lax.axis_size(axis))])


def bits_of(size):
    return [1 << i for i in range(size.bit_length() - 1)]


def along_edge(x, edge):
    n = lax.axis_size("tensor")
    return lax.ppermute(x, "tensor", [(edge, edge + 1), (n - 1 - edge, n - 2 - edge)])


def on_line(hidden, matrix, input_factor, output_factor, requests, token, request_count, n):
    shard = lax.axis_index("store")
    block = hidden.shape[0] // n
    width = input_factor.shape[2]
    rank_rows = output_factor.shape[1]
    piece = block + block * width // (matrix.shape[1] // 2)
    bundle = 2 * request_count * rank_rows

    def base(token, groups, half, grant, under=None):
        factor = input_factor if half == 0 else None
        return base_terms(token, requests, request_count, hidden, matrix, factor, groups, half, n, grant, under)

    def send(x, edge, token):
        return along_edge(after(x, token), edge)

    (s00,) = base(token, [[0]], 0, 58)
    token = after(token, s00)
    e0_1 = along_edge(s00, 0)
    kept, sent = select_rows(token, request_count, output_factor)
    token = after(token, kept, sent)
    swapped = swap(sent, "store", 1)
    token = after(token, swapped)
    side = shard // 2 % 2
    kept, swapped, _ = lax.optimization_barrier((kept, swapped, token))
    outgoing = kept[1 - side] + swapped[1 - side]
    rows = kept[side] + swapped[side]
    token = after(token, outgoing, rows)
    swapped = swap(outgoing, "store", 2)
    s01, s11 = base(token, [[0], [1]], 1, 50)

    token = after(token, s01)
    e0_2 = send(s01, 0, token)
    token, e0_1 = lax.optimization_barrier((token, e0_1))
    b10 = join(token, piece, s00, 0, e0_1, 0)
    token = after(token, b10)
    e1_2 = along_edge(b10, 1)
    token, swapped = lax.optimization_barrier((token, swapped))
    rows = rows + swapped
    token = after(token, rows)
    near = lax.ppermute(rows, "tensor", [(0, 1), (n - 1, n - 2), (1, 0), (n - 2, n - 1)])
    far = along_edge(rows, 1)
    s10_s11, s20, s30 = base(token, [[1], [2], [3]], 0, 50, s11)

    token = after(token, s10_s11)
    e0_3 = send(s10_s11, 0, token)
    token, e0_2 = lax.optimization_barrier((token, e0_2))
    b11 = join(token, block, s01, 0, e0_2, 0, weight=HEAVY)
    token, near = lax.optimization_barrier((after(token, b11), near))
    e1_3 = along_edge(b11, 1)
    far_2 = send(near, 1, token)
    token, e1_2, far = lax.optimization_barrier((token, e1_2, far))
    c20 = join(token, piece, s20, 0, e1_2, 0, far, 0, bundle)
    token = after(token, c20)
    e2_3 = along_edge(c20, 2)
    s21, s31 = base(token, [[2], [3]], 1, 50)

    token = after(token, s21)
    e0_4 = send(s20, 0, token)
    token, e0_3 = lax.optimization_barrier((token, e0_3))
    b20 = join(token, piece, s10_s11, 0, e0_3, 0)
    token = after(token, b20)
    e1_4 = along_edge(b20, 1)
    token, far_2 = lax.optimization_barrier((token, far_2))
    last_rows = send(far_2, 2, token)
    token, e1_3 = lax.optimization_barrier((token, e1_3))
    c21 = join(token, block, s21, 0, e1_3, 0, weight=HEAVY)
    token = after(token, c21)
    e2_4 = along_edge(c21, 2)
    token, e2_3 = lax.optimization_barrier((token, e2_3))
    e0_5 = send(s21, 0, token)
    b21 = join(token, block, s10_s11, piece, e0_3, piece)
    token = after(token, b21)
    e1_5 = along_edge(b21, 1)

    token, e0_4 = lax.optimization_barrier((token, e0_4))
    token, e1_4 = lax.optimization_barrier((token, e1_4))
    token, last_rows = lax.optimization_barrier((token, last_rows))
    e1_4 = after(e1_4, token)
    lora = s30[block:].astype(jnp.float32) + e0_4[block:].astype(jnp.float32)
    lora += e1_4[block:].astype(jnp.float32) + e2_3[block:piece].astype(jnp.float32)
    lora = lora.astype(jnp.bfloat16).reshape(piece - block, -1, width).swapaxes(0, 1).reshape(block, width)
    lora = lora + swap(lora, "store", 1)
    lora = lora + swap(lora, "store", 2)
    arrays = [s30, s31, rows, near, far, far_2, e2_3, last_rows, e0_4, e1_4]
    items = [
        (2, 0, [(z, z) for z in range(n)]),
        (3, 0, [(0, 1), (1, 0), (2, 3), (3, 2)]),
        (4, 0, [(1, 2), (2, 1)]),
        (5, 0, [(1, 3), (2, 0)]),
        (6, piece, [(0, 2), (3, 1)]),
        (7, 0, [(0, 3), (3, 0)]),
    ]
    added = [(0, 0, 0), (8, 0, 0), (9, 0, 0), (6, 0, 0), (1, 0, 1)]
    out = finish(token, requests, lora, arrays, items, added, request_count, rank_rows, n)
    return add_last(out, e0_5, e1_5, e2_4)


def anywhere(hidden, matrix, input_factor, output_factor, token_requests, meta):
    request_adapters, ranks, slots = meta
    held = input_factor.shape[0]
    width = input_factor.shape[2]
    rank, slot = ranks[request_adapters], slots[request_adapters]
    owned = slot // held == lax.axis_index("store")
    chosen = token_requests[:, None] == jnp.arange(request_adapters.shape[0])[None, :]
    lora = jnp.zeros((hidden.shape[0], width), jnp.float32)
    for r in range(request_adapters.shape[0]):
        product = jnp.dot(hidden, input_factor[slot[r] % held], preferred_element_type=jnp.float32)
        keep = (chosen[:, r] & owned[r])[:, None] & (jnp.arange(width) < rank[r])[None, :]
        lora = jnp.where(keep, product, lora)
    lora = lax.psum_scatter(lora.astype(jnp.bfloat16), "tensor", scatter_dimension=1, tiled=True)
    lora = lax.psum(lora, "store").astype(jnp.float32)
    rows = jnp.where(owned[:, None, None], output_factor[slot % held], jnp.zeros((), output_factor.dtype))
    rows = lax.psum_scatter(rows, "store", scatter_dimension=2, tiled=True)
    weights = jnp.where(chosen, 0.25 * width / rank.astype(jnp.float32)[None, :], 0.0)
    expanded = (weights[:, :, None] * lora[:, None, :]).reshape(hidden.shape[0], -1).astype(jnp.bfloat16)
    term = jnp.dot(hidden, matrix, preferred_element_type=jnp.float32)
    term += jnp.dot(expanded, rows.reshape(-1, rows.shape[2]), preferred_element_type=jnp.float32)
    return lax.psum_scatter(term.astype(jnp.bfloat16), "tensor", scatter_dimension=0, tiled=True)


def per_device(
    hidden_activations,
    down_matrix,
    adapter_input_factor,
    adapter_output_factor,
    token_requests,
    request_adapters,
    adapter_ranks,
    adapter_store_slot,
):
    n = lax.axis_size("tensor")
    meta = (request_adapters, adapter_ranks, adapter_store_slot)
    arrays = (hidden_activations, down_matrix, adapter_input_factor, adapter_output_factor)
    if n == LINE and lax.axis_size("store") == 2 * PAIRS and adapter_input_factor.shape[0] % 2 == 0:
        place = jnp.stack([lax.axis_index("tensor"), lax.axis_index("store")]).astype(jnp.int32)
        token = jnp.concatenate([place, *meta])
        return on_line(*arrays, token_requests.reshape(-1, LANES), token, request_adapters.shape[0], n)
    return anywhere(*arrays, token_requests, meta)


def solution(mesh):
    in_specs = (
        P("groups", "tensor"),
        P("tensor", "store"),
        P(("groups", "store"), "tensor", None),
        P(("groups", "store"), "tensor", None),
        P("groups"),
        P("groups"),
        P("groups"),
        P("groups"),
    )
    out_specs = P(("groups", "tensor"), "store")
    return jax.shard_map(
        per_device, mesh=mesh, in_specs=in_specs, out_specs=out_specs, check_vma=False
    )
```

```python
import functools

import jax
import jax.numpy as jnp
from jax import lax
from jax.experimental import pallas as pl
from jax.experimental.pallas import tpu as pltpu
from jax.sharding import PartitionSpec as P

LINE = 4
LANES = 128
AHEAD = 3
PAIRS = 2
HEAVY = 10**10
MIB = 1024 * 1024


def line_order(n):
    order = []
    for z in range(n):
        sends = [(t, z >= n // 2, n - 1 - t + z) for t in range(z, n - 1)]
        sends += [(t, z < n // 2, t - (n - 1 - z)) for t in range(n - 1 - z, n - 1)]
        order.append([block for _, _, block in sorted(sends)] + [z])
    return order


def first_divisor(size, choices):
    for choice in choices:
        if size % choice == 0:
            return choice
    return size


def after(token, *done):
    return lax.optimization_barrier((token, done))[0]


def params(mebibytes):
    return pltpu.CompilerParams(vmem_limit_bytes=mebibytes * MIB)


def small_cost():
    return pl.CostEstimate(flops=10**6, bytes_accessed=10**5, transcendentals=0)


def block_at(order, slot, place):
    picked = jnp.int32(order[0][slot])
    for z in range(1, len(order)):
        picked = jnp.where(place == z, order[z][slot], picked)
    return picked


def spans(requests_ref, count):
    requests = requests_ref[...]
    return [jnp.int32(0)] + [jnp.sum((requests <= r).astype(jnp.int32)) for r in range(count)]


class Meta:
    def __init__(self, ref, requests):
        self.ref, self.requests = ref, requests
        self.adapters = (ref.shape[0] - 2 - requests) // 2
        self.place, self.shard = ref[0], ref[1]

    def adapter(self, r):
        return self.ref[2 + r]

    def rank(self, r):
        return self.ref[2 + self.requests + self.adapter(r)]

    def local_slot(self, r, held):
        return self.ref[2 + self.requests + self.adapters + self.adapter(r)] - self.shard * held


def base_kernel(order, groups, inputs_for, half, held, request_count, handed_on, *refs):
    slots = [slot for group in groups for slot in group]
    count = len(slots)
    meta, refs = Meta(refs[0], request_count), refs[1:]
    if held:
        requests_ref, factor, refs = refs[0], refs[1], refs[2:]
    hidden, matrix, refs = refs[0], refs[1], refs[2:]
    under, refs = (refs[0], refs[1:]) if handed_on else (None, refs)
    outs, refs = refs[: len(groups)], refs[len(groups) :]
    (rows, right, sums, sems), refs = refs[:4], refs[4:]
    steps, _, tile = rows.shape
    columns = outs[0].shape[1]
    block = rows.shape[1] // count
    first_rows = [pl.multiple_of(block_at(order, slot, meta.place) * block, block) for slot in slots]

    def depth_of(k):
        return pl.ds(pl.multiple_of(k * tile, tile), tile)

    def copies(k):
        moves = [
            (hidden.at[pl.ds(first_rows[i], block), depth_of(k)], rows.at[k, pl.ds(i * block, block), :])
            for i in range(count)
        ]
        moves.append((matrix.at[depth_of(k), pl.ds(half * columns, columns)], right.at[k]))
        return [pltpu.make_async_copy(a, b, sems.at[k, i]) for i, (a, b) in enumerate(moves)]

    if held:
        factors, inputs, flags, factor_sems = refs
        width = factor.shape[2]

        def factor_copies(k, pair):
            return [
                pltpu.make_async_copy(
                    factor.at[2 * pair + i, depth_of(k), :],
                    factors.at[pair, k, :, pl.ds(i * width, width)],
                    factor_sems.at[k, 2 * pair + i],
                )
                for i in range(2)
            ]

    def start(k):
        for copy in copies(k):
            copy.start()

    def start_factors(k, pairs):
        for pair, used in enumerate(pairs):

            @pl.when(used)
            def _(pair=pair):
                for copy in factor_copies(k, pair):
                    copy.start()

    for k in range(min(AHEAD, steps)):
        start(k)
    used = []
    if held:
        bounds = spans(requests_ref, request_count)
        local = [meta.local_slot(r, held) for r in range(request_count)]
        top = slots.index(inputs_for[0])
        wide = len(inputs_for)
        for pair in range(held // 2):
            used_by = []
            for first in first_rows[top : top + wide]:
                wanted = jnp.bool_(False)
                for r, slot in enumerate(local):
                    here = jnp.maximum(bounds[r], first) < jnp.minimum(bounds[r + 1], first + block)
                    wanted = wanted | (here & (slot // 2 == pair) & (slot >= 0))
                flags[pair * wide + len(used_by)] = wanted.astype(jnp.int32)
                used_by.append(wanted)
            used.append(functools.reduce(jnp.logical_or, used_by))
        for k in range(min(AHEAD, steps)):
            start_factors(k, used)
    sums[...] = jnp.zeros_like(sums)

    def step(k, _):
        @pl.when(k + AHEAD < steps)
        def _():
            start(k + AHEAD)
            start_factors(k + AHEAD, used)

        for copy in copies(k):
            copy.wait()
        sums[...] += jnp.dot(rows[k], right[k], preferred_element_type=jnp.float32)
        return 0

    lax.fori_loop(0, steps, step, 0)

    if held:
        for pair, wanted in enumerate(used):

            @pl.when(wanted)
            def _(pair=pair):
                for k in range(steps):
                    for copy in factor_copies(k, pair):
                        copy.wait()

        def pair_block(j, _):
            pair, i = j // wide, j % wide

            @pl.when(flags[j] == 1)
            def _():
                own = pl.ds(pl.multiple_of((top + i) * block, block), block)
                total = jnp.dot(rows[0, own, :], factors[pair, 0], preferred_element_type=jnp.float32)
                for k in range(1, steps):
                    total += jnp.dot(rows[k, own, :], factors[pair, k], preferred_element_type=jnp.float32)
                inputs[pair, pl.ds(pl.multiple_of(i * block, block), block), :] = total

            return 0

        lax.fori_loop(0, held // 2 * wide, pair_block, 0)

    i = 0
    for out, group in zip(outs, groups):
        here = 0
        for slot in group:
            out[here : here + block, :] = sums[i * block : (i + 1) * block, :].astype(jnp.bfloat16)
            here += block
            if held and slot in inputs_for:
                own = pl.ds((i - top) * block, block)
                row = lax.broadcasted_iota(jnp.int32, (block, width), 0) + first_rows[i]
                column = lax.broadcasted_iota(jnp.int32, (block, width), 1)
                total = jnp.zeros((block, width), jnp.float32)
                for r, local_slot in enumerate(local):
                    last = jnp.where((local_slot >= 0) & (local_slot < held), bounds[r + 1], 0)
                    keep = (row >= bounds[r]) & (row < last) & (column < meta.rank(r))
                    local_slot = jnp.clip(local_slot, 0, held - 1)
                    lanes = pl.ds(pl.multiple_of(local_slot % 2 * width, width), width)
                    total = jnp.where(keep, inputs[local_slot // 2, own, lanes], total)
                total = total.astype(jnp.bfloat16)
                size = block * width // columns
                for j in range(columns // width):
                    lanes = slice(j * width, (j + 1) * width)
                    out[here : here + size, lanes] = total[j * size : (j + 1) * size, :]
                here += size
            i += 1
    if handed_on:
        outs[0][outs[0].shape[0] - under.shape[0] :, :] = under[...]


def base_terms(meta, requests, request_count, hidden, matrix, factor, groups, inputs_for, half, n, under=None):
    tokens, depth = hidden.shape
    block, columns = tokens // n, matrix.shape[1] // 2
    tile = first_divisor(depth, (1024, 512, 256, 128))
    steps = depth // tile
    count = sum(len(group) for group in groups)
    smem = pl.BlockSpec(memory_space=pltpu.SMEM)
    vmem = pl.BlockSpec(memory_space=pltpu.VMEM)
    hbm = pl.BlockSpec(memory_space=pltpu.HBM)
    held, extra = 0, 0
    operands, in_specs = [meta], [smem]
    scratch = [
        pltpu.VMEM((steps, count * block, tile), jnp.bfloat16),
        pltpu.VMEM((steps, tile, columns), jnp.bfloat16),
        pltpu.VMEM((count * block, columns), jnp.float32),
        pltpu.SemaphoreType.DMA((steps, count + 1)),
    ]
    if inputs_for:
        held, _, width = factor.shape
        extra = block * width // columns
        operands, in_specs = [meta, requests, factor], [smem, vmem, hbm]
        scratch += [
            pltpu.VMEM((held // 2, steps, tile, 2 * width), jnp.bfloat16),
            pltpu.VMEM((held // 2, len(inputs_for) * block, 2 * width), jnp.float32),
            pltpu.SMEM((held // 2 * len(inputs_for),), jnp.int32),
            pltpu.SemaphoreType.DMA((steps, held)),
        ]
    heights = [sum(block + (extra if slot in inputs_for else 0) for slot in group) for group in groups]
    operands, in_specs = operands + [hidden, matrix], in_specs + [hbm, hbm]
    if under is not None:
        heights[0] += under.shape[0]
        operands, in_specs = operands + [under], in_specs + [vmem]
    handed_on = under is not None
    return pl.pallas_call(
        lambda *refs: base_kernel(line_order(n), groups, inputs_for, half, held, request_count, handed_on, *refs),
        out_shape=[jax.ShapeDtypeStruct((height, columns), jnp.bfloat16) for height in heights],
        in_specs=in_specs,
        out_specs=[vmem] * len(groups),
        scratch_shapes=scratch,
        compiler_params=params(50 if half or count > 1 else 58),
        cost_estimate=small_cost(),
        name="base_terms",
    )(*operands)


def select_rows_kernel(request_count, meta_ref, factor, kept, sent):
    meta = Meta(meta_ref, request_count)
    held, rank_rows, _ = factor.shape
    width = factor.shape[2] // (2 * PAIRS)
    side = meta.shard % 2
    for r in range(request_count):
        slot = meta.local_slot(r, held)
        owned = (slot >= 0) & (slot < held)
        slot = jnp.clip(slot, 0, held - 1)
        for out, core in ((kept, side), (sent, 1 - side)):
            for i in range(PAIRS):
                for c in range(2):
                    first = (2 * i + core) * width + c * (width // 2)
                    rows = factor[slot, :, pl.ds(pl.multiple_of(first, LANES), width // 2)]
                    top = (c * request_count + r) * rank_rows
                    out[i, top : top + rank_rows, :] = jnp.where(owned, rows, jnp.zeros_like(rows))


def select_rows(meta, request_count, factor):
    _, rank_rows, model_width = factor.shape
    smem = pl.BlockSpec(memory_space=pltpu.SMEM)
    vmem = pl.BlockSpec(memory_space=pltpu.VMEM)
    shape = (PAIRS, 2 * request_count * rank_rows, model_width // (4 * PAIRS))
    out = jax.ShapeDtypeStruct(shape, factor.dtype)
    return pl.pallas_call(
        lambda *refs: select_rows_kernel(request_count, *refs),
        out_shape=[out, out],
        in_specs=[smem, vmem],
        out_specs=[vmem, vmem],
        compiler_params=params(16),
        cost_estimate=small_cost(),
        name="select_rows",
    )(meta, factor)


def expanded_inputs(meta, requests_ref, lora_ref):
    block, width = lora_ref.shape
    row = lax.broadcasted_iota(jnp.int32, (block, width), 0) + meta.place * block
    lora = lora_ref[...].astype(jnp.float32)
    bounds = spans(requests_ref, meta.requests)
    parts = []
    for r in range(meta.requests):
        scale = 0.25 * width / meta.rank(r).astype(jnp.float32)
        keep = (row >= bounds[r]) & (row < bounds[r + 1])
        parts.append(jnp.where(keep, lora * scale, 0.0).astype(jnp.bfloat16))
    return jnp.concatenate(parts, axis=1)


def finish_kernel(items, added, requests, rank_rows, n, *refs):
    meta_ref, requests_ref, lora_ref, refs = refs[0], refs[1], refs[2], refs[3:]
    arrays, out, rows = refs[:-2], refs[-2], refs[-1]
    meta = Meta(meta_ref, requests)
    rank = n * rank_rows
    half = out.shape[1] // 2
    for index, top, targets in items:
        for place, k in targets:

            @pl.when(meta.place == place)
            def _(piece=arrays[index], top=top, k=k):
                for r in range(requests):
                    first = r * rank + k * rank_rows
                    for c in range(2):
                        start = top + (c * requests + r) * rank_rows
                        rows[first : first + rank_rows, c * half : (c + 1) * half] = piece[start : start + rank_rows, :]

    expanded = expanded_inputs(meta, requests_ref, lora_ref)
    block = lora_ref.shape[0]
    for c in range(2):
        columns = slice(c * half, (c + 1) * half)
        total = jnp.dot(expanded, rows[:, columns], preferred_element_type=jnp.float32)
        for index, top, which in added:
            if which == c:
                total += arrays[index][top : top + block, :].astype(jnp.float32)
        out[:, columns] = total.astype(out.dtype)


def finish(meta, requests, lora, arrays, items, added, request_count, rank_rows, n):
    smem = pl.BlockSpec(memory_space=pltpu.SMEM)
    vmem = pl.BlockSpec(memory_space=pltpu.VMEM)
    width = 2 * arrays[0].shape[1]
    return pl.pallas_call(
        lambda *refs: finish_kernel(items, added, request_count, rank_rows, n, *refs),
        out_shape=jax.ShapeDtypeStruct((lora.shape[0], width), jnp.bfloat16),
        in_specs=[smem] + [vmem] * (2 + len(arrays)),
        out_specs=vmem,
        scratch_shapes=[pltpu.VMEM((request_count * n * rank_rows, width), jnp.bfloat16)],
        compiler_params=params(20),
        cost_estimate=small_cost(),
        name="finish",
    )(meta, requests, lora, *arrays)


def join_kernel(count, term_top, came_top, under_top, term, came, *refs):
    out = refs[-1]
    total = term[term_top : term_top + count, :].astype(jnp.float32)
    total += came[came_top : came_top + count, :].astype(jnp.float32)
    out[:count, :] = total.astype(out.dtype)
    if len(refs) > 1:
        under = refs[0]
        out[count:, :] = under[under_top : under_top + out.shape[0] - count, :]


def join(token, count, term, term_top, came, came_top, under=None, under_top=0, under_count=0, weight=10**6):
    arrays = [term, came] + ([] if under is None else [under])
    arrays = lax.optimization_barrier((arrays, token))[0]
    vmem = pl.BlockSpec(memory_space=pltpu.VMEM)
    return pl.pallas_call(
        lambda *refs: join_kernel(count, term_top, came_top, under_top, *refs),
        out_shape=jax.ShapeDtypeStruct((count + under_count, term.shape[1]), term.dtype),
        in_specs=[vmem] * len(arrays),
        out_specs=vmem,
        compiler_params=params(12),
        cost_estimate=pl.CostEstimate(flops=weight, bytes_accessed=10**5, transcendentals=0),
        name="join",
    )(*arrays)


def add_last_kernel(total, *refs):
    arrivals, out = refs[:-1], refs[-1]
    half = arrivals[0].shape[1]
    out[:, :half] = total[:, :half]
    last = total[:, half:].astype(jnp.float32)
    for arrival in arrivals:
        last += arrival[...].astype(jnp.float32)
    out[:, half:] = last.astype(out.dtype)


def add_last(total, *arrivals):
    vmem = pl.BlockSpec(memory_space=pltpu.VMEM)
    return pl.pallas_call(
        add_last_kernel,
        out_shape=jax.ShapeDtypeStruct(total.shape, total.dtype),
        in_specs=[vmem] * (1 + len(arrivals)),
        out_specs=vmem,
        compiler_params=params(12),
        cost_estimate=small_cost(),
        name="add_last",
    )(total, *arrivals)


def swap(x, axis, bit):
    return lax.ppermute(x, axis, [(i, i ^ bit) for i in range(lax.axis_size(axis))])


def bits_of(size):
    return [1 << i for i in range(size.bit_length() - 1)]


def along_edge(x, edge):
    n = lax.axis_size("tensor")
    return lax.ppermute(x, "tensor", [(edge, edge + 1), (n - 1 - edge, n - 2 - edge)])


def on_line(hidden, matrix, input_factor, output_factor, requests, token, request_count, n):
    shard = lax.axis_index("store")
    block = hidden.shape[0] // n
    width = input_factor.shape[2]
    rank_rows = output_factor.shape[1]
    piece = block + block * width // (matrix.shape[1] // 2)
    bundle = 2 * request_count * rank_rows

    def base(token, groups, inputs_for, half, under=None):
        return base_terms(
            token, requests, request_count, hidden, matrix, input_factor, groups, inputs_for, half, n, under
        )

    def send(x, edge, token):
        return along_edge(after(x, token), edge)

    (s00,) = base(token, [[0]], [0], 0)
    token = after(token, s00)
    e0_1 = along_edge(s00, 0)
    kept, sent = select_rows(token, request_count, output_factor)
    token = after(token, kept, sent)
    swapped = swap(sent, "store", 1)
    token = after(token, swapped)
    side = shard // 2 % 2
    kept, swapped, _ = lax.optimization_barrier((kept, swapped, token))
    outgoing = kept[1 - side] + swapped[1 - side]
    rows = kept[side] + swapped[side]
    token = after(token, outgoing, rows)
    swapped = swap(outgoing, "store", 2)
    s01, s11 = base(token, [[0], [1]], [], 1)

    token = after(token, s01)
    e0_2 = send(s01, 0, token)
    token, e0_1 = lax.optimization_barrier((token, e0_1))
    b10 = join(token, piece, s00, 0, e0_1, 0)
    token = after(token, b10)
    e1_2 = along_edge(b10, 1)
    token, swapped = lax.optimization_barrier((token, swapped))
    rows = rows + swapped
    token = after(token, rows)
    near = lax.ppermute(rows, "tensor", [(0, 1), (n - 1, n - 2), (1, 0), (n - 2, n - 1)])
    far = along_edge(rows, 1)
    s10_s11, s20, s30 = base(token, [[1], [2], [3]], [1, 2], 0, s11)

    token = after(token, s10_s11)
    e0_3 = send(s10_s11, 0, token)
    token, e0_2 = lax.optimization_barrier((token, e0_2))
    b11 = join(token, block, s01, 0, e0_2, 0, weight=HEAVY)
    token, near = lax.optimization_barrier((after(token, b11), near))
    e1_3 = along_edge(b11, 1)
    far_2 = send(near, 1, token)
    token, e1_2, far = lax.optimization_barrier((token, e1_2, far))
    c20 = join(token, piece, s20, 0, e1_2, 0, far, 0, bundle)
    token = after(token, c20)
    e2_3 = along_edge(c20, 2)
    s21, s31 = base(token, [[2], [3]], [3], 1)

    token = after(token, s21)
    e0_4 = send(s20, 0, token)
    token, e0_3 = lax.optimization_barrier((token, e0_3))
    b20 = join(token, piece, s10_s11, 0, e0_3, 0)
    token = after(token, b20)
    e1_4 = along_edge(b20, 1)
    token, far_2 = lax.optimization_barrier((token, far_2))
    last_rows = send(far_2, 2, token)
    token, e1_3 = lax.optimization_barrier((token, e1_3))
    c21 = join(token, block, s21, 0, e1_3, 0, weight=HEAVY)
    token = after(token, c21)
    e2_4 = along_edge(c21, 2)
    token, e2_3 = lax.optimization_barrier((token, e2_3))
    e0_5 = send(s21, 0, token)
    b21 = join(token, block, s10_s11, piece, e0_3, piece)
    token = after(token, b21)
    e1_5 = along_edge(b21, 1)

    token, e0_4 = lax.optimization_barrier((token, e0_4))
    token, e1_4 = lax.optimization_barrier((token, e1_4))
    token, last_rows = lax.optimization_barrier((token, last_rows))
    e1_4 = after(e1_4, token)
    lora = s31[block:].astype(jnp.float32) + e0_4[block:].astype(jnp.float32)
    lora += e1_4[block:].astype(jnp.float32) + e2_3[block:piece].astype(jnp.float32)
    lora = lora.astype(jnp.bfloat16).reshape(piece - block, -1, width).swapaxes(0, 1).reshape(block, width)
    lora = lora + swap(lora, "store", 1)
    lora = lora + swap(lora, "store", 2)
    arrays = [s30, s31, rows, near, far, far_2, e2_3, last_rows, e0_4, e1_4]
    items = [
        (2, 0, [(z, z) for z in range(n)]),
        (3, 0, [(0, 1), (1, 0), (2, 3), (3, 2)]),
        (4, 0, [(1, 2), (2, 1)]),
        (5, 0, [(1, 3), (2, 0)]),
        (6, piece, [(0, 2), (3, 1)]),
        (7, 0, [(0, 3), (3, 0)]),
    ]
    added = [(0, 0, 0), (8, 0, 0), (9, 0, 0), (6, 0, 0), (1, 0, 1)]
    out = finish(token, requests, lora, arrays, items, added, request_count, rank_rows, n)
    return add_last(out, e0_5, e1_5, e2_4)


def anywhere(hidden, matrix, input_factor, output_factor, token_requests, meta):
    request_adapters, ranks, slots = meta
    held = input_factor.shape[0]
    width = input_factor.shape[2]
    rank, slot = ranks[request_adapters], slots[request_adapters]
    owned = slot // held == lax.axis_index("store")
    chosen = token_requests[:, None] == jnp.arange(request_adapters.shape[0])[None, :]
    lora = jnp.zeros((hidden.shape[0], width), jnp.float32)
    for r in range(request_adapters.shape[0]):
        product = jnp.dot(hidden, input_factor[slot[r] % held], preferred_element_type=jnp.float32)
        keep = (chosen[:, r] & owned[r])[:, None] & (jnp.arange(width) < rank[r])[None, :]
        lora = jnp.where(keep, product, lora)
    lora = lax.psum_scatter(lora.astype(jnp.bfloat16), "tensor", scatter_dimension=1, tiled=True)
    lora = lax.psum(lora, "store").astype(jnp.float32)
    rows = jnp.where(owned[:, None, None], output_factor[slot % held], jnp.zeros((), output_factor.dtype))
    rows = lax.psum_scatter(rows, "store", scatter_dimension=2, tiled=True)
    weights = jnp.where(chosen, 0.25 * width / rank.astype(jnp.float32)[None, :], 0.0)
    expanded = (weights[:, :, None] * lora[:, None, :]).reshape(hidden.shape[0], -1).astype(jnp.bfloat16)
    term = jnp.dot(hidden, matrix, preferred_element_type=jnp.float32)
    term += jnp.dot(expanded, rows.reshape(-1, rows.shape[2]), preferred_element_type=jnp.float32)
    return lax.psum_scatter(term.astype(jnp.bfloat16), "tensor", scatter_dimension=0, tiled=True)


def per_device(
    hidden_activations,
    down_matrix,
    adapter_input_factor,
    adapter_output_factor,
    token_requests,
    request_adapters,
    adapter_ranks,
    adapter_store_slot,
):
    n = lax.axis_size("tensor")
    meta = (request_adapters, adapter_ranks, adapter_store_slot)
    arrays = (hidden_activations, down_matrix, adapter_input_factor, adapter_output_factor)
    if n == LINE and lax.axis_size("store") == 2 * PAIRS and adapter_input_factor.shape[0] % 2 == 0:
        place = jnp.stack([lax.axis_index("tensor"), lax.axis_index("store")]).astype(jnp.int32)
        token = jnp.concatenate([place, *meta])
        return on_line(*arrays, token_requests.reshape(-1, LANES), token, request_adapters.shape[0], n)
    return anywhere(*arrays, token_requests, meta)


def solution(mesh):
    in_specs = (
        P("groups", "tensor"),
        P("tensor", "store"),
        P(("groups", "store"), "tensor", None),
        P(("groups", "store"), "tensor", None),
        P("groups"),
        P("groups"),
        P("groups"),
        P("groups"),
    )
    out_specs = P(("groups", "tensor"), "store")
    return jax.shard_map(
        per_device, mesh=mesh, in_specs=in_specs, out_specs=out_specs, check_vma=False
    )
```

```python
import functools

import jax
import jax.numpy as jnp
from jax import lax
from jax.experimental import pallas as pl
from jax.experimental.pallas import tpu as pltpu
from jax.sharding import PartitionSpec as P

LINE = 4
LANES = 128
AHEAD = 3
PAIRS = 2
HEAVY = 10**10
MIB = 1024 * 1024


def line_order(n):
    order = []
    for z in range(n):
        sends = [(t, z >= n // 2, n - 1 - t + z) for t in range(z, n - 1)]
        sends += [(t, z < n // 2, t - (n - 1 - z)) for t in range(n - 1 - z, n - 1)]
        order.append([block for _, _, block in sorted(sends)] + [z])
    return order


def first_divisor(size, choices):
    for choice in choices:
        if size % choice == 0:
            return choice
    return size


def after(token, *done):
    return lax.optimization_barrier((token, done))[0]


def params(mebibytes):
    return pltpu.CompilerParams(vmem_limit_bytes=mebibytes * MIB)


def small_cost():
    return pl.CostEstimate(flops=10**6, bytes_accessed=10**5, transcendentals=0)


def block_at(order, slot, place):
    picked = jnp.int32(order[0][slot])
    for z in range(1, len(order)):
        picked = jnp.where(place == z, order[z][slot], picked)
    return picked


def spans(requests_ref, count):
    requests = requests_ref[...]
    return [jnp.int32(0)] + [jnp.sum((requests <= r).astype(jnp.int32)) for r in range(count)]


class Meta:
    def __init__(self, ref, requests):
        self.ref, self.requests = ref, requests
        self.adapters = (ref.shape[0] - 2 - requests) // 2
        self.place, self.shard = ref[0], ref[1]

    def adapter(self, r):
        return self.ref[2 + r]

    def rank(self, r):
        return self.ref[2 + self.requests + self.adapter(r)]

    def local_slot(self, r, held):
        return self.ref[2 + self.requests + self.adapters + self.adapter(r)] - self.shard * held


def base_kernel(order, groups, inputs_for, half, held, request_count, handed_on, *refs):
    slots = [slot for group in groups for slot in group]
    count = len(slots)
    meta, refs = Meta(refs[0], request_count), refs[1:]
    if held:
        requests_ref, factor, refs = refs[0], refs[1], refs[2:]
    hidden, matrix, refs = refs[0], refs[1], refs[2:]
    under, refs = (refs[0], refs[1:]) if handed_on else (None, refs)
    outs, refs = refs[: len(groups)], refs[len(groups) :]
    (rows, right, sums, sems), refs = refs[:4], refs[4:]
    steps, _, tile = rows.shape
    columns = outs[0].shape[1]
    block = rows.shape[1] // count
    first_rows = [pl.multiple_of(block_at(order, slot, meta.place) * block, block) for slot in slots]

    def depth_of(k):
        return pl.ds(pl.multiple_of(k * tile, tile), tile)

    def copies(k):
        moves = [
            (hidden.at[pl.ds(first_rows[i], block), depth_of(k)], rows.at[k, pl.ds(i * block, block), :])
            for i in range(count)
        ]
        moves.append((matrix.at[depth_of(k), pl.ds(half * columns, columns)], right.at[k]))
        return [pltpu.make_async_copy(a, b, sems.at[k, i]) for i, (a, b) in enumerate(moves)]

    if held:
        factors, inputs, flags, factor_sems = refs
        width = factor.shape[2]

        def factor_copies(k, pair):
            return [
                pltpu.make_async_copy(
                    factor.at[2 * pair + i, depth_of(k), :],
                    factors.at[pair, k, :, pl.ds(i * width, width)],
                    factor_sems.at[k, 2 * pair + i],
                )
                for i in range(2)
            ]

    def start(k):
        for copy in copies(k):
            copy.start()

    def start_factors(k, pairs):
        for pair, used in enumerate(pairs):

            @pl.when(used)
            def _(pair=pair):
                for copy in factor_copies(k, pair):
                    copy.start()

    for k in range(min(AHEAD, steps)):
        start(k)
    used = []
    if held:
        bounds = spans(requests_ref, request_count)
        local = [meta.local_slot(r, held) for r in range(request_count)]
        top = slots.index(inputs_for[0])
        wide = len(inputs_for)
        for pair in range(held // 2):
            used_by = []
            for first in first_rows[top : top + wide]:
                wanted = jnp.bool_(False)
                for r, slot in enumerate(local):
                    here = jnp.maximum(bounds[r], first) < jnp.minimum(bounds[r + 1], first + block)
                    wanted = wanted | (here & (slot // 2 == pair) & (slot >= 0))
                flags[pair * wide + len(used_by)] = wanted.astype(jnp.int32)
                used_by.append(wanted)
            used.append(functools.reduce(jnp.logical_or, used_by))
        for k in range(min(AHEAD, steps)):
            start_factors(k, used)
    sums[...] = jnp.zeros_like(sums)

    def step(k, _):
        @pl.when(k + AHEAD < steps)
        def _():
            start(k + AHEAD)
            start_factors(k + AHEAD, used)

        for copy in copies(k):
            copy.wait()
        sums[...] += jnp.dot(rows[k], right[k], preferred_element_type=jnp.float32)
        return 0

    lax.fori_loop(0, steps, step, 0)

    if held:
        for pair, wanted in enumerate(used):

            @pl.when(wanted)
            def _(pair=pair):
                for k in range(steps):
                    for copy in factor_copies(k, pair):
                        copy.wait()

        def pair_block(j, _):
            pair, i = j // wide, j % wide

            @pl.when(flags[j] == 1)
            def _():
                own = pl.ds(pl.multiple_of((top + i) * block, block), block)
                total = jnp.dot(rows[0, own, :], factors[pair, 0], preferred_element_type=jnp.float32)
                for k in range(1, steps):
                    total += jnp.dot(rows[k, own, :], factors[pair, k], preferred_element_type=jnp.float32)
                inputs[pair, pl.ds(pl.multiple_of(i * block, block), block), :] = total

            return 0

        lax.fori_loop(0, held // 2 * wide, pair_block, 0)

    i = 0
    for out, group in zip(outs, groups):
        here = 0
        for slot in group:
            out[here : here + block, :] = sums[i * block : (i + 1) * block, :].astype(jnp.bfloat16)
            here += block
            if held and slot in inputs_for:
                own = pl.ds((i - top) * block, block)
                row = lax.broadcasted_iota(jnp.int32, (block, width), 0) + first_rows[i]
                column = lax.broadcasted_iota(jnp.int32, (block, width), 1)
                total = jnp.zeros((block, width), jnp.float32)
                for r, local_slot in enumerate(local):
                    last = jnp.where((local_slot >= 0) & (local_slot < held), bounds[r + 1], 0)
                    keep = (row >= bounds[r]) & (row < last) & (column < meta.rank(r))
                    local_slot = jnp.clip(local_slot, 0, held - 1)
                    lanes = pl.ds(pl.multiple_of(local_slot % 2 * width, width), width)
                    total = jnp.where(keep, inputs[local_slot // 2, own, lanes], total)
                total = total.astype(jnp.bfloat16)
                size = block * width // columns
                for j in range(columns // width):
                    lanes = slice(j * width, (j + 1) * width)
                    out[here : here + size, lanes] = total[j * size : (j + 1) * size, :]
                here += size
            i += 1
    if handed_on:
        outs[0][outs[0].shape[0] - under.shape[0] :, :] = under[...]


def base_terms(meta, requests, request_count, hidden, matrix, factor, groups, inputs_for, half, n, under=None):
    tokens, depth = hidden.shape
    block, columns = tokens // n, matrix.shape[1] // 2
    tile = first_divisor(depth, (1024, 512, 256, 128))
    steps = depth // tile
    count = sum(len(group) for group in groups)
    smem = pl.BlockSpec(memory_space=pltpu.SMEM)
    vmem = pl.BlockSpec(memory_space=pltpu.VMEM)
    hbm = pl.BlockSpec(memory_space=pltpu.HBM)
    held, extra = 0, 0
    operands, in_specs = [meta], [smem]
    scratch = [
        pltpu.VMEM((steps, count * block, tile), jnp.bfloat16),
        pltpu.VMEM((steps, tile, columns), jnp.bfloat16),
        pltpu.VMEM((count * block, columns), jnp.float32),
        pltpu.SemaphoreType.DMA((steps, count + 1)),
    ]
    if inputs_for:
        held, _, width = factor.shape
        extra = block * width // columns
        operands, in_specs = [meta, requests, factor], [smem, vmem, hbm]
        scratch += [
            pltpu.VMEM((held // 2, steps, tile, 2 * width), jnp.bfloat16),
            pltpu.VMEM((held // 2, len(inputs_for) * block, 2 * width), jnp.float32),
            pltpu.SMEM((held // 2 * len(inputs_for),), jnp.int32),
            pltpu.SemaphoreType.DMA((steps, held)),
        ]
    heights = [sum(block + (extra if slot in inputs_for else 0) for slot in group) for group in groups]
    operands, in_specs = operands + [hidden, matrix], in_specs + [hbm, hbm]
    if under is not None:
        heights[0] += under.shape[0]
        operands, in_specs = operands + [under], in_specs + [vmem]
    handed_on = under is not None
    return pl.pallas_call(
        lambda *refs: base_kernel(line_order(n), groups, inputs_for, half, held, request_count, handed_on, *refs),
        out_shape=[jax.ShapeDtypeStruct((height, columns), jnp.bfloat16) for height in heights],
        in_specs=in_specs,
        out_specs=[vmem] * len(groups),
        scratch_shapes=scratch,
        compiler_params=params(50 if half or count > 1 else 58),
        cost_estimate=small_cost(),
        name="base_terms",
    )(*operands)


def select_rows_kernel(request_count, meta_ref, factor, kept, sent):
    meta = Meta(meta_ref, request_count)
    held, rank_rows, _ = factor.shape
    width = factor.shape[2] // (2 * PAIRS)
    side = meta.shard % 2
    for r in range(request_count):
        slot = meta.local_slot(r, held)
        owned = (slot >= 0) & (slot < held)
        slot = jnp.clip(slot, 0, held - 1)
        for out, core in ((kept, side), (sent, 1 - side)):
            for i in range(PAIRS):
                for c in range(2):
                    first = (2 * i + core) * width + c * (width // 2)
                    rows = factor[slot, :, pl.ds(pl.multiple_of(first, LANES), width // 2)]
                    top = (c * request_count + r) * rank_rows
                    out[i, top : top + rank_rows, :] = jnp.where(owned, rows, jnp.zeros_like(rows))


def select_rows(meta, request_count, factor):
    _, rank_rows, model_width = factor.shape
    smem = pl.BlockSpec(memory_space=pltpu.SMEM)
    vmem = pl.BlockSpec(memory_space=pltpu.VMEM)
    shape = (PAIRS, 2 * request_count * rank_rows, model_width // (4 * PAIRS))
    out = jax.ShapeDtypeStruct(shape, factor.dtype)
    return pl.pallas_call(
        lambda *refs: select_rows_kernel(request_count, *refs),
        out_shape=[out, out],
        in_specs=[smem, vmem],
        out_specs=[vmem, vmem],
        compiler_params=params(16),
        cost_estimate=small_cost(),
        name="select_rows",
    )(meta, factor)


def expanded_inputs(meta, requests_ref, lora_ref):
    block, width = lora_ref.shape
    row = lax.broadcasted_iota(jnp.int32, (block, width), 0) + meta.place * block
    lora = lora_ref[...].astype(jnp.float32)
    bounds = spans(requests_ref, meta.requests)
    parts = []
    for r in range(meta.requests):
        scale = 0.25 * width / meta.rank(r).astype(jnp.float32)
        keep = (row >= bounds[r]) & (row < bounds[r + 1])
        parts.append(jnp.where(keep, lora * scale, 0.0).astype(jnp.bfloat16))
    return jnp.concatenate(parts, axis=1)


def finish_kernel(items, added, requests, rank_rows, n, *refs):
    meta_ref, requests_ref, lora_ref, refs = refs[0], refs[1], refs[2], refs[3:]
    arrays, out, rows = refs[:-2], refs[-2], refs[-1]
    meta = Meta(meta_ref, requests)
    rank = n * rank_rows
    half = out.shape[1] // 2
    for index, targets in items:
        for place, k in targets:

            @pl.when(meta.place == place)
            def _(piece=arrays[index], k=k):
                for r in range(requests):
                    first = r * rank + k * rank_rows
                    for c in range(2):
                        start = (c * requests + r) * rank_rows
                        rows[first : first + rank_rows, c * half : (c + 1) * half] = piece[start : start + rank_rows, :]

    expanded = expanded_inputs(meta, requests_ref, lora_ref)
    block = lora_ref.shape[0]
    for c in range(2):
        columns = slice(c * half, (c + 1) * half)
        total = jnp.dot(expanded, rows[:, columns], preferred_element_type=jnp.float32)
        for index, which in added:
            if which == c:
                total += arrays[index][:block, :].astype(jnp.float32)
        out[:, columns] = total.astype(out.dtype)


def finish(meta, requests, lora, arrays, items, added, request_count, rank_rows, n):
    smem = pl.BlockSpec(memory_space=pltpu.SMEM)
    vmem = pl.BlockSpec(memory_space=pltpu.VMEM)
    width = 2 * arrays[0].shape[1]
    return pl.pallas_call(
        lambda *refs: finish_kernel(items, added, request_count, rank_rows, n, *refs),
        out_shape=jax.ShapeDtypeStruct((lora.shape[0], width), jnp.bfloat16),
        in_specs=[smem] + [vmem] * (2 + len(arrays)),
        out_specs=vmem,
        scratch_shapes=[pltpu.VMEM((request_count * n * rank_rows, width), jnp.bfloat16)],
        compiler_params=params(20),
        cost_estimate=pl.CostEstimate(flops=10**6, bytes_accessed=10**5, transcendentals=0),
        name="finish",
    )(meta, requests, lora, *arrays)


def join_kernel(count, term_top, came_top, term, came, out):
    total = term[term_top : term_top + count, :].astype(jnp.float32)
    total += came[came_top : came_top + count, :].astype(jnp.float32)
    out[...] = total.astype(out.dtype)


def join(token, count, term, term_top, came, came_top, weight=10**6):
    arrays = lax.optimization_barrier(((term, came), token))[0]
    vmem = pl.BlockSpec(memory_space=pltpu.VMEM)
    return pl.pallas_call(
        lambda *refs: join_kernel(count, term_top, came_top, *refs),
        out_shape=jax.ShapeDtypeStruct((count, term.shape[1]), term.dtype),
        in_specs=[vmem] * 2,
        out_specs=vmem,
        compiler_params=params(12),
        cost_estimate=pl.CostEstimate(flops=weight, bytes_accessed=10**5, transcendentals=0),
        name="join",
    )(*arrays)


def add_last_kernel(total, *refs):
    arrivals, out = refs[:-1], refs[-1]
    half = arrivals[0].shape[1]
    out[:, :half] = total[:, :half]
    last = total[:, half:].astype(jnp.float32)
    for arrival in arrivals:
        last += arrival[...].astype(jnp.float32)
    out[:, half:] = last.astype(out.dtype)


def add_last(total, *arrivals):
    vmem = pl.BlockSpec(memory_space=pltpu.VMEM)
    return pl.pallas_call(
        add_last_kernel,
        out_shape=jax.ShapeDtypeStruct(total.shape, total.dtype),
        in_specs=[vmem] * (1 + len(arrivals)),
        out_specs=vmem,
        compiler_params=params(12),
        cost_estimate=small_cost(),
        name="add_last",
    )(total, *arrivals)


def swap(x, axis, bit):
    return lax.ppermute(x, axis, [(i, i ^ bit) for i in range(lax.axis_size(axis))])


def bits_of(size):
    return [1 << i for i in range(size.bit_length() - 1)]


def along_edge(x, edge):
    n = lax.axis_size("tensor")
    return lax.ppermute(x, "tensor", [(edge, edge + 1), (n - 1 - edge, n - 2 - edge)])


def on_line(hidden, matrix, input_factor, output_factor, requests, token, request_count, n):
    shard = lax.axis_index("store")
    block = hidden.shape[0] // n
    width = input_factor.shape[2]
    rank_rows = output_factor.shape[1]
    piece = block + block * width // (matrix.shape[1] // 2)

    def base(token, groups, inputs_for, half, under=None):
        return base_terms(
            token, requests, request_count, hidden, matrix, input_factor, groups, inputs_for, half, n, under
        )

    def send(x, edge, token):
        return along_edge(after(x, token), edge)

    (s00,) = base(token, [[0]], [0], 0)
    token = after(token, s00)
    e0_1 = along_edge(s00, 0)
    kept, sent = select_rows(token, request_count, output_factor)
    token = after(token, kept, sent)
    swapped = swap(sent, "store", 1)
    token = after(token, swapped)
    side = shard // 2 % 2
    kept, swapped, _ = lax.optimization_barrier((kept, swapped, token))
    outgoing = kept[1 - side] + swapped[1 - side]
    rows = kept[side] + swapped[side]
    token = after(token, outgoing, rows)
    swapped = swap(outgoing, "store", 2)
    s01, s11 = base(token, [[0], [1]], [], 1)

    token = after(token, s01)
    e0_2 = send(s01, 0, token)
    token, e0_1 = lax.optimization_barrier((token, e0_1))
    b10 = join(token, piece, s00, 0, e0_1, 0)
    token = after(token, b10)
    e1_2 = along_edge(b10, 1)
    token, swapped = lax.optimization_barrier((token, swapped))
    rows = rows + swapped
    token = after(token, rows)
    near = lax.ppermute(rows, "tensor", [(0, 1), (n - 1, n - 2), (1, 0), (n - 2, n - 1)])
    far = along_edge(rows, 1)
    s10_s11, s20, s30 = base(token, [[1], [2], [3]], [1, 2], 0, s11)

    token = after(token, s10_s11)
    e0_3 = send(s10_s11, 0, token)
    token, far = lax.optimization_barrier((token, far))
    far_1 = send(far, 2, token)
    token, e0_2 = lax.optimization_barrier((token, e0_2))
    b11 = join(token, block, s01, 0, e0_2, 0, HEAVY)
    token, near = lax.optimization_barrier((after(token, b11), near))
    e1_3 = along_edge(b11, 1)
    far_2 = send(near, 1, token)
    token, e1_2 = lax.optimization_barrier((token, e1_2))
    c20 = join(token, piece, s20, 0, e1_2, 0)
    token = after(token, c20)
    e2_3 = along_edge(c20, 2)
    s21, s31 = base(token, [[2], [3]], [3], 1)

    token = after(token, s21)
    e0_4 = send(s20, 0, token)
    token, e0_3 = lax.optimization_barrier((token, e0_3))
    b20 = join(token, piece, s10_s11, 0, e0_3, 0)
    token = after(token, b20)
    e1_4 = along_edge(b20, 1)
    token, far_1 = lax.optimization_barrier((token, far_1))
    token, far_2 = lax.optimization_barrier((token, far_2))
    far_3 = send(far_2, 2, token)
    token, e1_3 = lax.optimization_barrier((token, e1_3))
    c21 = join(token, block, s21, 0, e1_3, 0, HEAVY)
    token = after(token, c21)
    e2_4 = along_edge(c21, 2)
    token, e2_3 = lax.optimization_barrier((token, e2_3))
    e0_5 = send(s21, 0, token)
    b21 = join(token, block, s10_s11, piece, e0_3, piece)
    token = after(token, b21)
    e1_5 = along_edge(b21, 1)

    token, e0_4 = lax.optimization_barrier((token, e0_4))
    token, e1_4 = lax.optimization_barrier((token, e1_4))
    token, far_3 = lax.optimization_barrier((token, far_3))
    e1_4 = after(e1_4, token)
    lora = s31[block:].astype(jnp.float32) + e0_4[block:].astype(jnp.float32)
    lora += e1_4[block:].astype(jnp.float32) + e2_3[block:piece].astype(jnp.float32)
    lora = lora.astype(jnp.bfloat16).reshape(piece - block, -1, width).swapaxes(0, 1).reshape(block, width)
    lora = sum((swap(lora, "store", other) for other in range(1, 2 * PAIRS)), lora)
    arrays = [s30, s31, rows, near, far, far_1, far_2, far_3, e0_4, e1_4, e2_3, e0_5]
    items = [
        (2, [(z, z) for z in range(n)]),
        (3, [(0, 1), (1, 0), (2, 3), (3, 2)]),
        (4, [(1, 2), (2, 1)]),
        (5, [(0, 2), (3, 1)]),
        (6, [(1, 3), (2, 0)]),
        (7, [(0, 3), (3, 0)]),
    ]
    added = [(0, 0), (8, 0), (9, 0), (10, 0), (1, 1), (11, 1)]
    out = finish(token, requests, lora, arrays, items, added, request_count, rank_rows, n)
    return add_last(out, e1_5, e2_4)


def anywhere(hidden, matrix, input_factor, output_factor, token_requests, meta):
    request_adapters, ranks, slots = meta
    held = input_factor.shape[0]
    width = input_factor.shape[2]
    rank, slot = ranks[request_adapters], slots[request_adapters]
    owned = slot // held == lax.axis_index("store")
    chosen = token_requests[:, None] == jnp.arange(request_adapters.shape[0])[None, :]
    lora = jnp.zeros((hidden.shape[0], width), jnp.float32)
    for r in range(request_adapters.shape[0]):
        product = jnp.dot(hidden, input_factor[slot[r] % held], preferred_element_type=jnp.float32)
        keep = (chosen[:, r] & owned[r])[:, None] & (jnp.arange(width) < rank[r])[None, :]
        lora = jnp.where(keep, product, lora)
    lora = lax.psum_scatter(lora.astype(jnp.bfloat16), "tensor", scatter_dimension=1, tiled=True)
    lora = lax.psum(lora, "store").astype(jnp.float32)
    rows = jnp.where(owned[:, None, None], output_factor[slot % held], jnp.zeros((), output_factor.dtype))
    rows = lax.psum_scatter(rows, "store", scatter_dimension=2, tiled=True)
    weights = jnp.where(chosen, 0.25 * width / rank.astype(jnp.float32)[None, :], 0.0)
    expanded = (weights[:, :, None] * lora[:, None, :]).reshape(hidden.shape[0], -1).astype(jnp.bfloat16)
    term = jnp.dot(hidden, matrix, preferred_element_type=jnp.float32)
    term += jnp.dot(expanded, rows.reshape(-1, rows.shape[2]), preferred_element_type=jnp.float32)
    return lax.psum_scatter(term.astype(jnp.bfloat16), "tensor", scatter_dimension=0, tiled=True)


def per_device(
    hidden_activations,
    down_matrix,
    adapter_input_factor,
    adapter_output_factor,
    token_requests,
    request_adapters,
    adapter_ranks,
    adapter_store_slot,
):
    n = lax.axis_size("tensor")
    meta = (request_adapters, adapter_ranks, adapter_store_slot)
    arrays = (hidden_activations, down_matrix, adapter_input_factor, adapter_output_factor)
    if n == LINE and lax.axis_size("store") == 2 * PAIRS and adapter_input_factor.shape[0] % 2 == 0:
        place = jnp.stack([lax.axis_index("tensor"), lax.axis_index("store")]).astype(jnp.int32)
        token = jnp.concatenate([place, *meta])
        return on_line(*arrays, token_requests.reshape(-1, LANES), token, request_adapters.shape[0], n)
    return anywhere(*arrays, token_requests, meta)


def solution(mesh):
    in_specs = (
        P("groups", "tensor"),
        P("tensor", "store"),
        P(("groups", "store"), "tensor", None),
        P(("groups", "store"), "tensor", None),
        P("groups"),
        P("groups"),
        P("groups"),
        P("groups"),
    )
    out_specs = P(("groups", "tensor"), "store")
    return jax.shard_map(
        per_device, mesh=mesh, in_specs=in_specs, out_specs=out_specs, check_vma=False
    )
```

```python
import functools

import jax
import jax.numpy as jnp
from jax import lax
from jax.experimental import pallas as pl
from jax.experimental.pallas import tpu as pltpu
from jax.sharding import PartitionSpec as P

LINE = 4
LANES = 128
AHEAD = 3
PAIRS = 2
HEAVY = 10**10
MIB = 1024 * 1024


def line_order(n):
    order = []
    for z in range(n):
        sends = [(t, z >= n // 2, n - 1 - t + z) for t in range(z, n - 1)]
        sends += [(t, z < n // 2, t - (n - 1 - z)) for t in range(n - 1 - z, n - 1)]
        order.append([block for _, _, block in sorted(sends)] + [z])
    return order


def first_divisor(size, choices):
    for choice in choices:
        if size % choice == 0:
            return choice
    return size


def after(token, *done):
    return lax.optimization_barrier((token, done))[0]


def params(mebibytes):
    return pltpu.CompilerParams(vmem_limit_bytes=mebibytes * MIB)


def small_cost():
    return pl.CostEstimate(flops=10**6, bytes_accessed=10**5, transcendentals=0)


def block_at(order, slot, place):
    picked = jnp.int32(order[0][slot])
    for z in range(1, len(order)):
        picked = jnp.where(place == z, order[z][slot], picked)
    return picked


def spans(requests_ref, count):
    requests = requests_ref[...]
    return [jnp.int32(0)] + [jnp.sum((requests <= r).astype(jnp.int32)) for r in range(count)]


class Meta:
    def __init__(self, ref, requests):
        self.ref, self.requests = ref, requests
        self.adapters = (ref.shape[0] - 2 - requests) // 2
        self.place, self.shard = ref[0], ref[1]

    def adapter(self, r):
        return self.ref[2 + r]

    def rank(self, r):
        return self.ref[2 + self.requests + self.adapter(r)]

    def local_slot(self, r, held):
        return self.ref[2 + self.requests + self.adapters + self.adapter(r)] - self.shard * held


def base_kernel(order, groups, inputs_for, half, held, request_count, handed_on, *refs):
    slots = [slot for group in groups for slot in group]
    count = len(slots)
    meta, refs = Meta(refs[0], request_count), refs[1:]
    if held:
        requests_ref, factor, refs = refs[0], refs[1], refs[2:]
    hidden, matrix, refs = refs[0], refs[1], refs[2:]
    under, refs = (refs[0], refs[1:]) if handed_on else (None, refs)
    outs, refs = refs[: len(groups)], refs[len(groups) :]
    (rows, right, sums, sems), refs = refs[:4], refs[4:]
    steps, _, tile = rows.shape
    columns = outs[0].shape[1]
    block = rows.shape[1] // count
    first_rows = [pl.multiple_of(block_at(order, slot, meta.place) * block, block) for slot in slots]

    def depth_of(k):
        return pl.ds(pl.multiple_of(k * tile, tile), tile)

    def copies(k):
        moves = [
            (hidden.at[pl.ds(first_rows[i], block), depth_of(k)], rows.at[k, pl.ds(i * block, block), :])
            for i in range(count)
        ]
        moves.append((matrix.at[depth_of(k), pl.ds(half * columns, columns)], right.at[k]))
        return [pltpu.make_async_copy(a, b, sems.at[k, i]) for i, (a, b) in enumerate(moves)]

    if held:
        factors, inputs, flags, factor_sems = refs
        width = factor.shape[2]

        def factor_copies(k, pair):
            return [
                pltpu.make_async_copy(
                    factor.at[2 * pair + i, depth_of(k), :],
                    factors.at[pair, k, :, pl.ds(i * width, width)],
                    factor_sems.at[k, 2 * pair + i],
                )
                for i in range(2)
            ]

    def start(k):
        for copy in copies(k):
            copy.start()

    def start_factors(k, pairs):
        for pair, used in enumerate(pairs):

            @pl.when(used)
            def _(pair=pair):
                for copy in factor_copies(k, pair):
                    copy.start()

    for k in range(min(AHEAD, steps)):
        start(k)
    used = []
    if held:
        bounds = spans(requests_ref, request_count)
        local = [meta.local_slot(r, held) for r in range(request_count)]
        top = slots.index(inputs_for[0])
        wide = len(inputs_for)
        for pair in range(held // 2):
            used_by = []
            for first in first_rows[top : top + wide]:
                wanted = jnp.bool_(False)
                for r, slot in enumerate(local):
                    here = jnp.maximum(bounds[r], first) < jnp.minimum(bounds[r + 1], first + block)
                    wanted = wanted | (here & (slot // 2 == pair) & (slot >= 0))
                flags[pair * wide + len(used_by)] = wanted.astype(jnp.int32)
                used_by.append(wanted)
            used.append(functools.reduce(jnp.logical_or, used_by))
        for k in range(min(AHEAD, steps)):
            start_factors(k, used)
    sums[...] = jnp.zeros_like(sums)

    def step(k, _):
        @pl.when(k + AHEAD < steps)
        def _():
            start(k + AHEAD)
            start_factors(k + AHEAD, used)

        for copy in copies(k):
            copy.wait()
        sums[...] += jnp.dot(rows[k], right[k], preferred_element_type=jnp.float32)
        return 0

    lax.fori_loop(0, steps, step, 0)

    if held:
        for pair, wanted in enumerate(used):

            @pl.when(wanted)
            def _(pair=pair):
                for k in range(steps):
                    for copy in factor_copies(k, pair):
                        copy.wait()

        def pair_block(j, _):
            pair, i = j // wide, j % wide

            @pl.when(flags[j] == 1)
            def _():
                own = pl.ds(pl.multiple_of((top + i) * block, block), block)
                total = jnp.dot(rows[0, own, :], factors[pair, 0], preferred_element_type=jnp.float32)
                for k in range(1, steps):
                    total += jnp.dot(rows[k, own, :], factors[pair, k], preferred_element_type=jnp.float32)
                inputs[pair, pl.ds(pl.multiple_of(i * block, block), block), :] = total

            return 0

        lax.fori_loop(0, held // 2 * wide, pair_block, 0)

    i = 0
    for out, group in zip(outs, groups):
        here = 0
        for slot in group:
            out[here : here + block, :] = sums[i * block : (i + 1) * block, :].astype(jnp.bfloat16)
            here += block
            if held and slot in inputs_for:
                own = pl.ds((i - top) * block, block)
                row = lax.broadcasted_iota(jnp.int32, (block, width), 0) + first_rows[i]
                column = lax.broadcasted_iota(jnp.int32, (block, width), 1)
                total = jnp.zeros((block, width), jnp.float32)
                for r, local_slot in enumerate(local):
                    last = jnp.where((local_slot >= 0) & (local_slot < held), bounds[r + 1], 0)
                    keep = (row >= bounds[r]) & (row < last) & (column < meta.rank(r))
                    local_slot = jnp.clip(local_slot, 0, held - 1)
                    lanes = pl.ds(pl.multiple_of(local_slot % 2 * width, width), width)
                    total = jnp.where(keep, inputs[local_slot // 2, own, lanes], total)
                total = total.astype(jnp.bfloat16)
                size = block * width // columns
                for j in range(columns // width):
                    lanes = slice(j * width, (j + 1) * width)
                    out[here : here + size, lanes] = total[j * size : (j + 1) * size, :]
                here += size
            i += 1
    if handed_on:
        outs[0][outs[0].shape[0] - under.shape[0] :, :] = under[...]


def base_terms(meta, requests, request_count, hidden, matrix, factor, groups, inputs_for, half, n, under=None):
    tokens, depth = hidden.shape
    block, columns = tokens // n, matrix.shape[1] // 2
    tile = first_divisor(depth, (1024, 512, 256, 128))
    steps = depth // tile
    count = sum(len(group) for group in groups)
    smem = pl.BlockSpec(memory_space=pltpu.SMEM)
    vmem = pl.BlockSpec(memory_space=pltpu.VMEM)
    hbm = pl.BlockSpec(memory_space=pltpu.HBM)
    held, extra = 0, 0
    operands, in_specs = [meta], [smem]
    scratch = [
        pltpu.VMEM((steps, count * block, tile), jnp.bfloat16),
        pltpu.VMEM((steps, tile, columns), jnp.bfloat16),
        pltpu.VMEM((count * block, columns), jnp.float32),
        pltpu.SemaphoreType.DMA((steps, count + 1)),
    ]
    if inputs_for:
        held, _, width = factor.shape
        extra = block * width // columns
        operands, in_specs = [meta, requests, factor], [smem, vmem, hbm]
        scratch += [
            pltpu.VMEM((held // 2, steps, tile, 2 * width), jnp.bfloat16),
            pltpu.VMEM((held // 2, len(inputs_for) * block, 2 * width), jnp.float32),
            pltpu.SMEM((held // 2 * len(inputs_for),), jnp.int32),
            pltpu.SemaphoreType.DMA((steps, held)),
        ]
    heights = [sum(block + (extra if slot in inputs_for else 0) for slot in group) for group in groups]
    operands, in_specs = operands + [hidden, matrix], in_specs + [hbm, hbm]
    if under is not None:
        heights[0] += under.shape[0]
        operands, in_specs = operands + [under], in_specs + [vmem]
    handed_on = under is not None
    return pl.pallas_call(
        lambda *refs: base_kernel(line_order(n), groups, inputs_for, half, held, request_count, handed_on, *refs),
        out_shape=[jax.ShapeDtypeStruct((height, columns), jnp.bfloat16) for height in heights],
        in_specs=in_specs,
        out_specs=[vmem] * len(groups),
        scratch_shapes=scratch,
        compiler_params=params(50 if half or count > 1 else 58),
        cost_estimate=small_cost(),
        name="base_terms",
    )(*operands)


def select_rows_kernel(request_count, meta_ref, factor, kept, sent):
    meta = Meta(meta_ref, request_count)
    held, rank_rows, _ = factor.shape
    width = factor.shape[2] // (2 * PAIRS)
    side = meta.shard % 2
    for r in range(request_count):
        slot = meta.local_slot(r, held)
        owned = (slot >= 0) & (slot < held)
        slot = jnp.clip(slot, 0, held - 1)
        for out, core in ((kept, side), (sent, 1 - side)):
            for i in range(PAIRS):
                for c in range(2):
                    first = (2 * i + core) * width + c * (width // 2)
                    rows = factor[slot, :, pl.ds(pl.multiple_of(first, LANES), width // 2)]
                    top = (c * request_count + r) * rank_rows
                    out[i, top : top + rank_rows, :] = jnp.where(owned, rows, jnp.zeros_like(rows))


def select_rows(meta, request_count, factor):
    _, rank_rows, model_width = factor.shape
    smem = pl.BlockSpec(memory_space=pltpu.SMEM)
    vmem = pl.BlockSpec(memory_space=pltpu.VMEM)
    shape = (PAIRS, 2 * request_count * rank_rows, model_width // (4 * PAIRS))
    out = jax.ShapeDtypeStruct(shape, factor.dtype)
    return pl.pallas_call(
        lambda *refs: select_rows_kernel(request_count, *refs),
        out_shape=[out, out],
        in_specs=[smem, vmem],
        out_specs=[vmem, vmem],
        compiler_params=params(16),
        cost_estimate=small_cost(),
        name="select_rows",
    )(meta, factor)


def expanded_inputs(meta, requests_ref, lora_ref):
    block, width = lora_ref.shape
    row = lax.broadcasted_iota(jnp.int32, (block, width), 0) + meta.place * block
    lora = lora_ref[...].astype(jnp.float32)
    bounds = spans(requests_ref, meta.requests)
    parts = []
    for r in range(meta.requests):
        scale = 0.25 * width / meta.rank(r).astype(jnp.float32)
        keep = (row >= bounds[r]) & (row < bounds[r + 1])
        parts.append(jnp.where(keep, lora * scale, 0.0).astype(jnp.bfloat16))
    return jnp.concatenate(parts, axis=1)


def finish_kernel(items, added, requests, rank_rows, n, *refs):
    meta_ref, requests_ref, lora_ref, refs = refs[0], refs[1], refs[2], refs[3:]
    arrays, out, rows = refs[:-2], refs[-2], refs[-1]
    meta = Meta(meta_ref, requests)
    rank = n * rank_rows
    half = out.shape[1] // 2
    for index, top, targets in items:
        for place, k in targets:

            @pl.when(meta.place == place)
            def _(piece=arrays[index], top=top, k=k):
                for r in range(requests):
                    first = r * rank + k * rank_rows
                    for c in range(2):
                        start = top + (c * requests + r) * rank_rows
                        rows[first : first + rank_rows, c * half : (c + 1) * half] = piece[start : start + rank_rows, :]

    expanded = expanded_inputs(meta, requests_ref, lora_ref)
    block = lora_ref.shape[0]
    for c in range(2):
        columns = slice(c * half, (c + 1) * half)
        total = jnp.dot(expanded, rows[:, columns], preferred_element_type=jnp.float32)
        for index, top, which in added:
            if which == c:
                total += arrays[index][top : top + block, :].astype(jnp.float32)
        out[:, columns] = total.astype(out.dtype)


def finish(meta, requests, lora, arrays, items, added, request_count, rank_rows, n):
    smem = pl.BlockSpec(memory_space=pltpu.SMEM)
    vmem = pl.BlockSpec(memory_space=pltpu.VMEM)
    width = 2 * arrays[0].shape[1]
    return pl.pallas_call(
        lambda *refs: finish_kernel(items, added, request_count, rank_rows, n, *refs),
        out_shape=jax.ShapeDtypeStruct((lora.shape[0], width), jnp.bfloat16),
        in_specs=[smem] + [vmem] * (2 + len(arrays)),
        out_specs=vmem,
        scratch_shapes=[pltpu.VMEM((request_count * n * rank_rows, width), jnp.bfloat16)],
        compiler_params=params(20),
        cost_estimate=small_cost(),
        name="finish",
    )(meta, requests, lora, *arrays)


def join_kernel(count, term_top, came_top, under_top, term, came, *refs):
    out = refs[-1]
    total = term[term_top : term_top + count, :].astype(jnp.float32)
    total += came[came_top : came_top + count, :].astype(jnp.float32)
    out[:count, :] = total.astype(out.dtype)
    if len(refs) > 1:
        under = refs[0]
        out[count:, :] = under[under_top : under_top + out.shape[0] - count, :]


def join(token, count, term, term_top, came, came_top, under=None, under_top=0, under_count=0, weight=10**6):
    arrays = [term, came] + ([] if under is None else [under])
    arrays = lax.optimization_barrier((arrays, token))[0]
    vmem = pl.BlockSpec(memory_space=pltpu.VMEM)
    return pl.pallas_call(
        lambda *refs: join_kernel(count, term_top, came_top, under_top, *refs),
        out_shape=jax.ShapeDtypeStruct((count + under_count, term.shape[1]), term.dtype),
        in_specs=[vmem] * len(arrays),
        out_specs=vmem,
        compiler_params=params(12),
        cost_estimate=pl.CostEstimate(flops=weight, bytes_accessed=10**5, transcendentals=0),
        name="join",
    )(*arrays)


def add_last_kernel(total, *refs):
    arrivals, out = refs[:-1], refs[-1]
    half = arrivals[0].shape[1]
    out[:, :half] = total[:, :half]
    last = total[:, half:].astype(jnp.float32)
    for arrival in arrivals:
        last += arrival[...].astype(jnp.float32)
    out[:, half:] = last.astype(out.dtype)


def add_last(total, *arrivals):
    vmem = pl.BlockSpec(memory_space=pltpu.VMEM)
    return pl.pallas_call(
        add_last_kernel,
        out_shape=jax.ShapeDtypeStruct(total.shape, total.dtype),
        in_specs=[vmem] * (1 + len(arrivals)),
        out_specs=vmem,
        compiler_params=params(12),
        cost_estimate=small_cost(),
        name="add_last",
    )(total, *arrivals)


def under_each_other_kernel(upper, lower, out):
    out[: upper.shape[0], :] = upper[...]
    out[upper.shape[0] :, :] = lower[...]


def under_each_other(upper, lower):
    vmem = pl.BlockSpec(memory_space=pltpu.VMEM)
    return pl.pallas_call(
        under_each_other_kernel,
        out_shape=jax.ShapeDtypeStruct((upper.shape[0] + lower.shape[0], upper.shape[1]), upper.dtype),
        in_specs=[vmem] * 2,
        out_specs=vmem,
        compiler_params=params(12),
        cost_estimate=small_cost(),
        name="under_each_other",
    )(upper, lower)


def swap(x, axis, bit):
    return lax.ppermute(x, axis, [(i, i ^ bit) for i in range(lax.axis_size(axis))])


def bits_of(size):
    return [1 << i for i in range(size.bit_length() - 1)]


def along_edge(x, edge):
    n = lax.axis_size("tensor")
    return lax.ppermute(x, "tensor", [(edge, edge + 1), (n - 1 - edge, n - 2 - edge)])


def on_line(hidden, matrix, input_factor, output_factor, requests, token, request_count, n):
    shard = lax.axis_index("store")
    block = hidden.shape[0] // n
    width = input_factor.shape[2]
    rank_rows = output_factor.shape[1]
    piece = block + block * width // (matrix.shape[1] // 2)
    bundle = 2 * request_count * rank_rows

    def base(token, groups, inputs_for, half, under=None):
        return base_terms(
            token, requests, request_count, hidden, matrix, input_factor, groups, inputs_for, half, n, under
        )

    def send(x, edge, token):
        return along_edge(after(x, token), edge)

    (s00,) = base(token, [[0]], [0], 0)
    token = after(token, s00)
    e0_1 = along_edge(s00, 0)
    kept, sent = select_rows(token, request_count, output_factor)
    token = after(token, kept, sent)
    swapped = swap(sent, "store", 1)
    token = after(token, swapped)
    side = shard // 2 % 2
    kept, swapped, _ = lax.optimization_barrier((kept, swapped, token))
    outgoing = kept[1 - side] + swapped[1 - side]
    token = after(token, outgoing)
    across = swap(outgoing, "store", 2)
    s01, s11 = base(token, [[0], [1]], [], 1)

    token = after(token, s01)
    e0_2 = send(s01, 0, token)
    token, e0_1 = lax.optimization_barrier((token, e0_1))
    b10 = join(token, piece, s00, 0, e0_1, 0)
    token = after(token, b10)
    e1_2 = along_edge(b10, 1)
    token, across, kept, swapped = lax.optimization_barrier((token, across, kept, swapped))
    rows = kept[side] + swapped[side] + across
    token = after(token, rows)
    near = lax.ppermute(rows, "tensor", [(0, 1), (n - 1, n - 2), (1, 0), (n - 2, n - 1)])
    far = along_edge(rows, 1)
    s10_s11, s20, s30 = base(token, [[1], [2], [3]], [1, 2], 0, s11)

    token = after(token, s10_s11)
    e0_3 = send(s10_s11, 0, token)
    token, e0_2 = lax.optimization_barrier((token, e0_2))
    b11 = join(token, block, s01, 0, e0_2, 0, weight=HEAVY)
    token, near = lax.optimization_barrier((after(token, b11), near))
    e1_3 = along_edge(under_each_other(b11, near), 1)
    token, e1_2, far = lax.optimization_barrier((token, e1_2, far))
    c20 = join(token, piece, s20, 0, e1_2, 0, far, 0, bundle)
    token = after(token, c20)
    e2_3 = along_edge(c20, 2)
    s21, s31 = base(token, [[2], [3]], [3], 1)

    token = after(token, s21)
    e0_4 = send(s20, 0, token)
    token, e0_3 = lax.optimization_barrier((token, e0_3))
    b20 = join(token, piece, s10_s11, 0, e0_3, 0)
    token = after(token, b20)
    e1_4 = along_edge(b20, 1)
    token, e1_3 = lax.optimization_barrier((token, e1_3))
    last_rows = send(e1_3[block:], 2, token)
    c21 = join(token, block, s21, 0, e1_3, 0, weight=HEAVY // 5)
    token = after(token, c21)
    e2_4 = along_edge(c21, 2)
    token, e2_3 = lax.optimization_barrier((token, e2_3))
    e0_5 = send(s21, 0, token)
    b21 = join(token, block, s10_s11, piece, e0_3, piece)
    token = after(token, b21)
    e1_5 = along_edge(b21, 1)

    token, e0_4 = lax.optimization_barrier((token, e0_4))
    token, e1_4 = lax.optimization_barrier((token, e1_4))
    token, last_rows = lax.optimization_barrier((token, last_rows))
    e1_4 = after(e1_4, token)
    lora = s31[block:].astype(jnp.float32) + e0_4[block:].astype(jnp.float32)
    lora += e1_4[block:].astype(jnp.float32) + e2_3[block:piece].astype(jnp.float32)
    lora = lora.astype(jnp.bfloat16).reshape(piece - block, -1, width).swapaxes(0, 1).reshape(block, width)
    lora = lora + swap(lora, "store", 1)
    lora = lora + swap(lora, "store", 2)
    arrays = [s30, s31, rows, near, far, e1_3, e2_3, last_rows, e0_4, e1_4]
    items = [
        (2, 0, [(z, z) for z in range(n)]),
        (3, 0, [(0, 1), (1, 0), (2, 3), (3, 2)]),
        (4, 0, [(1, 2), (2, 1)]),
        (5, block, [(1, 3), (2, 0)]),
        (6, piece, [(0, 2), (3, 1)]),
        (7, 0, [(0, 3), (3, 0)]),
    ]
    added = [(0, 0, 0), (8, 0, 0), (9, 0, 0), (6, 0, 0), (1, 0, 1)]
    out = finish(token, requests, lora, arrays, items, added, request_count, rank_rows, n)
    return add_last(out, e0_5, e1_5, e2_4)


def anywhere(hidden, matrix, input_factor, output_factor, token_requests, meta):
    request_adapters, ranks, slots = meta
    held = input_factor.shape[0]
    width = input_factor.shape[2]
    rank, slot = ranks[request_adapters], slots[request_adapters]
    owned = slot // held == lax.axis_index("store")
    chosen = token_requests[:, None] == jnp.arange(request_adapters.shape[0])[None, :]
    lora = jnp.zeros((hidden.shape[0], width), jnp.float32)
    for r in range(request_adapters.shape[0]):
        product = jnp.dot(hidden, input_factor[slot[r] % held], preferred_element_type=jnp.float32)
        keep = (chosen[:, r] & owned[r])[:, None] & (jnp.arange(width) < rank[r])[None, :]
        lora = jnp.where(keep, product, lora)
    lora = lax.psum_scatter(lora.astype(jnp.bfloat16), "tensor", scatter_dimension=1, tiled=True)
    lora = lax.psum(lora, "store").astype(jnp.float32)
    rows = jnp.where(owned[:, None, None], output_factor[slot % held], jnp.zeros((), output_factor.dtype))
    rows = lax.psum_scatter(rows, "store", scatter_dimension=2, tiled=True)
    weights = jnp.where(chosen, 0.25 * width / rank.astype(jnp.float32)[None, :], 0.0)
    expanded = (weights[:, :, None] * lora[:, None, :]).reshape(hidden.shape[0], -1).astype(jnp.bfloat16)
    term = jnp.dot(hidden, matrix, preferred_element_type=jnp.float32)
    term += jnp.dot(expanded, rows.reshape(-1, rows.shape[2]), preferred_element_type=jnp.float32)
    return lax.psum_scatter(term.astype(jnp.bfloat16), "tensor", scatter_dimension=0, tiled=True)


def per_device(
    hidden_activations,
    down_matrix,
    adapter_input_factor,
    adapter_output_factor,
    token_requests,
    request_adapters,
    adapter_ranks,
    adapter_store_slot,
):
    n = lax.axis_size("tensor")
    meta = (request_adapters, adapter_ranks, adapter_store_slot)
    arrays = (hidden_activations, down_matrix, adapter_input_factor, adapter_output_factor)
    if n == LINE and lax.axis_size("store") == 2 * PAIRS and adapter_input_factor.shape[0] % 2 == 0:
        place = jnp.stack([lax.axis_index("tensor"), lax.axis_index("store")]).astype(jnp.int32)
        token = jnp.concatenate([place, *meta])
        return on_line(*arrays, token_requests.reshape(-1, LANES), token, request_adapters.shape[0], n)
    return anywhere(*arrays, token_requests, meta)


def solution(mesh):
    in_specs = (
        P("groups", "tensor"),
        P("tensor", "store"),
        P(("groups", "store"), "tensor", None),
        P(("groups", "store"), "tensor", None),
        P("groups"),
        P("groups"),
        P("groups"),
        P("groups"),
    )
    out_specs = P(("groups", "tensor"), "store")
    return jax.shard_map(
        per_device, mesh=mesh, in_specs=in_specs, out_specs=out_specs, check_vma=False
    )
```

```python
import functools

import jax
import jax.numpy as jnp
from jax import lax
from jax.experimental import pallas as pl
from jax.experimental.pallas import tpu as pltpu
from jax.sharding import PartitionSpec as P

LINE = 4
LANES = 128
AHEAD = 3
PAIRS = 2
HEAVY = 10**10
MIB = 1024 * 1024


def line_order(n):
    order = []
    for z in range(n):
        sends = [(t, z >= n // 2, n - 1 - t + z) for t in range(z, n - 1)]
        sends += [(t, z < n // 2, t - (n - 1 - z)) for t in range(n - 1 - z, n - 1)]
        order.append([block for _, _, block in sorted(sends)] + [z])
    return order


def first_divisor(size, choices):
    for choice in choices:
        if size % choice == 0:
            return choice
    return size


def after(token, *done):
    return lax.optimization_barrier((token, done))[0]


def params(mebibytes):
    return pltpu.CompilerParams(vmem_limit_bytes=mebibytes * MIB)


def small_cost():
    return pl.CostEstimate(flops=10**6, bytes_accessed=10**5, transcendentals=0)


def block_at(order, slot, place):
    picked = jnp.int32(order[0][slot])
    for z in range(1, len(order)):
        picked = jnp.where(place == z, order[z][slot], picked)
    return picked


def spans(requests_ref, count):
    requests = requests_ref[...]
    return [jnp.int32(0)] + [jnp.sum((requests <= r).astype(jnp.int32)) for r in range(count)]


class Meta:
    def __init__(self, ref, requests):
        self.ref, self.requests = ref, requests
        self.adapters = (ref.shape[0] - 2 - requests) // 2
        self.place, self.shard = ref[0], ref[1]

    def adapter(self, r):
        return self.ref[2 + r]

    def rank(self, r):
        return self.ref[2 + self.requests + self.adapter(r)]

    def local_slot(self, r, held):
        return self.ref[2 + self.requests + self.adapters + self.adapter(r)] - self.shard * held


def base_kernel(order, groups, inputs_for, half, held, request_count, handed_on, *refs):
    slots = [slot for group in groups for slot in group]
    count = len(slots)
    meta, refs = Meta(refs[0], request_count), refs[1:]
    if held:
        requests_ref, factor, refs = refs[0], refs[1], refs[2:]
    hidden, matrix, refs = refs[0], refs[1], refs[2:]
    under, refs = (refs[0], refs[1:]) if handed_on else (None, refs)
    outs, refs = refs[: len(groups)], refs[len(groups) :]
    (rows, right, sums, sems), refs = refs[:4], refs[4:]
    steps, _, tile = rows.shape
    columns = outs[0].shape[1]
    block = rows.shape[1] // count
    first_rows = [pl.multiple_of(block_at(order, slot, meta.place) * block, block) for slot in slots]

    def depth_of(k):
        return pl.ds(pl.multiple_of(k * tile, tile), tile)

    def copies(k):
        moves = [
            (hidden.at[pl.ds(first_rows[i], block), depth_of(k)], rows.at[k, pl.ds(i * block, block), :])
            for i in range(count)
        ]
        moves.append((matrix.at[depth_of(k), pl.ds(half * columns, columns)], right.at[k]))
        return [pltpu.make_async_copy(a, b, sems.at[k, i]) for i, (a, b) in enumerate(moves)]

    if held:
        factors, inputs, flags, factor_sems = refs
        width = factor.shape[2]

        def factor_copies(k, pair):
            return [
                pltpu.make_async_copy(
                    factor.at[2 * pair + i, depth_of(k), :],
                    factors.at[pair, k, :, pl.ds(i * width, width)],
                    factor_sems.at[k, 2 * pair + i],
                )
                for i in range(2)
            ]

    def start(k):
        for copy in copies(k):
            copy.start()

    def start_factors(k, pairs):
        for pair, used in enumerate(pairs):

            @pl.when(used)
            def _(pair=pair):
                for copy in factor_copies(k, pair):
                    copy.start()

    for k in range(min(AHEAD, steps)):
        start(k)
    used = []
    if held:
        bounds = spans(requests_ref, request_count)
        local = [meta.local_slot(r, held) for r in range(request_count)]
        top = slots.index(inputs_for[0])
        wide = len(inputs_for)
        for pair in range(held // 2):
            used_by = []
            for first in first_rows[top : top + wide]:
                wanted = jnp.bool_(False)
                for r, slot in enumerate(local):
                    here = jnp.maximum(bounds[r], first) < jnp.minimum(bounds[r + 1], first + block)
                    wanted = wanted | (here & (slot // 2 == pair) & (slot >= 0))
                flags[pair * wide + len(used_by)] = wanted.astype(jnp.int32)
                used_by.append(wanted)
            used.append(functools.reduce(jnp.logical_or, used_by))
        for k in range(min(AHEAD, steps)):
            start_factors(k, used)
    sums[...] = jnp.zeros_like(sums)

    def step(k, _):
        @pl.when(k + AHEAD < steps)
        def _():
            start(k + AHEAD)
            start_factors(k + AHEAD, used)

        for copy in copies(k):
            copy.wait()
        sums[...] += jnp.dot(rows[k], right[k], preferred_element_type=jnp.float32)
        return 0

    lax.fori_loop(0, steps, step, 0)

    if held:
        for pair, wanted in enumerate(used):

            @pl.when(wanted)
            def _(pair=pair):
                for k in range(steps):
                    for copy in factor_copies(k, pair):
                        copy.wait()

        def pair_block(j, _):
            pair, i = j // wide, j % wide

            @pl.when(flags[j] == 1)
            def _():
                own = pl.ds(pl.multiple_of((top + i) * block, block), block)
                total = jnp.dot(rows[0, own, :], factors[pair, 0], preferred_element_type=jnp.float32)
                for k in range(1, steps):
                    total += jnp.dot(rows[k, own, :], factors[pair, k], preferred_element_type=jnp.float32)
                inputs[pair, pl.ds(pl.multiple_of(i * block, block), block), :] = total

            return 0

        lax.fori_loop(0, held // 2 * wide, pair_block, 0)

    i = 0
    for out, group in zip(outs, groups):
        here = 0
        for slot in group:
            out[here : here + block, :] = sums[i * block : (i + 1) * block, :].astype(jnp.bfloat16)
            here += block
            if held and slot in inputs_for:
                own = pl.ds((i - top) * block, block)
                row = lax.broadcasted_iota(jnp.int32, (block, width), 0) + first_rows[i]
                column = lax.broadcasted_iota(jnp.int32, (block, width), 1)
                total = jnp.zeros((block, width), jnp.float32)
                for r, local_slot in enumerate(local):
                    last = jnp.where((local_slot >= 0) & (local_slot < held), bounds[r + 1], 0)
                    keep = (row >= bounds[r]) & (row < last) & (column < meta.rank(r))
                    local_slot = jnp.clip(local_slot, 0, held - 1)
                    lanes = pl.ds(pl.multiple_of(local_slot % 2 * width, width), width)
                    total = jnp.where(keep, inputs[local_slot // 2, own, lanes], total)
                total = total.astype(jnp.bfloat16)
                size = block * width // columns
                for j in range(columns // width):
                    lanes = slice(j * width, (j + 1) * width)
                    out[here : here + size, lanes] = total[j * size : (j + 1) * size, :]
                here += size
            i += 1
    if handed_on:
        outs[0][outs[0].shape[0] - under.shape[0] :, :] = under[...]


def base_terms(meta, requests, request_count, hidden, matrix, factor, groups, inputs_for, half, n, under=None):
    tokens, depth = hidden.shape
    block, columns = tokens // n, matrix.shape[1] // 2
    tile = first_divisor(depth, (1024, 512, 256, 128))
    steps = depth // tile
    count = sum(len(group) for group in groups)
    smem = pl.BlockSpec(memory_space=pltpu.SMEM)
    vmem = pl.BlockSpec(memory_space=pltpu.VMEM)
    hbm = pl.BlockSpec(memory_space=pltpu.HBM)
    held, extra = 0, 0
    operands, in_specs = [meta], [smem]
    scratch = [
        pltpu.VMEM((steps, count * block, tile), jnp.bfloat16),
        pltpu.VMEM((steps, tile, columns), jnp.bfloat16),
        pltpu.VMEM((count * block, columns), jnp.float32),
        pltpu.SemaphoreType.DMA((steps, count + 1)),
    ]
    if inputs_for:
        held, _, width = factor.shape
        extra = block * width // columns
        operands, in_specs = [meta, requests, factor], [smem, vmem, hbm]
        scratch += [
            pltpu.VMEM((held // 2, steps, tile, 2 * width), jnp.bfloat16),
            pltpu.VMEM((held // 2, len(inputs_for) * block, 2 * width), jnp.float32),
            pltpu.SMEM((held // 2 * len(inputs_for),), jnp.int32),
            pltpu.SemaphoreType.DMA((steps, held)),
        ]
    heights = [sum(block + (extra if slot in inputs_for else 0) for slot in group) for group in groups]
    operands, in_specs = operands + [hidden, matrix], in_specs + [hbm, hbm]
    if under is not None:
        heights[0] += under.shape[0]
        operands, in_specs = operands + [under], in_specs + [vmem]
    handed_on = under is not None
    return pl.pallas_call(
        lambda *refs: base_kernel(line_order(n), groups, inputs_for, half, held, request_count, handed_on, *refs),
        out_shape=[jax.ShapeDtypeStruct((height, columns), jnp.bfloat16) for height in heights],
        in_specs=in_specs,
        out_specs=[vmem] * len(groups),
        scratch_shapes=scratch,
        compiler_params=params(50 if half or count > 1 else 58),
        cost_estimate=small_cost(),
        name="base_terms",
    )(*operands)


def select_rows_kernel(request_count, meta_ref, factor, kept, sent):
    meta = Meta(meta_ref, request_count)
    held, rank_rows, _ = factor.shape
    width = factor.shape[2] // (2 * PAIRS)
    side = meta.shard % 2
    for r in range(request_count):
        slot = meta.local_slot(r, held)
        owned = (slot >= 0) & (slot < held)
        slot = jnp.clip(slot, 0, held - 1)
        for out, core in ((kept, side), (sent, 1 - side)):
            for i in range(PAIRS):
                for c in range(2):
                    first = (2 * i + core) * width + c * (width // 2)
                    rows = factor[slot, :, pl.ds(pl.multiple_of(first, LANES), width // 2)]
                    top = (c * request_count + r) * rank_rows
                    out[i, top : top + rank_rows, :] = jnp.where(owned, rows, jnp.zeros_like(rows))


def select_rows(meta, request_count, factor):
    _, rank_rows, model_width = factor.shape
    smem = pl.BlockSpec(memory_space=pltpu.SMEM)
    vmem = pl.BlockSpec(memory_space=pltpu.VMEM)
    shape = (PAIRS, 2 * request_count * rank_rows, model_width // (4 * PAIRS))
    out = jax.ShapeDtypeStruct(shape, factor.dtype)
    return pl.pallas_call(
        lambda *refs: select_rows_kernel(request_count, *refs),
        out_shape=[out, out],
        in_specs=[smem, vmem],
        out_specs=[vmem, vmem],
        compiler_params=params(16),
        cost_estimate=small_cost(),
        name="select_rows",
    )(meta, factor)


def expanded_inputs(meta, requests_ref, lora_ref):
    block, width = lora_ref.shape
    row = lax.broadcasted_iota(jnp.int32, (block, width), 0) + meta.place * block
    lora = lora_ref[...].astype(jnp.float32)
    bounds = spans(requests_ref, meta.requests)
    parts = []
    for r in range(meta.requests):
        scale = 0.25 * width / meta.rank(r).astype(jnp.float32)
        keep = (row >= bounds[r]) & (row < bounds[r + 1])
        parts.append(jnp.where(keep, lora * scale, 0.0).astype(jnp.bfloat16))
    return jnp.concatenate(parts, axis=1)


def finish_kernel(items, added, requests, rank_rows, n, *refs):
    meta_ref, requests_ref, lora_ref, refs = refs[0], refs[1], refs[2], refs[3:]
    arrays, out, rows = refs[:-2], refs[-2], refs[-1]
    meta = Meta(meta_ref, requests)
    rank = n * rank_rows
    half = out.shape[1] // 2
    for index, top, targets in items:
        for place, k in targets:

            @pl.when(meta.place == place)
            def _(piece=arrays[index], top=top, k=k):
                for r in range(requests):
                    first = r * rank + k * rank_rows
                    for c in range(2):
                        start = top + (c * requests + r) * rank_rows
                        rows[first : first + rank_rows, c * half : (c + 1) * half] = piece[start : start + rank_rows, :]

    expanded = expanded_inputs(meta, requests_ref, lora_ref)
    block = lora_ref.shape[0]
    for c in range(2):
        columns = slice(c * half, (c + 1) * half)
        total = jnp.dot(expanded, rows[:, columns], preferred_element_type=jnp.float32)
        for index, top, which in added:
            if which == c:
                total += arrays[index][top : top + block, :].astype(jnp.float32)
        out[:, columns] = total.astype(out.dtype)


def finish(meta, requests, lora, arrays, items, added, request_count, rank_rows, n):
    smem = pl.BlockSpec(memory_space=pltpu.SMEM)
    vmem = pl.BlockSpec(memory_space=pltpu.VMEM)
    width = 2 * arrays[0].shape[1]
    return pl.pallas_call(
        lambda *refs: finish_kernel(items, added, request_count, rank_rows, n, *refs),
        out_shape=jax.ShapeDtypeStruct((lora.shape[0], width), jnp.bfloat16),
        in_specs=[smem] + [vmem] * (2 + len(arrays)),
        out_specs=vmem,
        scratch_shapes=[pltpu.VMEM((request_count * n * rank_rows, width), jnp.bfloat16)],
        compiler_params=params(20),
        cost_estimate=small_cost(),
        name="finish",
    )(meta, requests, lora, *arrays)


def join_kernel(count, term_top, came_top, under_top, term, came, *refs):
    out = refs[-1]
    total = term[term_top : term_top + count, :].astype(jnp.float32)
    total += came[came_top : came_top + count, :].astype(jnp.float32)
    out[:count, :] = total.astype(out.dtype)
    if len(refs) > 1:
        under = refs[0]
        out[count:, :] = under[under_top : under_top + out.shape[0] - count, :]


def join(token, count, term, term_top, came, came_top, under=None, under_top=0, under_count=0, weight=10**6):
    arrays = [term, came] + ([] if under is None else [under])
    arrays = lax.optimization_barrier((arrays, token))[0]
    vmem = pl.BlockSpec(memory_space=pltpu.VMEM)
    return pl.pallas_call(
        lambda *refs: join_kernel(count, term_top, came_top, under_top, *refs),
        out_shape=jax.ShapeDtypeStruct((count + under_count, term.shape[1]), term.dtype),
        in_specs=[vmem] * len(arrays),
        out_specs=vmem,
        compiler_params=params(12),
        cost_estimate=pl.CostEstimate(flops=weight, bytes_accessed=10**5, transcendentals=0),
        name="join",
    )(*arrays)


def add_last_kernel(total, *refs):
    arrivals, out = refs[:-1], refs[-1]
    half = arrivals[0].shape[1]
    out[:, :half] = total[:, :half]
    last = total[:, half:].astype(jnp.float32)
    for arrival in arrivals:
        last += arrival[...].astype(jnp.float32)
    out[:, half:] = last.astype(out.dtype)


def add_last(total, *arrivals):
    vmem = pl.BlockSpec(memory_space=pltpu.VMEM)
    return pl.pallas_call(
        add_last_kernel,
        out_shape=jax.ShapeDtypeStruct(total.shape, total.dtype),
        in_specs=[vmem] * (1 + len(arrivals)),
        out_specs=vmem,
        compiler_params=params(12),
        cost_estimate=small_cost(),
        name="add_last",
    )(total, *arrivals)


def under_each_other_kernel(upper, lower, out):
    out[: upper.shape[0], :] = upper[...]
    out[upper.shape[0] :, :] = lower[...]


def under_each_other(upper, lower):
    vmem = pl.BlockSpec(memory_space=pltpu.VMEM)
    return pl.pallas_call(
        under_each_other_kernel,
        out_shape=jax.ShapeDtypeStruct((upper.shape[0] + lower.shape[0], upper.shape[1]), upper.dtype),
        in_specs=[vmem] * 2,
        out_specs=vmem,
        compiler_params=params(12),
        cost_estimate=small_cost(),
        name="under_each_other",
    )(upper, lower)


def swap(x, axis, bit):
    return lax.ppermute(x, axis, [(i, i ^ bit) for i in range(lax.axis_size(axis))])


def bits_of(size):
    return [1 << i for i in range(size.bit_length() - 1)]


def along_edge(x, edge):
    n = lax.axis_size("tensor")
    return lax.ppermute(x, "tensor", [(edge, edge + 1), (n - 1 - edge, n - 2 - edge)])


def on_line(hidden, matrix, input_factor, output_factor, requests, token, request_count, n):
    shard = lax.axis_index("store")
    block = hidden.shape[0] // n
    width = input_factor.shape[2]
    rank_rows = output_factor.shape[1]
    piece = block + block * width // (matrix.shape[1] // 2)
    bundle = 2 * request_count * rank_rows

    def base(token, groups, inputs_for, half, under=None):
        return base_terms(
            token, requests, request_count, hidden, matrix, input_factor, groups, inputs_for, half, n, under
        )

    def send(x, edge, token):
        return along_edge(after(x, token), edge)

    (s00,) = base(token, [[0]], [0], 0)
    token = after(token, s00)
    e0_1 = along_edge(s00, 0)
    kept, sent = select_rows(token, request_count, output_factor)
    token = after(token, kept, sent)
    swapped = swap(sent, "store", 1)
    token = after(token, swapped)
    side = shard // 2 % 2
    kept, swapped, _ = lax.optimization_barrier((kept, swapped, token))
    outgoing = kept[1 - side] + swapped[1 - side]
    rows = kept[side] + swapped[side]
    token = after(token, outgoing, rows)
    across = swap(outgoing, "store", 2)
    s01, s11 = base(token, [[0], [1]], [], 1)

    token = after(token, s01)
    e0_2 = send(s01, 0, token)
    token, e0_1 = lax.optimization_barrier((token, e0_1))
    b10 = join(token, piece, s00, 0, e0_1, 0)
    token = after(token, b10)
    e1_2 = along_edge(b10, 1)
    token, across = lax.optimization_barrier((token, across))
    rows = rows + across
    token = after(token, rows)
    near = lax.ppermute(rows, "tensor", [(0, 1), (n - 1, n - 2), (1, 0), (n - 2, n - 1)])
    far = along_edge(rows, 1)
    s10_s11, s20, s30 = base(token, [[1], [2], [3]], [1, 2], 0, s11)

    token = after(token, s10_s11)
    e0_3 = send(s10_s11, 0, token)
    token, e0_2 = lax.optimization_barrier((token, e0_2))
    b11 = join(token, block, s01, 0, e0_2, 0, weight=HEAVY)
    token, near = lax.optimization_barrier((after(token, b11), near))
    e1_3 = along_edge(under_each_other(b11, near), 1)
    token, e1_2, far = lax.optimization_barrier((token, e1_2, far))
    c20 = join(token, piece, s20, 0, e1_2, 0, far, 0, bundle)
    token = after(token, c20)
    e2_3 = along_edge(c20, 2)
    s21, s31 = base(token, [[2], [3]], [3], 1)

    token = after(token, s21)
    e0_4 = send(s20, 0, token)
    token, e0_3 = lax.optimization_barrier((token, e0_3))
    b20 = join(token, piece, s10_s11, 0, e0_3, 0)
    token = after(token, b20)
    e1_4 = along_edge(b20, 1)
    token, e1_3 = lax.optimization_barrier((token, e1_3))
    last_rows = send(e1_3[block:], 2, token)
    c21 = join(token, block, s21, 0, e1_3, 0, weight=HEAVY // 5)
    token = after(token, c21)
    e2_4 = along_edge(c21, 2)
    token, e2_3 = lax.optimization_barrier((token, e2_3))
    e0_5 = send(s21, 0, token)
    b21 = join(token, block, s10_s11, piece, e0_3, piece)
    token = after(token, b21)
    e1_5 = along_edge(b21, 1)

    token, e0_4 = lax.optimization_barrier((token, e0_4))
    token, e1_4 = lax.optimization_barrier((token, e1_4))
    token, last_rows = lax.optimization_barrier((token, last_rows))
    e1_4 = after(e1_4, token)
    lora = s31[block:].astype(jnp.float32) + e0_4[block:].astype(jnp.float32)
    lora += e1_4[block:].astype(jnp.float32) + e2_3[block:piece].astype(jnp.float32)
    lora = lora.astype(jnp.bfloat16).reshape(piece - block, -1, width).swapaxes(0, 1).reshape(block, width)
    lora = lora + swap(lora, "store", 1)
    lora = lora + swap(lora, "store", 2)
    arrays = [s30, s31, rows, near, far, e1_3, e2_3, last_rows, e0_4, e1_4]
    items = [
        (2, 0, [(z, z) for z in range(n)]),
        (3, 0, [(0, 1), (1, 0), (2, 3), (3, 2)]),
        (4, 0, [(1, 2), (2, 1)]),
        (5, block, [(1, 3), (2, 0)]),
        (6, piece, [(0, 2), (3, 1)]),
        (7, 0, [(0, 3), (3, 0)]),
    ]
    added = [(0, 0, 0), (8, 0, 0), (9, 0, 0), (6, 0, 0), (1, 0, 1)]
    out = finish(token, requests, lora, arrays, items, added, request_count, rank_rows, n)
    return add_last(out, e0_5, e1_5, e2_4)


def anywhere(hidden, matrix, input_factor, output_factor, token_requests, meta):
    request_adapters, ranks, slots = meta
    held = input_factor.shape[0]
    width = input_factor.shape[2]
    rank, slot = ranks[request_adapters], slots[request_adapters]
    owned = slot // held == lax.axis_index("store")
    chosen = token_requests[:, None] == jnp.arange(request_adapters.shape[0])[None, :]
    lora = jnp.zeros((hidden.shape[0], width), jnp.float32)
    for r in range(request_adapters.shape[0]):
        product = jnp.dot(hidden, input_factor[slot[r] % held], preferred_element_type=jnp.float32)
        keep = (chosen[:, r] & owned[r])[:, None] & (jnp.arange(width) < rank[r])[None, :]
        lora = jnp.where(keep, product, lora)
    lora = lax.psum_scatter(lora.astype(jnp.bfloat16), "tensor", scatter_dimension=1, tiled=True)
    lora = lax.psum(lora, "store").astype(jnp.float32)
    rows = jnp.where(owned[:, None, None], output_factor[slot % held], jnp.zeros((), output_factor.dtype))
    rows = lax.psum_scatter(rows, "store", scatter_dimension=2, tiled=True)
    weights = jnp.where(chosen, 0.25 * width / rank.astype(jnp.float32)[None, :], 0.0)
    expanded = (weights[:, :, None] * lora[:, None, :]).reshape(hidden.shape[0], -1).astype(jnp.bfloat16)
    term = jnp.dot(hidden, matrix, preferred_element_type=jnp.float32)
    term += jnp.dot(expanded, rows.reshape(-1, rows.shape[2]), preferred_element_type=jnp.float32)
    return lax.psum_scatter(term.astype(jnp.bfloat16), "tensor", scatter_dimension=0, tiled=True)


def per_device(
    hidden_activations,
    down_matrix,
    adapter_input_factor,
    adapter_output_factor,
    token_requests,
    request_adapters,
    adapter_ranks,
    adapter_store_slot,
):
    n = lax.axis_size("tensor")
    meta = (request_adapters, adapter_ranks, adapter_store_slot)
    arrays = (hidden_activations, down_matrix, adapter_input_factor, adapter_output_factor)
    if n == LINE and lax.axis_size("store") == 2 * PAIRS and adapter_input_factor.shape[0] % 2 == 0:
        place = jnp.stack([lax.axis_index("tensor"), lax.axis_index("store")]).astype(jnp.int32)
        token = jnp.concatenate([place, *meta])
        return on_line(*arrays, token_requests.reshape(-1, LANES), token, request_adapters.shape[0], n)
    return anywhere(*arrays, token_requests, meta)


def solution(mesh):
    in_specs = (
        P("groups", "tensor"),
        P("tensor", "store"),
        P(("groups", "store"), "tensor", None),
        P(("groups", "store"), "tensor", None),
        P("groups"),
        P("groups"),
        P("groups"),
        P("groups"),
    )
    out_specs = P(("groups", "tensor"), "store")
    return jax.shard_map(
        per_device, mesh=mesh, in_specs=in_specs, out_specs=out_specs, check_vma=False
    )
```

```python
import functools

import jax
import jax.numpy as jnp
from jax import lax
from jax.experimental import pallas as pl
from jax.experimental.pallas import tpu as pltpu
from jax.sharding import PartitionSpec as P

LINE = 4
LANES = 128
AHEAD = 5
PAIRS = 2
HEAVY = 10**10
MIB = 1024 * 1024


def line_order(n):
    order = []
    for z in range(n):
        sends = [(t, z >= n // 2, n - 1 - t + z) for t in range(z, n - 1)]
        sends += [(t, z < n // 2, t - (n - 1 - z)) for t in range(n - 1 - z, n - 1)]
        order.append([block for _, _, block in sorted(sends)] + [z])
    return order


def first_divisor(size, choices):
    for choice in choices:
        if size % choice == 0:
            return choice
    return size


def after(token, *done):
    return lax.optimization_barrier((token, done))[0]


def params(mebibytes):
    return pltpu.CompilerParams(vmem_limit_bytes=mebibytes * MIB)


def small_cost():
    return pl.CostEstimate(flops=10**6, bytes_accessed=10**5, transcendentals=0)


def block_at(order, slot, place):
    picked = jnp.int32(order[0][slot])
    for z in range(1, len(order)):
        picked = jnp.where(place == z, order[z][slot], picked)
    return picked


def spans(requests_ref, count):
    requests = requests_ref[...]
    return [jnp.int32(0)] + [jnp.sum((requests <= r).astype(jnp.int32)) for r in range(count)]


class Meta:
    def __init__(self, ref, requests):
        self.ref, self.requests = ref, requests
        self.adapters = (ref.shape[0] - 2 - requests) // 2
        self.place, self.shard = ref[0], ref[1]

    def adapter(self, r):
        return self.ref[2 + r]

    def rank(self, r):
        return self.ref[2 + self.requests + self.adapter(r)]

    def local_slot(self, r, held):
        return self.ref[2 + self.requests + self.adapters + self.adapter(r)] - self.shard * held


def base_kernel(order, groups, inputs_for, half, held, request_count, handed_on, *refs):
    slots = [slot for group in groups for slot in group]
    count = len(slots)
    meta, refs = Meta(refs[0], request_count), refs[1:]
    if held:
        requests_ref, factor, refs = refs[0], refs[1], refs[2:]
    hidden, matrix, refs = refs[0], refs[1], refs[2:]
    under, refs = (refs[0], refs[1:]) if handed_on else (None, refs)
    outs, refs = refs[: len(groups)], refs[len(groups) :]
    (rows, right, sums, sems), refs = refs[:4], refs[4:]
    steps, _, tile = rows.shape
    columns = outs[0].shape[1]
    block = rows.shape[1] // count
    first_rows = [pl.multiple_of(block_at(order, slot, meta.place) * block, block) for slot in slots]

    def depth_of(k):
        return pl.ds(pl.multiple_of(k * tile, tile), tile)

    def copies(k):
        moves = [
            (hidden.at[pl.ds(first_rows[i], block), depth_of(k)], rows.at[k, pl.ds(i * block, block), :])
            for i in range(count)
        ]
        moves.append((matrix.at[depth_of(k), pl.ds(half * columns, columns)], right.at[k]))
        return [pltpu.make_async_copy(a, b, sems.at[k, i]) for i, (a, b) in enumerate(moves)]

    if held:
        factors, inputs, flags, factor_sems = refs
        width = factor.shape[2]

        def factor_copies(k, pair):
            return [
                pltpu.make_async_copy(
                    factor.at[2 * pair + i, depth_of(k), :],
                    factors.at[pair, k, :, pl.ds(i * width, width)],
                    factor_sems.at[k, 2 * pair + i],
                )
                for i in range(2)
            ]

    def start(k):
        for copy in copies(k):
            copy.start()

    def start_factors(k, pairs):
        for pair, used in enumerate(pairs):

            @pl.when(used)
            def _(pair=pair):
                for copy in factor_copies(k, pair):
                    copy.start()

    for k in range(min(AHEAD, steps)):
        start(k)
    used = []
    if held:
        bounds = spans(requests_ref, request_count)
        local = [meta.local_slot(r, held) for r in range(request_count)]
        top = slots.index(inputs_for[0])
        wide = len(inputs_for)
        for pair in range(held // 2):
            used_by = []
            for first in first_rows[top : top + wide]:
                wanted = jnp.bool_(False)
                for r, slot in enumerate(local):
                    here = jnp.maximum(bounds[r], first) < jnp.minimum(bounds[r + 1], first + block)
                    wanted = wanted | (here & (slot // 2 == pair) & (slot >= 0))
                flags[pair * wide + len(used_by)] = wanted.astype(jnp.int32)
                used_by.append(wanted)
            used.append(functools.reduce(jnp.logical_or, used_by))
        for k in range(min(AHEAD, steps)):
            start_factors(k, used)
    sums[...] = jnp.zeros_like(sums)

    def step(k, _):
        @pl.when(k + AHEAD < steps)
        def _():
            start(k + AHEAD)
            start_factors(k + AHEAD, used)

        for copy in copies(k):
            copy.wait()
        sums[...] += jnp.dot(rows[k], right[k], preferred_element_type=jnp.float32)
        return 0

    lax.fori_loop(0, steps, step, 0)

    if held:
        for pair, wanted in enumerate(used):

            @pl.when(wanted)
            def _(pair=pair):
                for k in range(steps):
                    for copy in factor_copies(k, pair):
                        copy.wait()

        def pair_block(j, _):
            pair, i = j // wide, j % wide

            @pl.when(flags[j] == 1)
            def _():
                own = pl.ds(pl.multiple_of((top + i) * block, block), block)
                total = jnp.dot(rows[0, own, :], factors[pair, 0], preferred_element_type=jnp.float32)
                for k in range(1, steps):
                    total += jnp.dot(rows[k, own, :], factors[pair, k], preferred_element_type=jnp.float32)
                inputs[pair, pl.ds(pl.multiple_of(i * block, block), block), :] = total

            return 0

        lax.fori_loop(0, held // 2 * wide, pair_block, 0)

    i = 0
    for out, group in zip(outs, groups):
        here = 0
        for slot in group:
            out[here : here + block, :] = sums[i * block : (i + 1) * block, :].astype(jnp.bfloat16)
            here += block
            if held and slot in inputs_for:
                own = pl.ds((i - top) * block, block)
                row = lax.broadcasted_iota(jnp.int32, (block, width), 0) + first_rows[i]
                column = lax.broadcasted_iota(jnp.int32, (block, width), 1)
                total = jnp.zeros((block, width), jnp.float32)
                for r, local_slot in enumerate(local):
                    last = jnp.where((local_slot >= 0) & (local_slot < held), bounds[r + 1], 0)
                    keep = (row >= bounds[r]) & (row < last) & (column < meta.rank(r))
                    local_slot = jnp.clip(local_slot, 0, held - 1)
                    lanes = pl.ds(pl.multiple_of(local_slot % 2 * width, width), width)
                    total = jnp.where(keep, inputs[local_slot // 2, own, lanes], total)
                total = total.astype(jnp.bfloat16)
                size = block * width // columns
                for j in range(columns // width):
                    lanes = slice(j * width, (j + 1) * width)
                    out[here : here + size, lanes] = total[j * size : (j + 1) * size, :]
                here += size
            i += 1
    if handed_on:
        outs[0][outs[0].shape[0] - under.shape[0] :, :] = under[...]


def base_terms(meta, requests, request_count, hidden, matrix, factor, groups, inputs_for, half, n, under=None):
    tokens, depth = hidden.shape
    block, columns = tokens // n, matrix.shape[1] // 2
    tile = first_divisor(depth, (1024, 512, 256, 128))
    steps = depth // tile
    count = sum(len(group) for group in groups)
    smem = pl.BlockSpec(memory_space=pltpu.SMEM)
    vmem = pl.BlockSpec(memory_space=pltpu.VMEM)
    hbm = pl.BlockSpec(memory_space=pltpu.HBM)
    held, extra = 0, 0
    operands, in_specs = [meta], [smem]
    scratch = [
        pltpu.VMEM((steps, count * block, tile), jnp.bfloat16),
        pltpu.VMEM((steps, tile, columns), jnp.bfloat16),
        pltpu.VMEM((count * block, columns), jnp.float32),
        pltpu.SemaphoreType.DMA((steps, count + 1)),
    ]
    if inputs_for:
        held, _, width = factor.shape
        extra = block * width // columns
        operands, in_specs = [meta, requests, factor], [smem, vmem, hbm]
        scratch += [
            pltpu.VMEM((held // 2, steps, tile, 2 * width), jnp.bfloat16),
            pltpu.VMEM((held // 2, len(inputs_for) * block, 2 * width), jnp.float32),
            pltpu.SMEM((held // 2 * len(inputs_for),), jnp.int32),
            pltpu.SemaphoreType.DMA((steps, held)),
        ]
    heights = [sum(block + (extra if slot in inputs_for else 0) for slot in group) for group in groups]
    operands, in_specs = operands + [hidden, matrix], in_specs + [hbm, hbm]
    if under is not None:
        heights[0] += under.shape[0]
        operands, in_specs = operands + [under], in_specs + [vmem]
    handed_on = under is not None
    return pl.pallas_call(
        lambda *refs: base_kernel(line_order(n), groups, inputs_for, half, held, request_count, handed_on, *refs),
        out_shape=[jax.ShapeDtypeStruct((height, columns), jnp.bfloat16) for height in heights],
        in_specs=in_specs,
        out_specs=[vmem] * len(groups),
        scratch_shapes=scratch,
        compiler_params=params(50 if half or count > 1 else 58),
        cost_estimate=small_cost(),
        name="base_terms",
    )(*operands)


def select_rows_kernel(request_count, meta_ref, factor, kept, sent):
    meta = Meta(meta_ref, request_count)
    held, rank_rows, _ = factor.shape
    width = factor.shape[2] // (2 * PAIRS)
    side = meta.shard % 2
    for r in range(request_count):
        slot = meta.local_slot(r, held)
        owned = (slot >= 0) & (slot < held)
        slot = jnp.clip(slot, 0, held - 1)
        for out, core in ((kept, side), (sent, 1 - side)):
            for i in range(PAIRS):
                for c in range(2):
                    first = (2 * i + core) * width + c * (width // 2)
                    rows = factor[slot, :, pl.ds(pl.multiple_of(first, LANES), width // 2)]
                    top = (c * request_count + r) * rank_rows
                    out[i, top : top + rank_rows, :] = jnp.where(owned, rows, jnp.zeros_like(rows))


def select_rows(meta, request_count, factor):
    _, rank_rows, model_width = factor.shape
    smem = pl.BlockSpec(memory_space=pltpu.SMEM)
    vmem = pl.BlockSpec(memory_space=pltpu.VMEM)
    shape = (PAIRS, 2 * request_count * rank_rows, model_width // (4 * PAIRS))
    out = jax.ShapeDtypeStruct(shape, factor.dtype)
    return pl.pallas_call(
        lambda *refs: select_rows_kernel(request_count, *refs),
        out_shape=[out, out],
        in_specs=[smem, vmem],
        out_specs=[vmem, vmem],
        compiler_params=params(16),
        cost_estimate=small_cost(),
        name="select_rows",
    )(meta, factor)


def expanded_inputs(meta, requests_ref, lora_ref):
    block, width = lora_ref.shape
    row = lax.broadcasted_iota(jnp.int32, (block, width), 0) + meta.place * block
    lora = lora_ref[...].astype(jnp.float32)
    bounds = spans(requests_ref, meta.requests)
    parts = []
    for r in range(meta.requests):
        scale = 0.25 * width / meta.rank(r).astype(jnp.float32)
        keep = (row >= bounds[r]) & (row < bounds[r + 1])
        parts.append(jnp.where(keep, lora * scale, 0.0).astype(jnp.bfloat16))
    return jnp.concatenate(parts, axis=1)


def finish_kernel(items, added, requests, rank_rows, n, *refs):
    meta_ref, requests_ref, lora_ref, refs = refs[0], refs[1], refs[2], refs[3:]
    arrays, out, rows = refs[:-2], refs[-2], refs[-1]
    meta = Meta(meta_ref, requests)
    rank = n * rank_rows
    half = out.shape[1] // 2
    for index, top, targets in items:
        for place, k in targets:

            @pl.when(meta.place == place)
            def _(piece=arrays[index], top=top, k=k):
                for r in range(requests):
                    first = r * rank + k * rank_rows
                    for c in range(2):
                        start = top + (c * requests + r) * rank_rows
                        rows[first : first + rank_rows, c * half : (c + 1) * half] = piece[start : start + rank_rows, :]

    expanded = expanded_inputs(meta, requests_ref, lora_ref)
    block = lora_ref.shape[0]
    for c in range(2):
        columns = slice(c * half, (c + 1) * half)
        total = jnp.dot(expanded, rows[:, columns], preferred_element_type=jnp.float32)
        for index, top, which in added:
            if which == c:
                total += arrays[index][top : top + block, :].astype(jnp.float32)
        out[:, columns] = total.astype(out.dtype)


def finish(meta, requests, lora, arrays, items, added, request_count, rank_rows, n):
    smem = pl.BlockSpec(memory_space=pltpu.SMEM)
    vmem = pl.BlockSpec(memory_space=pltpu.VMEM)
    width = 2 * arrays[0].shape[1]
    return pl.pallas_call(
        lambda *refs: finish_kernel(items, added, request_count, rank_rows, n, *refs),
        out_shape=jax.ShapeDtypeStruct((lora.shape[0], width), jnp.bfloat16),
        in_specs=[smem] + [vmem] * (2 + len(arrays)),
        out_specs=vmem,
        scratch_shapes=[pltpu.VMEM((request_count * n * rank_rows, width), jnp.bfloat16)],
        compiler_params=params(20),
        cost_estimate=small_cost(),
        name="finish",
    )(meta, requests, lora, *arrays)


def join_kernel(count, term_top, came_top, under_top, term, came, *refs):
    out = refs[-1]
    total = term[term_top : term_top + count, :].astype(jnp.float32)
    total += came[came_top : came_top + count, :].astype(jnp.float32)
    out[:count, :] = total.astype(out.dtype)
    if len(refs) > 1:
        under = refs[0]
        out[count:, :] = under[under_top : under_top + out.shape[0] - count, :]


def join(token, count, term, term_top, came, came_top, under=None, under_top=0, under_count=0, weight=10**6):
    arrays = [term, came] + ([] if under is None else [under])
    arrays = lax.optimization_barrier((arrays, token))[0]
    vmem = pl.BlockSpec(memory_space=pltpu.VMEM)
    return pl.pallas_call(
        lambda *refs: join_kernel(count, term_top, came_top, under_top, *refs),
        out_shape=jax.ShapeDtypeStruct((count + under_count, term.shape[1]), term.dtype),
        in_specs=[vmem] * len(arrays),
        out_specs=vmem,
        compiler_params=params(12),
        cost_estimate=pl.CostEstimate(flops=weight, bytes_accessed=10**5, transcendentals=0),
        name="join",
    )(*arrays)


def add_last_kernel(total, *refs):
    arrivals, out = refs[:-1], refs[-1]
    half = arrivals[0].shape[1]
    out[:, :half] = total[:, :half]
    last = total[:, half:].astype(jnp.float32)
    for arrival in arrivals:
        last += arrival[...].astype(jnp.float32)
    out[:, half:] = last.astype(out.dtype)


def add_last(total, *arrivals):
    vmem = pl.BlockSpec(memory_space=pltpu.VMEM)
    return pl.pallas_call(
        add_last_kernel,
        out_shape=jax.ShapeDtypeStruct(total.shape, total.dtype),
        in_specs=[vmem] * (1 + len(arrivals)),
        out_specs=vmem,
        compiler_params=params(12),
        cost_estimate=small_cost(),
        name="add_last",
    )(total, *arrivals)


def under_each_other_kernel(upper, lower, out):
    out[: upper.shape[0], :] = upper[...]
    out[upper.shape[0] :, :] = lower[...]


def under_each_other(upper, lower):
    vmem = pl.BlockSpec(memory_space=pltpu.VMEM)
    return pl.pallas_call(
        under_each_other_kernel,
        out_shape=jax.ShapeDtypeStruct((upper.shape[0] + lower.shape[0], upper.shape[1]), upper.dtype),
        in_specs=[vmem] * 2,
        out_specs=vmem,
        compiler_params=params(12),
        cost_estimate=small_cost(),
        name="under_each_other",
    )(upper, lower)


def swap(x, axis, bit):
    return lax.ppermute(x, axis, [(i, i ^ bit) for i in range(lax.axis_size(axis))])


def bits_of(size):
    return [1 << i for i in range(size.bit_length() - 1)]


def along_edge(x, edge):
    n = lax.axis_size("tensor")
    return lax.ppermute(x, "tensor", [(edge, edge + 1), (n - 1 - edge, n - 2 - edge)])


def on_line(hidden, matrix, input_factor, output_factor, requests, token, request_count, n):
    shard = lax.axis_index("store")
    block = hidden.shape[0] // n
    width = input_factor.shape[2]
    rank_rows = output_factor.shape[1]
    piece = block + block * width // (matrix.shape[1] // 2)
    bundle = 2 * request_count * rank_rows

    def base(token, groups, inputs_for, half, under=None):
        return base_terms(
            token, requests, request_count, hidden, matrix, input_factor, groups, inputs_for, half, n, under
        )

    def send(x, edge, token):
        return along_edge(after(x, token), edge)

    (s00,) = base(token, [[0]], [0], 0)
    token = after(token, s00)
    e0_1 = along_edge(s00, 0)
    kept, sent = select_rows(token, request_count, output_factor)
    token = after(token, kept, sent)
    swapped = swap(sent, "store", 1)
    token = after(token, swapped)
    side = shard // 2 % 2
    kept, swapped, _ = lax.optimization_barrier((kept, swapped, token))
    outgoing = kept[1 - side] + swapped[1 - side]
    rows = kept[side] + swapped[side]
    token = after(token, outgoing, rows)
    across = swap(outgoing, "store", 2)
    s01, s11 = base(token, [[0], [1]], [], 1)

    token = after(token, s01)
    e0_2 = send(s01, 0, token)
    token, e0_1 = lax.optimization_barrier((token, e0_1))
    b10 = join(token, piece, s00, 0, e0_1, 0)
    token = after(token, b10)
    e1_2 = along_edge(b10, 1)
    token, across = lax.optimization_barrier((token, across))
    rows = rows + across
    token = after(token, rows)
    near = lax.ppermute(rows, "tensor", [(0, 1), (n - 1, n - 2), (1, 0), (n - 2, n - 1)])
    far = along_edge(rows, 1)
    s10_s11, s20, s30 = base(token, [[1], [2], [3]], [1, 2], 0, s11)

    token = after(token, s10_s11)
    e0_3 = send(s10_s11, 0, token)
    token, e0_2 = lax.optimization_barrier((token, e0_2))
    b11 = join(token, block, s01, 0, e0_2, 0, weight=HEAVY)
    token, near = lax.optimization_barrier((after(token, b11), near))
    e1_3 = along_edge(under_each_other(b11, near), 1)
    token, e1_2, far = lax.optimization_barrier((token, e1_2, far))
    c20 = join(token, piece, s20, 0, e1_2, 0, far, 0, bundle)
    token = after(token, c20)
    e2_3 = along_edge(c20, 2)
    s21, s31 = base(token, [[2], [3]], [3], 1)

    token = after(token, s21)
    e0_4 = send(s20, 0, token)
    token, e0_3 = lax.optimization_barrier((token, e0_3))
    b20 = join(token, piece, s10_s11, 0, e0_3, 0)
    token = after(token, b20)
    e1_4 = along_edge(b20, 1)
    token, e1_3 = lax.optimization_barrier((token, e1_3))
    last_rows = send(e1_3[block:], 2, token)
    c21 = join(token, block, s21, 0, e1_3, 0, weight=HEAVY // 5)
    token = after(token, c21)
    e2_4 = along_edge(c21, 2)
    token, e2_3 = lax.optimization_barrier((token, e2_3))
    e0_5 = send(s21, 0, token)
    b21 = join(token, block, s10_s11, piece, e0_3, piece)
    token = after(token, b21)
    e1_5 = along_edge(b21, 1)

    token, e0_4 = lax.optimization_barrier((token, e0_4))
    token, e1_4 = lax.optimization_barrier((token, e1_4))
    token, last_rows = lax.optimization_barrier((token, last_rows))
    e1_4 = after(e1_4, token)
    lora = s31[block:].astype(jnp.float32) + e0_4[block:].astype(jnp.float32)
    lora += e1_4[block:].astype(jnp.float32) + e2_3[block:piece].astype(jnp.float32)
    lora = lora.astype(jnp.bfloat16).reshape(piece - block, -1, width).swapaxes(0, 1).reshape(block, width)
    lora = lora + swap(lora, "store", 1)
    lora = lora + swap(lora, "store", 2)
    arrays = [s30, s31, rows, near, far, e1_3, e2_3, last_rows, e0_4, e1_4]
    items = [
        (2, 0, [(z, z) for z in range(n)]),
        (3, 0, [(0, 1), (1, 0), (2, 3), (3, 2)]),
        (4, 0, [(1, 2), (2, 1)]),
        (5, block, [(1, 3), (2, 0)]),
        (6, piece, [(0, 2), (3, 1)]),
        (7, 0, [(0, 3), (3, 0)]),
    ]
    added = [(0, 0, 0), (8, 0, 0), (9, 0, 0), (6, 0, 0), (1, 0, 1)]
    out = finish(token, requests, lora, arrays, items, added, request_count, rank_rows, n)
    return add_last(out, e0_5, e1_5, e2_4)


def anywhere(hidden, matrix, input_factor, output_factor, token_requests, meta):
    request_adapters, ranks, slots = meta
    held = input_factor.shape[0]
    width = input_factor.shape[2]
    rank, slot = ranks[request_adapters], slots[request_adapters]
    owned = slot // held == lax.axis_index("store")
    chosen = token_requests[:, None] == jnp.arange(request_adapters.shape[0])[None, :]
    lora = jnp.zeros((hidden.shape[0], width), jnp.float32)
    for r in range(request_adapters.shape[0]):
        product = jnp.dot(hidden, input_factor[slot[r] % held], preferred_element_type=jnp.float32)
        keep = (chosen[:, r] & owned[r])[:, None] & (jnp.arange(width) < rank[r])[None, :]
        lora = jnp.where(keep, product, lora)
    lora = lax.psum_scatter(lora.astype(jnp.bfloat16), "tensor", scatter_dimension=1, tiled=True)
    lora = lax.psum(lora, "store").astype(jnp.float32)
    rows = jnp.where(owned[:, None, None], output_factor[slot % held], jnp.zeros((), output_factor.dtype))
    rows = lax.psum_scatter(rows, "store", scatter_dimension=2, tiled=True)
    weights = jnp.where(chosen, 0.25 * width / rank.astype(jnp.float32)[None, :], 0.0)
    expanded = (weights[:, :, None] * lora[:, None, :]).reshape(hidden.shape[0], -1).astype(jnp.bfloat16)
    term = jnp.dot(hidden, matrix, preferred_element_type=jnp.float32)
    term += jnp.dot(expanded, rows.reshape(-1, rows.shape[2]), preferred_element_type=jnp.float32)
    return lax.psum_scatter(term.astype(jnp.bfloat16), "tensor", scatter_dimension=0, tiled=True)


def per_device(
    hidden_activations,
    down_matrix,
    adapter_input_factor,
    adapter_output_factor,
    token_requests,
    request_adapters,
    adapter_ranks,
    adapter_store_slot,
):
    n = lax.axis_size("tensor")
    meta = (request_adapters, adapter_ranks, adapter_store_slot)
    arrays = (hidden_activations, down_matrix, adapter_input_factor, adapter_output_factor)
    if n == LINE and lax.axis_size("store") == 2 * PAIRS and adapter_input_factor.shape[0] % 2 == 0:
        place = jnp.stack([lax.axis_index("tensor"), lax.axis_index("store")]).astype(jnp.int32)
        token = jnp.concatenate([place, *meta])
        return on_line(*arrays, token_requests.reshape(-1, LANES), token, request_adapters.shape[0], n)
    return anywhere(*arrays, token_requests, meta)


def solution(mesh):
    in_specs = (
        P("groups", "tensor"),
        P("tensor", "store"),
        P(("groups", "store"), "tensor", None),
        P(("groups", "store"), "tensor", None),
        P("groups"),
        P("groups"),
        P("groups"),
        P("groups"),
    )
    out_specs = P(("groups", "tensor"), "store")
    return jax.shard_map(
        per_device, mesh=mesh, in_specs=in_specs, out_specs=out_specs, check_vma=False
    )
```

```python
import functools

import jax
import jax.numpy as jnp
from jax import lax
from jax.experimental import pallas as pl
from jax.experimental.pallas import tpu as pltpu
from jax.sharding import PartitionSpec as P

LINE = 4
LANES = 128
AHEAD = 3
PAIRS = 2
HEAVY = 10**10
MIB = 1024 * 1024


def line_order(n):
    order = []
    for z in range(n):
        sends = [(t, z >= n // 2, n - 1 - t + z) for t in range(z, n - 1)]
        sends += [(t, z < n // 2, t - (n - 1 - z)) for t in range(n - 1 - z, n - 1)]
        order.append([block for _, _, block in sorted(sends)] + [z])
    return order


def first_divisor(size, choices):
    for choice in choices:
        if size % choice == 0:
            return choice
    return size


def after(token, *done):
    return lax.optimization_barrier((token, done))[0]


def params(mebibytes):
    return pltpu.CompilerParams(vmem_limit_bytes=mebibytes * MIB)


def small_cost():
    return pl.CostEstimate(flops=10**6, bytes_accessed=10**5, transcendentals=0)


def block_at(order, slot, place):
    picked = jnp.int32(order[0][slot])
    for z in range(1, len(order)):
        picked = jnp.where(place == z, order[z][slot], picked)
    return picked


def spans(requests_ref, count):
    requests = requests_ref[...]
    return [jnp.int32(0)] + [jnp.sum((requests <= r).astype(jnp.int32)) for r in range(count)]


class Meta:
    def __init__(self, ref, requests):
        self.ref, self.requests = ref, requests
        self.adapters = (ref.shape[0] - 2 - requests) // 2
        self.place, self.shard = ref[0], ref[1]

    def adapter(self, r):
        return self.ref[2 + r]

    def rank(self, r):
        return self.ref[2 + self.requests + self.adapter(r)]

    def local_slot(self, r, held):
        return self.ref[2 + self.requests + self.adapters + self.adapter(r)] - self.shard * held


def base_kernel(order, groups, inputs_for, half, held, request_count, handed_on, *refs):
    slots = [slot for group in groups for slot in group]
    count = len(slots)
    meta, refs = Meta(refs[0], request_count), refs[1:]
    if held:
        requests_ref, factor, refs = refs[0], refs[1], refs[2:]
    hidden, matrix, refs = refs[0], refs[1], refs[2:]
    under, refs = (refs[0], refs[1:]) if handed_on else (None, refs)
    outs, refs = refs[: len(groups)], refs[len(groups) :]
    (rows, right, sums, sems), refs = refs[:4], refs[4:]
    steps, _, tile = rows.shape
    columns = outs[0].shape[1]
    block = rows.shape[1] // count
    first_rows = [pl.multiple_of(block_at(order, slot, meta.place) * block, block) for slot in slots]

    def depth_of(k):
        return pl.ds(pl.multiple_of(k * tile, tile), tile)

    def copies(k):
        moves = [
            (hidden.at[pl.ds(first_rows[i], block), depth_of(k)], rows.at[k, pl.ds(i * block, block), :])
            for i in range(count)
        ]
        moves.append((matrix.at[depth_of(k), pl.ds(half * columns, columns)], right.at[k]))
        return [pltpu.make_async_copy(a, b, sems.at[k, i]) for i, (a, b) in enumerate(moves)]

    if held:
        factors, inputs, flags, factor_sems = refs
        width = factor.shape[2]

        def factor_copies(k, pair):
            return [
                pltpu.make_async_copy(
                    factor.at[2 * pair + i, depth_of(k), :],
                    factors.at[pair, k, :, pl.ds(i * width, width)],
                    factor_sems.at[k, 2 * pair + i],
                )
                for i in range(2)
            ]

    def start(k):
        for copy in copies(k):
            copy.start()

    def start_factors(k, pairs):
        for pair, used in enumerate(pairs):

            @pl.when(used)
            def _(pair=pair):
                for copy in factor_copies(k, pair):
                    copy.start()

    for k in range(min(AHEAD, steps)):
        start(k)
    used = []
    if held:
        bounds = spans(requests_ref, request_count)
        local = [meta.local_slot(r, held) for r in range(request_count)]
        top = slots.index(inputs_for[0])
        wide = len(inputs_for)
        for pair in range(held // 2):
            used_by = []
            for first in first_rows[top : top + wide]:
                wanted = jnp.bool_(False)
                for r, slot in enumerate(local):
                    here = jnp.maximum(bounds[r], first) < jnp.minimum(bounds[r + 1], first + block)
                    wanted = wanted | (here & (slot // 2 == pair) & (slot >= 0))
                flags[pair * wide + len(used_by)] = wanted.astype(jnp.int32)
                used_by.append(wanted)
            used.append(functools.reduce(jnp.logical_or, used_by))
        for k in range(min(AHEAD, steps)):
            start_factors(k, used)
    sums[...] = jnp.zeros_like(sums)

    def step(k, _):
        @pl.when(k + AHEAD < steps)
        def _():
            start(k + AHEAD)
            start_factors(k + AHEAD, used)

        for copy in copies(k):
            copy.wait()
        sums[...] += jnp.dot(rows[k], right[k], preferred_element_type=jnp.float32)
        return 0

    lax.fori_loop(0, steps, step, 0)

    if held:
        for pair, wanted in enumerate(used):

            @pl.when(wanted)
            def _(pair=pair):
                for k in range(steps):
                    for copy in factor_copies(k, pair):
                        copy.wait()

        def pair_block(j, _):
            pair, i = j // wide, j % wide

            @pl.when(flags[j] == 1)
            def _():
                own = pl.ds(pl.multiple_of((top + i) * block, block), block)
                total = jnp.dot(rows[0, own, :], factors[pair, 0], preferred_element_type=jnp.float32)
                for k in range(1, steps):
                    total += jnp.dot(rows[k, own, :], factors[pair, k], preferred_element_type=jnp.float32)
                inputs[pair, pl.ds(pl.multiple_of(i * block, block), block), :] = total

            return 0

        lax.fori_loop(0, held // 2 * wide, pair_block, 0)

    i = 0
    for out, group in zip(outs, groups):
        here = 0
        for slot in group:
            out[here : here + block, :] = sums[i * block : (i + 1) * block, :].astype(jnp.bfloat16)
            here += block
            if held and slot in inputs_for:
                own = pl.ds((i - top) * block, block)
                row = lax.broadcasted_iota(jnp.int32, (block, width), 0) + first_rows[i]
                column = lax.broadcasted_iota(jnp.int32, (block, width), 1)
                total = jnp.zeros((block, width), jnp.float32)
                for r, local_slot in enumerate(local):
                    last = jnp.where((local_slot >= 0) & (local_slot < held), bounds[r + 1], 0)
                    keep = (row >= bounds[r]) & (row < last) & (column < meta.rank(r))
                    local_slot = jnp.clip(local_slot, 0, held - 1)
                    lanes = pl.ds(pl.multiple_of(local_slot % 2 * width, width), width)
                    total = jnp.where(keep, inputs[local_slot // 2, own, lanes], total)
                total = total.astype(jnp.bfloat16)
                size = block * width // columns
                for j in range(columns // width):
                    lanes = slice(j * width, (j + 1) * width)
                    out[here : here + size, lanes] = total[j * size : (j + 1) * size, :]
                here += size
            i += 1
    if handed_on:
        outs[0][outs[0].shape[0] - under.shape[0] :, :] = under[...]


def base_terms(meta, requests, request_count, hidden, matrix, factor, groups, inputs_for, half, n, under=None):
    tokens, depth = hidden.shape
    block, columns = tokens // n, matrix.shape[1] // 2
    tile = first_divisor(depth, (1024, 512, 256, 128))
    steps = depth // tile
    count = sum(len(group) for group in groups)
    smem = pl.BlockSpec(memory_space=pltpu.SMEM)
    vmem = pl.BlockSpec(memory_space=pltpu.VMEM)
    hbm = pl.BlockSpec(memory_space=pltpu.HBM)
    held, extra = 0, 0
    operands, in_specs = [meta], [smem]
    scratch = [
        pltpu.VMEM((steps, count * block, tile), jnp.bfloat16),
        pltpu.VMEM((steps, tile, columns), jnp.bfloat16),
        pltpu.VMEM((count * block, columns), jnp.float32),
        pltpu.SemaphoreType.DMA((steps, count + 1)),
    ]
    if inputs_for:
        held, _, width = factor.shape
        extra = block * width // columns
        operands, in_specs = [meta, requests, factor], [smem, vmem, hbm]
        scratch += [
            pltpu.VMEM((held // 2, steps, tile, 2 * width), jnp.bfloat16),
            pltpu.VMEM((held // 2, len(inputs_for) * block, 2 * width), jnp.float32),
            pltpu.SMEM((held // 2 * len(inputs_for),), jnp.int32),
            pltpu.SemaphoreType.DMA((steps, held)),
        ]
    heights = [sum(block + (extra if slot in inputs_for else 0) for slot in group) for group in groups]
    operands, in_specs = operands + [hidden, matrix], in_specs + [hbm, hbm]
    if under is not None:
        heights[0] += under.shape[0]
        operands, in_specs = operands + [under], in_specs + [vmem]
    handed_on = under is not None
    return pl.pallas_call(
        lambda *refs: base_kernel(line_order(n), groups, inputs_for, half, held, request_count, handed_on, *refs),
        out_shape=[jax.ShapeDtypeStruct((height, columns), jnp.bfloat16) for height in heights],
        in_specs=in_specs,
        out_specs=[vmem] * len(groups),
        scratch_shapes=scratch,
        compiler_params=params(50 if half or count > 1 else 58),
        cost_estimate=small_cost(),
        name="base_terms",
    )(*operands)


def select_rows_kernel(request_count, meta_ref, factor, kept, sent):
    meta = Meta(meta_ref, request_count)
    held, rank_rows, _ = factor.shape
    width = factor.shape[2] // (2 * PAIRS)
    side = meta.shard % 2
    for r in range(request_count):
        slot = meta.local_slot(r, held)
        owned = (slot >= 0) & (slot < held)
        slot = jnp.clip(slot, 0, held - 1)
        for out, core in ((kept, side), (sent, 1 - side)):
            for i in range(PAIRS):
                for c in range(2):
                    first = (2 * i + core) * width + c * (width // 2)
                    rows = factor[slot, :, pl.ds(pl.multiple_of(first, LANES), width // 2)]
                    top = (c * request_count + r) * rank_rows
                    out[i, top : top + rank_rows, :] = jnp.where(owned, rows, jnp.zeros_like(rows))


def select_rows(meta, request_count, factor):
    _, rank_rows, model_width = factor.shape
    smem = pl.BlockSpec(memory_space=pltpu.SMEM)
    vmem = pl.BlockSpec(memory_space=pltpu.VMEM)
    shape = (PAIRS, 2 * request_count * rank_rows, model_width // (4 * PAIRS))
    out = jax.ShapeDtypeStruct(shape, factor.dtype)
    return pl.pallas_call(
        lambda *refs: select_rows_kernel(request_count, *refs),
        out_shape=[out, out],
        in_specs=[smem, vmem],
        out_specs=[vmem, vmem],
        compiler_params=params(16),
        cost_estimate=small_cost(),
        name="select_rows",
    )(meta, factor)


def expanded_inputs(meta, requests_ref, lora_ref):
    block, width = lora_ref.shape
    row = lax.broadcasted_iota(jnp.int32, (block, width), 0) + meta.place * block
    lora = lora_ref[...].astype(jnp.float32)
    bounds = spans(requests_ref, meta.requests)
    parts = []
    for r in range(meta.requests):
        scale = 0.25 * width / meta.rank(r).astype(jnp.float32)
        keep = (row >= bounds[r]) & (row < bounds[r + 1])
        parts.append(jnp.where(keep, lora * scale, 0.0).astype(jnp.bfloat16))
    return jnp.concatenate(parts, axis=1)


def finish_kernel(items, added, requests, rank_rows, n, *refs):
    meta_ref, requests_ref, lora_ref, refs = refs[0], refs[1], refs[2], refs[3:]
    arrays, out, rows = refs[:-2], refs[-2], refs[-1]
    meta = Meta(meta_ref, requests)
    rank = n * rank_rows
    half = out.shape[1] // 2
    for index, top, targets in items:
        for place, k in targets:

            @pl.when(meta.place == place)
            def _(piece=arrays[index], top=top, k=k):
                for r in range(requests):
                    first = r * rank + k * rank_rows
                    for c in range(2):
                        start = top + (c * requests + r) * rank_rows
                        rows[first : first + rank_rows, c * half : (c + 1) * half] = piece[start : start + rank_rows, :]

    expanded = expanded_inputs(meta, requests_ref, lora_ref)
    block = lora_ref.shape[0]
    for c in range(2):
        columns = slice(c * half, (c + 1) * half)
        total = jnp.dot(expanded, rows[:, columns], preferred_element_type=jnp.float32)
        for index, top, which in added:
            if which == c:
                total += arrays[index][top : top + block, :].astype(jnp.float32)
        out[:, columns] = total.astype(out.dtype)


def finish(meta, requests, lora, arrays, items, added, request_count, rank_rows, n):
    smem = pl.BlockSpec(memory_space=pltpu.SMEM)
    vmem = pl.BlockSpec(memory_space=pltpu.VMEM)
    width = 2 * arrays[0].shape[1]
    return pl.pallas_call(
        lambda *refs: finish_kernel(items, added, request_count, rank_rows, n, *refs),
        out_shape=jax.ShapeDtypeStruct((lora.shape[0], width), jnp.bfloat16),
        in_specs=[smem] + [vmem] * (2 + len(arrays)),
        out_specs=vmem,
        scratch_shapes=[pltpu.VMEM((request_count * n * rank_rows, width), jnp.bfloat16)],
        compiler_params=params(20),
        cost_estimate=small_cost(),
        name="finish",
    )(meta, requests, lora, *arrays)


def join_kernel(count, term_top, came_top, under_top, term, came, *refs):
    out = refs[-1]
    total = term[term_top : term_top + count, :].astype(jnp.float32)
    total += came[came_top : came_top + count, :].astype(jnp.float32)
    out[:count, :] = total.astype(out.dtype)
    if len(refs) > 1:
        under = refs[0]
        out[count:, :] = under[under_top : under_top + out.shape[0] - count, :]


def join(token, count, term, term_top, came, came_top, under=None, under_top=0, under_count=0, weight=10**6):
    arrays = [term, came] + ([] if under is None else [under])
    arrays = lax.optimization_barrier((arrays, token))[0]
    vmem = pl.BlockSpec(memory_space=pltpu.VMEM)
    return pl.pallas_call(
        lambda *refs: join_kernel(count, term_top, came_top, under_top, *refs),
        out_shape=jax.ShapeDtypeStruct((count + under_count, term.shape[1]), term.dtype),
        in_specs=[vmem] * len(arrays),
        out_specs=vmem,
        compiler_params=params(12),
        cost_estimate=pl.CostEstimate(flops=weight, bytes_accessed=10**5, transcendentals=0),
        name="join",
    )(*arrays)


def under_each_other_kernel(upper, lower, out):
    out[: upper.shape[0], :] = upper[...]
    out[upper.shape[0] :, :] = lower[...]


def under_each_other(upper, lower):
    vmem = pl.BlockSpec(memory_space=pltpu.VMEM)
    return pl.pallas_call(
        under_each_other_kernel,
        out_shape=jax.ShapeDtypeStruct((upper.shape[0] + lower.shape[0], upper.shape[1]), upper.dtype),
        in_specs=[vmem] * 2,
        out_specs=vmem,
        compiler_params=params(12),
        cost_estimate=small_cost(),
        name="under_each_other",
    )(upper, lower)


def swap(x, axis, bit):
    return lax.ppermute(x, axis, [(i, i ^ bit) for i in range(lax.axis_size(axis))])


def bits_of(size):
    return [1 << i for i in range(size.bit_length() - 1)]


def along_edge(x, edge):
    n = lax.axis_size("tensor")
    return lax.ppermute(x, "tensor", [(edge, edge + 1), (n - 1 - edge, n - 2 - edge)])


def on_line(hidden, matrix, input_factor, output_factor, requests, token, request_count, n):
    shard = lax.axis_index("store")
    block = hidden.shape[0] // n
    width = input_factor.shape[2]
    rank_rows = output_factor.shape[1]
    piece = block + block * width // (matrix.shape[1] // 2)
    bundle = 2 * request_count * rank_rows

    def base(token, groups, inputs_for, half, under=None):
        return base_terms(
            token, requests, request_count, hidden, matrix, input_factor, groups, inputs_for, half, n, under
        )

    def send(x, edge, token):
        return along_edge(after(x, token), edge)

    (s00,) = base(token, [[0]], [0], 0)
    token = after(token, s00)
    e0_1 = along_edge(s00, 0)
    kept, sent = select_rows(token, request_count, output_factor)
    token = after(token, kept, sent)
    swapped = swap(sent, "store", 1)
    token = after(token, swapped)
    side = shard // 2 % 2
    kept, swapped, _ = lax.optimization_barrier((kept, swapped, token))
    outgoing = kept[1 - side] + swapped[1 - side]
    rows = kept[side] + swapped[side]
    token = after(token, outgoing, rows)
    across = swap(outgoing, "store", 2)
    s01, s11 = base(token, [[0], [1]], [], 1)

    token = after(token, s01)
    e0_2 = send(s01, 0, token)
    token, e0_1 = lax.optimization_barrier((token, e0_1))
    b10 = join(token, piece, s00, 0, e0_1, 0)
    token = after(token, b10)
    e1_2 = along_edge(b10, 1)
    token, across = lax.optimization_barrier((token, across))
    rows = rows + across
    token = after(token, rows)
    near = lax.ppermute(rows, "tensor", [(0, 1), (n - 1, n - 2), (1, 0), (n - 2, n - 1)])
    far = along_edge(rows, 1)
    s10_s11, s20, s30 = base(token, [[1], [2], [3]], [1, 2], 0, s11)

    token = after(token, s10_s11)
    e0_3 = send(s10_s11, 0, token)
    token, e0_2 = lax.optimization_barrier((token, e0_2))
    b11 = join(token, block, s01, 0, e0_2, 0, weight=HEAVY)
    token, near = lax.optimization_barrier((after(token, b11), near))
    e1_3 = along_edge(under_each_other(b11, near), 1)
    token, e1_2, far = lax.optimization_barrier((token, e1_2, far))
    c20 = join(token, piece, s20, 0, e1_2, 0, far, 0, bundle)
    token = after(token, c20)
    e2_3 = along_edge(c20, 2)
    s21, s31 = base(token, [[2], [3]], [3], 1)

    token = after(token, s21)
    e0_4 = send(s20, 0, token)
    token, e0_3 = lax.optimization_barrier((token, e0_3))
    b20 = join(token, piece, s10_s11, 0, e0_3, 0)
    token = after(token, b20)
    e1_4 = along_edge(b20, 1)
    token, e1_3 = lax.optimization_barrier((token, e1_3))
    last_rows = send(e1_3[block:], 2, token)
    c21 = join(token, block, s21, 0, e1_3, 0, weight=HEAVY // 5)
    token = after(token, c21)
    e2_4 = along_edge(c21, 2)
    token, e2_3 = lax.optimization_barrier((token, e2_3))
    e0_5 = send(s21, 0, token)
    b21 = join(token, block, s10_s11, piece, e0_3, piece)
    token = after(token, b21)
    e1_5 = along_edge(b21, 1)

    token, e0_4 = lax.optimization_barrier((token, e0_4))
    token, e1_4 = lax.optimization_barrier((token, e1_4))
    token, last_rows = lax.optimization_barrier((token, last_rows))
    e1_4 = after(e1_4, token)
    lora = s31[block:].astype(jnp.float32) + e0_4[block:].astype(jnp.float32)
    lora += e1_4[block:].astype(jnp.float32) + e2_3[block:piece].astype(jnp.float32)
    lora = lora.astype(jnp.bfloat16).reshape(piece - block, -1, width).swapaxes(0, 1).reshape(block, width)
    lora = lora + swap(lora, "store", 1)
    lora = lora + swap(lora, "store", 2)
    arrays = [s30, s31, rows, near, far, e1_3, e2_3, last_rows, e0_4, e1_4]
    items = [
        (2, 0, [(z, z) for z in range(n)]),
        (3, 0, [(0, 1), (1, 0), (2, 3), (3, 2)]),
        (4, 0, [(1, 2), (2, 1)]),
        (5, block, [(1, 3), (2, 0)]),
        (6, piece, [(0, 2), (3, 1)]),
        (7, 0, [(0, 3), (3, 0)]),
    ]
    arrays += [e0_5, e1_5, e2_4]
    added = [(0, 0, 0), (8, 0, 0), (9, 0, 0), (6, 0, 0), (1, 0, 1), (10, 0, 1), (11, 0, 1), (12, 0, 1)]
    return finish(token, requests, lora, arrays, items, added, request_count, rank_rows, n)


def anywhere(hidden, matrix, input_factor, output_factor, token_requests, meta):
    request_adapters, ranks, slots = meta
    held = input_factor.shape[0]
    width = input_factor.shape[2]
    rank, slot = ranks[request_adapters], slots[request_adapters]
    owned = slot // held == lax.axis_index("store")
    chosen = token_requests[:, None] == jnp.arange(request_adapters.shape[0])[None, :]
    lora = jnp.zeros((hidden.shape[0], width), jnp.float32)
    for r in range(request_adapters.shape[0]):
        product = jnp.dot(hidden, input_factor[slot[r] % held], preferred_element_type=jnp.float32)
        keep = (chosen[:, r] & owned[r])[:, None] & (jnp.arange(width) < rank[r])[None, :]
        lora = jnp.where(keep, product, lora)
    lora = lax.psum_scatter(lora.astype(jnp.bfloat16), "tensor", scatter_dimension=1, tiled=True)
    lora = lax.psum(lora, "store").astype(jnp.float32)
    rows = jnp.where(owned[:, None, None], output_factor[slot % held], jnp.zeros((), output_factor.dtype))
    rows = lax.psum_scatter(rows, "store", scatter_dimension=2, tiled=True)
    weights = jnp.where(chosen, 0.25 * width / rank.astype(jnp.float32)[None, :], 0.0)
    expanded = (weights[:, :, None] * lora[:, None, :]).reshape(hidden.shape[0], -1).astype(jnp.bfloat16)
    term = jnp.dot(hidden, matrix, preferred_element_type=jnp.float32)
    term += jnp.dot(expanded, rows.reshape(-1, rows.shape[2]), preferred_element_type=jnp.float32)
    return lax.psum_scatter(term.astype(jnp.bfloat16), "tensor", scatter_dimension=0, tiled=True)


def per_device(
    hidden_activations,
    down_matrix,
    adapter_input_factor,
    adapter_output_factor,
    token_requests,
    request_adapters,
    adapter_ranks,
    adapter_store_slot,
):
    n = lax.axis_size("tensor")
    meta = (request_adapters, adapter_ranks, adapter_store_slot)
    arrays = (hidden_activations, down_matrix, adapter_input_factor, adapter_output_factor)
    if n == LINE and lax.axis_size("store") == 2 * PAIRS and adapter_input_factor.shape[0] % 2 == 0:
        place = jnp.stack([lax.axis_index("tensor"), lax.axis_index("store")]).astype(jnp.int32)
        token = jnp.concatenate([place, *meta])
        return on_line(*arrays, token_requests.reshape(-1, LANES), token, request_adapters.shape[0], n)
    return anywhere(*arrays, token_requests, meta)


def solution(mesh):
    in_specs = (
        P("groups", "tensor"),
        P("tensor", "store"),
        P(("groups", "store"), "tensor", None),
        P(("groups", "store"), "tensor", None),
        P("groups"),
        P("groups"),
        P("groups"),
        P("groups"),
    )
    out_specs = P(("groups", "tensor"), "store")
    return jax.shard_map(
        per_device, mesh=mesh, in_specs=in_specs, out_specs=out_specs, check_vma=False
    )
```

```python
import functools

import jax
import jax.numpy as jnp
from jax import lax
from jax.experimental import pallas as pl
from jax.experimental.pallas import tpu as pltpu
from jax.sharding import PartitionSpec as P

LINE = 4
LANES = 128
AHEAD = 3
PAIRS = 2
HEAVY = 10**10
MIB = 1024 * 1024


def line_order(n):
    order = []
    for z in range(n):
        sends = [(t, z >= n // 2, n - 1 - t + z) for t in range(z, n - 1)]
        sends += [(t, z < n // 2, t - (n - 1 - z)) for t in range(n - 1 - z, n - 1)]
        order.append([block for _, _, block in sorted(sends)] + [z])
    return order


def first_divisor(size, choices):
    for choice in choices:
        if size % choice == 0:
            return choice
    return size


def after(token, *done):
    return lax.optimization_barrier((token, done))[0]


def params(mebibytes):
    return pltpu.CompilerParams(vmem_limit_bytes=mebibytes * MIB)


def small_cost():
    return pl.CostEstimate(flops=10**6, bytes_accessed=10**5, transcendentals=0)


def block_at(order, slot, place):
    picked = jnp.int32(order[0][slot])
    for z in range(1, len(order)):
        picked = jnp.where(place == z, order[z][slot], picked)
    return picked


def spans(requests_ref, count):
    requests = requests_ref[...]
    return [jnp.int32(0)] + [jnp.sum((requests <= r).astype(jnp.int32)) for r in range(count)]


class Meta:
    def __init__(self, ref, requests):
        self.ref, self.requests = ref, requests
        self.adapters = (ref.shape[0] - 2 - requests) // 2
        self.place, self.shard = ref[0], ref[1]

    def adapter(self, r):
        return self.ref[2 + r]

    def rank(self, r):
        return self.ref[2 + self.requests + self.adapter(r)]

    def local_slot(self, r, held):
        return self.ref[2 + self.requests + self.adapters + self.adapter(r)] - self.shard * held


def base_kernel(order, groups, inputs_for, half, held, request_count, handed_on, *refs):
    slots = [slot for group in groups for slot in group]
    count = len(slots)
    meta, refs = Meta(refs[0], request_count), refs[1:]
    if held:
        requests_ref, factor, refs = refs[0], refs[1], refs[2:]
    hidden, matrix, refs = refs[0], refs[1], refs[2:]
    under, refs = (refs[0], refs[1:]) if handed_on else (None, refs)
    outs, refs = refs[: len(groups)], refs[len(groups) :]
    (rows, right, sums, sems), refs = refs[:4], refs[4:]
    steps, _, tile = rows.shape
    columns = outs[0].shape[1]
    block = rows.shape[1] // count
    first_rows = [pl.multiple_of(block_at(order, slot, meta.place) * block, block) for slot in slots]

    def depth_of(k):
        return pl.ds(pl.multiple_of(k * tile, tile), tile)

    def copies(k):
        moves = [
            (hidden.at[pl.ds(first_rows[i], block), depth_of(k)], rows.at[k, pl.ds(i * block, block), :])
            for i in range(count)
        ]
        moves.append((matrix.at[depth_of(k), pl.ds(half * columns, columns)], right.at[k]))
        return [pltpu.make_async_copy(a, b, sems.at[k, i]) for i, (a, b) in enumerate(moves)]

    if held:
        factors, inputs, flags, factor_sems = refs
        width = factor.shape[2]

        def factor_copies(k, pair):
            return [
                pltpu.make_async_copy(
                    factor.at[2 * pair + i, depth_of(k), :],
                    factors.at[pair, k, :, pl.ds(i * width, width)],
                    factor_sems.at[k, 2 * pair + i],
                )
                for i in range(2)
            ]

    def start(k):
        for copy in copies(k):
            copy.start()

    def start_factors(k, pairs):
        for pair, used in enumerate(pairs):

            @pl.when(used)
            def _(pair=pair):
                for copy in factor_copies(k, pair):
                    copy.start()

    for k in range(min(AHEAD, steps)):
        start(k)
    used = []
    if held:
        bounds = spans(requests_ref, request_count)
        local = [meta.local_slot(r, held) for r in range(request_count)]
        top = slots.index(inputs_for[0])
        wide = len(inputs_for)
        for pair in range(held // 2):
            used_by = []
            for first in first_rows[top : top + wide]:
                wanted = jnp.bool_(False)
                for r, slot in enumerate(local):
                    here = jnp.maximum(bounds[r], first) < jnp.minimum(bounds[r + 1], first + block)
                    wanted = wanted | (here & (slot // 2 == pair) & (slot >= 0))
                flags[pair * wide + len(used_by)] = wanted.astype(jnp.int32)
                used_by.append(wanted)
            used.append(functools.reduce(jnp.logical_or, used_by))
        for k in range(min(AHEAD, steps)):
            start_factors(k, used)
    sums[...] = jnp.zeros_like(sums)

    def step(k, _):
        @pl.when(k + AHEAD < steps)
        def _():
            start(k + AHEAD)
            start_factors(k + AHEAD, used)

        for copy in copies(k):
            copy.wait()
        sums[...] += jnp.dot(rows[k], right[k], preferred_element_type=jnp.float32)
        return 0

    lax.fori_loop(0, steps, step, 0)

    if held:
        for pair, wanted in enumerate(used):

            @pl.when(wanted)
            def _(pair=pair):
                for k in range(steps):
                    for copy in factor_copies(k, pair):
                        copy.wait()

        def pair_block(j, _):
            pair, i = j // wide, j % wide

            @pl.when(flags[j] == 1)
            def _():
                own = pl.ds(pl.multiple_of((top + i) * block, block), block)
                total = jnp.dot(rows[0, own, :], factors[pair, 0], preferred_element_type=jnp.float32)
                for k in range(1, steps):
                    total += jnp.dot(rows[k, own, :], factors[pair, k], preferred_element_type=jnp.float32)
                inputs[pair, pl.ds(pl.multiple_of(i * block, block), block), :] = total

            return 0

        lax.fori_loop(0, held // 2 * wide, pair_block, 0)

    i = 0
    for out, group in zip(outs, groups):
        here = 0
        for slot in group:
            out[here : here + block, :] = sums[i * block : (i + 1) * block, :].astype(jnp.bfloat16)
            here += block
            if held and slot in inputs_for:
                own = pl.ds((i - top) * block, block)
                row = lax.broadcasted_iota(jnp.int32, (block, width), 0) + first_rows[i]
                column = lax.broadcasted_iota(jnp.int32, (block, width), 1)
                total = jnp.zeros((block, width), jnp.float32)
                for r, local_slot in enumerate(local):
                    last = jnp.where((local_slot >= 0) & (local_slot < held), bounds[r + 1], 0)
                    keep = (row >= bounds[r]) & (row < last) & (column < meta.rank(r))
                    local_slot = jnp.clip(local_slot, 0, held - 1)
                    lanes = pl.ds(pl.multiple_of(local_slot % 2 * width, width), width)
                    total = jnp.where(keep, inputs[local_slot // 2, own, lanes], total)
                total = total.astype(jnp.bfloat16)
                size = block * width // columns
                for j in range(columns // width):
                    lanes = slice(j * width, (j + 1) * width)
                    out[here : here + size, lanes] = total[j * size : (j + 1) * size, :]
                here += size
            i += 1
    if handed_on:
        outs[0][outs[0].shape[0] - under.shape[0] :, :] = under[...]


def base_terms(meta, requests, request_count, hidden, matrix, factor, groups, inputs_for, half, n, under=None):
    tokens, depth = hidden.shape
    block, columns = tokens // n, matrix.shape[1] // 2
    tile = first_divisor(depth, (1024, 512, 256, 128))
    steps = depth // tile
    count = sum(len(group) for group in groups)
    smem = pl.BlockSpec(memory_space=pltpu.SMEM)
    vmem = pl.BlockSpec(memory_space=pltpu.VMEM)
    hbm = pl.BlockSpec(memory_space=pltpu.HBM)
    held, extra = 0, 0
    operands, in_specs = [meta], [smem]
    scratch = [
        pltpu.VMEM((steps, count * block, tile), jnp.bfloat16),
        pltpu.VMEM((steps, tile, columns), jnp.bfloat16),
        pltpu.VMEM((count * block, columns), jnp.float32),
        pltpu.SemaphoreType.DMA((steps, count + 1)),
    ]
    if inputs_for:
        held, _, width = factor.shape
        extra = block * width // columns
        operands, in_specs = [meta, requests, factor], [smem, vmem, hbm]
        scratch += [
            pltpu.VMEM((held // 2, steps, tile, 2 * width), jnp.bfloat16),
            pltpu.VMEM((held // 2, len(inputs_for) * block, 2 * width), jnp.float32),
            pltpu.SMEM((held // 2 * len(inputs_for),), jnp.int32),
            pltpu.SemaphoreType.DMA((steps, held)),
        ]
    heights = [sum(block + (extra if slot in inputs_for else 0) for slot in group) for group in groups]
    operands, in_specs = operands + [hidden, matrix], in_specs + [hbm, hbm]
    if under is not None:
        heights[0] += under.shape[0]
        operands, in_specs = operands + [under], in_specs + [vmem]
    handed_on = under is not None
    return pl.pallas_call(
        lambda *refs: base_kernel(line_order(n), groups, inputs_for, half, held, request_count, handed_on, *refs),
        out_shape=[jax.ShapeDtypeStruct((height, columns), jnp.bfloat16) for height in heights],
        in_specs=in_specs,
        out_specs=[vmem] * len(groups),
        scratch_shapes=scratch,
        compiler_params=params(50 if half or count > 1 else 58),
        cost_estimate=small_cost(),
        name="base_terms",
    )(*operands)


def select_rows_kernel(request_count, meta_ref, factor, kept, sent):
    meta = Meta(meta_ref, request_count)
    held, rank_rows, _ = factor.shape
    width = factor.shape[2] // (2 * PAIRS)
    side = meta.shard % 2
    for r in range(request_count):
        slot = meta.local_slot(r, held)
        owned = (slot >= 0) & (slot < held)
        slot = jnp.clip(slot, 0, held - 1)
        for out, core in ((kept, side), (sent, 1 - side)):
            for i in range(PAIRS):
                for c in range(2):
                    first = (2 * i + core) * width + c * (width // 2)
                    rows = factor[slot, :, pl.ds(pl.multiple_of(first, LANES), width // 2)]
                    top = (c * request_count + r) * rank_rows
                    out[i, top : top + rank_rows, :] = jnp.where(owned, rows, jnp.zeros_like(rows))


def select_rows(meta, request_count, factor):
    _, rank_rows, model_width = factor.shape
    smem = pl.BlockSpec(memory_space=pltpu.SMEM)
    vmem = pl.BlockSpec(memory_space=pltpu.VMEM)
    shape = (PAIRS, 2 * request_count * rank_rows, model_width // (4 * PAIRS))
    out = jax.ShapeDtypeStruct(shape, factor.dtype)
    return pl.pallas_call(
        lambda *refs: select_rows_kernel(request_count, *refs),
        out_shape=[out, out],
        in_specs=[smem, vmem],
        out_specs=[vmem, vmem],
        compiler_params=params(16),
        cost_estimate=small_cost(),
        name="select_rows",
    )(meta, factor)


def expanded_inputs(meta, requests_ref, lora_ref):
    block, width = lora_ref.shape
    row = lax.broadcasted_iota(jnp.int32, (block, width), 0) + meta.place * block
    lora = lora_ref[...].astype(jnp.float32)
    bounds = spans(requests_ref, meta.requests)
    parts = []
    for r in range(meta.requests):
        scale = 0.25 * width / meta.rank(r).astype(jnp.float32)
        keep = (row >= bounds[r]) & (row < bounds[r + 1])
        parts.append(jnp.where(keep, lora * scale, 0.0).astype(jnp.bfloat16))
    return jnp.concatenate(parts, axis=1)


def finish_kernel(items, added, requests, rank_rows, n, *refs):
    meta_ref, requests_ref, lora_ref, refs = refs[0], refs[1], refs[2], refs[3:]
    arrays, out, rows = refs[:-2], refs[-2], refs[-1]
    meta = Meta(meta_ref, requests)
    rank = n * rank_rows
    half = out.shape[1] // 2
    for index, top, targets in items:
        for place, k in targets:

            @pl.when(meta.place == place)
            def _(piece=arrays[index], top=top, k=k):
                for r in range(requests):
                    first = r * rank + k * rank_rows
                    for c in range(2):
                        start = top + (c * requests + r) * rank_rows
                        rows[first : first + rank_rows, c * half : (c + 1) * half] = piece[start : start + rank_rows, :]

    expanded = expanded_inputs(meta, requests_ref, lora_ref)
    block = lora_ref.shape[0]
    for c in range(2):
        columns = slice(c * half, (c + 1) * half)
        total = jnp.dot(expanded, rows[:, columns], preferred_element_type=jnp.float32)
        for index, top, which in added:
            if which == c:
                total += arrays[index][top : top + block, :].astype(jnp.float32)
        out[:, columns] = total.astype(out.dtype)


def finish(meta, requests, lora, arrays, items, added, request_count, rank_rows, n):
    smem = pl.BlockSpec(memory_space=pltpu.SMEM)
    vmem = pl.BlockSpec(memory_space=pltpu.VMEM)
    width = 2 * arrays[0].shape[1]
    return pl.pallas_call(
        lambda *refs: finish_kernel(items, added, request_count, rank_rows, n, *refs),
        out_shape=jax.ShapeDtypeStruct((lora.shape[0], width), jnp.bfloat16),
        in_specs=[smem] + [vmem] * (2 + len(arrays)),
        out_specs=vmem,
        scratch_shapes=[pltpu.VMEM((request_count * n * rank_rows, width), jnp.bfloat16)],
        compiler_params=params(20),
        cost_estimate=small_cost(),
        name="finish",
    )(meta, requests, lora, *arrays)


def join_kernel(count, term_top, came_top, under_top, term, came, *refs):
    out = refs[-1]
    total = term[term_top : term_top + count, :].astype(jnp.float32)
    total += came[came_top : came_top + count, :].astype(jnp.float32)
    out[:count, :] = total.astype(out.dtype)
    if len(refs) > 1:
        under = refs[0]
        out[count:, :] = under[under_top : under_top + out.shape[0] - count, :]


def join(token, count, term, term_top, came, came_top, under=None, under_top=0, under_count=0, weight=10**6):
    arrays = [term, came] + ([] if under is None else [under])
    arrays = lax.optimization_barrier((arrays, token))[0]
    vmem = pl.BlockSpec(memory_space=pltpu.VMEM)
    return pl.pallas_call(
        lambda *refs: join_kernel(count, term_top, came_top, under_top, *refs),
        out_shape=jax.ShapeDtypeStruct((count + under_count, term.shape[1]), term.dtype),
        in_specs=[vmem] * len(arrays),
        out_specs=vmem,
        compiler_params=params(12),
        cost_estimate=pl.CostEstimate(flops=weight, bytes_accessed=10**5, transcendentals=0),
        name="join",
    )(*arrays)


def add_last_kernel(total, *refs):
    arrivals, out = refs[:-1], refs[-1]
    half = arrivals[0].shape[1]
    out[:, :half] = total[:, :half]
    last = total[:, half:].astype(jnp.float32)
    for arrival in arrivals:
        last += arrival[...].astype(jnp.float32)
    out[:, half:] = last.astype(out.dtype)


def add_last(total, *arrivals):
    vmem = pl.BlockSpec(memory_space=pltpu.VMEM)
    return pl.pallas_call(
        add_last_kernel,
        out_shape=jax.ShapeDtypeStruct(total.shape, total.dtype),
        in_specs=[vmem] * (1 + len(arrivals)),
        out_specs=vmem,
        compiler_params=params(12),
        cost_estimate=small_cost(),
        name="add_last",
    )(total, *arrivals)


def under_each_other_kernel(upper, lower, out):
    out[: upper.shape[0], :] = upper[...]
    out[upper.shape[0] :, :] = lower[...]


def under_each_other(upper, lower):
    vmem = pl.BlockSpec(memory_space=pltpu.VMEM)
    return pl.pallas_call(
        under_each_other_kernel,
        out_shape=jax.ShapeDtypeStruct((upper.shape[0] + lower.shape[0], upper.shape[1]), upper.dtype),
        in_specs=[vmem] * 2,
        out_specs=vmem,
        compiler_params=params(12),
        cost_estimate=small_cost(),
        name="under_each_other",
    )(upper, lower)


def swap(x, axis, bit):
    return lax.ppermute(x, axis, [(i, i ^ bit) for i in range(lax.axis_size(axis))])


def bits_of(size):
    return [1 << i for i in range(size.bit_length() - 1)]


def along_edge(x, edge):
    n = lax.axis_size("tensor")
    return lax.ppermute(x, "tensor", [(edge, edge + 1), (n - 1 - edge, n - 2 - edge)])


def on_line(hidden, matrix, input_factor, output_factor, requests, token, request_count, n):
    shard = lax.axis_index("store")
    block = hidden.shape[0] // n
    width = input_factor.shape[2]
    rank_rows = output_factor.shape[1]
    piece = block + block * width // (matrix.shape[1] // 2)
    bundle = 2 * request_count * rank_rows

    def base(token, groups, inputs_for, half, under=None):
        return base_terms(
            token, requests, request_count, hidden, matrix, input_factor, groups, inputs_for, half, n, under
        )

    def send(x, edge, token):
        return along_edge(after(x, token), edge)

    (s00,) = base(token, [[0]], [0], 0)
    token = after(token, s00)
    e0_1 = along_edge(s00, 0)
    kept, sent = select_rows(token, request_count, output_factor)
    token = after(token, kept, sent)
    swapped = swap(sent, "store", 1)
    token = after(token, swapped)
    side = shard // 2 % 2
    kept, swapped, _ = lax.optimization_barrier((kept, swapped, token))
    outgoing = kept[1 - side] + swapped[1 - side]
    rows = kept[side] + swapped[side]
    token = after(token, outgoing, rows)
    across = swap(outgoing, "store", 2)
    s01, s11 = base(token, [[0], [1]], [], 1)

    token = after(token, s01)
    e0_2 = send(s01, 0, token)
    token, e0_1 = lax.optimization_barrier((token, e0_1))
    b10 = join(token, piece, s00, 0, e0_1, 0)
    token = after(token, b10)
    e1_2 = along_edge(b10, 1)
    token, across = lax.optimization_barrier((token, across))
    rows = rows + across
    token = after(token, rows)
    near = lax.ppermute(rows, "tensor", [(0, 1), (n - 1, n - 2), (1, 0), (n - 2, n - 1)])
    far = along_edge(rows, 1)
    s10_s11, s20, s30 = base(token, [[1], [2], [3]], [1, 2], 0, s11)

    token = after(token, s10_s11)
    e0_3 = send(s10_s11, 0, token)
    token, e0_2 = lax.optimization_barrier((token, e0_2))
    b11 = join(token, block, s01, 0, e0_2, 0, weight=HEAVY)
    token, near = lax.optimization_barrier((after(token, b11), near))
    e1_3 = along_edge(under_each_other(b11, near), 1)
    token, e1_2, far = lax.optimization_barrier((token, e1_2, far))
    c20 = join(token, piece, s20, 0, e1_2, 0, far, 0, bundle)
    token = after(token, c20)
    e2_3 = along_edge(c20, 2)
    s21, s31 = base(token, [[2], [3]], [3], 1)

    token = after(token, s21)
    e0_4 = send(s20, 0, token)
    token, e0_3 = lax.optimization_barrier((token, e0_3))
    b20 = join(token, piece, s10_s11, 0, e0_3, 0)
    token = after(token, b20)
    e1_4 = along_edge(b20, 1)
    token, e1_3 = lax.optimization_barrier((token, e1_3))
    last_rows = send(e1_3[block:], 2, token)
    token, e2_3 = lax.optimization_barrier((token, e2_3))
    c21 = join(token, block, s21, 0, e1_3, 0, weight=HEAVY // 5)
    token = after(token, c21)
    e2_4 = along_edge(c21, 2)
    e0_5 = send(s21, 0, token)
    b21 = join(token, block, s10_s11, piece, e0_3, piece)
    token = after(token, b21)
    e1_5 = along_edge(b21, 1)

    token, e0_4 = lax.optimization_barrier((token, e0_4))
    token, e1_4 = lax.optimization_barrier((token, e1_4))
    e1_4 = after(e1_4, token)
    lora = s31[block:].astype(jnp.float32) + e0_4[block:].astype(jnp.float32)
    lora += e1_4[block:].astype(jnp.float32) + e2_3[block:piece].astype(jnp.float32)
    lora = lora.astype(jnp.bfloat16).reshape(piece - block, -1, width).swapaxes(0, 1).reshape(block, width)
    lora = lora + swap(lora, "store", 1)
    lora = lora + swap(lora, "store", 2)
    arrays = [s30, s31, rows, near, far, e1_3, e2_3, last_rows, e0_4, e1_4]
    items = [
        (2, 0, [(z, z) for z in range(n)]),
        (3, 0, [(0, 1), (1, 0), (2, 3), (3, 2)]),
        (4, 0, [(1, 2), (2, 1)]),
        (5, block, [(1, 3), (2, 0)]),
        (6, piece, [(0, 2), (3, 1)]),
        (7, 0, [(0, 3), (3, 0)]),
    ]
    added = [(0, 0, 0), (8, 0, 0), (9, 0, 0), (6, 0, 0), (1, 0, 1)]
    out = finish(token, requests, lora, arrays, items, added, request_count, rank_rows, n)
    return add_last(out, e0_5, e1_5, e2_4)


def anywhere(hidden, matrix, input_factor, output_factor, token_requests, meta):
    request_adapters, ranks, slots = meta
    held = input_factor.shape[0]
    width = input_factor.shape[2]
    rank, slot = ranks[request_adapters], slots[request_adapters]
    owned = slot // held == lax.axis_index("store")
    chosen = token_requests[:, None] == jnp.arange(request_adapters.shape[0])[None, :]
    lora = jnp.zeros((hidden.shape[0], width), jnp.float32)
    for r in range(request_adapters.shape[0]):
        product = jnp.dot(hidden, input_factor[slot[r] % held], preferred_element_type=jnp.float32)
        keep = (chosen[:, r] & owned[r])[:, None] & (jnp.arange(width) < rank[r])[None, :]
        lora = jnp.where(keep, product, lora)
    lora = lax.psum_scatter(lora.astype(jnp.bfloat16), "tensor", scatter_dimension=1, tiled=True)
    lora = lax.psum(lora, "store").astype(jnp.float32)
    rows = jnp.where(owned[:, None, None], output_factor[slot % held], jnp.zeros((), output_factor.dtype))
    rows = lax.psum_scatter(rows, "store", scatter_dimension=2, tiled=True)
    weights = jnp.where(chosen, 0.25 * width / rank.astype(jnp.float32)[None, :], 0.0)
    expanded = (weights[:, :, None] * lora[:, None, :]).reshape(hidden.shape[0], -1).astype(jnp.bfloat16)
    term = jnp.dot(hidden, matrix, preferred_element_type=jnp.float32)
    term += jnp.dot(expanded, rows.reshape(-1, rows.shape[2]), preferred_element_type=jnp.float32)
    return lax.psum_scatter(term.astype(jnp.bfloat16), "tensor", scatter_dimension=0, tiled=True)


def per_device(
    hidden_activations,
    down_matrix,
    adapter_input_factor,
    adapter_output_factor,
    token_requests,
    request_adapters,
    adapter_ranks,
    adapter_store_slot,
):
    n = lax.axis_size("tensor")
    meta = (request_adapters, adapter_ranks, adapter_store_slot)
    arrays = (hidden_activations, down_matrix, adapter_input_factor, adapter_output_factor)
    if n == LINE and lax.axis_size("store") == 2 * PAIRS and adapter_input_factor.shape[0] % 2 == 0:
        place = jnp.stack([lax.axis_index("tensor"), lax.axis_index("store")]).astype(jnp.int32)
        token = jnp.concatenate([place, *meta])
        return on_line(*arrays, token_requests.reshape(-1, LANES), token, request_adapters.shape[0], n)
    return anywhere(*arrays, token_requests, meta)


def solution(mesh):
    in_specs = (
        P("groups", "tensor"),
        P("tensor", "store"),
        P(("groups", "store"), "tensor", None),
        P(("groups", "store"), "tensor", None),
        P("groups"),
        P("groups"),
        P("groups"),
        P("groups"),
    )
    out_specs = P(("groups", "tensor"), "store")
    return jax.shard_map(
        per_device, mesh=mesh, in_specs=in_specs, out_specs=out_specs, check_vma=False
    )
```
